32 devices in a mesh: seq: 4 (over z), fsdp: 8 (over y, x, core).
Axes of the slice: x: 2, y: 2, z: 4, core: 2. Of those that a mesh axis runs over, the one named last changes fastest.
Arguments:
- inputs: bfloat16 [2, 8192, 1024], P(None, ('seq', 'fsdp')), may hold values from -6 to 6
- cotangent: bfloat16 [2, 8192, 1024], P(None, ('seq', 'fsdp')), may hold values from -6 to 6
- segment_ids: int32 [2, 8192], replicated, may hold values from 0 to 3, as said below
- norm1_gain: bfloat16 [1024], P('fsdp'), may hold values from 0.099609375 to 1.8984375
- norm1_bias: bfloat16 [1024], P('fsdp'), may hold values from -3 to 3
- qkv_weight: bfloat16 [1024, 3072], P(None, 'fsdp'), may hold values from -0.1875 to 0.1875
- qv_bias: bfloat16 [16, 128], P('fsdp'), may hold values from -3 to 3
- out_weight: bfloat16 [1024, 1024], P('fsdp'), may hold values from -1.5 to 1.5
- out_bias: bfloat16 [1024], P('fsdp'), may hold values from -3 to 3
- norm2_gain: bfloat16 [1024], P('fsdp'), may hold values from 0.099609375 to 1.8984375
- norm2_bias: bfloat16 [1024], P('fsdp'), may hold values from -3 to 3
- fc_weight: bfloat16 [1024, 4096], P(None, 'fsdp'), may hold values from -0.1875 to 0.1875
- fc_bias: bfloat16 [4096], P('fsdp'), may hold values from -3 to 3
- proj_weight: bfloat16 [4096, 1024], P('fsdp'), may hold values from -0.09375 to 0.09375
- proj_bias: bfloat16 [1024], P('fsdp'), may hold values from -3 to 3
Outputs:
- layer_output: bfloat16 [2, 8192, 1024], P(None, ('seq', 'fsdp'))
- input_grad: bfloat16 [2, 8192, 1024], P(None, ('seq', 'fsdp'))
- norm1_gain_grad: float32 [1024], P('fsdp')
- norm1_bias_grad: float32 [1024], P('fsdp')
- qkv_weight_grad: float32 [1024, 3072], P(None, 'fsdp')
- qv_bias_grad: float32 [16, 128], P('fsdp')
- out_weight_grad: float32 [1024, 1024], P('fsdp')
- out_bias_grad: float32 [1024], P('fsdp')
- norm2_gain_grad: float32 [1024], P('fsdp')
- norm2_bias_grad: float32 [1024], P('fsdp')
- fc_weight_grad: float32 [1024, 4096], P(None, 'fsdp')
- fc_bias_grad: float32 [4096], P('fsdp')
- proj_weight_grad: float32 [4096, 1024], P('fsdp')
- proj_bias_grad: float32 [1024], P('fsdp')
The draws below stay inside these ranges and needn't reach their ends.
Inputs may be any that keep to these rules, and one draw needn't show every extreme that they name: `segment_ids`: along each sequence the ids start at 0 and never fall, rising by at most one from a token to the next. In every draw one sequence, chosen by the seed, is a single document; every other sequence holds exactly 4 documents.
All inputs are finite; a program needn't handle non-finite values.
Results may differ from the reference program's by a relative error of at most 0.012.
The reference program's roundings to bfloat16 on the way count: a program that leaves them out, or rounds other values in their place, can miss the bound.
Values may be sent and summed in bfloat16 or wider, within the bound.
A program may use at most 256 MiB of HBM per device.

```python
import functools
import math
import jax
import jax.numpy as jnp
from jax import lax

D = 1024
H = 16
HD = 64
FF = 4096
WINDOW = 1024
SEQS = 2
LEN = 8192
QBLOCK = 512


def draw_segment_ids(key, part):
    key = jax.random.fold_in(key, 11)
    mark_key, pick_key = jax.random.split(key)
    doc_count = LEN // (2 * WINDOW)
    seq_keys = jax.random.split(mark_key, SEQS)

    def boundary_marks(row_key):
        shuffled = jax.random.permutation(row_key, LEN - 1).astype(jnp.int32) + 1
        starts = shuffled[:doc_count - 1]
        return jnp.zeros((LEN,), jnp.int32).at[starts].add(1)
    marks = jax.vmap(boundary_marks)(seq_keys)
    chosen = jax.random.randint(pick_key, (), 0, SEQS)
    lanes = jnp.arange(SEQS, dtype=jnp.int32)[:, None]
    marks = jnp.where(lanes == chosen, 0, marks)
    return jnp.cumsum(marks, axis=1).astype(jnp.int32)


def shard_levels(rng, shape, pieces, low, high):
    level = 1.0
    for position, parts in pieces:
        steps = jax.random.uniform(jax.random.fold_in(jax.random.fold_in(rng, 6), position), (parts,), jnp.float32, low / len(pieces), high / len(pieces))
        level = level * jnp.repeat(jnp.exp(steps), shape[position] // parts).reshape((-1,) + (1,) * (len(shape) - 1 - position))
    return level


def noise(key, extent, deviation, most, shards=(), kind=jnp.bfloat16):
    values = jax.random.normal(key, extent, jnp.float32) * deviation
    if len(shards) > 0:
        values = shard_levels(key, extent, shards, -0.22, 0.18) * values
    return jnp.clip(values, min=-most, max=most).astype(kind)


def setup_inputs(seed: int = 0) -> dict:
    splits = jax.random.split(jax.random.key(seed), 16)
    return {
        "inputs": noise(splits[0], (SEQS, LEN, D), 1.0, 6.0, ((1, 32),)),
        "cotangent": noise(splits[1], (SEQS, LEN, D), 1.0, 6.0, ((1, 32),)),
        "segment_ids": draw_segment_ids(jax.random.fold_in(splits[15], 71), 0),
        "norm1_gain": jnp.clip(1.0 + 0.18 * jax.random.normal(splits[3], (D,), jnp.float32), 0.099609375, 1.8984375).astype(jnp.bfloat16),
        "norm1_bias": noise(splits[4], (D,), 0.5, 3.0, ((0, 8),)),
        "qkv_weight": noise(splits[5], (D, 3 * D), D ** -0.5, 0.1875, ((1, 8),)),
        "qv_bias": noise(splits[6], (H, 2 * HD), 0.5, 3.0, ((0, 8),)),
        "out_weight": noise(splits[7], (D, D), (D // 64) ** -0.5, 1.5, ((0, 8),)),
        "out_bias": noise(splits[8], (D,), 0.5, 3.0, ((0, 8),)),
        "norm2_gain": jnp.clip(1.0 + 0.18 * jax.random.normal(splits[9], (D,), jnp.float32), 0.099609375, 1.8984375).astype(jnp.bfloat16),
        "norm2_bias": noise(splits[10], (D,), 0.5, 3.0, ((0, 8),)),
        "fc_weight": noise(splits[11], (D, FF), D ** -0.5, 0.1875, ((1, 8),)),
        "fc_bias": noise(splits[12], (FF,), 0.5, 3.0, ((0, 8),)),
        "proj_weight": noise(splits[13], (FF, D), FF ** -0.5, 0.09375, ((0, 8),)),
        "proj_bias": noise(splits[14], (D,), 0.5, 3.0, ((0, 8),)),
    }


@jax.custom_vjp
def low(v):
    return lax.optimization_barrier(v.astype(jnp.bfloat16)).astype(jnp.float32)

@jax.custom_vjp
def low_back(v):
    return v

def low_keep(v):
    return (low(v), None)

def low_pass(kept, grad):
    return (grad,)

def back_keep(v):
    return (v, None)

def back_low(kept, grad):
    return (low(grad),)
low.defvjp(low_keep, low_pass)
low_back.defvjp(back_keep, back_low)
precise = lax.Precision.HIGHEST
norm_eps = 1e-05
neg_fill = -1e+30

def layer_norm(values, gain, offset):
    centre = values - lax.optimization_barrier(jnp.mean(values, axis=-1, keepdims=True))
    spread = lax.optimization_barrier(jnp.mean(centre * centre, axis=-1, keepdims=True))
    return centre * lax.rsqrt(spread + norm_eps) * gain + offset

def full_bias(bias_rows):
    head_size = bias_rows.shape[1] // 2
    query_part = bias_rows[:, :head_size]
    stacked = jnp.stack([query_part, jnp.zeros_like(query_part), bias_rows[:, head_size:]], axis=1)
    return stacked.reshape(-1)

def window_attention(queries, key_rows, value_rows, seg_rows):
    length = queries.shape[1]
    key_pad = jnp.pad(key_rows, ((0, 0), (WINDOW, 0), (0, 0)))
    value_pad = jnp.pad(value_rows, ((0, 0), (WINDOW, 0), (0, 0)))
    id_pad = jnp.concatenate([jnp.full((WINDOW,), -1, jnp.int32), seg_rows.astype(jnp.int32)])
    row_pos = lax.broadcasted_iota(jnp.int32, (QBLOCK, WINDOW + QBLOCK), 0)
    col_pos = lax.broadcasted_iota(jnp.int32, (QBLOCK, WINDOW + QBLOCK), 1)
    in_window = (col_pos > row_pos) & (col_pos <= row_pos + WINDOW)
    score_scale = 1.0 / math.sqrt(HD)

    def window_block(block_start):
        query_block = lax.dynamic_slice_in_dim(queries, block_start, QBLOCK, 1)
        key_block = lax.dynamic_slice_in_dim(key_pad, block_start, WINDOW + QBLOCK, 1)
        value_block = lax.dynamic_slice_in_dim(value_pad, block_start, WINDOW + QBLOCK, 1)
        query_ids = lax.dynamic_slice_in_dim(seg_rows.astype(jnp.int32), block_start, QBLOCK, 0)
        key_ids = lax.dynamic_slice_in_dim(id_pad, block_start, WINDOW + QBLOCK, 0)
        allowed = in_window & (query_ids[:, None] == key_ids[None, :])
        scores = low_back(jnp.einsum('hqd,hkd->hqk', query_block, key_block, precision=precise) * score_scale)
        scores = jnp.where(allowed[None], scores, neg_fill)
        row_peak = lax.optimization_barrier(jnp.max(scores, axis=-1, keepdims=True))
        exponent = jnp.exp(scores - row_peak)
        weights_low = low(exponent / lax.optimization_barrier(jnp.sum(exponent, axis=-1, keepdims=True)))
        return jnp.einsum('hqk,hkd->hqd', weights_low, value_block, precision=precise)
    block_starts = jnp.arange(length // QBLOCK, dtype=jnp.int32) * QBLOCK
    blocks = lax.map(jax.checkpoint(window_block), block_starts)
    return jnp.transpose(blocks, (1, 0, 2, 3)).reshape(queries.shape[0], length, HD)

def block_layer(tokens_in, norm1_gain, norm1_bias, qkv_weight, qv_bias, out_weight, out_bias, norm2_gain, norm2_bias, fc_weight, fc_bias, proj_weight, proj_bias, seg_rows):
    length = tokens_in.shape[0]
    normed = low(layer_norm(tokens_in, norm1_gain, norm1_bias))
    projected = jnp.dot(normed, qkv_weight, precision=precise, preferred_element_type=jnp.float32) + full_bias(qv_bias)
    projected = low(low_back(projected)).reshape(length, H, 3, HD)
    queries = jnp.transpose(projected[:, :, 0], (1, 0, 2))
    key_rows = jnp.transpose(projected[:, :, 1], (1, 0, 2))
    value_rows = jnp.transpose(projected[:, :, 2], (1, 0, 2))
    head_out = window_attention(queries, key_rows, value_rows, seg_rows)
    merged = low(low_back(jnp.transpose(head_out, (1, 0, 2)).reshape(length, D)))
    attn_out = low_back(jnp.dot(merged, out_weight, precision=precise, preferred_element_type=jnp.float32) + out_bias)
    residual = tokens_in + attn_out
    normed2 = low(layer_norm(residual, norm2_gain, norm2_bias))
    hidden = low_back(jnp.dot(normed2, fc_weight, precision=precise, preferred_element_type=jnp.float32) + fc_bias)
    active = low(jax.nn.gelu(hidden, approximate=True))
    outcome = low_back(jnp.dot(active, proj_weight, precision=precise, preferred_element_type=jnp.float32) + proj_bias)
    return residual + outcome

def reference(inputs, cotangent, segment_ids, norm1_gain, norm1_bias, qkv_weight, qv_bias, out_weight, out_bias, norm2_gain, norm2_bias, fc_weight, fc_bias, proj_weight, proj_bias):
    weights = (norm1_gain.astype(jnp.float32), norm1_bias.astype(jnp.float32), qkv_weight.astype(jnp.float32), qv_bias.astype(jnp.float32), out_weight.astype(jnp.float32), out_bias.astype(jnp.float32), norm2_gain.astype(jnp.float32), norm2_bias.astype(jnp.float32), fc_weight.astype(jnp.float32), fc_bias.astype(jnp.float32), proj_weight.astype(jnp.float32), proj_bias.astype(jnp.float32))

    def per_sequence(running, scan_entry):
        tokens_in, grad_in, seg_rows = scan_entry
        outcome, pullback = jax.vjp(functools.partial(block_layer, seg_rows=seg_rows), tokens_in.astype(jnp.float32), *weights)
        gradients = pullback(grad_in.astype(jnp.float32))
        running = tuple((earlier + update for earlier, update in zip(running, gradients[1:])))
        return (running, (outcome.astype(jnp.bfloat16), gradients[0].astype(jnp.bfloat16)))
    zero_grads = tuple((jnp.zeros_like(weight) for weight in weights))
    totals, (layer_output, input_grad) = lax.scan(per_sequence, zero_grads, (inputs, cotangent, segment_ids))
    return (layer_output, input_grad, totals[0], totals[1], totals[2], totals[3], totals[4], totals[5], totals[6], totals[7], totals[8], totals[9], totals[10], totals[11])
```

```python
import functools
import jax, jax.numpy as jnp
from jax import lax
from jax.experimental import pallas as pl
from jax.experimental.pallas import tpu as pltpu
from jax.sharding import PartitionSpec as P

HD = 64
WINDOW = 1024
BLK = 256
PENALTY = 1e30


def nt(a, b):
    return lax.dot_general(a, b, (((1,), (1,)), ((), ())), preferred_element_type=jnp.float32)


def nn(a, b):
    return lax.dot_general(a, b, (((1,), (0,)), ((), ())), preferred_element_type=jnp.float32)


def tn(a, b):
    return lax.dot_general(a, b, (((0,), (0,)), ((), ())), preferred_element_type=jnp.float32)


def split3(v):
    hi = v.astype(jnp.bfloat16).astype(jnp.float32)
    rest = v - hi
    mid = rest.astype(jnp.bfloat16).astype(jnp.float32)
    return hi, mid, rest - mid


def merge_edges(mask, tiles):
    return [jnp.where(mask, tiles[0], tiles[-1])] + tiles[1:-1]


def spread_edges(mask, tiles):
    zero = jnp.zeros_like(tiles[0])
    return [jnp.where(mask, tiles[0], zero)] + tiles[1:] + [jnp.where(mask, zero, tiles[0])]


def edge_mask():
    rows = lax.broadcasted_iota(jnp.int32, (BLK, BLK), 0)
    cols = lax.broadcasted_iota(jnp.int32, (BLK, BLK), 1)
    return rows > cols


def fill_keys(heads, qkv_ref, halo_ref, augk_ref, keys, values):
    halo_rows = halo_ref.shape[1]
    rows = qkv_ref.shape[1]
    ones = jnp.ones((1, HD), jnp.bfloat16)
    for h in range(heads):
        c = h * 2 * HD
        for source, base, size in ((halo_ref, 0, halo_rows), (qkv_ref, halo_rows, rows)):
            pair = source[0, :, c : c + 2 * HD]
            keys[h, base : base + size, :] = jnp.concatenate(
                [pair[:, :HD], augk_ref[0, base : base + size, :]], axis=1
            )
            values[h, base : base + size, :] = jnp.concatenate(
                [pair[:, HD:], jnp.broadcast_to(ones, (size, HD))], axis=1
            )


def attend_kernel(heads, qkv_ref, halo_ref, augk_ref, augq_ref, out_ref, q2_ref, keys, values, values_t):
    step = pl.program_id(1)
    nkeys = keys.shape[1]

    @pl.when(step == 0)
    def _():
        fill_keys(heads, qkv_ref, halo_ref, augk_ref, keys, values)
        for h in range(heads):
            for b in range(nkeys // BLK):
                values_t[h, :, b * BLK : (b + 1) * BLK] = values[h, b * BLK : (b + 1) * BLK, :].T

    mask = edge_mask()
    tiles = WINDOW // BLK + 1
    start = pl.multiple_of(step * BLK, BLK)
    lane = lax.broadcasted_iota(jnp.int32, (BLK, 2 * HD), 1)
    lse_lane = augq_ref.shape[2] + HD - 3
    for h in range(heads):
        qc = heads * 2 * HD + h * HD
        q = jnp.concatenate([qkv_ref[0, pl.ds(start, BLK), qc : qc + HD] * 0.125, augq_ref[0]], axis=1)
        scores = [nt(keys[h, pl.ds(start + b * BLK, BLK), :], q) for b in range(tiles)]
        scores = merge_edges(mask, scores)
        peak = functools.reduce(jnp.maximum, scores)
        peak = jnp.max(peak, axis=0, keepdims=True)
        weights = spread_edges(mask, [jnp.exp(s - peak).astype(jnp.bfloat16) for s in scores])
        total = sum(
            nn(values_t[h, :, pl.ds(pl.multiple_of(start + b * BLK, BLK), BLK)], w) for b, w in enumerate(weights)
        )
        sub = lax.broadcasted_iota(jnp.int32, total.shape, 0)
        total = jnp.where(sub == HD + 1, peak, total).T
        norm = total[:, HD : HD + 1]
        out_ref[0, :, h * HD : (h + 1) * HD] = (total[:, :HD] / norm).astype(out_ref.dtype)
        lse = total[:, HD + 1 : HD + 2] + jnp.log(norm)
        hi, mid, low = split3(-lse)
        q2 = q.astype(jnp.float32)
        q2 = jnp.where(lane == lse_lane, hi, q2)
        q2 = jnp.where(lane == lse_lane + 1, mid, q2)
        q2 = jnp.where(lane == lse_lane + 2, low, q2)
        q2_ref[0, h] = q2.astype(jnp.bfloat16)


def attend(qkv, halo, augk, augq, heads):
    seqs, rows, cols = qkv.shape
    ext = augk.shape[1]
    return pl.pallas_call(
        functools.partial(attend_kernel, heads),
        grid=(seqs, rows // BLK),
        in_specs=[
            pl.BlockSpec((1, rows, cols), lambda s, i: (s, 0, 0)),
            pl.BlockSpec((1, WINDOW, heads * 2 * HD), lambda s, i: (s, 0, 0)),
            pl.BlockSpec((1, ext, HD), lambda s, i: (s, 0, 0)),
            pl.BlockSpec((1, BLK, HD), lambda s, i: (s, i, 0)),
        ],
        out_specs=[
            pl.BlockSpec((1, BLK, heads * HD), lambda s, i: (s, i, 0)),
            pl.BlockSpec((1, heads, BLK, 2 * HD), lambda s, i: (s, 0, i, 0)),
        ],
        out_shape=[
            jax.ShapeDtypeStruct((seqs, rows, heads * HD), jnp.bfloat16),
            jax.ShapeDtypeStruct((seqs, heads, rows, 2 * HD), jnp.bfloat16),
        ],
        scratch_shapes=[
            pltpu.VMEM((heads, ext, 2 * HD), jnp.bfloat16),
            pltpu.VMEM((heads, ext, 2 * HD), jnp.bfloat16),
            pltpu.VMEM((heads, 2 * HD, ext), jnp.bfloat16),
        ],
        compiler_params=pltpu.CompilerParams(vmem_limit_bytes=48 * 2**20),
        name="attend",
    )(qkv, halo, augk, augq)


def attend_back_kernel(
    heads, qkv_ref, halo_ref, augk_ref, q2_ref, out_ref, grad_ref, dq_ref, dkv_ref, dhalo_ref,
    keys, values, keys_t, dkeys, dvalues,
):
    step = pl.program_id(1)
    nkeys = keys.shape[1]

    @pl.when(step == 0)
    def _():
        fill_keys(heads, qkv_ref, halo_ref, augk_ref, keys, values)
        for h in range(heads):
            for b in range(nkeys // BLK):
                keys_t[h, :, b * BLK : (b + 1) * BLK] = keys[h, b * BLK : (b + 1) * BLK, :].T
        dkeys[...] = jnp.zeros_like(dkeys)
        dvalues[...] = jnp.zeros_like(dvalues)

    mask = edge_mask()
    tiles = WINDOW // BLK + 1
    start = pl.multiple_of(step * BLK, BLK)
    lane = lax.broadcasted_iota(jnp.int32, (BLK, 2 * HD), 1)
    for h in range(heads):
        q = q2_ref[0, h]
        g = grad_ref[0, :, h * HD : (h + 1) * HD]
        g32 = g.astype(jnp.float32)
        centre = jnp.sum(g32 * out_ref[0, :, h * HD : (h + 1) * HD].astype(jnp.float32), axis=1, keepdims=True)
        hi, mid, low = split3(-centre)
        g2 = jnp.concatenate([g32, jnp.zeros((BLK, HD), jnp.float32)], axis=1)
        g2 = jnp.where(lane == HD, hi, g2)
        g2 = jnp.where(lane == HD + 1, mid, g2)
        g2 = jnp.where(lane == HD + 2, low, g2).astype(jnp.bfloat16)
        spans = [pl.ds(pl.multiple_of(start + b * BLK, BLK), BLK) for b in range(tiles)]
        scores = merge_edges(mask, [nt(keys[h, s, :], q) for s in spans])
        wgrads = merge_edges(mask, [nt(values[h, s, :], g2) for s in spans])
        weights = [jnp.exp(s) for s in scores]
        sgrads = spread_edges(mask, [(w * d).astype(jnp.bfloat16) for w, d in zip(weights, wgrads)])
        weights = spread_edges(mask, [w.astype(jnp.bfloat16) for w in weights])
        for s, w, d in zip(spans, weights, sgrads):
            dvalues[h, s, :] += nn(w, g2)
            dkeys[h, s, :] += nn(d, q)
        dq = sum(nn(keys_t[h, :, s], d) for s, d in zip(spans, sgrads))
        dq_ref[0, :, h * HD : (h + 1) * HD] = (dq.T[:, :HD] * 0.125).astype(dq_ref.dtype)

    @pl.when(step == pl.num_programs(1) - 1)
    def _():
        for h in range(heads):
            c = h * 2 * HD
            dhalo_ref[0, :, c : c + 2 * HD] = jnp.concatenate(
                [dkeys[h, :WINDOW, :HD], dvalues[h, :WINDOW, :HD]], axis=1
            ).astype(dhalo_ref.dtype)
            dkv_ref[0, :, c : c + 2 * HD] = jnp.concatenate(
                [dkeys[h, WINDOW:, :HD], dvalues[h, WINDOW:, :HD]], axis=1
            ).astype(dkv_ref.dtype)


def attend_back(qkv, halo, augk, q2, out, grad, heads):
    seqs, rows, cols = qkv.shape
    ext = augk.shape[1]
    return pl.pallas_call(
        functools.partial(attend_back_kernel, heads),
        grid=(seqs, rows // BLK),
        in_specs=[
            pl.BlockSpec((1, rows, cols), lambda s, i: (s, 0, 0)),
            pl.BlockSpec((1, WINDOW, heads * 2 * HD), lambda s, i: (s, 0, 0)),
            pl.BlockSpec((1, ext, HD), lambda s, i: (s, 0, 0)),
            pl.BlockSpec((1, heads, BLK, 2 * HD), lambda s, i: (s, 0, i, 0)),
            pl.BlockSpec((1, BLK, heads * HD), lambda s, i: (s, i, 0)),
            pl.BlockSpec((1, BLK, heads * HD), lambda s, i: (s, i, 0)),
        ],
        out_specs=[
            pl.BlockSpec((1, BLK, heads * HD), lambda s, i: (s, i, 0)),
            pl.BlockSpec((1, rows, heads * 2 * HD), lambda s, i: (s, 0, 0)),
            pl.BlockSpec((1, WINDOW, heads * 2 * HD), lambda s, i: (s, 0, 0)),
        ],
        out_shape=[
            jax.ShapeDtypeStruct((seqs, rows, heads * HD), jnp.bfloat16),
            jax.ShapeDtypeStruct((seqs, rows, heads * 2 * HD), jnp.float32),
            jax.ShapeDtypeStruct((seqs, WINDOW, heads * 2 * HD), jnp.bfloat16),
        ],
        scratch_shapes=[
            pltpu.VMEM((heads, ext, 2 * HD), jnp.bfloat16),
            pltpu.VMEM((heads, ext, 2 * HD), jnp.bfloat16),
            pltpu.VMEM((heads, 2 * HD, ext), jnp.bfloat16),
            pltpu.VMEM((heads, ext, 2 * HD), jnp.float32),
            pltpu.VMEM((heads, ext, 2 * HD), jnp.float32),
        ],
        compiler_params=pltpu.CompilerParams(vmem_limit_bytes=56 * 2**20),
        name="attend_back",
    )(qkv, halo, augk, q2, out, grad)


def mask_features(segment_ext, docs):
    doc = jnp.arange(docs, dtype=jnp.int32)
    hot = (segment_ext[..., None] == doc).astype(jnp.bfloat16)
    outside = (segment_ext < 0).astype(jnp.bfloat16)[..., None]
    pad = HD - docs - 4
    one = jnp.ones(segment_ext.shape + (3,), jnp.bfloat16)
    zero = jnp.zeros(segment_ext.shape + (pad,), jnp.bfloat16)
    keys = jnp.concatenate([-hot, -outside, zero, one], axis=-1)
    own = hot[:, WINDOW:]
    queries = jnp.concatenate(
        [
            (1 - own) * jnp.bfloat16(PENALTY),
            jnp.full(own.shape[:2] + (1,), PENALTY, jnp.bfloat16),
            jnp.zeros(own.shape[:2] + (pad + 3,), jnp.bfloat16),
        ],
        axis=-1,
    )
    return keys, queries


norm_eps = 1e-05


def standardize(values):
    centre = values - jnp.mean(values, axis=-1, keepdims=True)
    spread = jnp.mean(centre * centre, axis=-1, keepdims=True)
    rate = lax.rsqrt(spread + norm_eps)
    return centre * rate, rate


def norm_grad(direction, z, rate):
    mean_d = jnp.mean(direction, axis=-1, keepdims=True)
    mean_dz = jnp.mean(direction * z, axis=-1, keepdims=True)
    return rate * (direction - mean_d - z * mean_dz)


def from_behind(block, axis, distance):
    devices = range(lax.axis_size(axis))
    route = [(i - distance, i) for i in devices if i - distance in devices]
    return lax.ppermute(block, axis, route)


def pack_columns(array, heads):
    parts = array.reshape(array.shape[:-1] + (heads, 3 * HD))
    lead = array.shape[:-1]
    return jnp.concatenate(
        [parts[..., HD:].reshape(lead + (-1,)), parts[..., :HD].reshape(lead + (-1,))], axis=-1
    )


def unpack_columns(array, heads):
    lead = array.shape[:-1]
    pairs = array[..., : heads * 2 * HD].reshape(lead + (heads, 2 * HD))
    queries = array[..., heads * 2 * HD :].reshape(lead + (heads, HD))
    return jnp.concatenate([queries, pairs], axis=-1).reshape(lead + (-1,))


def dot(subscripts, a, b):
    return jnp.einsum(subscripts, a, b, preferred_element_type=jnp.float32)


def body(
    inputs, cotangent, segment_ids, norm1_gain, norm1_bias, qkv_weight, qv_bias, out_weight, out_bias,
    norm2_gain, norm2_bias, fc_weight, fc_bias, proj_weight, proj_bias,
):
    group = lax.axis_size("fsdp")
    seqs, local_rows, width = inputs.shape
    part_rows = local_rows * group
    heads = qkv_weight.shape[1] // (3 * HD)
    docs = segment_ids.shape[1] // (2 * WINDOW)
    seq_index = lax.axis_index("seq")
    shard = norm1_gain.shape[0]

    small = jnp.concatenate([norm1_gain, norm1_bias, out_bias, norm2_gain, norm2_bias, proj_bias, fc_bias])
    small = lax.all_gather(small, "fsdp")
    gain1, offset1, out_off, gain2, offset2, proj_off = (
        small[:, i * shard : (i + 1) * shard].reshape(-1).astype(jnp.float32) for i in range(6)
    )
    fc_off = small[:, 6 * shard :].reshape(-1).astype(jnp.float32)
    out_all = lax.all_gather(out_weight, "fsdp", axis=0, tiled=True)
    fc_all = lax.all_gather(fc_weight, "fsdp")
    proj_all = lax.all_gather(proj_weight, "fsdp")

    padded_ids = jnp.concatenate([jnp.full((seqs, WINDOW), -1, jnp.int32), segment_ids], axis=1)
    segment_ext = lax.dynamic_slice_in_dim(padded_ids, seq_index * part_rows, WINDOW + part_rows, 1)
    augk, augq = mask_features(segment_ext, docs)

    x = inputs.astype(jnp.float32)
    z1, rate1 = standardize(x)
    normed1 = (z1 * gain1 + offset1).astype(jnp.bfloat16)
    normed1 = lax.all_gather(normed1, "fsdp", axis=1, tiled=True)
    packed_weight = pack_columns(qkv_weight, heads)
    head_bias = qv_bias.astype(jnp.float32)
    head_bias = jnp.concatenate(
        [head_bias[:, :HD], jnp.zeros((heads, HD), jnp.float32), head_bias[:, HD:]], axis=1
    ).reshape(-1)
    packed_bias = pack_columns(head_bias, heads)
    qkv = (dot("sre,ef->srf", normed1, packed_weight) + packed_bias).astype(jnp.bfloat16)
    halo = from_behind(qkv[:, part_rows - WINDOW :, : heads * 2 * HD], "seq", 1)
    head_out, q2 = attend(qkv, halo, augk, augq, heads)
    merged = lax.all_to_all(head_out, "fsdp", split_axis=1, concat_axis=2, tiled=True)
    resid = x + dot("sre,ef->srf", merged, out_all) + out_off
    z2, rate2 = standardize(resid)
    normed2 = (z2 * gain2 + offset2).astype(jnp.bfloat16)
    fc_offset = fc_off.reshape(group, -1)
    hidden = dot("sre,gef->gsrf", normed2, fc_all) + fc_offset[:, None, None]
    active, gelu_back = jax.vjp(lambda v: jax.nn.gelu(v, approximate=True), hidden)
    active = active.astype(jnp.bfloat16)
    layer_output = (resid + dot("gsrf,gfd->srd", active, proj_all) + proj_off).astype(jnp.bfloat16)

    cot32 = cotangent.astype(jnp.float32)
    proj_bias_part = jnp.sum(cot32, axis=(0, 1))
    proj_weight_part = dot("gsrf,srd->gfd", active, cotangent)
    g_hidden = gelu_back(dot("srd,gfd->gsrf", cotangent, proj_all))[0].astype(jnp.bfloat16)
    fc_bias_part = jnp.sum(g_hidden, axis=(1, 2), dtype=jnp.float32).reshape(-1)
    fc_weight_part = dot("sre,gsrf->gef", normed2, g_hidden)
    g_norm2 = dot("gsrf,gef->sre", g_hidden, fc_all)
    gain2_part = jnp.sum(g_norm2 * z2, axis=(0, 1))
    offset2_part = jnp.sum(g_norm2, axis=(0, 1))
    g_resid = cot32 + norm_grad(g_norm2 * gain2, z2, rate2)
    g_attn = g_resid.astype(jnp.bfloat16)
    out_bias_part = jnp.sum(g_attn, axis=(0, 1), dtype=jnp.float32)
    out_weight_part = dot("sre,srd->ed", merged, g_attn)
    g_merged = dot("srd,ed->sre", g_attn, out_all).astype(jnp.bfloat16)
    g_heads = lax.all_to_all(g_merged, "fsdp", split_axis=2, concat_axis=1, tiled=True)

    low = jnp.bfloat16
    fc_grad = lax.psum_scatter(fc_weight_part.astype(low), "fsdp")
    proj_grad = lax.psum_scatter(proj_weight_part.astype(low), "fsdp")
    out_grad = lax.psum_scatter(out_weight_part.astype(low), "fsdp", scatter_dimension=0, tiled=True)
    fc_grad, proj_grad, out_grad = lax.psum((fc_grad, proj_grad, out_grad), "seq")

    dq, dkv, dhalo = attend_back(qkv, halo, augk, q2, head_out, g_heads, heads)
    edge = from_behind(dhalo, "seq", -1)
    edge = jnp.pad(edge.astype(jnp.float32), ((0, 0), (part_rows - WINDOW, 0), (0, 0)))
    g_qkv = jnp.concatenate([(dkv + edge).astype(jnp.bfloat16), dq], axis=-1)
    qkv_grad = dot("sre,srf->ef", normed1, g_qkv)
    qkv_colsum = jnp.sum(g_qkv, axis=(0, 1), dtype=jnp.float32)
    g_norm1 = dot("srf,ef->sre", g_qkv, packed_weight).astype(jnp.bfloat16)
    g_norm1 = lax.psum_scatter(g_norm1, "fsdp", scatter_dimension=1, tiled=True).astype(jnp.float32)
    gain1_part = jnp.sum(g_norm1 * z1, axis=(0, 1))
    offset1_part = jnp.sum(g_norm1, axis=(0, 1))
    input_grad = (g_resid + norm_grad(g_norm1 * gain1, z1, rate1)).astype(jnp.bfloat16)

    qkv_grad = lax.psum(qkv_grad.astype(low), "seq").astype(jnp.float32)
    qkv_grad = unpack_columns(qkv_grad, heads)
    col = unpack_columns(qkv_colsum, heads).reshape(heads, 3 * HD)
    col = lax.psum(jnp.concatenate([col[:, :HD], col[:, 2 * HD :]], axis=1), "seq")
    vectors = jnp.concatenate(
        [
            v.reshape(group, -1)
            for v in (gain1_part, offset1_part, out_bias_part, gain2_part, offset2_part, proj_bias_part, fc_bias_part)
        ],
        axis=1,
    )
    vectors = lax.psum_scatter(vectors, "fsdp")
    vectors = lax.psum(vectors, "seq")
    parts = [vectors[i * shard : (i + 1) * shard] for i in range(6)] + [vectors[6 * shard :]]
    f32 = jnp.float32
    return (
        layer_output, input_grad, parts[0], parts[1], qkv_grad, col, out_grad.astype(f32), parts[2], parts[3],
        parts[4], fc_grad.astype(f32), parts[6], proj_grad.astype(f32), parts[5],
    )


def solution(mesh):
    tokens = P(None, ("seq", "fsdp"), None)
    rows, cols, vec = P("fsdp", None), P(None, "fsdp"), P("fsdp")
    return jax.shard_map(
        body,
        mesh=mesh,
        in_specs=(tokens, tokens, P(), vec, vec, cols, rows, rows, vec, vec, vec, cols, vec, rows, vec),
        out_specs=(tokens, tokens, vec, vec, cols, rows, rows, vec, vec, vec, cols, vec, rows, vec),
        check_vma=False,
    )
```

```python
import functools
import jax, jax.numpy as jnp
from jax import lax
from jax.experimental import pallas as pl
from jax.experimental.pallas import tpu as pltpu
from jax.sharding import PartitionSpec as P

HD = 64
WINDOW = 1024
BLK = 256
PENALTY = 1e30


def nt(a, b):
    return lax.dot_general(a, b, (((1,), (1,)), ((), ())), preferred_element_type=jnp.float32)


def nn(a, b):
    return lax.dot_general(a, b, (((1,), (0,)), ((), ())), preferred_element_type=jnp.float32)


def tn(a, b):
    return lax.dot_general(a, b, (((0,), (0,)), ((), ())), preferred_element_type=jnp.float32)


def split3(v):
    hi = v.astype(jnp.bfloat16).astype(jnp.float32)
    rest = v - hi
    mid = rest.astype(jnp.bfloat16).astype(jnp.float32)
    return hi, mid, rest - mid


def merge_edges(mask, tiles):
    return [jnp.where(mask, tiles[0], tiles[-1])] + tiles[1:-1]


def spread_edges(mask, tiles):
    zero = jnp.zeros_like(tiles[0])
    return [jnp.where(mask, tiles[0], zero)] + tiles[1:] + [jnp.where(mask, zero, tiles[0])]


def edge_mask():
    rows = lax.broadcasted_iota(jnp.int32, (BLK, BLK), 0)
    cols = lax.broadcasted_iota(jnp.int32, (BLK, BLK), 1)
    return rows > cols


def fill_keys(heads, qkv_ref, halo_ref, augk_ref, keys, values):
    halo_rows = halo_ref.shape[1]
    rows = qkv_ref.shape[1]
    ones = jnp.ones((1, HD), jnp.bfloat16)
    for h in range(heads):
        c = h * 2 * HD
        for source, base, size in ((halo_ref, 0, halo_rows), (qkv_ref, halo_rows, rows)):
            pair = source[0, :, c : c + 2 * HD]
            keys[h, base : base + size, :] = jnp.concatenate(
                [pair[:, :HD], augk_ref[0, base : base + size, :]], axis=1
            )
            values[h, base : base + size, :] = jnp.concatenate(
                [pair[:, HD:], jnp.broadcast_to(ones, (size, HD))], axis=1
            )


def xor(a, b, size):
    total, bit = 0, 1
    while bit < size:
        total = total + bit * lax.rem(lax.div(a, bit) + lax.div(b, bit), 2)
        bit *= 2
    return total


def enter(peers):
    barrier = pltpu.get_barrier_semaphore()
    for peer in peers:
        pl.semaphore_signal(barrier, inc=1, device_id={"fsdp": peer}, device_id_type=pl.DeviceIdType.MESH)
    pl.semaphore_wait(barrier, len(peers))


def attend_kernel(
    heads, group, qkv_ref, halo_ref, augk_ref, augq_ref, out_ref, q2_ref, merged_ref,
    keys, values, values_t, sent, local_sems, send_sems, recv_sems,
):
    seq, step = pl.program_id(0), pl.program_id(1)
    me = lax.axis_index("fsdp")
    nkeys = keys.shape[1]
    place = xor(me, step, group)

    @pl.when((seq == 0) & (step == 0))
    def _():
        enter([xor(me, k, group) for k in range(1, group)])

    @pl.when(step == 0)
    def _():
        fill_keys(heads, qkv_ref, halo_ref, augk_ref, keys, values)
        for h in range(heads):
            for b in range(nkeys // BLK):
                values_t[h, :, b * BLK : (b + 1) * BLK] = values[h, b * BLK : (b + 1) * BLK, :].T

    mask = edge_mask()
    tiles = WINDOW // BLK + 1
    start = pl.multiple_of(place * BLK, BLK)
    lane = lax.broadcasted_iota(jnp.int32, (BLK, 2 * HD), 1)
    lse_lane = augq_ref.shape[2] + HD - 3
    for h in range(heads):
        qc = heads * 2 * HD + h * HD
        q = jnp.concatenate([qkv_ref[0, pl.ds(start, BLK), qc : qc + HD] * 0.125, augq_ref[0, pl.ds(start, BLK), :]], axis=1)
        scores = [nt(keys[h, pl.ds(pl.multiple_of(start + b * BLK, BLK), BLK), :], q) for b in range(tiles)]
        scores = merge_edges(mask, scores)
        peak = functools.reduce(jnp.maximum, scores)
        peak = jnp.max(peak, axis=0, keepdims=True)
        weights = spread_edges(mask, [jnp.exp(s - peak).astype(jnp.bfloat16) for s in scores])
        total = sum(
            nn(values_t[h, :, pl.ds(pl.multiple_of(start + b * BLK, BLK), BLK)], w) for b, w in enumerate(weights)
        )
        sub = lax.broadcasted_iota(jnp.int32, total.shape, 0)
        total = jnp.where(sub == HD + 1, peak, total).T
        norm = total[:, HD : HD + 1]
        part = (total[:, :HD] / norm).astype(out_ref.dtype)
        out_ref[0, pl.ds(start, BLK), h * HD : (h + 1) * HD] = part
        sent[seq, step, :, h * HD : (h + 1) * HD] = part
        lse = total[:, HD + 1 : HD + 2] + jnp.log(norm)
        hi, mid, low = split3(-lse)
        q2 = q.astype(jnp.float32)
        q2 = jnp.where(lane == lse_lane, hi, q2)
        q2 = jnp.where(lane == lse_lane + 1, mid, q2)
        q2 = jnp.where(lane == lse_lane + 2, low, q2)
        q2_ref[0, h, pl.ds(start, BLK), :] = q2.astype(jnp.bfloat16)

    def own(s):
        return pltpu.make_async_copy(sent.at[s, 0], merged_ref.at[0, s], local_sems.at[s])

    def away(s, k):
        return pltpu.make_async_remote_copy(
            src_ref=sent.at[s, k],
            dst_ref=merged_ref.at[k, s],
            send_sem=send_sems.at[s, k],
            recv_sem=recv_sems.at[s, k],
            device_id={"fsdp": xor(me, k, group)},
            device_id_type=pl.DeviceIdType.MESH,
        )

    @pl.when(step == 0)
    def _():
        own(seq).start()

    @pl.when(step > 0)
    def _():
        away(seq, step).start()

    @pl.when((seq == pl.num_programs(0) - 1) & (step == pl.num_programs(1) - 1))
    def _():
        for s in range(merged_ref.shape[1]):
            own(s).wait()
            for k in range(1, group):
                away(s, k).wait()


def attend(qkv, halo, augk, augq, heads, group):
    seqs, rows, cols = qkv.shape
    ext = augk.shape[1]
    assert rows // BLK == group
    return pl.pallas_call(
        functools.partial(attend_kernel, heads, group),
        grid=(seqs, rows // BLK),
        in_specs=[
            pl.BlockSpec((1, rows, cols), lambda s, i: (s, 0, 0)),
            pl.BlockSpec((1, WINDOW, heads * 2 * HD), lambda s, i: (s, 0, 0)),
            pl.BlockSpec((1, ext, HD), lambda s, i: (s, 0, 0)),
            pl.BlockSpec((1, rows, HD), lambda s, i: (s, 0, 0)),
        ],
        out_specs=[
            pl.BlockSpec((1, rows, heads * HD), lambda s, i: (s, 0, 0)),
            pl.BlockSpec((1, heads, rows, 2 * HD), lambda s, i: (s, 0, 0, 0)),
            pl.BlockSpec(memory_space=pl.ANY),
        ],
        out_shape=[
            jax.ShapeDtypeStruct((seqs, rows, heads * HD), jnp.bfloat16),
            jax.ShapeDtypeStruct((seqs, heads, rows, 2 * HD), jnp.bfloat16),
            jax.ShapeDtypeStruct((group, seqs, BLK, heads * HD), jnp.bfloat16),
        ],
        scratch_shapes=[
            pltpu.VMEM((heads, ext, 2 * HD), jnp.bfloat16),
            pltpu.VMEM((heads, ext, 2 * HD), jnp.bfloat16),
            pltpu.VMEM((heads, 2 * HD, ext), jnp.bfloat16),
            pltpu.VMEM((seqs, group, BLK, heads * HD), jnp.bfloat16),
            pltpu.SemaphoreType.DMA((seqs,)),
            pltpu.SemaphoreType.DMA((seqs, group)),
            pltpu.SemaphoreType.DMA((seqs, group)),
        ],
        compiler_params=pltpu.CompilerParams(vmem_limit_bytes=48 * 2**20, collective_id=1, has_side_effects=True),
        name="attend",
    )(qkv, halo, augk, augq)


def attend_back_kernel(
    heads, qkv_ref, halo_ref, augk_ref, q2_ref, out_ref, grad_ref, dq_ref, dkv_ref, dhalo_ref,
    keys, values, keys_t, dkeys, dvalues,
):
    step = pl.program_id(1)
    nkeys = keys.shape[1]

    @pl.when(step == 0)
    def _():
        fill_keys(heads, qkv_ref, halo_ref, augk_ref, keys, values)
        for h in range(heads):
            for b in range(nkeys // BLK):
                keys_t[h, :, b * BLK : (b + 1) * BLK] = keys[h, b * BLK : (b + 1) * BLK, :].T
        dkeys[...] = jnp.zeros_like(dkeys)
        dvalues[...] = jnp.zeros_like(dvalues)

    mask = edge_mask()
    tiles = WINDOW // BLK + 1
    start = pl.multiple_of(step * BLK, BLK)
    lane = lax.broadcasted_iota(jnp.int32, (BLK, 2 * HD), 1)
    for h in range(heads):
        q = q2_ref[0, h]
        g = grad_ref[0, :, h * HD : (h + 1) * HD]
        g32 = g.astype(jnp.float32)
        centre = jnp.sum(g32 * out_ref[0, :, h * HD : (h + 1) * HD].astype(jnp.float32), axis=1, keepdims=True)
        hi, mid, low = split3(-centre)
        g2 = jnp.concatenate([g32, jnp.zeros((BLK, HD), jnp.float32)], axis=1)
        g2 = jnp.where(lane == HD, hi, g2)
        g2 = jnp.where(lane == HD + 1, mid, g2)
        g2 = jnp.where(lane == HD + 2, low, g2).astype(jnp.bfloat16)
        spans = [pl.ds(pl.multiple_of(start + b * BLK, BLK), BLK) for b in range(tiles)]
        scores = merge_edges(mask, [nt(keys[h, s, :], q) for s in spans])
        wgrads = merge_edges(mask, [nt(values[h, s, :], g2) for s in spans])
        weights = [jnp.exp(s) for s in scores]
        sgrads = spread_edges(mask, [(w * d).astype(jnp.bfloat16) for w, d in zip(weights, wgrads)])
        weights = spread_edges(mask, [w.astype(jnp.bfloat16) for w in weights])
        for s, w, d in zip(spans, weights, sgrads):
            dvalues[h, s, :] += nn(w, g2)
            dkeys[h, s, :] += nn(d, q)
        dq = sum(nn(keys_t[h, :, s], d) for s, d in zip(spans, sgrads))
        dq_ref[0, :, h * HD : (h + 1) * HD] = (dq.T[:, :HD] * 0.125).astype(dq_ref.dtype)

    @pl.when(step == pl.num_programs(1) - 1)
    def _():
        for h in range(heads):
            c = h * 2 * HD
            dhalo_ref[0, :, c : c + 2 * HD] = jnp.concatenate(
                [dkeys[h, :WINDOW, :HD], dvalues[h, :WINDOW, :HD]], axis=1
            ).astype(dhalo_ref.dtype)
            dkv_ref[0, :, c : c + 2 * HD] = jnp.concatenate(
                [dkeys[h, WINDOW:, :HD], dvalues[h, WINDOW:, :HD]], axis=1
            ).astype(dkv_ref.dtype)


def attend_back(qkv, halo, augk, q2, out, grad, heads):
    seqs, rows, cols = qkv.shape
    ext = augk.shape[1]
    return pl.pallas_call(
        functools.partial(attend_back_kernel, heads),
        grid=(seqs, rows // BLK),
        in_specs=[
            pl.BlockSpec((1, rows, cols), lambda s, i: (s, 0, 0)),
            pl.BlockSpec((1, WINDOW, heads * 2 * HD), lambda s, i: (s, 0, 0)),
            pl.BlockSpec((1, ext, HD), lambda s, i: (s, 0, 0)),
            pl.BlockSpec((1, heads, BLK, 2 * HD), lambda s, i: (s, 0, i, 0)),
            pl.BlockSpec((1, BLK, heads * HD), lambda s, i: (s, i, 0)),
            pl.BlockSpec((1, BLK, heads * HD), lambda s, i: (s, i, 0)),
        ],
        out_specs=[
            pl.BlockSpec((1, BLK, heads * HD), lambda s, i: (s, i, 0)),
            pl.BlockSpec((1, rows, heads * 2 * HD), lambda s, i: (s, 0, 0)),
            pl.BlockSpec((1, WINDOW, heads * 2 * HD), lambda s, i: (s, 0, 0)),
        ],
        out_shape=[
            jax.ShapeDtypeStruct((seqs, rows, heads * HD), jnp.bfloat16),
            jax.ShapeDtypeStruct((seqs, rows, heads * 2 * HD), jnp.float32),
            jax.ShapeDtypeStruct((seqs, WINDOW, heads * 2 * HD), jnp.bfloat16),
        ],
        scratch_shapes=[
            pltpu.VMEM((heads, ext, 2 * HD), jnp.bfloat16),
            pltpu.VMEM((heads, ext, 2 * HD), jnp.bfloat16),
            pltpu.VMEM((heads, 2 * HD, ext), jnp.bfloat16),
            pltpu.VMEM((heads, ext, 2 * HD), jnp.float32),
            pltpu.VMEM((heads, ext, 2 * HD), jnp.float32),
        ],
        compiler_params=pltpu.CompilerParams(vmem_limit_bytes=56 * 2**20),
        name="attend_back",
    )(qkv, halo, augk, q2, out, grad)


def mask_features(segment_ext, docs):
    doc = jnp.arange(docs, dtype=jnp.int32)
    hot = (segment_ext[..., None] == doc).astype(jnp.bfloat16)
    outside = (segment_ext < 0).astype(jnp.bfloat16)[..., None]
    pad = HD - docs - 4
    one = jnp.ones(segment_ext.shape + (3,), jnp.bfloat16)
    zero = jnp.zeros(segment_ext.shape + (pad,), jnp.bfloat16)
    keys = jnp.concatenate([-hot, -outside, zero, one], axis=-1)
    own = hot[:, WINDOW:]
    queries = jnp.concatenate(
        [
            (1 - own) * jnp.bfloat16(PENALTY),
            jnp.full(own.shape[:2] + (1,), PENALTY, jnp.bfloat16),
            jnp.zeros(own.shape[:2] + (pad + 3,), jnp.bfloat16),
        ],
        axis=-1,
    )
    return keys, queries


norm_eps = 1e-05


def standardize(values):
    centre = values - jnp.mean(values, axis=-1, keepdims=True)
    spread = jnp.mean(centre * centre, axis=-1, keepdims=True)
    rate = lax.rsqrt(spread + norm_eps)
    return centre * rate, rate


def norm_grad(direction, z, rate):
    mean_d = jnp.mean(direction, axis=-1, keepdims=True)
    mean_dz = jnp.mean(direction * z, axis=-1, keepdims=True)
    return rate * (direction - mean_d - z * mean_dz)


def from_behind(block, axis, distance):
    devices = range(lax.axis_size(axis))
    route = [(i - distance, i) for i in devices if i - distance in devices]
    return lax.ppermute(block, axis, route)


def pack_columns(array, heads):
    parts = array.reshape(array.shape[:-1] + (heads, 3 * HD))
    lead = array.shape[:-1]
    return jnp.concatenate(
        [parts[..., HD:].reshape(lead + (-1,)), parts[..., :HD].reshape(lead + (-1,))], axis=-1
    )


def unpack_columns(array, heads):
    lead = array.shape[:-1]
    pairs = array[..., : heads * 2 * HD].reshape(lead + (heads, 2 * HD))
    queries = array[..., heads * 2 * HD :].reshape(lead + (heads, HD))
    return jnp.concatenate([queries, pairs], axis=-1).reshape(lead + (-1,))


def dot(subscripts, a, b):
    return jnp.einsum(subscripts, a, b, preferred_element_type=jnp.float32)


def body(
    inputs, cotangent, segment_ids, norm1_gain, norm1_bias, qkv_weight, qv_bias, out_weight, out_bias,
    norm2_gain, norm2_bias, fc_weight, fc_bias, proj_weight, proj_bias,
):
    group = lax.axis_size("fsdp")
    seqs, local_rows, width = inputs.shape
    part_rows = local_rows * group
    heads = qkv_weight.shape[1] // (3 * HD)
    docs = segment_ids.shape[1] // (2 * WINDOW)
    seq_index = lax.axis_index("seq")
    shard = norm1_gain.shape[0]

    small = jnp.concatenate([norm1_gain, norm1_bias, out_bias, norm2_gain, norm2_bias, proj_bias, fc_bias])
    small = lax.all_gather(small, "fsdp")
    gain1, offset1, out_off, gain2, offset2, proj_off = (
        small[:, i * shard : (i + 1) * shard].reshape(-1).astype(jnp.float32) for i in range(6)
    )
    fc_off = small[:, 6 * shard :].reshape(-1).astype(jnp.float32)
    out_all = lax.all_gather(out_weight, "fsdp", axis=0, tiled=True)
    fc_all = lax.all_gather(fc_weight, "fsdp")
    proj_all = lax.all_gather(proj_weight, "fsdp")

    padded_ids = jnp.concatenate([jnp.full((seqs, WINDOW), -1, jnp.int32), segment_ids], axis=1)
    segment_ext = lax.dynamic_slice_in_dim(padded_ids, seq_index * part_rows, WINDOW + part_rows, 1)
    augk, augq = mask_features(segment_ext, docs)

    x = inputs.astype(jnp.float32)
    z1, rate1 = standardize(x)
    normed1 = (z1 * gain1 + offset1).astype(jnp.bfloat16)
    normed1 = lax.all_gather(normed1, "fsdp", axis=1, tiled=True)
    packed_weight = pack_columns(qkv_weight, heads)
    head_bias = qv_bias.astype(jnp.float32)
    head_bias = jnp.concatenate(
        [head_bias[:, :HD], jnp.zeros((heads, HD), jnp.float32), head_bias[:, HD:]], axis=1
    ).reshape(-1)
    packed_bias = pack_columns(head_bias, heads)
    qkv = (dot("sre,ef->srf", normed1, packed_weight) + packed_bias).astype(jnp.bfloat16)
    halo = from_behind(qkv[:, part_rows - WINDOW :, : heads * 2 * HD], "seq", 1)
    head_out, q2, merged = attend(qkv, halo, augk, augq, heads, group)
    me = lax.axis_index("fsdp")
    merged = jnp.stack([lax.dynamic_index_in_dim(merged, xor(me, k, group), 0, False) for k in range(group)], axis=2).reshape(seqs, local_rows, width)
    resid = x + dot("sre,ef->srf", merged, out_all) + out_off
    z2, rate2 = standardize(resid)
    normed2 = (z2 * gain2 + offset2).astype(jnp.bfloat16)
    fc_offset = fc_off.reshape(group, -1)
    hidden = dot("sre,gef->gsrf", normed2, fc_all) + fc_offset[:, None, None]
    active, gelu_back = jax.vjp(lambda v: jax.nn.gelu(v, approximate=True), hidden)
    active = active.astype(jnp.bfloat16)
    layer_output = (resid + dot("gsrf,gfd->srd", active, proj_all) + proj_off).astype(jnp.bfloat16)

    cot32 = cotangent.astype(jnp.float32)
    proj_bias_part = jnp.sum(cot32, axis=(0, 1))
    proj_weight_part = dot("gsrf,srd->gfd", active, cotangent)
    g_hidden = gelu_back(dot("srd,gfd->gsrf", cotangent, proj_all))[0].astype(jnp.bfloat16)
    fc_bias_part = jnp.sum(g_hidden, axis=(1, 2), dtype=jnp.float32).reshape(-1)
    fc_weight_part = dot("sre,gsrf->gef", normed2, g_hidden)
    g_norm2 = dot("gsrf,gef->sre", g_hidden, fc_all)
    gain2_part = jnp.sum(g_norm2 * z2, axis=(0, 1))
    offset2_part = jnp.sum(g_norm2, axis=(0, 1))
    g_resid = cot32 + norm_grad(g_norm2 * gain2, z2, rate2)
    g_attn = g_resid.astype(jnp.bfloat16)
    out_bias_part = jnp.sum(g_attn, axis=(0, 1), dtype=jnp.float32)
    out_weight_part = dot("sre,srd->ed", merged, g_attn)
    g_merged = dot("srd,ed->sre", g_attn, out_all).astype(jnp.bfloat16)
    g_heads = lax.all_to_all(g_merged, "fsdp", split_axis=2, concat_axis=1, tiled=True)

    low = jnp.bfloat16
    fc_grad = lax.psum_scatter(fc_weight_part.astype(low), "fsdp")
    proj_grad = lax.psum_scatter(proj_weight_part.astype(low), "fsdp")
    out_grad = lax.psum_scatter(out_weight_part.astype(low), "fsdp", scatter_dimension=0, tiled=True)
    fc_grad, proj_grad, out_grad = lax.psum((fc_grad, proj_grad, out_grad), "seq")

    dq, dkv, dhalo = attend_back(qkv, halo, augk, q2, head_out, g_heads, heads)
    edge = from_behind(dhalo, "seq", -1)
    edge = jnp.pad(edge.astype(jnp.float32), ((0, 0), (part_rows - WINDOW, 0), (0, 0)))
    g_qkv = jnp.concatenate([(dkv + edge).astype(jnp.bfloat16), dq], axis=-1)
    qkv_grad = dot("sre,srf->ef", normed1, g_qkv)
    qkv_colsum = jnp.sum(g_qkv, axis=(0, 1), dtype=jnp.float32)
    g_norm1 = dot("srf,ef->sre", g_qkv, packed_weight).astype(jnp.bfloat16)
    g_norm1 = lax.psum_scatter(g_norm1, "fsdp", scatter_dimension=1, tiled=True).astype(jnp.float32)
    gain1_part = jnp.sum(g_norm1 * z1, axis=(0, 1))
    offset1_part = jnp.sum(g_norm1, axis=(0, 1))
    input_grad = (g_resid + norm_grad(g_norm1 * gain1, z1, rate1)).astype(jnp.bfloat16)

    qkv_grad = lax.psum(qkv_grad.astype(low), "seq").astype(jnp.float32)
    qkv_grad = unpack_columns(qkv_grad, heads)
    col = unpack_columns(qkv_colsum, heads).reshape(heads, 3 * HD)
    col = lax.psum(jnp.concatenate([col[:, :HD], col[:, 2 * HD :]], axis=1), "seq")
    vectors = jnp.concatenate(
        [
            v.reshape(group, -1)
            for v in (gain1_part, offset1_part, out_bias_part, gain2_part, offset2_part, proj_bias_part, fc_bias_part)
        ],
        axis=1,
    )
    vectors = lax.psum_scatter(vectors, "fsdp")
    vectors = lax.psum(vectors, "seq")
    parts = [vectors[i * shard : (i + 1) * shard] for i in range(6)] + [vectors[6 * shard :]]
    f32 = jnp.float32
    return (
        layer_output, input_grad, parts[0], parts[1], qkv_grad, col, out_grad.astype(f32), parts[2], parts[3],
        parts[4], fc_grad.astype(f32), parts[6], proj_grad.astype(f32), parts[5],
    )


def solution(mesh):
    tokens = P(None, ("seq", "fsdp"), None)
    rows, cols, vec = P("fsdp", None), P(None, "fsdp"), P("fsdp")
    return jax.shard_map(
        body,
        mesh=mesh,
        in_specs=(tokens, tokens, P(), vec, vec, cols, rows, rows, vec, vec, vec, cols, vec, rows, vec),
        out_specs=(tokens, tokens, vec, vec, cols, rows, rows, vec, vec, vec, cols, vec, rows, vec),
        check_vma=False,
    )
```

```python
import functools
import math

import jax
import jax.numpy as jnp
from jax import lax
from jax.experimental import pallas as pl
from jax.experimental.pallas import tpu as pltpu
from jax.sharding import PartitionSpec as P


def standardize(values):
    centre = values - jnp.mean(values, axis=-1, keepdims=True)
    spread = jnp.mean(centre * centre, axis=-1, keepdims=True)
    rate = lax.rsqrt(spread + norm_eps)
    return centre * rate, rate


def norm_grad(direction, z, rate):
    mean_d = jnp.mean(direction, axis=-1, keepdims=True)
    mean_dz = jnp.mean(direction * z, axis=-1, keepdims=True)
    return rate * (direction - mean_d - z * mean_dz)


norm_eps = 1e-05

HD = 64
WINDOW = 1024
BLK = 256
PENALTY = 1e30


def nt(a, b):
    return lax.dot_general(a, b, (((1,), (1,)), ((), ())), preferred_element_type=jnp.float32)


def nn(a, b):
    return lax.dot_general(a, b, (((1,), (0,)), ((), ())), preferred_element_type=jnp.float32)


def tn(a, b):
    return lax.dot_general(a, b, (((0,), (0,)), ((), ())), preferred_element_type=jnp.float32)


def split3(v):
    hi = v.astype(jnp.bfloat16).astype(jnp.float32)
    rest = v - hi
    mid = rest.astype(jnp.bfloat16).astype(jnp.float32)
    return hi, mid, rest - mid


def merge_edges(mask, tiles):
    return [jnp.where(mask, tiles[0], tiles[-1])] + tiles[1:-1]


def spread_edges(mask, tiles):
    zero = jnp.zeros_like(tiles[0])
    return [jnp.where(mask, tiles[0], zero)] + tiles[1:] + [jnp.where(mask, zero, tiles[0])]


def edge_mask():
    rows = lax.broadcasted_iota(jnp.int32, (BLK, BLK), 0)
    cols = lax.broadcasted_iota(jnp.int32, (BLK, BLK), 1)
    return rows > cols


def xor(a, b, size):
    total, bit = 0, 1
    while bit < size:
        total = total + bit * lax.rem(lax.div(a, bit) + lax.div(b, bit), 2)
        bit *= 2
    return total


MESH = pl.DeviceIdType.MESH
SLOT_AT = (1, 3, 5, 2, 4, 0, 7, 6)
STEP_OF = tuple(SLOT_AT.index(r) for r in range(8))
NEAR = 6


def enter(peers):
    barrier = pltpu.get_barrier_semaphore()
    for peer in peers:
        pl.semaphore_signal(barrier, inc=1, device_id={"fsdp": peer}, device_id_type=MESH)
    pl.semaphore_wait(barrier, len(peers))


def attend_kernel(
    heads, group, qkv_ref, augk_ref, augq_ref, out_w, fc_w, proj_w,
    out_ref, q2_ref, halo_ref, merged_ref, out_all, fc_all, proj_all,
    keys, values, values_t, sent, behind, own_sems, send_sems, recv_sems, halo_sems, w_own, w_send, w_recv,
):
    step = pl.program_id(0)
    last = pl.num_programs(0) - 1
    me = lax.axis_index("fsdp")
    line = lax.axis_index("seq")
    line_end = lax.axis_size("seq") - 1
    at = [xor(me, k, group) for k in range(group)]
    seqs, rows = qkv_ref.shape[0], qkv_ref.shape[1]
    half = group // 2
    seq = lax.rem(lax.div(step, half), 2)
    lower = lax.div(step, group)
    place = (1 - lower) * half + lax.rem(step + me, half)
    width = heads * 2 * HD
    low = jnp.bfloat16

    def halo_copy():
        return pltpu.make_async_remote_copy(
            src_ref=qkv_ref.at[:, pl.ds(rows - WINDOW, WINDOW), pl.ds(0, width)],
            dst_ref=behind, send_sem=halo_sems.at[0], recv_sem=halo_sems.at[1],
            device_id={"seq": lax.rem(line + 1, line_end + 1)}, device_id_type=MESH,
        )

    weights = ((out_w, out_all, False), (fc_w, fc_all, True), (proj_w, proj_all, True))

    def slot(a, r):
        return weights[a][1].at[STEP_OF[r] if weights[a][2] else r]

    def w_copy(a, r, second=False):
        to = at[1] if r % 2 else at[r]
        src = weights[a][0] if r in (1, 2, 4) else slot(a, r - 1) if r % 2 else None
        dst, sem = slot(a, r), r
        if r == 6:
            size = weights[a][0].shape[0] // 2
            part = pl.ds(size if second else 0, size)
            src = slot(a, 4 if second else 2).at[part]
            to = at[2] if second else at[4]
            dst, sem = dst.at[part], 0 if second else 6
        return pltpu.make_async_remote_copy(
            src_ref=src, dst_ref=dst, send_sem=w_send.at[a, sem], recv_sem=w_recv.at[a, sem],
            device_id={"fsdp": to}, device_id_type=MESH,
        )

    def w_keep(a):
        return pltpu.make_async_copy(weights[a][0], slot(a, 0), w_own.at[a])

    def forward(a):
        w_copy(a, 2).wait_recv()
        w_copy(a, 3).start()
        w_copy(a, 4).wait_recv()
        w_copy(a, 5).start()
        if not weights[a][2]:
            w_copy(a, 6).start()
            w_copy(a, 6, True).start()

    @pl.when(step == 0)
    def _():
        barrier = pltpu.get_barrier_semaphore()
        for peer in at[1:]:
            pl.semaphore_signal(barrier, inc=1, device_id={"fsdp": peer}, device_id_type=MESH)

        pl.semaphore_signal(
            barrier, inc=1, device_id={"seq": lax.rem(line + line_end, line_end + 1)}, device_id_type=MESH
        )
        pl.semaphore_wait(barrier, group)

        @pl.when(line < line_end)
        def _():
            halo_copy().start()

        for a in range(3):
            for r in (2, 4, 1):
                w_copy(a, r).start()
            w_keep(a).start()
        for s in range(seqs):
            fill_keys(s, heads, qkv_ref, augk_ref, WINDOW, keys, values, values_t, None)

    @pl.when(step == group)
    def _():
        @pl.when(line > 0)
        def _():
            halo_copy().wait_recv()

        @pl.when(line == 0)
        def _():
            behind[...] = jnp.zeros_like(behind)

        halo_ref[...] = behind[...]
        for s in range(seqs):
            fill_keys(s, heads, behind, augk_ref, 0, keys, values, values_t, None)

    mask = edge_mask()
    tiles = WINDOW // BLK + 1
    start = pl.multiple_of(place * BLK, BLK)
    lane = lax.broadcasted_iota(jnp.int32, (BLK, 2 * HD), 1)
    lse_lane = augq_ref.shape[2] + HD - 3
    slot_k = xor(me, place, group)
    spans = [pl.ds(pl.multiple_of(start + b * BLK, BLK), BLK) for b in range(tiles)]
    for h in range(heads):
        sh = seq * heads + h
        qc = heads * 2 * HD + h * HD
        q = jnp.concatenate(
            [qkv_ref[seq, pl.ds(start, BLK), qc : qc + HD] * 0.125, augq_ref[seq, pl.ds(start, BLK), :]], axis=1
        )
        scores = merge_edges(mask, [nt(keys[sh, s, :], q) for s in spans])
        peak = functools.reduce(jnp.maximum, scores)
        peak = jnp.max(peak, axis=0, keepdims=True)
        weights_ = spread_edges(mask, [jnp.exp(s - peak).astype(low) for s in scores])
        total = sum(nn(values_t[sh, :, s], w) for s, w in zip(spans, weights_))
        sub = lax.broadcasted_iota(jnp.int32, total.shape, 0)
        total = jnp.where(sub == HD + 1, peak, total).T
        norm = total[:, HD : HD + 1]
        part = (total[:, :HD] / norm).astype(low)
        out_ref[seq, pl.ds(start, BLK), h * HD : (h + 1) * HD] = part
        sent[step, :, h * HD : (h + 1) * HD] = part
        lse = total[:, HD + 1 : HD + 2] + jnp.log(norm)
        hi, mid, lo = split3(-lse)
        q2 = q.astype(jnp.float32)
        q2 = jnp.where(lane == lse_lane, hi, q2)
        q2 = jnp.where(lane == lse_lane + 1, mid, q2)
        q2 = jnp.where(lane == lse_lane + 2, lo, q2)
        q2_ref[seq, h, pl.ds(start, BLK), :] = q2.astype(low)

    span = sent.shape[2]

    def landing(s, k):
        return merged_ref.at[s, :, pl.ds(pl.multiple_of(k * span, span), span)]

    def own(s):
        return pltpu.make_async_copy(sent.at[step], landing(s, 0), own_sems.at[s])

    def away(s, k, to):
        return pltpu.make_async_remote_copy(
            src_ref=sent.at[step], dst_ref=landing(s, k), send_sem=send_sems.at[s, k], recv_sem=recv_sems.at[s, k],
            device_id={"fsdp": to}, device_id_type=MESH,
        )

    @pl.when(place == me)
    def _():
        own(seq).start()

    @pl.when(place != me)
    def _():
        away(seq, slot_k, place).start()

    @pl.when(step == last - 3)
    def _():
        forward(0)

    @pl.when(step == last - 1)
    def _():
        forward(1)

    @pl.when(step == last)
    def _():
        forward(2)
        w_copy(0, 6).wait_recv()
        w_copy(0, 6, True).wait_recv()
        w_copy(0, 7).start()
        for s in range(seqs):
            own(s).wait()
            for k in range(1, group):
                away(s, k, at[k]).wait()
        for a in range(3):
            w_keep(a).wait()
            for r in (1, 2, 3, 4, 5):
                w_copy(a, r).wait_send()
            for r in (1, 3, 5):
                w_copy(a, r).wait_recv()
        w_copy(0, 6).wait_send()
        w_copy(0, 6, True).wait_send()
        w_copy(0, 7).wait()

        @pl.when(line < line_end)
        def _():
            halo_copy().wait_send()


def fill_keys(s, heads, source, augk_ref, base, keys, values, values_t, keys_t):
    size = BLK
    ones = jnp.ones((size, HD), jnp.bfloat16)
    first = source.shape[1] - WINDOW if base == 0 else 0
    for h in range(heads):
        c = h * 2 * HD
        for i in range(source.shape[1] // size):
            pair = source[s, i * size : (i + 1) * size, c : c + 2 * HD]
            span = slice(base + i * size, base + (i + 1) * size)
            k = jnp.concatenate([pair[:, :HD], augk_ref[s, span, :]], axis=1)
            v = jnp.concatenate([pair[:, HD:], ones], axis=1)
            keys[s * heads + h, span, :] = k
            values[s * heads + h, span, :] = v
            if values_t is not None:
                values_t[s * heads + h, :, span] = v.T
            if keys_t is not None:
                keys_t[s * heads + h, :, span] = k.T


def attend(qkv, augk, augq, out_w, fc_w, proj_w, heads, group):
    seqs, rows, cols = qkv.shape
    ext = augk.shape[1]
    assert rows // BLK == group
    low = jnp.bfloat16
    vmem = pl.BlockSpec(memory_space=pltpu.VMEM)
    hbm = pl.BlockSpec(memory_space=pl.ANY)
    every = seqs * heads
    return pl.pallas_call(
        functools.partial(attend_kernel, heads, group),
        grid=(seqs * rows // BLK,),
        in_specs=[vmem] * 3 + [hbm] * 3,
        out_specs=[vmem] * 3 + [hbm] * 4,
        out_shape=[
            jax.ShapeDtypeStruct((seqs, rows, heads * HD), low),
            jax.ShapeDtypeStruct((seqs, heads, rows, 2 * HD), low),
            jax.ShapeDtypeStruct((seqs, WINDOW, heads * 2 * HD), low),
            jax.ShapeDtypeStruct((seqs, BLK, group * heads * HD), low),
        ]
        + [jax.ShapeDtypeStruct((n,) + w.shape, low) for n, w in ((group, out_w), (NEAR, fc_w), (NEAR, proj_w))],
        scratch_shapes=[
            pltpu.VMEM((every, ext, 2 * HD), low),
            pltpu.VMEM((every, ext, 2 * HD), low),
            pltpu.VMEM((every, 2 * HD, ext), low),
            pltpu.VMEM((seqs * rows // BLK, BLK, heads * HD), low),
            pltpu.VMEM((seqs, WINDOW, heads * 2 * HD), low),
            pltpu.SemaphoreType.DMA((seqs,)),
            pltpu.SemaphoreType.DMA((seqs, group)),
            pltpu.SemaphoreType.DMA((seqs, group)),
            pltpu.SemaphoreType.DMA((2,)),
            pltpu.SemaphoreType.DMA((3,)),
            pltpu.SemaphoreType.DMA((3, group)),
            pltpu.SemaphoreType.DMA((3, group)),
        ],
        compiler_params=pltpu.CompilerParams(vmem_limit_bytes=56 * 2**20, collective_id=1, has_side_effects=True),
        name="attend",
    )(qkv, augk, augq, out_w, fc_w, proj_w)


def attend_back_kernel(
    heads, qkv_ref, halo_ref, augk_ref, q2_ref, out_ref, grad_ref, dq_ref, dkv_ref, dhalo_ref,
    keys, values, keys_t, dkeys, dvalues,
):
    step = pl.program_id(1)
    nkeys = keys.shape[1]

    @pl.when(step == 0)
    def _():
        plain_fill(heads, qkv_ref, halo_ref, augk_ref, keys, values)
        for h in range(heads):
            for b in range(nkeys // BLK):
                keys_t[h, :, b * BLK : (b + 1) * BLK] = keys[h, b * BLK : (b + 1) * BLK, :].T
        dkeys[...] = jnp.zeros_like(dkeys)
        dvalues[...] = jnp.zeros_like(dvalues)

    mask = edge_mask()
    tiles = WINDOW // BLK + 1
    start = pl.multiple_of(step * BLK, BLK)
    lane = lax.broadcasted_iota(jnp.int32, (BLK, 2 * HD), 1)
    for h in range(heads):
        q = q2_ref[0, h]
        g = grad_ref[0, :, h * HD : (h + 1) * HD]
        g32 = g.astype(jnp.float32)
        centre = jnp.sum(g32 * out_ref[0, :, h * HD : (h + 1) * HD].astype(jnp.float32), axis=1, keepdims=True)
        hi, mid, low = split3(-centre)
        g2 = jnp.concatenate([g32, jnp.zeros((BLK, HD), jnp.float32)], axis=1)
        g2 = jnp.where(lane == HD, hi, g2)
        g2 = jnp.where(lane == HD + 1, mid, g2)
        g2 = jnp.where(lane == HD + 2, low, g2).astype(jnp.bfloat16)
        spans = [pl.ds(pl.multiple_of(start + b * BLK, BLK), BLK) for b in range(tiles)]
        scores = merge_edges(mask, [nt(keys[h, s, :], q) for s in spans])
        wgrads = merge_edges(mask, [nt(values[h, s, :], g2) for s in spans])
        weights = [jnp.exp(s) for s in scores]
        sgrads = spread_edges(mask, [(w * d).astype(jnp.bfloat16) for w, d in zip(weights, wgrads)])
        weights = spread_edges(mask, [w.astype(jnp.bfloat16) for w in weights])
        for s, w, d in zip(spans, weights, sgrads):
            dvalues[h, s, :] += nn(w, g2)
            dkeys[h, s, :] += nn(d, q)
        dq = sum(nn(keys_t[h, :, s], d) for s, d in zip(spans, sgrads))
        dq_ref[0, :, h * HD : (h + 1) * HD] = (dq.T[:, :HD] * 0.125).astype(dq_ref.dtype)

    @pl.when(step == pl.num_programs(1) - 1)
    def _():
        for h in range(heads):
            c = h * 2 * HD
            dhalo_ref[0, :, c : c + 2 * HD] = jnp.concatenate(
                [dkeys[h, :WINDOW, :HD], dvalues[h, :WINDOW, :HD]], axis=1
            ).astype(dhalo_ref.dtype)
            dkv_ref[0, :, c : c + 2 * HD] = jnp.concatenate(
                [dkeys[h, WINDOW:, :HD], dvalues[h, WINDOW:, :HD]], axis=1
            ).astype(dkv_ref.dtype)


def attend_back(qkv, halo, augk, q2, out, grad, heads):
    seqs, rows, cols = qkv.shape
    ext = augk.shape[1]
    return pl.pallas_call(
        functools.partial(attend_back_kernel, heads),
        grid=(seqs, rows // BLK),
        in_specs=[
            pl.BlockSpec((1, rows, cols), lambda s, i: (s, 0, 0)),
            pl.BlockSpec((1, WINDOW, heads * 2 * HD), lambda s, i: (s, 0, 0)),
            pl.BlockSpec((1, ext, HD), lambda s, i: (s, 0, 0)),
            pl.BlockSpec((1, heads, BLK, 2 * HD), lambda s, i: (s, 0, i, 0)),
            pl.BlockSpec((1, BLK, heads * HD), lambda s, i: (s, i, 0)),
            pl.BlockSpec((1, BLK, heads * HD), lambda s, i: (s, i, 0)),
        ],
        out_specs=[
            pl.BlockSpec((1, BLK, heads * HD), lambda s, i: (s, i, 0)),
            pl.BlockSpec((1, rows, heads * 2 * HD), lambda s, i: (s, 0, 0)),
            pl.BlockSpec((1, WINDOW, heads * 2 * HD), lambda s, i: (s, 0, 0)),
        ],
        out_shape=[
            jax.ShapeDtypeStruct((seqs, rows, heads * HD), jnp.bfloat16),
            jax.ShapeDtypeStruct((seqs, rows, heads * 2 * HD), jnp.float32),
            jax.ShapeDtypeStruct((seqs, WINDOW, heads * 2 * HD), jnp.bfloat16),
        ],
        scratch_shapes=[
            pltpu.VMEM((heads, ext, 2 * HD), jnp.bfloat16),
            pltpu.VMEM((heads, ext, 2 * HD), jnp.bfloat16),
            pltpu.VMEM((heads, 2 * HD, ext), jnp.bfloat16),
            pltpu.VMEM((heads, ext, 2 * HD), jnp.float32),
            pltpu.VMEM((heads, ext, 2 * HD), jnp.float32),
        ],
        compiler_params=pltpu.CompilerParams(vmem_limit_bytes=56 * 2**20),
        name="attend_back",
    )(qkv, halo, augk, q2, out, grad)


def mask_features(segment_ext, docs):
    doc = jnp.arange(docs, dtype=jnp.int32)
    hot = (segment_ext[..., None] == doc).astype(jnp.bfloat16)
    rows = segment_ext.shape[1]
    outside = (segment_ext < 0).astype(jnp.bfloat16)[..., None]
    pad = HD - docs - 4
    one = jnp.ones(segment_ext.shape + (3,), jnp.bfloat16)
    zero = jnp.zeros(segment_ext.shape + (pad,), jnp.bfloat16)
    keys = jnp.concatenate([-hot, -outside, zero, one], axis=-1)
    own = hot[:, WINDOW:]
    queries = jnp.concatenate(
        [
            (1 - own) * jnp.bfloat16(PENALTY),
            jnp.full(own.shape[:2] + (1,), PENALTY, jnp.bfloat16),
            jnp.zeros(own.shape[:2] + (pad + 3,), jnp.bfloat16),
        ],
        axis=-1,
    )
    return keys, queries


def gather_project_kernel(
    x_ref, small_ref, w_ref, b_ref, all_small_ref, normed_out, qkv_ref,
    z1, normed, smalls, small_send, small_recv, send_sems, recv_sems, out_sems,
):
    group = all_small_ref.shape[0]
    me = lax.axis_index("fsdp")
    at = [xor(me, k, group) for k in range(group)]
    rows = x_ref.shape[0] // 2
    f32, low = jnp.float32, jnp.bfloat16
    enter(at[1:])

    def small_copy(k):
        return pltpu.make_async_remote_copy(
            src_ref=small_ref, dst_ref=smalls.at[me], send_sem=small_send.at[k], recv_sem=small_recv.at[k],
            device_id={"fsdp": at[k]}, device_id_type=MESH,
        )

    for k in range(1, group):
        small_copy(k).start()
    smalls[me] = small_ref[...]
    for s in range(2):
        z, _ = standardize(x_ref[s * rows : (s + 1) * rows, :].astype(f32))
        z1[s * rows : (s + 1) * rows, :] = z
    for k in range(1, group):
        small_copy(k).wait()
    all_small_ref[...] = smalls[...]
    gain = jnp.concatenate([smalls[f, 0:1, :] for f in range(group)], axis=1).astype(f32)
    offset = jnp.concatenate([smalls[f, 1:2, :] for f in range(group)], axis=1).astype(f32)

    def chunk(p, s):
        return normed.at[p, s]

    def move(r, s):
        if r % 2:
            piece, to = at[r - 1], at[1]
        elif r == 6:
            piece, to = (at[2], at[4]) if s == 0 else (at[4], at[2])
        else:
            piece, to = me, at[r]
        return pltpu.make_async_remote_copy(
            src_ref=chunk(piece, s), dst_ref=chunk(piece, s), send_sem=send_sems.at[r, s], recv_sem=recv_sems.at[r, s],
            device_id={"fsdp": to}, device_id_type=MESH,
        )

    def keep(k, s):
        return pltpu.make_async_copy(chunk(at[k], s), normed_out.at[at[k], s], out_sems.at[k, s])

    def project(k, s):
        keep(k, s).start()
        start = pl.multiple_of(at[k] * rows, rows)
        qkv_ref[s, pl.ds(start, rows), :] = (nn(normed[at[k], s], w_ref[...]) + b_ref[...]).astype(low)

    for s in range(2):
        normed[me, s] = (z1[s * rows : (s + 1) * rows, :] * gain + offset).astype(low)
        move(2, s).start()
        move(4, s).start()
        move(1, s).start()
    for s in range(2):
        project(0, s)
    for s in range(2):
        move(1, s).wait_recv()
        project(1, s)
    for s in range(2):
        move(2, s).wait_recv()
        if s == 0:
            move(6, 0).start()
        move(3, s).start()
        move(4, s).wait_recv()
        if s == 1:
            move(6, 1).start()
        move(5, s).start()
        project(2, s)
        project(4, s)
    for s in range(2):
        move(3, s).wait_recv()
        project(3, s)
        move(5, s).wait_recv()
        project(5, s)
    for s in range(2):
        move(6, s).wait_recv()
        move(7, s).start()
        project(6, s)
    for s in range(2):
        move(7, s).wait_recv()
        project(7, s)
    for s in range(2):
        for r in range(1, group):
            move(r, s).wait_send()
        for k in range(group):
            keep(k, s).wait()


def gather_project(x, small, weight, bias, group):
    rows, width = x.shape
    cols = weight.shape[1]
    half = rows // 2
    vmem = pl.BlockSpec(memory_space=pltpu.VMEM)
    low = jnp.bfloat16
    return pl.pallas_call(
        gather_project_kernel,
        in_specs=[vmem] * 4,
        out_specs=[vmem, pl.BlockSpec(memory_space=pl.ANY), vmem],
        out_shape=[
            jax.ShapeDtypeStruct((group,) + small.shape, low),
            jax.ShapeDtypeStruct((group, 2, half, width), low),
            jax.ShapeDtypeStruct((2, group * half, cols), low),
        ],
        scratch_shapes=[
            pltpu.VMEM((rows, width), jnp.float32),
            pltpu.VMEM((group, 2, half, width), low),
            pltpu.VMEM((group,) + small.shape, low),
            pltpu.SemaphoreType.DMA((group,)),
            pltpu.SemaphoreType.DMA((group,)),
            pltpu.SemaphoreType.DMA((group, 2)),
            pltpu.SemaphoreType.DMA((group, 2)),
            pltpu.SemaphoreType.DMA((group, 2)),
        ],
        compiler_params=pltpu.CompilerParams(
            vmem_limit_bytes=48 * 2**20, collective_id=2, has_side_effects=True
        ),
        name="gather_project",
    )(x, small, weight, bias)


def gelu_both(v):
    c = math.sqrt(2.0 / math.pi)
    square = v * v
    t = jnp.tanh(v * (c + (c * 0.044715) * square))
    half = 0.5 * (1.0 + t)
    slope = half + (0.5 * v) * (1.0 - t * t) * (c + (3.0 * 0.044715 * c) * square)
    return v * half, slope


def column_sums(array):
    return jnp.sum(array, axis=0, keepdims=True)


def feed_forward_kernel(
    group, x_ref, cot_ref, merged_ref, out_ref, fc_ref, proj_ref, fc_near, proj_near, fcb_ref, vec_ref,
    layer_ref, gres_ref, gheads_ref, keep_ref, gout_ref, gvec_ref, gfcb_ref,
    resid, z2, rate, normed, total, gnormed, fc_far, proj_far, given, taken, gmerged, gout_given, gout_taken,
    far_send, far_recv, pair_send, pair_recv, head_send, head_recv, own_sem, gout_sems,
):
    step = pl.program_id(0)
    last = group - 1
    me = lax.axis_index("fsdp")
    at = [xor(me, k, group) for k in range(group)]
    rows = x_ref.shape[0]
    block = rows // 2
    f32, low = jnp.float32, jnp.bfloat16
    span = merged_ref.shape[1] // group

    def far_copy(a, way):
        near, far = ((fc_near, fc_far), (proj_near, proj_far))[a]
        size = near.shape[1] // 2
        if way == 2:
            src, dst, to = far.at[1], far.at[0], at[1]
        else:
            part = pl.ds(way * size, size)
            src, dst = near.at[STEP_OF[(2, 4)[way]], part], far.at[1, part]
            to = at[(4, 2)[way]]
        return pltpu.make_async_remote_copy(
            src_ref=src, dst_ref=dst, send_sem=far_send.at[a, way], recv_sem=far_recv.at[a, way],
            device_id={"fsdp": to}, device_id_type=MESH,
        )

    def pair_copy(j):
        return pltpu.make_async_remote_copy(
            src_ref=given.at[j % 2], dst_ref=taken.at[j], send_sem=pair_send.at[j], recv_sem=pair_recv.at[j],
            device_id={"fsdp": at[1]}, device_id_type=MESH,
        )

    def head_copy(k):
        src = gmerged.at[:, :, pl.ds(k * span, span)]
        dst = gheads_ref.at[:, pl.ds(pl.multiple_of(me * block, block), block), :]
        if k == 0:
            return pltpu.make_async_copy(src, dst, own_sem)
        return pltpu.make_async_remote_copy(
            src_ref=src, dst_ref=dst, send_sem=head_send.at[k], recv_sem=head_recv.at[k],
            device_id={"fsdp": at[k]}, device_id_type=MESH,
        )

    def gout_copy():
        return pltpu.make_async_remote_copy(
            src_ref=gout_given, dst_ref=gout_taken, send_sem=gout_sems.at[0], recv_sem=gout_sems.at[1],
            device_id={"fsdp": at[1]}, device_id_type=MESH,
        )

    @pl.when(step == 0)
    def _():
        enter(at[1:])
        for a in range(2):
            far_copy(a, 0).start()
            far_copy(a, 1).start()
        acc = x_ref[...].astype(f32) + vec_ref[0:1, :] + nn(merged_ref[...], out_ref[...])
        resid[...] = acc
        z, r = standardize(acc)
        z2[...] = z
        rate[...] = jnp.broadcast_to(r, rate.shape)
        normed[...] = (z * vec_ref[1:2, :] + vec_ref[2:3, :]).astype(low)
        total[...] = jnp.zeros_like(total)
        gnormed[...] = jnp.zeros_like(gnormed)

    def work(fc, proj, store):
        cot = cot_ref[...]
        hidden = nn(normed[...], fc[...]) + fcb_ref[0]
        gactive = nt(cot, proj[...])
        active, slope = gelu_both(hidden)
        active = active.astype(low)
        ghidden = gactive * slope
        gfcb_ref[0] = column_sums(ghidden)
        ghidden = ghidden.astype(low)
        total[...] += nn(active, proj[...])
        gnormed[...] += nt(ghidden, fc[...])
        gfc = tn(normed[...], ghidden)
        gproj = tn(active, cot)
        w, size = gfc.shape[1], gproj.shape[0]
        store(0, slice(None), gfc)
        for i in range(gproj.shape[1] // w):
            store(1, slice(i * size, (i + 1) * size), gproj[:, i * w : (i + 1) * w])

    def give(j):
        def store(a, part, value):
            given[j % 2, a, part, :] = value.astype(low)

        return store

    def sum_with(j):
        def store(a, part, value):
            keep_ref[0, a, part, :] = (value.astype(low).astype(f32) + taken[j, a, part, :].astype(f32)).astype(low)

        return store

    for i in range(group):
        slot = SLOT_AT[i]
        j = slot // 2

        @pl.when(step == i)
        def _(i=i, slot=slot, j=j):
            fc, proj = (fc_ref.at[0], proj_ref.at[0]) if i < NEAR else (fc_far.at[i - NEAR], proj_far.at[i - NEAR])
            if i == NEAR:
                for a in range(2):
                    far_copy(a, 2).wait_recv()
            if slot % 2:
                if j >= 2:
                    pair_copy(j - 2).wait_send()
                work(fc, proj, give(j))
                pair_copy(j).start()
            else:
                pair_copy(j).wait_recv()
                work(fc, proj, sum_with(j))
            if i == NEAR - 1:
                for a in range(2):
                    far_copy(a, 0).wait_recv()
                    far_copy(a, 1).wait_recv()
                    far_copy(a, 2).start()

    @pl.when(step == last)
    def _():
        cot32 = cot_ref[...].astype(f32)
        g, z = gnormed[...], z2[...]
        gres = cot32 + norm_grad(g * vec_ref[1:2, :], z, rate[:, :1])
        gres_ref[...] = gres
        gattn = gres.astype(low)
        back = nt(gattn, out_ref[...]).astype(low)
        for s in range(2):
            gmerged[s] = back[s * block : (s + 1) * block, :]
        for k in (6, 2, 4, 3, 5, 7, 1, 0):
            head_copy(k).start()
        gout = tn(merged_ref[...], gattn)
        for k in range(1, group, 2):
            gout_given[k // 2] = gout[k * span : (k + 1) * span, :].astype(low)
        gout_copy().start()
        layer_ref[...] = (resid[...] + total[...] + vec_ref[3:4, :]).astype(low)
        gvec_ref[0:1, :] = column_sums(gattn.astype(f32))
        gvec_ref[1:2, :] = column_sums(g * z)
        gvec_ref[2:3, :] = column_sums(g)
        gvec_ref[3:4, :] = column_sums(cot32)
        gout_copy().wait_recv()
        for k in range(0, group, 2):
            mine = gout[k * span : (k + 1) * span, :].astype(low).astype(f32)
            gout_ref[k // 2] = (mine + gout_taken[k // 2].astype(f32)).astype(low)
        for k in range(group):
            head_copy(k).wait()
        gout_copy().wait_send()
        for a in range(2):
            for way in range(3):
                far_copy(a, way).wait_send()
        pair_copy(2).wait_send()
        pair_copy(3).wait_send()


def feed_forward(x, cot, merged, out_all, fc_near, proj_near, fc_bias, vectors):
    rows, width = x.shape
    group, part = fc_bias.shape[0], fc_near.shape[2]
    span = width // group
    f32, low = jnp.float32, jnp.bfloat16
    vmem = pl.BlockSpec(memory_space=pltpu.VMEM)
    hbm = pl.BlockSpec(memory_space=pl.ANY)
    near = lambda i: jnp.minimum(i, NEAR - 1)
    kept = lambda i: jnp.where(i == group - 1, 3, jnp.clip(i - 3, 0, 2))
    return pl.pallas_call(
        functools.partial(feed_forward_kernel, group),
        grid=(group,),
        in_specs=[
            vmem, vmem, vmem, vmem,
            pl.BlockSpec((1, width, part), lambda i: (near(i), 0, 0)),
            pl.BlockSpec((1, part, width), lambda i: (near(i), 0, 0)),
            hbm, hbm,
            pl.BlockSpec((1, 1, part), lambda i: (i, 0, 0)),
            vmem,
        ],
        out_specs=[
            vmem, vmem, hbm,
            pl.BlockSpec((1, 2, width, part), lambda i: (kept(i), 0, 0, 0)),
            vmem, vmem,
            pl.BlockSpec((1, 1, part), lambda i: (i, 0, 0)),
        ],
        out_shape=[
            jax.ShapeDtypeStruct((rows, width), low),
            jax.ShapeDtypeStruct((rows, width), f32),
            jax.ShapeDtypeStruct((2, group * rows // 2, span), low),
            jax.ShapeDtypeStruct((group // 2, 2, width, part), low),
            jax.ShapeDtypeStruct((group // 2, span, width), low),
            jax.ShapeDtypeStruct((8, width), f32),
            jax.ShapeDtypeStruct((group, 1, part), f32),
        ],
        scratch_shapes=[
            pltpu.VMEM((rows, width), f32),
            pltpu.VMEM((rows, width), f32),
            pltpu.VMEM((rows, 128), f32),
            pltpu.VMEM((rows, width), low),
            pltpu.VMEM((rows, width), f32),
            pltpu.VMEM((rows, width), f32),
            pltpu.VMEM((2, width, part), low),
            pltpu.VMEM((2, part, width), low),
            pltpu.VMEM((2, 2, width, part), low),
            pltpu.VMEM((group // 2, 2, width, part), low),
            pltpu.VMEM((2, rows // 2, width), low),
            pltpu.VMEM((group // 2, span, width), low),
            pltpu.VMEM((group // 2, span, width), low),
            pltpu.SemaphoreType.DMA((2, 3)),
            pltpu.SemaphoreType.DMA((2, 3)),
            pltpu.SemaphoreType.DMA((group // 2,)),
            pltpu.SemaphoreType.DMA((group // 2,)),
            pltpu.SemaphoreType.DMA((group,)),
            pltpu.SemaphoreType.DMA((group,)),
            pltpu.SemaphoreType.DMA,
            pltpu.SemaphoreType.DMA((2,)),
        ],
        compiler_params=pltpu.CompilerParams(vmem_limit_bytes=62 * 2**20, collective_id=3, has_side_effects=True),
        name="feed_forward",
    )(x, cot, merged, out_all, fc_near, proj_near, fc_near, proj_near, fc_bias, vectors)


def plain_fill(heads, qkv_ref, halo_ref, augk_ref, keys, values):
    halo_rows = halo_ref.shape[1]
    rows = qkv_ref.shape[1]
    ones = jnp.ones((1, HD), jnp.bfloat16)
    for h in range(heads):
        c = h * 2 * HD
        for source, base, size in ((halo_ref, 0, halo_rows), (qkv_ref, halo_rows, rows)):
            pair = source[0, :, c : c + 2 * HD]
            keys[h, base : base + size, :] = jnp.concatenate(
                [pair[:, :HD], augk_ref[0, base : base + size, :]], axis=1
            )
            values[h, base : base + size, :] = jnp.concatenate(
                [pair[:, HD:], jnp.broadcast_to(ones, (size, HD))], axis=1
            )


def plain_attend_kernel(heads, qkv_ref, halo_ref, augk_ref, augq_ref, out_ref, q2_ref, keys, values, values_t):
    step = pl.program_id(1)
    nkeys = keys.shape[1]

    @pl.when(step == 0)
    def _():
        plain_fill(heads, qkv_ref, halo_ref, augk_ref, keys, values)
        for h in range(heads):
            for b in range(nkeys // BLK):
                values_t[h, :, b * BLK : (b + 1) * BLK] = values[h, b * BLK : (b + 1) * BLK, :].T

    mask = edge_mask()
    tiles = WINDOW // BLK + 1
    start = pl.multiple_of(step * BLK, BLK)
    lane = lax.broadcasted_iota(jnp.int32, (BLK, 2 * HD), 1)
    lse_lane = augq_ref.shape[2] + HD - 3
    for h in range(heads):
        qc = heads * 2 * HD + h * HD
        q = jnp.concatenate([qkv_ref[0, pl.ds(start, BLK), qc : qc + HD] * 0.125, augq_ref[0]], axis=1)
        scores = [nt(keys[h, pl.ds(start + b * BLK, BLK), :], q) for b in range(tiles)]
        scores = merge_edges(mask, scores)
        peak = functools.reduce(jnp.maximum, scores)
        peak = jnp.max(peak, axis=0, keepdims=True)
        weights = spread_edges(mask, [jnp.exp(s - peak).astype(jnp.bfloat16) for s in scores])
        total = sum(
            nn(values_t[h, :, pl.ds(pl.multiple_of(start + b * BLK, BLK), BLK)], w) for b, w in enumerate(weights)
        )
        sub = lax.broadcasted_iota(jnp.int32, total.shape, 0)
        total = jnp.where(sub == HD + 1, peak, total).T
        norm = total[:, HD : HD + 1]
        out_ref[0, :, h * HD : (h + 1) * HD] = (total[:, :HD] / norm).astype(out_ref.dtype)
        lse = total[:, HD + 1 : HD + 2] + jnp.log(norm)
        hi, mid, low = split3(-lse)
        q2 = q.astype(jnp.float32)
        q2 = jnp.where(lane == lse_lane, hi, q2)
        q2 = jnp.where(lane == lse_lane + 1, mid, q2)
        q2 = jnp.where(lane == lse_lane + 2, low, q2)
        q2_ref[0, h] = q2.astype(jnp.bfloat16)


def plain_attend(qkv, halo, augk, augq, heads):
    seqs, rows, cols = qkv.shape
    ext = augk.shape[1]
    return pl.pallas_call(
        functools.partial(plain_attend_kernel, heads),
        grid=(seqs, rows // BLK),
        in_specs=[
            pl.BlockSpec((1, rows, cols), lambda s, i: (s, 0, 0)),
            pl.BlockSpec((1, WINDOW, heads * 2 * HD), lambda s, i: (s, 0, 0)),
            pl.BlockSpec((1, ext, HD), lambda s, i: (s, 0, 0)),
            pl.BlockSpec((1, BLK, HD), lambda s, i: (s, i, 0)),
        ],
        out_specs=[
            pl.BlockSpec((1, BLK, heads * HD), lambda s, i: (s, i, 0)),
            pl.BlockSpec((1, heads, BLK, 2 * HD), lambda s, i: (s, 0, i, 0)),
        ],
        out_shape=[
            jax.ShapeDtypeStruct((seqs, rows, heads * HD), jnp.bfloat16),
            jax.ShapeDtypeStruct((seqs, heads, rows, 2 * HD), jnp.bfloat16),
        ],
        scratch_shapes=[
            pltpu.VMEM((heads, ext, 2 * HD), jnp.bfloat16),
            pltpu.VMEM((heads, ext, 2 * HD), jnp.bfloat16),
            pltpu.VMEM((heads, 2 * HD, ext), jnp.bfloat16),
        ],
        compiler_params=pltpu.CompilerParams(vmem_limit_bytes=48 * 2**20),
        name="plain_attend",
    )(qkv, halo, augk, augq)


def from_behind(block, axis, distance):
    devices = range(lax.axis_size(axis))
    route = [(i - distance, i) for i in devices if i - distance in devices]
    return lax.ppermute(block, axis, route)


def pack_columns(array, heads):
    parts = array.reshape(array.shape[:-1] + (heads, 3 * HD))
    lead = array.shape[:-1]
    return jnp.concatenate(
        [parts[..., HD:].reshape(lead + (-1,)), parts[..., :HD].reshape(lead + (-1,))], axis=-1
    )


def unpack_columns(array, heads):
    lead = array.shape[:-1]
    pairs = array[..., : heads * 2 * HD].reshape(lead + (heads, 2 * HD))
    queries = array[..., heads * 2 * HD :].reshape(lead + (heads, HD))
    return jnp.concatenate([queries, pairs], axis=-1).reshape(lead + (-1,))


def dot(subscripts, a, b):
    return jnp.einsum(subscripts, a, b, preferred_element_type=jnp.float32)


def general_body(
    inputs, cotangent, segment_ids, norm1_gain, norm1_bias, qkv_weight, qv_bias, out_weight, out_bias,
    norm2_gain, norm2_bias, fc_weight, fc_bias, proj_weight, proj_bias,
):
    group = lax.axis_size("fsdp")
    seqs, local_rows, width = inputs.shape
    part_rows = local_rows * group
    heads = qkv_weight.shape[1] // (3 * HD)
    docs = segment_ids.shape[1] // (2 * WINDOW)
    seq_index = lax.axis_index("seq")
    shard = norm1_gain.shape[0]

    small = jnp.concatenate([norm1_gain, norm1_bias, out_bias, norm2_gain, norm2_bias, proj_bias, fc_bias])
    small = lax.all_gather(small, "fsdp")
    gain1, offset1, out_off, gain2, offset2, proj_off = (
        small[:, i * shard : (i + 1) * shard].reshape(-1).astype(jnp.float32) for i in range(6)
    )
    fc_off = small[:, 6 * shard :].reshape(-1).astype(jnp.float32)
    out_all = lax.all_gather(out_weight, "fsdp", axis=0, tiled=True)
    fc_all = lax.all_gather(fc_weight, "fsdp")
    proj_all = lax.all_gather(proj_weight, "fsdp")

    padded_ids = jnp.concatenate([jnp.full((seqs, WINDOW), -1, jnp.int32), segment_ids], axis=1)
    segment_ext = lax.dynamic_slice_in_dim(padded_ids, seq_index * part_rows, WINDOW + part_rows, 1)
    augk, augq = mask_features(segment_ext, docs)

    x = inputs.astype(jnp.float32)
    z1, rate1 = standardize(x)
    normed1 = (z1 * gain1 + offset1).astype(jnp.bfloat16)
    normed1 = lax.all_gather(normed1, "fsdp", axis=1, tiled=True)
    packed_weight = pack_columns(qkv_weight, heads)
    head_bias = qv_bias.astype(jnp.float32)
    head_bias = jnp.concatenate(
        [head_bias[:, :HD], jnp.zeros((heads, HD), jnp.float32), head_bias[:, HD:]], axis=1
    ).reshape(-1)
    packed_bias = pack_columns(head_bias, heads)
    qkv = (dot("sre,ef->srf", normed1, packed_weight) + packed_bias).astype(jnp.bfloat16)
    halo = from_behind(qkv[:, part_rows - WINDOW :, : heads * 2 * HD], "seq", 1)
    head_out, q2 = plain_attend(qkv, halo, augk, augq, heads)
    merged = lax.all_to_all(head_out, "fsdp", split_axis=1, concat_axis=2, tiled=True)
    resid = x + dot("sre,ef->srf", merged, out_all) + out_off
    z2, rate2 = standardize(resid)
    normed2 = (z2 * gain2 + offset2).astype(jnp.bfloat16)
    fc_offset = fc_off.reshape(group, -1)
    hidden = dot("sre,gef->gsrf", normed2, fc_all) + fc_offset[:, None, None]
    active, gelu_back = jax.vjp(lambda v: jax.nn.gelu(v, approximate=True), hidden)
    active = active.astype(jnp.bfloat16)
    layer_output = (resid + dot("gsrf,gfd->srd", active, proj_all) + proj_off).astype(jnp.bfloat16)

    cot32 = cotangent.astype(jnp.float32)
    proj_bias_part = jnp.sum(cot32, axis=(0, 1))
    proj_weight_part = dot("gsrf,srd->gfd", active, cotangent)
    g_hidden = gelu_back(dot("srd,gfd->gsrf", cotangent, proj_all))[0].astype(jnp.bfloat16)
    fc_bias_part = jnp.sum(g_hidden, axis=(1, 2), dtype=jnp.float32).reshape(-1)
    fc_weight_part = dot("sre,gsrf->gef", normed2, g_hidden)
    g_norm2 = dot("gsrf,gef->sre", g_hidden, fc_all)
    gain2_part = jnp.sum(g_norm2 * z2, axis=(0, 1))
    offset2_part = jnp.sum(g_norm2, axis=(0, 1))
    g_resid = cot32 + norm_grad(g_norm2 * gain2, z2, rate2)
    g_attn = g_resid.astype(jnp.bfloat16)
    out_bias_part = jnp.sum(g_attn, axis=(0, 1), dtype=jnp.float32)
    out_weight_part = dot("sre,srd->ed", merged, g_attn)
    g_merged = dot("srd,ed->sre", g_attn, out_all).astype(jnp.bfloat16)
    g_heads = lax.all_to_all(g_merged, "fsdp", split_axis=2, concat_axis=1, tiled=True)

    low = jnp.bfloat16
    fc_grad = lax.psum_scatter(fc_weight_part.astype(low), "fsdp")
    proj_grad = lax.psum_scatter(proj_weight_part.astype(low), "fsdp")
    out_grad = lax.psum_scatter(out_weight_part.astype(low), "fsdp", scatter_dimension=0, tiled=True)
    fc_grad, proj_grad, out_grad = lax.psum((fc_grad, proj_grad, out_grad), "seq")

    dq, dkv, dhalo = attend_back(qkv, halo, augk, q2, head_out, g_heads, heads)
    edge = from_behind(dhalo, "seq", -1)
    edge = jnp.pad(edge.astype(jnp.float32), ((0, 0), (part_rows - WINDOW, 0), (0, 0)))
    g_qkv = jnp.concatenate([(dkv + edge).astype(jnp.bfloat16), dq], axis=-1)
    qkv_grad = dot("sre,srf->ef", normed1, g_qkv)
    qkv_colsum = jnp.sum(g_qkv, axis=(0, 1), dtype=jnp.float32)
    g_norm1 = dot("srf,ef->sre", g_qkv, packed_weight).astype(jnp.bfloat16)
    g_norm1 = lax.psum_scatter(g_norm1, "fsdp", scatter_dimension=1, tiled=True).astype(jnp.float32)
    gain1_part = jnp.sum(g_norm1 * z1, axis=(0, 1))
    offset1_part = jnp.sum(g_norm1, axis=(0, 1))
    input_grad = (g_resid + norm_grad(g_norm1 * gain1, z1, rate1)).astype(jnp.bfloat16)

    qkv_grad = lax.psum(qkv_grad.astype(low), "seq").astype(jnp.float32)
    qkv_grad = unpack_columns(qkv_grad, heads)
    col = unpack_columns(qkv_colsum, heads).reshape(heads, 3 * HD)
    col = lax.psum(jnp.concatenate([col[:, :HD], col[:, 2 * HD :]], axis=1), "seq")
    vectors = jnp.concatenate(
        [
            v.reshape(group, -1)
            for v in (gain1_part, offset1_part, out_bias_part, gain2_part, offset2_part, proj_bias_part, fc_bias_part)
        ],
        axis=1,
    )
    vectors = lax.psum_scatter(vectors, "fsdp")
    vectors = lax.psum(vectors, "seq")
    parts = [vectors[i * shard : (i + 1) * shard] for i in range(6)] + [vectors[6 * shard :]]
    f32 = jnp.float32
    return (
        layer_output, input_grad, parts[0], parts[1], qkv_grad, col, out_grad.astype(f32), parts[2], parts[3],
        parts[4], fc_grad.astype(f32), parts[6], proj_grad.astype(f32), parts[5],
    )


def cube_body(
    inputs, cotangent, segment_ids, norm1_gain, norm1_bias, qkv_weight, qv_bias, out_weight, out_bias,
    norm2_gain, norm2_bias, fc_weight, fc_bias, proj_weight, proj_bias,
):
    group = lax.axis_size("fsdp")
    seqs, local_rows, width = inputs.shape
    part_rows = local_rows * group
    heads = qkv_weight.shape[1] // (3 * HD)
    docs = segment_ids.shape[1] // (2 * WINDOW)
    seq_index = lax.axis_index("seq")
    me = lax.axis_index("fsdp")
    shard = norm1_gain.shape[0]
    f32, low = jnp.float32, jnp.bfloat16

    small = jnp.concatenate([norm1_gain, norm1_bias, out_bias, norm2_gain, norm2_bias, proj_bias, fc_bias])
    small = jnp.pad(small, (0, 16 * shard - small.shape[0])).reshape(16, shard)
    padded_ids = jnp.concatenate([jnp.full((seqs, WINDOW), -1, jnp.int32), segment_ids], axis=1)
    segment_ext = lax.dynamic_slice_in_dim(padded_ids, seq_index * part_rows, WINDOW + part_rows, 1)
    augk, augq = mask_features(segment_ext, docs)
    packed_weight = pack_columns(qkv_weight, heads)
    head_bias = qv_bias.astype(f32)
    head_bias = jnp.concatenate(
        [head_bias[:, :HD], jnp.zeros((heads, HD), f32), head_bias[:, HD:]], axis=1
    ).reshape(-1)
    packed_bias = pack_columns(head_bias, heads)

    x = inputs.reshape(seqs * local_rows, width)
    cot = cotangent.reshape(seqs * local_rows, width)
    all_small, normed1, qkv = gather_project(x, small, packed_weight, packed_bias[None], group)
    head_out, q2, halo, merged, out_all, fc_near, proj_near = attend(
        qkv, augk, augq, out_weight, fc_weight, proj_weight, heads, group
    )
    full = lambda i: all_small[:, i].reshape(-1).astype(f32)
    gain1 = full(0)
    vectors = jnp.stack([full(2), full(3), full(4), full(5)] + [jnp.zeros((width,), f32)] * 4)
    slots = jnp.stack([xor(me, r, group) for r in SLOT_AT])
    fc_off = jnp.take(all_small[:, 6:10].reshape(group, -1), slots, axis=0).astype(f32)[:, None]
    layer_output, g_resid, g_heads, kept, out_kept, gvec, gfcb = feed_forward(
        x, cot, merged.reshape(x.shape), out_all.reshape(width, width), fc_near, proj_near, fc_off, vectors
    )
    dq, dkv, dhalo = attend_back(qkv, halo, augk, q2, head_out, g_heads, heads)

    def swap(v, bit):
        return lax.ppermute(v, "fsdp", [(i, i ^ bit) for i in range(group)])

    def add(u, v):
        return (u.astype(f32) + v.astype(f32)).astype(low)

    def scatter(first, second, s2, s4, s0, s6):
        r2, r6 = swap(s2, first), swap(s6, first)
        return add(add(s0, r2), swap(add(s4, r6), second))

    f2, f4, f0, f6 = (kept[i, 0] for i in range(4))
    p2, p4, p0, p6 = (kept[i, 1] for i in range(4))
    fc_grad = scatter(2, 4, f2, f4, f0, f6)
    proj_grad = scatter(4, 2, p4, p2, p0, p6)
    out_grad = scatter(2, 4, out_kept[1], out_kept[2], out_kept[0], out_kept[3])
    w = proj_grad.shape[1]
    proj_grad = jnp.concatenate([proj_grad[: proj_grad.shape[0] // 2], proj_grad[proj_grad.shape[0] // 2 :]], axis=1)
    fc_grad, proj_grad, out_grad = lax.psum((fc_grad, proj_grad, out_grad), "seq")

    edge = from_behind(dhalo, "seq", -1)
    edge = jnp.pad(edge.astype(f32), ((0, 0), (part_rows - WINDOW, 0), (0, 0)))
    g_qkv = jnp.concatenate([(dkv + edge).astype(low), dq], axis=-1)
    qkv_colsum = jnp.sum(g_qkv, axis=(0, 1), dtype=f32)
    g_norm1 = dot("srf,ef->sre", g_qkv, packed_weight).astype(low)
    g_norm1 = lax.psum_scatter(g_norm1, "fsdp", scatter_dimension=1, tiled=True).astype(f32)
    qkv_grad = dot("fsre,sfrc->ec", normed1, g_qkv.reshape(seqs, group, local_rows, -1))
    z1, rate1 = standardize(inputs.astype(f32))
    gain1_part = jnp.sum(g_norm1 * z1, axis=(0, 1))
    offset1_part = jnp.sum(g_norm1, axis=(0, 1))
    g_resid = g_resid.reshape(inputs.shape)
    input_grad = (g_resid + norm_grad(g_norm1 * gain1, z1, rate1)).astype(low)
    qkv_grad = lax.psum(qkv_grad.astype(low), "seq").astype(f32)
    qkv_grad = unpack_columns(qkv_grad, heads)
    col = unpack_columns(qkv_colsum, heads).reshape(heads, 3 * HD)
    col = lax.psum(jnp.concatenate([col[:, :HD], col[:, 2 * HD :]], axis=1), "seq")
    back = jnp.zeros((group, fc_bias.shape[0]), f32).at[slots].set(gfcb[:, 0])
    vecs = jnp.concatenate(
        [v.reshape(group, -1) for v in (gain1_part, offset1_part, gvec[0], gvec[1], gvec[2], gvec[3], back)], axis=1
    )
    vecs = lax.psum(lax.psum_scatter(vecs, "fsdp"), "seq")
    parts = [vecs[i * shard : (i + 1) * shard] for i in range(6)] + [vecs[6 * shard :]]
    return (
        layer_output.reshape(inputs.shape), input_grad, parts[0], parts[1], qkv_grad, col, out_grad.astype(f32),
        parts[2], parts[3], parts[4], fc_grad.astype(f32), parts[6], proj_grad.astype(f32), parts[5],
    )


def solution(mesh):
    tokens = P(None, ("seq", "fsdp"), None)
    rows, cols, vec = P("fsdp", None), P(None, "fsdp"), P("fsdp")
    return jax.shard_map(
        cube_body if mesh.shape["fsdp"] == 8 and mesh.shape["seq"] == 4 else general_body,
        mesh=mesh,
        in_specs=(tokens, tokens, P(), vec, vec, cols, rows, rows, vec, vec, vec, cols, vec, rows, vec),
        out_specs=(tokens, tokens, vec, vec, cols, rows, rows, vec, vec, vec, cols, vec, rows, vec),
        check_vma=False,
    )
```

```python
import functools
import math

import jax
import jax.numpy as jnp
from jax import lax
from jax.experimental import pallas as pl
from jax.experimental.pallas import tpu as pltpu
from jax.sharding import PartitionSpec as P


def standardize(values):
    centre = values - jnp.mean(values, axis=-1, keepdims=True)
    spread = jnp.mean(centre * centre, axis=-1, keepdims=True)
    rate = lax.rsqrt(spread + norm_eps)
    return centre * rate, rate


def norm_grad(direction, z, rate):
    mean_d = jnp.mean(direction, axis=-1, keepdims=True)
    mean_dz = jnp.mean(direction * z, axis=-1, keepdims=True)
    return rate * (direction - mean_d - z * mean_dz)


norm_eps = 1e-05

HD = 64
WINDOW = 1024
BLK = 256
PENALTY = 1e30


def nt(a, b):
    return lax.dot_general(a, b, (((1,), (1,)), ((), ())), preferred_element_type=jnp.float32)


def nn(a, b):
    return lax.dot_general(a, b, (((1,), (0,)), ((), ())), preferred_element_type=jnp.float32)


def tn(a, b):
    return lax.dot_general(a, b, (((0,), (0,)), ((), ())), preferred_element_type=jnp.float32)


def split3(v):
    hi = v.astype(jnp.bfloat16).astype(jnp.float32)
    rest = v - hi
    mid = rest.astype(jnp.bfloat16).astype(jnp.float32)
    return hi, mid, rest - mid


def merge_edges(mask, tiles):
    return [jnp.where(mask, tiles[0], tiles[-1])] + tiles[1:-1]


def spread_edges(mask, tiles):
    zero = jnp.zeros_like(tiles[0])
    return [jnp.where(mask, tiles[0], zero)] + tiles[1:] + [jnp.where(mask, zero, tiles[0])]


def edge_mask():
    rows = lax.broadcasted_iota(jnp.int32, (BLK, BLK), 0)
    cols = lax.broadcasted_iota(jnp.int32, (BLK, BLK), 1)
    return rows > cols


def xor(a, b, size):
    total, bit = 0, 1
    while bit < size:
        total = total + bit * lax.rem(lax.div(a, bit) + lax.div(b, bit), 2)
        bit *= 2
    return total


MESH = pl.DeviceIdType.MESH
SLOT_AT = (3, 2, 5, 4, 1, 0, 7, 6)
STEP_OF = tuple(SLOT_AT.index(r) for r in range(8))
NEAR = 6


def enter(peers):
    barrier = pltpu.get_barrier_semaphore()
    for peer in peers:
        pl.semaphore_signal(barrier, inc=1, device_id={"fsdp": peer}, device_id_type=MESH)
    pl.semaphore_wait(barrier, len(peers))


def attend_kernel(
    heads, group, qkv_ref, augk_ref, augq_ref, out_w, fc_w, proj_w,
    out_ref, q2_ref, halo_ref, merged_ref, out_all, fc_all, proj_all,
    keys, values, values_t, sent, behind, own_sems, send_sems, recv_sems, halo_sems, w_own, w_send, w_recv,
):
    step = pl.program_id(0)
    last = pl.num_programs(0) - 1
    me = lax.axis_index("fsdp")
    line = lax.axis_index("seq")
    line_end = lax.axis_size("seq") - 1
    at = [xor(me, k, group) for k in range(group)]
    seqs, rows = qkv_ref.shape[0], qkv_ref.shape[1]
    half = group // 2
    seq = lax.rem(lax.div(step, half), 2)
    lower = lax.div(step, group)
    place = (1 - lower) * half + lax.rem(step + me, half)
    width = heads * 2 * HD
    low = jnp.bfloat16

    def halo_copy():
        return pltpu.make_async_remote_copy(
            src_ref=qkv_ref.at[:, pl.ds(rows - WINDOW, WINDOW), pl.ds(0, width)],
            dst_ref=behind, send_sem=halo_sems.at[0], recv_sem=halo_sems.at[1],
            device_id={"seq": lax.rem(line + 1, line_end + 1)}, device_id_type=MESH,
        )

    weights = ((out_w, out_all, False), (fc_w, fc_all, True), (proj_w, proj_all, True))

    def slot(a, r):
        return weights[a][1].at[STEP_OF[r] if weights[a][2] else r]

    def w_copy(a, r, second=False):
        to = at[1] if r % 2 else at[r]
        src = weights[a][0] if r in (1, 2, 4) else slot(a, r - 1) if r % 2 else None
        dst, sem = slot(a, r), r
        if r == 6:
            size = weights[a][0].shape[0] // 2
            part = pl.ds(size if second else 0, size)
            src = slot(a, 4 if second else 2).at[part]
            to = at[2] if second else at[4]
            dst, sem = dst.at[part], 0 if second else 6
        return pltpu.make_async_remote_copy(
            src_ref=src, dst_ref=dst, send_sem=w_send.at[a, sem], recv_sem=w_recv.at[a, sem],
            device_id={"fsdp": to}, device_id_type=MESH,
        )

    def w_keep(a):
        return pltpu.make_async_copy(weights[a][0], slot(a, 0), w_own.at[a])

    def forward(a):
        w_copy(a, 2).wait_recv()
        w_copy(a, 3).start()
        w_copy(a, 4).wait_recv()
        w_copy(a, 5).start()
        if not weights[a][2]:
            w_copy(a, 6).start()
            w_copy(a, 6, True).start()

    @pl.when(step == 0)
    def _():
        barrier = pltpu.get_barrier_semaphore()
        for peer in at[1:]:
            pl.semaphore_signal(barrier, inc=1, device_id={"fsdp": peer}, device_id_type=MESH)

        pl.semaphore_signal(
            barrier, inc=1, device_id={"seq": lax.rem(line + line_end, line_end + 1)}, device_id_type=MESH
        )
        pl.semaphore_wait(barrier, group)

        @pl.when(line < line_end)
        def _():
            halo_copy().start()

        for a in range(3):
            for r in (2, 4, 1):
                w_copy(a, r).start()
            w_keep(a).start()
        for s in range(seqs):
            fill_keys(s, heads, qkv_ref, augk_ref, WINDOW, keys, values, values_t, None)

    @pl.when(step == group)
    def _():
        @pl.when(line > 0)
        def _():
            halo_copy().wait_recv()

        @pl.when(line == 0)
        def _():
            behind[...] = jnp.zeros_like(behind)

        halo_ref[...] = behind[...]
        for s in range(seqs):
            fill_keys(s, heads, behind, augk_ref, 0, keys, values, values_t, None)

    mask = edge_mask()
    tiles = WINDOW // BLK + 1
    start = pl.multiple_of(place * BLK, BLK)
    lane = lax.broadcasted_iota(jnp.int32, (BLK, 2 * HD), 1)
    lse_lane = augq_ref.shape[2] + HD - 3
    slot_k = xor(me, place, group)
    spans = [pl.ds(pl.multiple_of(start + b * BLK, BLK), BLK) for b in range(tiles)]
    for h in range(heads):
        sh = seq * heads + h
        qc = heads * 2 * HD + h * HD
        q = jnp.concatenate(
            [qkv_ref[seq, pl.ds(start, BLK), qc : qc + HD] * 0.125, augq_ref[seq, pl.ds(start, BLK), :]], axis=1
        )
        scores = merge_edges(mask, [nt(keys[sh, s, :], q) for s in spans])
        peak = functools.reduce(jnp.maximum, scores)
        peak = jnp.max(peak, axis=0, keepdims=True)
        weights_ = spread_edges(mask, [jnp.exp(s - peak).astype(low) for s in scores])
        total = sum(nn(values_t[sh, :, s], w) for s, w in zip(spans, weights_))
        sub = lax.broadcasted_iota(jnp.int32, total.shape, 0)
        total = jnp.where(sub == HD + 1, peak, total).T
        norm = total[:, HD : HD + 1]
        part = (total[:, :HD] / norm).astype(low)
        out_ref[seq, pl.ds(start, BLK), h * HD : (h + 1) * HD] = part
        sent[step, :, h * HD : (h + 1) * HD] = part
        lse = total[:, HD + 1 : HD + 2] + jnp.log(norm)
        hi, mid, lo = split3(-lse)
        q2 = q.astype(jnp.float32)
        q2 = jnp.where(lane == lse_lane, hi, q2)
        q2 = jnp.where(lane == lse_lane + 1, mid, q2)
        q2 = jnp.where(lane == lse_lane + 2, lo, q2)
        q2_ref[seq, h, pl.ds(start, BLK), :] = q2.astype(low)

    span = sent.shape[2]

    def landing(s, k):
        return merged_ref.at[s, :, pl.ds(pl.multiple_of(k * span, span), span)]

    def own(s):
        return pltpu.make_async_copy(sent.at[step], landing(s, 0), own_sems.at[s])

    def away(s, k, to):
        return pltpu.make_async_remote_copy(
            src_ref=sent.at[step], dst_ref=landing(s, k), send_sem=send_sems.at[s, k], recv_sem=recv_sems.at[s, k],
            device_id={"fsdp": to}, device_id_type=MESH,
        )

    @pl.when(place == me)
    def _():
        own(seq).start()

    @pl.when(place != me)
    def _():
        away(seq, slot_k, place).start()

    @pl.when(step == last - 3)
    def _():
        forward(0)

    @pl.when(step == last - 1)
    def _():
        forward(1)

    @pl.when(step == last)
    def _():
        forward(2)
        w_copy(0, 6).wait_recv()
        w_copy(0, 6, True).wait_recv()
        w_copy(0, 7).start()
        for s in range(seqs):
            own(s).wait()
            for k in range(1, group):
                away(s, k, at[k]).wait()
        for a in range(3):
            w_keep(a).wait()
            for r in (1, 2, 3, 4, 5):
                w_copy(a, r).wait_send()
            for r in (1, 3, 5):
                w_copy(a, r).wait_recv()
        w_copy(0, 6).wait_send()
        w_copy(0, 6, True).wait_send()
        w_copy(0, 7).wait()

        @pl.when(line < line_end)
        def _():
            halo_copy().wait_send()


def fill_keys(s, heads, source, augk_ref, base, keys, values, values_t, keys_t):
    size = BLK
    ones = jnp.ones((size, HD), jnp.bfloat16)
    first = source.shape[1] - WINDOW if base == 0 else 0
    for h in range(heads):
        c = h * 2 * HD
        for i in range(source.shape[1] // size):
            pair = source[s, i * size : (i + 1) * size, c : c + 2 * HD]
            span = slice(base + i * size, base + (i + 1) * size)
            k = jnp.concatenate([pair[:, :HD], augk_ref[s, span, :]], axis=1)
            v = jnp.concatenate([pair[:, HD:], ones], axis=1)
            keys[s * heads + h, span, :] = k
            values[s * heads + h, span, :] = v
            if values_t is not None:
                values_t[s * heads + h, :, span] = v.T
            if keys_t is not None:
                keys_t[s * heads + h, :, span] = k.T


def attend(qkv, augk, augq, out_w, fc_w, proj_w, heads, group):
    seqs, rows, cols = qkv.shape
    ext = augk.shape[1]
    assert rows // BLK == group
    low = jnp.bfloat16
    vmem = pl.BlockSpec(memory_space=pltpu.VMEM)
    hbm = pl.BlockSpec(memory_space=pl.ANY)
    every = seqs * heads
    return pl.pallas_call(
        functools.partial(attend_kernel, heads, group),
        grid=(seqs * rows // BLK,),
        in_specs=[vmem] * 3 + [hbm] * 3,
        out_specs=[vmem] * 3 + [hbm] * 4,
        out_shape=[
            jax.ShapeDtypeStruct((seqs, rows, heads * HD), low),
            jax.ShapeDtypeStruct((seqs, heads, rows, 2 * HD), low),
            jax.ShapeDtypeStruct((seqs, WINDOW, heads * 2 * HD), low),
            jax.ShapeDtypeStruct((seqs, BLK, group * heads * HD), low),
        ]
        + [jax.ShapeDtypeStruct((n,) + w.shape, low) for n, w in ((group, out_w), (NEAR, fc_w), (NEAR, proj_w))],
        scratch_shapes=[
            pltpu.VMEM((every, ext, 2 * HD), low),
            pltpu.VMEM((every, ext, 2 * HD), low),
            pltpu.VMEM((every, 2 * HD, ext), low),
            pltpu.VMEM((seqs * rows // BLK, BLK, heads * HD), low),
            pltpu.VMEM((seqs, WINDOW, heads * 2 * HD), low),
            pltpu.SemaphoreType.DMA((seqs,)),
            pltpu.SemaphoreType.DMA((seqs, group)),
            pltpu.SemaphoreType.DMA((seqs, group)),
            pltpu.SemaphoreType.DMA((2,)),
            pltpu.SemaphoreType.DMA((3,)),
            pltpu.SemaphoreType.DMA((3, group)),
            pltpu.SemaphoreType.DMA((3, group)),
        ],
        compiler_params=pltpu.CompilerParams(vmem_limit_bytes=56 * 2**20, collective_id=1, has_side_effects=True),
        name="attend",
    )(qkv, augk, augq, out_w, fc_w, proj_w)


def mask_features(segment_ext, docs):
    doc = jnp.arange(docs, dtype=jnp.int32)
    hot = (segment_ext[..., None] == doc).astype(jnp.bfloat16)
    rows = segment_ext.shape[1]
    outside = (segment_ext < 0).astype(jnp.bfloat16)[..., None]
    pad = HD - docs - 4
    one = jnp.ones(segment_ext.shape + (3,), jnp.bfloat16)
    zero = jnp.zeros(segment_ext.shape + (pad,), jnp.bfloat16)
    keys = jnp.concatenate([-hot, -outside, zero, one], axis=-1)
    own = hot[:, WINDOW:]
    queries = jnp.concatenate(
        [
            (1 - own) * jnp.bfloat16(PENALTY),
            jnp.full(own.shape[:2] + (1,), PENALTY, jnp.bfloat16),
            jnp.zeros(own.shape[:2] + (pad + 3,), jnp.bfloat16),
        ],
        axis=-1,
    )
    return keys, queries


def gather_project_kernel(
    x_ref, small_ref, w_ref, b_ref, all_small_ref, pieces_out, qkv_ref,
    z1, pieces, smalls, small_send, small_recv, send_sems, recv_sems, out_sems,
):
    group = all_small_ref.shape[0]
    me = lax.axis_index("fsdp")
    at = [xor(me, k, group) for k in range(group)]
    rows = x_ref.shape[0] // 2
    f32, low = jnp.float32, jnp.bfloat16
    enter(at[1:])

    def small_copy(k):
        return pltpu.make_async_remote_copy(
            src_ref=small_ref, dst_ref=smalls.at[me], send_sem=small_send.at[k], recv_sem=small_recv.at[k],
            device_id={"fsdp": at[k]}, device_id_type=MESH,
        )

    for k in range(1, group):
        small_copy(k).start()
    smalls[me] = small_ref[...]

    def chunk(p, s):
        return pieces.at[p, s]

    def move(r, s):
        if r % 2:
            piece, to = at[r - 1], at[1]
        elif r == 6:
            piece, to = (at[2], at[4]) if s == 0 else (at[4], at[2])
        else:
            piece, to = me, at[r]
        return pltpu.make_async_remote_copy(
            src_ref=chunk(piece, s), dst_ref=chunk(piece, s), send_sem=send_sems.at[r, s], recv_sem=recv_sems.at[r, s],
            device_id={"fsdp": to}, device_id_type=MESH,
        )

    def keep(k, s):
        return pltpu.make_async_copy(chunk(at[k], s), pieces_out.at[s, pl.ds(pl.multiple_of(at[k] * rows, rows), rows)], out_sems.at[k, s])

    def project(k, s):
        keep(k, s).start()
        start = pl.multiple_of(at[k] * rows, rows)
        qkv_ref[s, pl.ds(start, rows), :] = (nn(pieces[at[k], s], w_ref[...]) + b_ref[...]).astype(low)

    for s in range(2):
        z1[s * rows : (s + 1) * rows, :] = standardize(x_ref[s * rows : (s + 1) * rows, :].astype(f32))[0]
    for k in range(1, group):
        small_copy(k).wait()
    gain = jnp.concatenate([smalls[f, 0:1, :] for f in range(group)], axis=1).astype(f32)
    offset = jnp.concatenate([smalls[f, 1:2, :] for f in range(group)], axis=1).astype(f32)
    for s in range(2):
        pieces[me, s] = (z1[s * rows : (s + 1) * rows, :] * gain + offset).astype(low)
        move(2, s).start()
        move(4, s).start()
        move(1, s).start()
    all_small_ref[...] = smalls[...]
    for s in range(2):
        project(0, s)
    for s in range(2):
        move(1, s).wait_recv()
        project(1, s)
    for s in range(2):
        move(2, s).wait_recv()
        if s == 0:
            move(6, 0).start()
        move(3, s).start()
        move(4, s).wait_recv()
        if s == 1:
            move(6, 1).start()
        move(5, s).start()
        project(2, s)
        project(4, s)
    for s in range(2):
        move(3, s).wait_recv()
        project(3, s)
        move(5, s).wait_recv()
        project(5, s)
    for s in range(2):
        move(6, s).wait_recv()
        move(7, s).start()
        project(6, s)
    for s in range(2):
        move(7, s).wait_recv()
        project(7, s)
    for s in range(2):
        for r in range(1, group):
            move(r, s).wait_send()
        for k in range(group):
            keep(k, s).wait()


def gather_project(x, small, weight, bias, group):
    rows, width = x.shape
    cols = weight.shape[1]
    half = rows // 2
    vmem = pl.BlockSpec(memory_space=pltpu.VMEM)
    low = jnp.bfloat16
    return pl.pallas_call(
        gather_project_kernel,
        in_specs=[vmem] * 4,
        out_specs=[vmem, pl.BlockSpec(memory_space=pl.ANY), vmem],
        out_shape=[
            jax.ShapeDtypeStruct((group,) + small.shape, low),
            jax.ShapeDtypeStruct((2, group * half, width), low),
            jax.ShapeDtypeStruct((2, group * half, cols), low),
        ],
        scratch_shapes=[
            pltpu.VMEM((rows, width), jnp.float32),
            pltpu.VMEM((group, 2, half, width), low),
            pltpu.VMEM((group,) + small.shape, low),
            pltpu.SemaphoreType.DMA((group,)),
            pltpu.SemaphoreType.DMA((group,)),
            pltpu.SemaphoreType.DMA((group, 2)),
            pltpu.SemaphoreType.DMA((group, 2)),
            pltpu.SemaphoreType.DMA((group, 2)),
        ],
        compiler_params=pltpu.CompilerParams(
            vmem_limit_bytes=48 * 2**20, collective_id=2, has_side_effects=True
        ),
        name="gather_project",
    )(x, small, weight, bias)


def gelu_both(v):
    c = math.sqrt(2.0 / math.pi)
    square = v * v
    t = jnp.tanh(v * (c + (c * 0.044715) * square))
    half = 0.5 * (1.0 + t)
    slope = half + (0.5 * v) * (1.0 - t * t) * (c + (3.0 * 0.044715 * c) * square)
    return v * half, slope


def column_sums(array):
    return jnp.sum(array, axis=0, keepdims=True)


def feed_forward_kernel(
    group, x_ref, cot_ref, merged_ref, out_ref, fc_near, proj_near, fcb_ref, vec_ref,
    layer_ref, gres_ref, gheads_ref, keep_ref, side_ref, gout_ref, gvec_ref, gfcb_ref,
    resid, z2, rate, normed, total, gnormed, fc_w, proj_w, given, taken, gmerged, gout_given, gout_taken,
    load_sems, far_send, far_recv, pair_send, pair_recv, side_send, side_recv, keep_sems, head_send, head_recv,
    own_sem, gout_sems,
):
    step = pl.program_id(0)
    last = group - 1
    me = lax.axis_index("fsdp")
    at = [xor(me, k, group) for k in range(group)]
    rows = x_ref.shape[0]
    block = rows // 2
    f32, low = jnp.float32, jnp.bfloat16
    span = merged_ref.shape[1] // group

    def load(a, i):
        near, here = ((fc_near, fc_w), (proj_near, proj_w))[a]
        return pltpu.make_async_copy(near.at[i], here.at[lax.rem(i, 2)], load_sems.at[a, lax.rem(i, 2)])

    def far_copy(a, way):
        near, here = ((fc_near, fc_w), (proj_near, proj_w))[a]
        size = near.shape[1] // 2
        if way == 2:
            src, dst, to = here.at[3], here.at[2], at[1]
        else:
            part = pl.ds(way * size, size)
            src, dst = near.at[STEP_OF[(2, 4)[way]], part], here.at[3, part]
            to = at[(4, 2)[way]]
        return pltpu.make_async_remote_copy(
            src_ref=src, dst_ref=dst, send_sem=far_send.at[a, way], recv_sem=far_recv.at[a, way],
            device_id={"fsdp": to}, device_id_type=MESH,
        )

    def pair_copy(j):
        return pltpu.make_async_remote_copy(
            src_ref=given.at[lax.rem(j, 2)], dst_ref=taken.at[j], send_sem=pair_send.at[j], recv_sem=pair_recv.at[j],
            device_id={"fsdp": at[1]}, device_id_type=MESH,
        )

    def side_copy(a):
        return pltpu.make_async_remote_copy(
            src_ref=taken.at[a, a], dst_ref=side_ref.at[a], send_sem=side_send.at[a], recv_sem=side_recv.at[a],
            device_id={"fsdp": at[(2, 4)[a]]}, device_id_type=MESH,
        )

    def keep_copy(j):
        return pltpu.make_async_copy(taken.at[j], keep_ref.at[j], keep_sems.at[j])

    def head_copy(k):
        src = gmerged.at[:, :, pl.ds(k * span, span)]
        dst = gheads_ref.at[:, pl.ds(pl.multiple_of(me * block, block), block), :]
        if k == 0:
            return pltpu.make_async_copy(src, dst, own_sem)
        return pltpu.make_async_remote_copy(
            src_ref=src, dst_ref=dst, send_sem=head_send.at[k], recv_sem=head_recv.at[k],
            device_id={"fsdp": at[k]}, device_id_type=MESH,
        )

    def gout_copy():
        return pltpu.make_async_remote_copy(
            src_ref=gout_given, dst_ref=gout_taken, send_sem=gout_sems.at[0], recv_sem=gout_sems.at[1],
            device_id={"fsdp": at[1]}, device_id_type=MESH,
        )

    @pl.when(step == 0)
    def _():
        enter(at[1:])
        for a in range(2):
            load(a, 0).start()
        for a in range(2):
            far_copy(a, 0).start()
            far_copy(a, 1).start()
        acc = x_ref[...].astype(f32) + vec_ref[0:1, :] + nn(merged_ref[...], out_ref[...])
        resid[...] = acc
        z, r = standardize(acc)
        z2[...] = z
        rate[...] = jnp.broadcast_to(r, rate.shape)
        normed[...] = (z * vec_ref[1:2, :] + vec_ref[2:3, :]).astype(low)
        total[...] = jnp.zeros_like(total)
        gnormed[...] = jnp.zeros_like(gnormed)

    j = lax.div(step, 2)
    odd = lax.rem(step, 2)

    @pl.when(step < NEAR)
    def _():
        for a in range(2):
            load(a, step).wait()

    @pl.when(step + 1 < NEAR)
    def _():
        for a in range(2):
            load(a, step + 1).start()

    @pl.when(step == NEAR)
    def _():
        for a in range(2):
            far_copy(a, 2).wait_recv()

    @pl.when((odd == 0) & (j >= 2))
    def _():
        pair_copy(j - 2).wait_send()

    here = jnp.where(step < NEAR, lax.rem(step, 2), step - NEAR + 2)
    fresh = jnp.where(odd == 0, lax.rem(j, 2), 2)
    hidden = nn(normed[...], fc_w[here]) + fcb_ref[0]
    gactive = nt(cot_ref[...], proj_w[here])
    active, slope = gelu_both(hidden)
    active = active.astype(low)
    ghidden = gactive * slope
    gfcb_ref[0] = column_sums(ghidden)
    ghidden = ghidden.astype(low)
    total[...] += nn(active, proj_w[here])
    gnormed[...] += nt(ghidden, fc_w[here])
    given[fresh, 0] = tn(normed[...], ghidden).astype(low)
    gproj = tn(active, cot_ref[...]).astype(low)
    size, part = gproj.shape[0], fc_w.shape[2]
    for i in range(gproj.shape[1] // part):
        given[fresh, 1, i * size : (i + 1) * size, :] = gproj[:, i * part : (i + 1) * part]

    @pl.when(odd == 0)
    def _():
        pair_copy(j).start()

    @pl.when(odd == 1)
    def _():
        pair_copy(j).wait_recv()

        def add(i, _):
            part = pl.ds(pl.multiple_of(lax.rem(i, 8) * 128, 128), 128)
            a = lax.div(i, 8)
            taken[j, a, part, :] = (taken[j, a, part, :].astype(f32) + given[2, a, part, :].astype(f32)).astype(low)
            return 0

        lax.fori_loop(0, 16, add, 0)
        keep_copy(j).start()

    for a in range(2):
        @pl.when(step == 1 + 2 * a)
        def _(a=a):
            side_copy(a).start()

    @pl.when(step == 3)
    def _():
        for a in range(2):
            far_copy(a, 0).wait_recv()
            far_copy(a, 1).wait_recv()
            far_copy(a, 2).start()

    @pl.when(step == last)
    def _():
        cot32 = cot_ref[...].astype(f32)
        g, z = gnormed[...], z2[...]
        gres = cot32 + norm_grad(g * vec_ref[1:2, :], z, rate[:, :1])
        gres_ref[...] = gres
        gattn = gres.astype(low)
        back = nt(gattn, out_ref[...]).astype(low)
        for s in range(2):
            gmerged[s] = back[s * block : (s + 1) * block, :]
        for k in (6, 2, 4, 3, 5, 7, 1, 0):
            head_copy(k).start()
        gout = tn(merged_ref[...], gattn)
        for k in range(1, group, 2):
            gout_given[k // 2] = gout[k * span : (k + 1) * span, :].astype(low)
        gout_copy().start()
        layer_ref[...] = (resid[...] + total[...] + vec_ref[3:4, :]).astype(low)
        gvec_ref[0:1, :] = column_sums(gattn.astype(f32))
        gvec_ref[1:2, :] = column_sums(g * z)
        gvec_ref[2:3, :] = column_sums(g)
        gvec_ref[3:4, :] = column_sums(cot32)
        gout_copy().wait_recv()
        for k in range(0, group, 2):
            mine = gout[k * span : (k + 1) * span, :].astype(low).astype(f32)
            gout_ref[k // 2] = (mine + gout_taken[k // 2].astype(f32)).astype(low)
        for k in range(group):
            head_copy(k).wait()
        gout_copy().wait_send()
        for a in range(2):
            for way in range(3):
                far_copy(a, way).wait_send()
        pair_copy(2).wait_send()
        pair_copy(3).wait_send()
        side_copy(0).wait()
        side_copy(1).wait()
        for i in range(group // 2):
            keep_copy(i).wait()


def feed_forward(x, cot, merged, out_all, fc_near, proj_near, fc_bias, vectors):
    rows, width = x.shape
    group, part = fc_bias.shape[0], fc_near.shape[2]
    span = width // group
    f32, low = jnp.float32, jnp.bfloat16
    vmem = pl.BlockSpec(memory_space=pltpu.VMEM)
    hbm = pl.BlockSpec(memory_space=pl.ANY)
    return pl.pallas_call(
        functools.partial(feed_forward_kernel, group),
        grid=(group,),
        in_specs=[
            vmem, vmem, vmem, vmem,
            hbm, hbm,
            pl.BlockSpec((1, 1, part), lambda i: (i, 0, 0)),
            vmem,
        ],
        out_specs=[
            vmem, vmem, hbm,
            hbm, hbm, vmem, vmem,
            pl.BlockSpec((1, 1, part), lambda i: (i, 0, 0)),
        ],
        out_shape=[
            jax.ShapeDtypeStruct((rows, width), low),
            jax.ShapeDtypeStruct((rows, width), f32),
            jax.ShapeDtypeStruct((2, group * rows // 2, span), low),
            jax.ShapeDtypeStruct((group // 2, 2, width, part), low),
            jax.ShapeDtypeStruct((2, width, part), low),
            jax.ShapeDtypeStruct((group // 2, span, width), low),
            jax.ShapeDtypeStruct((8, width), f32),
            jax.ShapeDtypeStruct((group, 1, part), f32),
        ],
        scratch_shapes=[
            pltpu.VMEM((rows, width), f32),
            pltpu.VMEM((rows, width), f32),
            pltpu.VMEM((rows, 128), f32),
            pltpu.VMEM((rows, width), low),
            pltpu.VMEM((rows, width), f32),
            pltpu.VMEM((rows, width), f32),
            pltpu.VMEM((4, width, part), low),
            pltpu.VMEM((4, part, width), low),
            pltpu.VMEM((3, 2, width, part), low),
            pltpu.VMEM((group // 2, 2, width, part), low),
            pltpu.VMEM((2, rows // 2, width), low),
            pltpu.VMEM((group // 2, span, width), low),
            pltpu.VMEM((group // 2, span, width), low),
            pltpu.SemaphoreType.DMA((2, 2)),
            pltpu.SemaphoreType.DMA((2, 3)),
            pltpu.SemaphoreType.DMA((2, 3)),
            pltpu.SemaphoreType.DMA((group // 2,)),
            pltpu.SemaphoreType.DMA((group // 2,)),
            pltpu.SemaphoreType.DMA((2,)),
            pltpu.SemaphoreType.DMA((2,)),
            pltpu.SemaphoreType.DMA((group // 2,)),
            pltpu.SemaphoreType.DMA((group,)),
            pltpu.SemaphoreType.DMA((group,)),
            pltpu.SemaphoreType.DMA,
            pltpu.SemaphoreType.DMA((2,)),
        ],
        compiler_params=pltpu.CompilerParams(vmem_limit_bytes=62 * 2**20, collective_id=3, has_side_effects=True),
        name="feed_forward",
    )(x, cot, merged, out_all, fc_near, proj_near, fc_bias, vectors)


def attend_back_kernel(
    heads, group, qkv_ref, halo_ref, augk_ref, q2_ref, out_ref, grad_ref, kept, side, out_kept,
    gqkv_ref, sums_ref, out_sum_ref,
    keys, values, keys_t, dkeys, dvalues, edge, ahead, mid, near, far, mine, met, out_mine, out_near, out_far,
    edge_sems, load_sems, near_send, near_recv, far_send, far_recv, out_load, out_send, out_recv,
):
    step = pl.program_id(0)
    last = pl.num_programs(0) - 1
    me = lax.axis_index("fsdp")
    line = lax.axis_index("seq")
    line_end = lax.axis_size("seq") - 1
    at = [xor(me, k, group) for k in range(group)]
    seqs, rows = qkv_ref.shape[0], qkv_ref.shape[1]
    half = group // 2
    seq = lax.rem(lax.div(step, half), 2)
    place = lax.div(step, group) * half + lax.rem(step, half)
    f32, low = jnp.float32, jnp.bfloat16
    pieces = 2
    size = mid.shape[1] // pieces

    def edge_copy():
        return pltpu.make_async_remote_copy(
            src_ref=edge, dst_ref=ahead, send_sem=edge_sems.at[0], recv_sem=edge_sems.at[1],
            device_id={"seq": lax.rem(line + line_end, line_end + 1)}, device_id_type=MESH,
        )

    first, second = (at[2], at[4]), (at[4], at[2])

    def near_copy(a, h):
        part = pl.ds(h * size, size)
        return pltpu.make_async_remote_copy(
            src_ref=kept.at[3, a, part], dst_ref=near.at[a, part], send_sem=near_send.at[a, h],
            recv_sem=near_recv.at[a, h], device_id={"fsdp": first[a]}, device_id_type=MESH,
        )

    def far_copy(a, h):
        part = pl.ds(h * size, size)
        return pltpu.make_async_remote_copy(
            src_ref=mid.at[a, part], dst_ref=far.at[a, part], send_sem=far_send.at[a, h],
            recv_sem=far_recv.at[a, h], device_id={"fsdp": second[a]}, device_id_type=MESH,
        )

    def loads():
        for a in range(2):
            yield pltpu.make_async_copy(kept.at[1 - a, a], mid.at[a], load_sems.at[0, a])
            yield pltpu.make_async_copy(kept.at[2, a], mine.at[a], load_sems.at[1, a])
            yield pltpu.make_async_copy(side.at[a], met.at[a], load_sems.at[2, a])
        yield pltpu.make_async_copy(out_kept, out_mine, out_load)

    cut = out_mine.shape[1] // 2
    out_first = ((0, 1, 0), (0, 3, 1), (1, 2, 0), (1, 3, 1))

    def out_near_copy(n):
        h, slot, j = out_first[n]
        return pltpu.make_async_remote_copy(
            src_ref=out_kept.at[slot, pl.ds(h * cut, cut)], dst_ref=out_near.at[h, j], send_sem=out_send.at[n],
            recv_sem=out_recv.at[n], device_id={"fsdp": first[h]}, device_id_type=MESH,
        )

    def out_far_copy(h):
        return pltpu.make_async_remote_copy(
            src_ref=out_mine.at[2 - h, pl.ds(h * cut, cut)], dst_ref=out_far.at[h], send_sem=out_send.at[4 + h],
            recv_sem=out_recv.at[4 + h], device_id={"fsdp": second[h]}, device_id_type=MESH,
        )

    def plus(u, *more):
        total = u.astype(f32)
        for v in more:
            total += v.astype(f32)
        return total.astype(low)

    @pl.when(step == 0)
    def _():
        barrier = pltpu.get_barrier_semaphore()
        for peer in (at[2], at[4]):
            pl.semaphore_signal(barrier, inc=1, device_id={"fsdp": peer}, device_id_type=MESH)
        pl.semaphore_signal(
            barrier, inc=1, device_id={"seq": lax.rem(line + 1, line_end + 1)}, device_id_type=MESH
        )
        pl.semaphore_wait(barrier, 3)
        for h in range(pieces):
            for a in range(2):
                near_copy(a, h).start()
        for n in range(4):
            out_near_copy(n).start()
        for load in loads():
            load.start()
        for s in range(seqs):
            fill_keys(s, heads, halo_ref, augk_ref, 0, keys, values, None, keys_t)
            fill_keys(s, heads, qkv_ref, augk_ref, WINDOW, keys, values, None, keys_t)
        dkeys[...] = jnp.zeros_like(dkeys)
        dvalues[...] = jnp.zeros_like(dvalues)

    @pl.when((step == group) & (line > 0))
    def _():
        for s in range(seqs):
            for h in range(heads):
                c = h * 2 * HD
                edge[s, :, c : c + 2 * HD] = jnp.concatenate(
                    [dkeys[s * heads + h, :WINDOW, :HD], dvalues[s * heads + h, :WINDOW, :HD]], axis=1
                ).astype(low)
        edge_copy().start()

    mask = edge_mask()
    tiles = WINDOW // BLK + 1
    start = pl.multiple_of(place * BLK, BLK)
    lane = lax.broadcasted_iota(jnp.int32, (BLK, 2 * HD), 1)
    spans = [pl.ds(pl.multiple_of(start + b * BLK, BLK), BLK) for b in range(tiles)]
    for h in range(heads):
        sh = seq * heads + h
        q = q2_ref[0, h]
        g32 = grad_ref[0, :, h * HD : (h + 1) * HD].astype(f32)
        centre = jnp.sum(g32 * out_ref[0, :, h * HD : (h + 1) * HD].astype(f32), axis=1, keepdims=True)
        hi, md, lo = split3(-centre)
        g2 = jnp.concatenate([g32, jnp.zeros((BLK, HD), f32)], axis=1)
        g2 = jnp.where(lane == HD, hi, g2)
        g2 = jnp.where(lane == HD + 1, md, g2)
        g2 = jnp.where(lane == HD + 2, lo, g2).astype(low)
        scores = merge_edges(mask, [nt(keys[sh, s, :], q) for s in spans])
        wgrads = merge_edges(mask, [nt(values[sh, s, :], g2) for s in spans])
        weights = [jnp.exp(s) for s in scores]
        sgrads = spread_edges(mask, [(w * d).astype(low) for w, d in zip(weights, wgrads)])
        weights = spread_edges(mask, [w.astype(low) for w in weights])
        for s, w, d in zip(spans, weights, sgrads):
            dvalues[sh, s, :] += nn(w, g2)
            dkeys[sh, s, :] += nn(d, q)
        dq = sum(nn(keys_t[sh, :, s], d) for s, d in zip(spans, sgrads))
        qc = heads * 2 * HD + h * HD
        gqkv_ref[seq, pl.ds(start, BLK), qc : qc + HD] = (dq.T[:, :HD] * 0.125).astype(low)

    def relay(h):
        part = slice(h * size, (h + 1) * size)
        for a in range(2):
            near_copy(a, h).wait_recv()
            mid[a, part] = plus(mid[a, part], near[a, part])
            far_copy(a, h).start()

    @pl.when(step == 5)
    def _():
        for load in loads():
            load.wait()
        relay(0)

    @pl.when(step == 9)
    def _():
        relay(1)
        for n in range(4):
            out_near_copy(n).wait_recv()
        for h in range(2):
            part = slice(h * cut, (h + 1) * cut)
            out_mine[2 - h, part] = plus(out_mine[2 - h, part], out_near[h, 1])
            out_far_copy(h).start()

    @pl.when(step == last)
    def _():
        for s in range(seqs):
            for h in range(heads):
                c = h * 2 * HD
                own = jnp.concatenate(
                    [dkeys[s * heads + h, WINDOW:, :HD], dvalues[s * heads + h, WINDOW:, :HD]], axis=1
                )
                gqkv_ref[s, : rows - WINDOW, c : c + 2 * HD] = own[: rows - WINDOW].astype(low)
                dkeys[s * heads + h, WINDOW:, :] = own

        @pl.when(line < line_end)
        def _():
            edge_copy().wait_recv()

        @pl.when(line == line_end)
        def _():
            ahead[...] = jnp.zeros_like(ahead)

        for s in range(seqs):
            for h in range(heads):
                c = h * 2 * HD
                own = dkeys[s * heads + h, rows:, :]
                gqkv_ref[s, rows - WINDOW :, c : c + 2 * HD] = (
                    own + ahead[s, :, c : c + 2 * HD].astype(f32)
                ).astype(low)

        for h in range(pieces):
            part = slice(h * size, (h + 1) * size)
            for a in range(2):
                far_copy(a, h).wait_recv()
                sums_ref[a, part] = plus(mine[a, part], met[a, part], far[a, part])
        for h in range(2):
            out_far_copy(h).wait_recv()
            part = slice(h * cut, (h + 1) * cut)
            out_sum_ref[part] = plus(out_mine[0, part], out_near[h, 0], out_far[h])
        for a in range(2):
            for h in range(pieces):
                near_copy(a, h).wait_send()
                far_copy(a, h).wait_send()
        for n in range(4):
            out_near_copy(n).wait_send()
        for h in range(2):
            out_far_copy(h).wait_send()

        @pl.when(line > 0)
        def _():
            edge_copy().wait_send()


def attend_back(qkv, halo, augk, q2, out, grad, kept, side, out_kept, heads, group):
    seqs, rows, cols = qkv.shape
    ext = augk.shape[1]
    half = group // 2
    f32, low = jnp.float32, jnp.bfloat16
    vmem = pl.BlockSpec(memory_space=pltpu.VMEM)
    hbm = pl.BlockSpec(memory_space=pl.ANY)
    every = seqs * heads
    part = kept.shape[2:]
    out_part = out_kept.shape[1:]
    seq_of = lambda i: lax.rem(lax.div(i, half), 2)
    place_of = lambda i: lax.div(i, group) * half + lax.rem(i, half)
    edge = pltpu.VMEM((seqs, WINDOW, heads * 2 * HD), low)
    pair = pltpu.VMEM((2,) + part, low)
    return pl.pallas_call(
        functools.partial(attend_back_kernel, heads, group),
        grid=(seqs * rows // BLK,),
        in_specs=[
            vmem, vmem, vmem,
            pl.BlockSpec((1, heads, BLK, 2 * HD), lambda i: (seq_of(i), 0, place_of(i), 0)),
            pl.BlockSpec((1, BLK, heads * HD), lambda i: (seq_of(i), place_of(i), 0)),
            pl.BlockSpec((1, BLK, heads * HD), lambda i: (seq_of(i), place_of(i), 0)),
            hbm, hbm, hbm,
        ],
        out_specs=[vmem, vmem, vmem],
        out_shape=[
            jax.ShapeDtypeStruct((seqs, rows, cols), low),
            jax.ShapeDtypeStruct((2,) + part, low),
            jax.ShapeDtypeStruct(out_part, low),
        ],
        scratch_shapes=[
            pltpu.VMEM((every, ext, 2 * HD), low),
            pltpu.VMEM((every, ext, 2 * HD), low),
            pltpu.VMEM((every, 2 * HD, ext), low),
            pltpu.VMEM((every, ext, 2 * HD), f32),
            pltpu.VMEM((every, ext, 2 * HD), f32),
            edge, edge, pair, pair, pair, pair, pair,
            pltpu.VMEM(out_kept.shape, low),
            pltpu.VMEM((2, 2, out_part[0] // 2, out_part[1]), low),
            pltpu.VMEM((2, out_part[0] // 2, out_part[1]), low),
            pltpu.SemaphoreType.DMA((2,)),
            pltpu.SemaphoreType.DMA((3, 2)),
            pltpu.SemaphoreType.DMA((2, 2)),
            pltpu.SemaphoreType.DMA((2, 2)),
            pltpu.SemaphoreType.DMA((2, 2)),
            pltpu.SemaphoreType.DMA((2, 2)),
            pltpu.SemaphoreType.DMA,
            pltpu.SemaphoreType.DMA((6,)),
            pltpu.SemaphoreType.DMA((6,)),
        ],
        compiler_params=pltpu.CompilerParams(vmem_limit_bytes=62 * 2**20, collective_id=4, has_side_effects=True),
        name="attend_back",
    )(qkv, halo, augk, q2, out, grad, kept, side, out_kept)


def finish_kernel(
    g_ref, wt_ref, x_ref, gres_ref, small_ref, sums_ref, out_sum_ref, gvec_ref, gfcb_ref, z_hbm,
    input_grad_ref, total_ref, out_total_ref, qkv_total_ref, vec_ref,
    z_all, odd, odd_in, even, mine, first_in, second_in, mt, rows6, vec_out, vec_in, vec_line,
    acc, acc_out, acc_q, left, left_out, left_q, right, right_out, right_q,
    z_sem, odd_send, odd_recv, near_send, near_recv, far_send, far_recv,
    vec_send, vec_recv, vl_send, vl_recv, line_send, line_recv,
):
    group = small_ref.shape[0]
    me = lax.axis_index("fsdp")
    line = lax.axis_index("seq")
    line_size = 4
    at = [xor(me, k, group) for k in range(group)]
    block = x_ref.shape[0] // 2
    f32, low = jnp.float32, jnp.bfloat16
    width = x_ref.shape[1]
    span = small_ref.shape[2]
    heads = wt_ref.shape[0] // (3 * HD)
    outer = (line == 0) | (line == line_size - 1)
    inner = (line > 0) & (line < line_size - 1)

    def remote(src, dst, send, recv, to):
        return pltpu.make_async_remote_copy(
            src_ref=src, dst_ref=dst, send_sem=send, recv_sem=recv, device_id=to, device_id_type=MESH
        )

    barrier = pltpu.get_barrier_semaphore()
    for peer in at[1:]:
        pl.semaphore_signal(barrier, inc=1, device_id={"fsdp": peer}, device_id_type=MESH)
    others = [lax.rem(line + d, line_size) for d in range(1, line_size)]
    for other in others:
        pl.semaphore_signal(barrier, inc=1, device_id={"seq": other}, device_id_type=MESH)
    pl.semaphore_wait(barrier, group - 1 + line_size - 1)

    cut = sums_ref.shape[1] // 2
    chunks = []
    for a in range(2):
        for h in range(2):
            part = pl.ds(h * cut, cut)
            chunks.append([r.at[a, part] for r in (sums_ref, acc, left, right, total_ref)])
    chunks.insert(3, [acc_q, acc_q, left_q, right_q, qkv_total_ref])
    chunks.append([out_sum_ref, acc_out, left_out, right_out, out_total_ref])

    def inwards(c):
        return remote(
            chunks[c][0], chunks[c][2], line_send.at[0, c], line_recv.at[0, c], {"seq": 1 + lax.div(line, line_size - 1)}
        )

    def across(c):
        return remote(
            chunks[c][1], chunks[c][3], line_send.at[1, c], line_recv.at[1, c], {"seq": line_size - 1 - line}
        )

    def outwards(c):
        return remote(
            chunks[c][4], chunks[c][3], line_send.at[2, c], line_recv.at[2, c],
            {"seq": lax.rem((line + line_size - 1) * (line_size - 1), 2 * (line_size - 1))},
        )

    def begin(cs):
        @pl.when(outer)
        def _():
            for c in cs:
                inwards(c).start()

    def collect(c):
        @pl.when(inner)
        def _():
            inwards(c).wait_recv()
            own, acc_c, left_c = chunks[c][:3]
            acc_c[...] = (own[...].astype(f32) + left_c[...].astype(f32)).astype(low)
            across(c).start()

    def settle(c):
        @pl.when(inner)
        def _():
            across(c).wait_recv()
            chunks[c][4][...] = (chunks[c][1][...].astype(f32) + chunks[c][3][...].astype(f32)).astype(low)
            outwards(c).start()

    def receive(c):
        @pl.when(outer)
        def _():
            outwards(c).wait_recv()
            chunks[c][4][...] = chunks[c][3][...]

    begin((0, 1, 2))
    load = pltpu.make_async_copy(z_hbm, z_all, z_sem)
    load.start()

    def product(r, s):
        start = pl.multiple_of(at[r] * block, block)
        return nn(g_ref[s, pl.ds(start, block), :], wt_ref[...])

    def odd_copy(j):
        return remote(odd.at[j], odd_in.at[j], odd_send.at[j], odd_recv.at[j], {"fsdp": at[1]})

    for j in (3, 1, 2, 0):
        for s in range(2):
            odd[j, s] = product(2 * j + 1, s).astype(low)
        odd_copy(j).start()

    ways = (at[2], at[4])

    def near_copy(s, i):
        j = 3 if i == 0 else 1 + s
        return remote(even.at[j, s], first_in.at[s, i], near_send.at[s, i], near_recv.at[s, i], {"fsdp": ways[s]})

    def far_copy(s):
        return remote(even.at[2 - s, s], second_in.at[s], far_send.at[s], far_recv.at[s], {"fsdp": ways[1 - s]})

    for j in (3, 1, 2, 0):
        for s in range(2):
            part = product(2 * j, s)
            if s == 0:
                odd_copy(j).wait_recv()
            part += odd_in[j, s].astype(f32)
            if j == 0:
                mine[s] = part
            else:
                even[j, s] = part.astype(low)
                if j == 3:
                    near_copy(s, 0).start()
                elif j == 1 + s:
                    near_copy(s, 1).start()

    collect(0)

    def wide(index):
        return jnp.concatenate([small_ref[f, index : index + 1, :] for f in range(group)], axis=1).astype(f32)

    gain = wide(0)
    load.wait()
    mt[...] = jnp.zeros_like(mt)
    steps = z_all.shape[1] // 512
    ones = jnp.ones((512, 128), low)

    def add_product(i, sums):
        rows = pl.ds(pl.multiple_of(lax.rem(i, steps) * 512, 512), 512)
        g = g_ref[lax.div(i, steps), rows, :]
        mt[...] += tn(g, z_all[lax.div(i, steps), rows, :])
        return sums + tn(g, ones)

    column = lax.fori_loop(0, 2 * steps, add_product, jnp.zeros((g_ref.shape[2], 128), f32))
    acc_q[...] = mt[...].astype(low)
    begin((3, 4, 5))
    collect(1)

    def vec_copy(k):
        return remote(vec_out.at[k], vec_in.at[k], vec_send.at[k], vec_recv.at[k], {"fsdp": at[k]})

    for s in range(2):
        near_copy(s, 0).wait_recv()
        even[2 - s, s] = (even[2 - s, s].astype(f32) + first_in[s, 0].astype(f32)).astype(low)
        far_copy(s).start()

    collect(2)
    settle(0)

    def line_copy(d):
        return remote(vec_line.at[line], vec_line.at[line], vl_send.at[d], vl_recv.at[d], {"seq": others[d]})

    settle(1)
    receive(0)
    gain_grad = offset_grad = jnp.zeros((1, width), f32)
    for s in range(2):
        near_copy(s, 1).wait_recv()
        far_copy(s).wait_recv()
        rows = slice(s * block, (s + 1) * block)
        e = mine[s] + first_in[s, 1].astype(f32) + second_in[s].astype(f32)
        z, rate = standardize(x_ref[rows, :].astype(f32))
        gain_grad += column_sums(e * z)
        offset_grad += column_sums(e)
        input_grad_ref[rows, :] = (gres_ref[rows, :] + norm_grad(e * gain, z, rate)).astype(low)
    rows6[0:1, :] = gain_grad
    rows6[1:2, :] = offset_grad
    rows6[2:6, :] = gvec_ref[0:4, :]
    row = column.T[0:1, :]
    vec_out[...] = jnp.zeros_like(vec_out)
    for k in range(group):
        vec_out[k, 0:6, :] = rows6[0:6, pl.ds(pl.multiple_of(at[k] * span, span), span)]
        for i in range(4):
            vec_out[k, 6 + i : 7 + i, :] = gfcb_ref[STEP_OF[k], :, i * span : (i + 1) * span]
    for h in range(heads):
        base = heads * 2 * HD + h * HD
        vec_out[0, 10 + h : 11 + h, :] = jnp.concatenate(
            [row[:, base : base + HD], row[:, h * 2 * HD + HD : (h + 1) * 2 * HD]], axis=1
        )

    for k in range(1, group):
        vec_copy(k).start()

    collect(3)
    settle(2)
    receive(1)
    total = vec_out[0]
    for k in range(1, group):
        vec_copy(k).wait_recv()
        total += vec_in[k]
    vec_line[line] = total

    for d in range(line_size - 1):
        line_copy(d).start()

    collect(4)
    settle(3)
    collect(5)
    receive(2)
    for d in range(line_size - 1):
        line_copy(d).wait_recv()
    vec_ref[...] = vec_line[0] + vec_line[1] + vec_line[2] + vec_line[3]
    settle(4)
    settle(5)
    for c in (3, 4, 5):
        receive(c)
    for j in range(4):
        odd_copy(j).wait_send()
    for s in range(2):
        near_copy(s, 0).wait_send()
        near_copy(s, 1).wait_send()
        far_copy(s).wait_send()
    for k in range(1, group):
        vec_copy(k).wait_send()
    for d in range(line_size - 1):
        line_copy(d).wait_send()

    @pl.when(outer)
    def _():
        for c in range(6):
            inwards(c).wait_send()

    @pl.when(inner)
    def _():
        for c in range(6):
            across(c).wait_send()
            outwards(c).wait_send()


def finish(g, wt, x, gres, small, sums, out_sum, gvec, gfcb, z_all):
    rows, width = x.shape
    group = small.shape[0]
    half = rows // 2
    span = small.shape[2]
    f32, low = jnp.float32, jnp.bfloat16
    vmem = pl.BlockSpec(memory_space=pltpu.VMEM)
    dma = pltpu.SemaphoreType.DMA
    buffers = [pltpu.VMEM(sums.shape, low), pltpu.VMEM(out_sum.shape, low), pltpu.VMEM(wt.shape, low)]
    return pl.pallas_call(
        finish_kernel,
        in_specs=[vmem] * 9 + [pl.BlockSpec(memory_space=pl.ANY)],
        out_specs=[vmem] * 5,
        out_shape=[
            jax.ShapeDtypeStruct((rows, width), low),
            jax.ShapeDtypeStruct(sums.shape, low),
            jax.ShapeDtypeStruct(out_sum.shape, low),
            jax.ShapeDtypeStruct(wt.shape, low),
            jax.ShapeDtypeStruct((16, span), f32),
        ],
        scratch_shapes=[
            pltpu.VMEM(z_all.shape, low),
            pltpu.VMEM((group // 2, 2, half, width), low),
            pltpu.VMEM((group // 2, 2, half, width), low),
            pltpu.VMEM((group // 2, 2, half, width), low),
            pltpu.VMEM((2, half, width), f32),
            pltpu.VMEM((2, 2, half, width), low),
            pltpu.VMEM((2, half, width), low),
            pltpu.VMEM(wt.shape, f32),
            pltpu.VMEM((8, width), f32),
            pltpu.VMEM((group, 16, span), f32),
            pltpu.VMEM((group, 16, span), f32),
            pltpu.VMEM((4, 16, span), f32),
        ]
        + buffers * 3
        + [dma, dma((4,)), dma((4,)), dma((2, 2)), dma((2, 2)), dma((2,)), dma((2,))]
        + [dma((group,)), dma((group,)), dma((3,)), dma((3,)), dma((3, 6)), dma((3, 6))],
        compiler_params=pltpu.CompilerParams(vmem_limit_bytes=62 * 2**20, collective_id=5, has_side_effects=True),
        name="finish",
    )(g, wt, x, gres, small, sums, out_sum, gvec, gfcb, z_all)


def plain_fill_keys(heads, qkv_ref, halo_ref, augk_ref, keys, values):
    halo_rows = halo_ref.shape[1]
    rows = qkv_ref.shape[1]
    ones = jnp.ones((1, HD), jnp.bfloat16)
    for h in range(heads):
        c = h * 2 * HD
        for source, base, size in ((halo_ref, 0, halo_rows), (qkv_ref, halo_rows, rows)):
            pair = source[0, :, c : c + 2 * HD]
            keys[h, base : base + size, :] = jnp.concatenate(
                [pair[:, :HD], augk_ref[0, base : base + size, :]], axis=1
            )
            values[h, base : base + size, :] = jnp.concatenate(
                [pair[:, HD:], jnp.broadcast_to(ones, (size, HD))], axis=1
            )


def plain_attend_kernel(heads, qkv_ref, halo_ref, augk_ref, augq_ref, out_ref, q2_ref, keys, values, values_t):
    step = pl.program_id(1)
    nkeys = keys.shape[1]

    @pl.when(step == 0)
    def _():
        plain_fill_keys(heads, qkv_ref, halo_ref, augk_ref, keys, values)
        for h in range(heads):
            for b in range(nkeys // BLK):
                values_t[h, :, b * BLK : (b + 1) * BLK] = values[h, b * BLK : (b + 1) * BLK, :].T

    mask = edge_mask()
    tiles = WINDOW // BLK + 1
    start = pl.multiple_of(step * BLK, BLK)
    lane = lax.broadcasted_iota(jnp.int32, (BLK, 2 * HD), 1)
    lse_lane = augq_ref.shape[2] + HD - 3
    for h in range(heads):
        qc = heads * 2 * HD + h * HD
        q = jnp.concatenate([qkv_ref[0, pl.ds(start, BLK), qc : qc + HD] * 0.125, augq_ref[0]], axis=1)
        scores = [nt(keys[h, pl.ds(start + b * BLK, BLK), :], q) for b in range(tiles)]
        scores = merge_edges(mask, scores)
        peak = functools.reduce(jnp.maximum, scores)
        peak = jnp.max(peak, axis=0, keepdims=True)
        weights = spread_edges(mask, [jnp.exp(s - peak).astype(jnp.bfloat16) for s in scores])
        total = sum(
            nn(values_t[h, :, pl.ds(pl.multiple_of(start + b * BLK, BLK), BLK)], w) for b, w in enumerate(weights)
        )
        sub = lax.broadcasted_iota(jnp.int32, total.shape, 0)
        total = jnp.where(sub == HD + 1, peak, total).T
        norm = total[:, HD : HD + 1]
        out_ref[0, :, h * HD : (h + 1) * HD] = (total[:, :HD] / norm).astype(out_ref.dtype)
        lse = total[:, HD + 1 : HD + 2] + jnp.log(norm)
        hi, mid, low = split3(-lse)
        q2 = q.astype(jnp.float32)
        q2 = jnp.where(lane == lse_lane, hi, q2)
        q2 = jnp.where(lane == lse_lane + 1, mid, q2)
        q2 = jnp.where(lane == lse_lane + 2, low, q2)
        q2_ref[0, h] = q2.astype(jnp.bfloat16)


def plain_attend(qkv, halo, augk, augq, heads):
    seqs, rows, cols = qkv.shape
    ext = augk.shape[1]
    return pl.pallas_call(
        functools.partial(plain_attend_kernel, heads),
        grid=(seqs, rows // BLK),
        in_specs=[
            pl.BlockSpec((1, rows, cols), lambda s, i: (s, 0, 0)),
            pl.BlockSpec((1, WINDOW, heads * 2 * HD), lambda s, i: (s, 0, 0)),
            pl.BlockSpec((1, ext, HD), lambda s, i: (s, 0, 0)),
            pl.BlockSpec((1, BLK, HD), lambda s, i: (s, i, 0)),
        ],
        out_specs=[
            pl.BlockSpec((1, BLK, heads * HD), lambda s, i: (s, i, 0)),
            pl.BlockSpec((1, heads, BLK, 2 * HD), lambda s, i: (s, 0, i, 0)),
        ],
        out_shape=[
            jax.ShapeDtypeStruct((seqs, rows, heads * HD), jnp.bfloat16),
            jax.ShapeDtypeStruct((seqs, heads, rows, 2 * HD), jnp.bfloat16),
        ],
        scratch_shapes=[
            pltpu.VMEM((heads, ext, 2 * HD), jnp.bfloat16),
            pltpu.VMEM((heads, ext, 2 * HD), jnp.bfloat16),
            pltpu.VMEM((heads, 2 * HD, ext), jnp.bfloat16),
        ],
        compiler_params=pltpu.CompilerParams(vmem_limit_bytes=48 * 2**20),
        name="plain_attend",
    )(qkv, halo, augk, augq)


def plain_attend_back_kernel(
    heads, qkv_ref, halo_ref, augk_ref, q2_ref, out_ref, grad_ref, dq_ref, dkv_ref, dhalo_ref,
    keys, values, keys_t, dkeys, dvalues,
):
    step = pl.program_id(1)
    nkeys = keys.shape[1]

    @pl.when(step == 0)
    def _():
        plain_fill_keys(heads, qkv_ref, halo_ref, augk_ref, keys, values)
        for h in range(heads):
            for b in range(nkeys // BLK):
                keys_t[h, :, b * BLK : (b + 1) * BLK] = keys[h, b * BLK : (b + 1) * BLK, :].T
        dkeys[...] = jnp.zeros_like(dkeys)
        dvalues[...] = jnp.zeros_like(dvalues)

    mask = edge_mask()
    tiles = WINDOW // BLK + 1
    start = pl.multiple_of(step * BLK, BLK)
    lane = lax.broadcasted_iota(jnp.int32, (BLK, 2 * HD), 1)
    for h in range(heads):
        q = q2_ref[0, h]
        g = grad_ref[0, :, h * HD : (h + 1) * HD]
        g32 = g.astype(jnp.float32)
        centre = jnp.sum(g32 * out_ref[0, :, h * HD : (h + 1) * HD].astype(jnp.float32), axis=1, keepdims=True)
        hi, mid, low = split3(-centre)
        g2 = jnp.concatenate([g32, jnp.zeros((BLK, HD), jnp.float32)], axis=1)
        g2 = jnp.where(lane == HD, hi, g2)
        g2 = jnp.where(lane == HD + 1, mid, g2)
        g2 = jnp.where(lane == HD + 2, low, g2).astype(jnp.bfloat16)
        spans = [pl.ds(pl.multiple_of(start + b * BLK, BLK), BLK) for b in range(tiles)]
        scores = merge_edges(mask, [nt(keys[h, s, :], q) for s in spans])
        wgrads = merge_edges(mask, [nt(values[h, s, :], g2) for s in spans])
        weights = [jnp.exp(s) for s in scores]
        sgrads = spread_edges(mask, [(w * d).astype(jnp.bfloat16) for w, d in zip(weights, wgrads)])
        weights = spread_edges(mask, [w.astype(jnp.bfloat16) for w in weights])
        for s, w, d in zip(spans, weights, sgrads):
            dvalues[h, s, :] += nn(w, g2)
            dkeys[h, s, :] += nn(d, q)
        dq = sum(nn(keys_t[h, :, s], d) for s, d in zip(spans, sgrads))
        dq_ref[0, :, h * HD : (h + 1) * HD] = (dq.T[:, :HD] * 0.125).astype(dq_ref.dtype)

    @pl.when(step == pl.num_programs(1) - 1)
    def _():
        for h in range(heads):
            c = h * 2 * HD
            dhalo_ref[0, :, c : c + 2 * HD] = jnp.concatenate(
                [dkeys[h, :WINDOW, :HD], dvalues[h, :WINDOW, :HD]], axis=1
            ).astype(dhalo_ref.dtype)
            dkv_ref[0, :, c : c + 2 * HD] = jnp.concatenate(
                [dkeys[h, WINDOW:, :HD], dvalues[h, WINDOW:, :HD]], axis=1
            ).astype(dkv_ref.dtype)


def plain_attend_back(qkv, halo, augk, q2, out, grad, heads):
    seqs, rows, cols = qkv.shape
    ext = augk.shape[1]
    return pl.pallas_call(
        functools.partial(plain_attend_back_kernel, heads),
        grid=(seqs, rows // BLK),
        in_specs=[
            pl.BlockSpec((1, rows, cols), lambda s, i: (s, 0, 0)),
            pl.BlockSpec((1, WINDOW, heads * 2 * HD), lambda s, i: (s, 0, 0)),
            pl.BlockSpec((1, ext, HD), lambda s, i: (s, 0, 0)),
            pl.BlockSpec((1, heads, BLK, 2 * HD), lambda s, i: (s, 0, i, 0)),
            pl.BlockSpec((1, BLK, heads * HD), lambda s, i: (s, i, 0)),
            pl.BlockSpec((1, BLK, heads * HD), lambda s, i: (s, i, 0)),
        ],
        out_specs=[
            pl.BlockSpec((1, BLK, heads * HD), lambda s, i: (s, i, 0)),
            pl.BlockSpec((1, rows, heads * 2 * HD), lambda s, i: (s, 0, 0)),
            pl.BlockSpec((1, WINDOW, heads * 2 * HD), lambda s, i: (s, 0, 0)),
        ],
        out_shape=[
            jax.ShapeDtypeStruct((seqs, rows, heads * HD), jnp.bfloat16),
            jax.ShapeDtypeStruct((seqs, rows, heads * 2 * HD), jnp.float32),
            jax.ShapeDtypeStruct((seqs, WINDOW, heads * 2 * HD), jnp.bfloat16),
        ],
        scratch_shapes=[
            pltpu.VMEM((heads, ext, 2 * HD), jnp.bfloat16),
            pltpu.VMEM((heads, ext, 2 * HD), jnp.bfloat16),
            pltpu.VMEM((heads, 2 * HD, ext), jnp.bfloat16),
            pltpu.VMEM((heads, ext, 2 * HD), jnp.float32),
            pltpu.VMEM((heads, ext, 2 * HD), jnp.float32),
        ],
        compiler_params=pltpu.CompilerParams(vmem_limit_bytes=56 * 2**20),
        name="plain_attend_back",
    )(qkv, halo, augk, q2, out, grad)


def from_behind(block, axis, distance):
    devices = range(lax.axis_size(axis))
    route = [(i - distance, i) for i in devices if i - distance in devices]
    return lax.ppermute(block, axis, route)


def pack_columns(array, heads):
    parts = array.reshape(array.shape[:-1] + (heads, 3 * HD))
    lead = array.shape[:-1]
    return jnp.concatenate(
        [parts[..., HD:].reshape(lead + (-1,)), parts[..., :HD].reshape(lead + (-1,))], axis=-1
    )


def unpack_columns(array, heads):
    lead = array.shape[:-1]
    pairs = array[..., : heads * 2 * HD].reshape(lead + (heads, 2 * HD))
    queries = array[..., heads * 2 * HD :].reshape(lead + (heads, HD))
    return jnp.concatenate([queries, pairs], axis=-1).reshape(lead + (-1,))


def dot(subscripts, a, b):
    return jnp.einsum(subscripts, a, b, preferred_element_type=jnp.float32)


def general_body(
    inputs, cotangent, segment_ids, norm1_gain, norm1_bias, qkv_weight, qv_bias, out_weight, out_bias,
    norm2_gain, norm2_bias, fc_weight, fc_bias, proj_weight, proj_bias,
):
    group = lax.axis_size("fsdp")
    seqs, local_rows, width = inputs.shape
    part_rows = local_rows * group
    heads = qkv_weight.shape[1] // (3 * HD)
    docs = segment_ids.shape[1] // (2 * WINDOW)
    seq_index = lax.axis_index("seq")
    shard = norm1_gain.shape[0]

    small = jnp.concatenate([norm1_gain, norm1_bias, out_bias, norm2_gain, norm2_bias, proj_bias, fc_bias])
    small = lax.all_gather(small, "fsdp")
    gain1, offset1, out_off, gain2, offset2, proj_off = (
        small[:, i * shard : (i + 1) * shard].reshape(-1).astype(jnp.float32) for i in range(6)
    )
    fc_off = small[:, 6 * shard :].reshape(-1).astype(jnp.float32)
    out_all = lax.all_gather(out_weight, "fsdp", axis=0, tiled=True)
    fc_all = lax.all_gather(fc_weight, "fsdp")
    proj_all = lax.all_gather(proj_weight, "fsdp")

    padded_ids = jnp.concatenate([jnp.full((seqs, WINDOW), -1, jnp.int32), segment_ids], axis=1)
    segment_ext = lax.dynamic_slice_in_dim(padded_ids, seq_index * part_rows, WINDOW + part_rows, 1)
    augk, augq = mask_features(segment_ext, docs)

    x = inputs.astype(jnp.float32)
    z1, rate1 = standardize(x)
    normed1 = (z1 * gain1 + offset1).astype(jnp.bfloat16)
    normed1 = lax.all_gather(normed1, "fsdp", axis=1, tiled=True)
    packed_weight = pack_columns(qkv_weight, heads)
    head_bias = qv_bias.astype(jnp.float32)
    head_bias = jnp.concatenate(
        [head_bias[:, :HD], jnp.zeros((heads, HD), jnp.float32), head_bias[:, HD:]], axis=1
    ).reshape(-1)
    packed_bias = pack_columns(head_bias, heads)
    qkv = (dot("sre,ef->srf", normed1, packed_weight) + packed_bias).astype(jnp.bfloat16)
    halo = from_behind(qkv[:, part_rows - WINDOW :, : heads * 2 * HD], "seq", 1)
    head_out, q2 = plain_attend(qkv, halo, augk, augq, heads)
    merged = lax.all_to_all(head_out, "fsdp", split_axis=1, concat_axis=2, tiled=True)
    resid = x + dot("sre,ef->srf", merged, out_all) + out_off
    z2, rate2 = standardize(resid)
    normed2 = (z2 * gain2 + offset2).astype(jnp.bfloat16)
    fc_offset = fc_off.reshape(group, -1)
    hidden = dot("sre,gef->gsrf", normed2, fc_all) + fc_offset[:, None, None]
    active, gelu_back = jax.vjp(lambda v: jax.nn.gelu(v, approximate=True), hidden)
    active = active.astype(jnp.bfloat16)
    layer_output = (resid + dot("gsrf,gfd->srd", active, proj_all) + proj_off).astype(jnp.bfloat16)

    cot32 = cotangent.astype(jnp.float32)
    proj_bias_part = jnp.sum(cot32, axis=(0, 1))
    proj_weight_part = dot("gsrf,srd->gfd", active, cotangent)
    g_hidden = gelu_back(dot("srd,gfd->gsrf", cotangent, proj_all))[0].astype(jnp.bfloat16)
    fc_bias_part = jnp.sum(g_hidden, axis=(1, 2), dtype=jnp.float32).reshape(-1)
    fc_weight_part = dot("sre,gsrf->gef", normed2, g_hidden)
    g_norm2 = dot("gsrf,gef->sre", g_hidden, fc_all)
    gain2_part = jnp.sum(g_norm2 * z2, axis=(0, 1))
    offset2_part = jnp.sum(g_norm2, axis=(0, 1))
    g_resid = cot32 + norm_grad(g_norm2 * gain2, z2, rate2)
    g_attn = g_resid.astype(jnp.bfloat16)
    out_bias_part = jnp.sum(g_attn, axis=(0, 1), dtype=jnp.float32)
    out_weight_part = dot("sre,srd->ed", merged, g_attn)
    g_merged = dot("srd,ed->sre", g_attn, out_all).astype(jnp.bfloat16)
    g_heads = lax.all_to_all(g_merged, "fsdp", split_axis=2, concat_axis=1, tiled=True)

    low = jnp.bfloat16
    fc_grad = lax.psum_scatter(fc_weight_part.astype(low), "fsdp")
    proj_grad = lax.psum_scatter(proj_weight_part.astype(low), "fsdp")
    out_grad = lax.psum_scatter(out_weight_part.astype(low), "fsdp", scatter_dimension=0, tiled=True)
    fc_grad, proj_grad, out_grad = lax.psum((fc_grad, proj_grad, out_grad), "seq")

    dq, dkv, dhalo = plain_attend_back(qkv, halo, augk, q2, head_out, g_heads, heads)
    edge = from_behind(dhalo, "seq", -1)
    edge = jnp.pad(edge.astype(jnp.float32), ((0, 0), (part_rows - WINDOW, 0), (0, 0)))
    g_qkv = jnp.concatenate([(dkv + edge).astype(jnp.bfloat16), dq], axis=-1)
    qkv_grad = dot("sre,srf->ef", normed1, g_qkv)
    qkv_colsum = jnp.sum(g_qkv, axis=(0, 1), dtype=jnp.float32)
    g_norm1 = dot("srf,ef->sre", g_qkv, packed_weight).astype(jnp.bfloat16)
    g_norm1 = lax.psum_scatter(g_norm1, "fsdp", scatter_dimension=1, tiled=True).astype(jnp.float32)
    gain1_part = jnp.sum(g_norm1 * z1, axis=(0, 1))
    offset1_part = jnp.sum(g_norm1, axis=(0, 1))
    input_grad = (g_resid + norm_grad(g_norm1 * gain1, z1, rate1)).astype(jnp.bfloat16)

    qkv_grad = lax.psum(qkv_grad.astype(low), "seq").astype(jnp.float32)
    qkv_grad = unpack_columns(qkv_grad, heads)
    col = unpack_columns(qkv_colsum, heads).reshape(heads, 3 * HD)
    col = lax.psum(jnp.concatenate([col[:, :HD], col[:, 2 * HD :]], axis=1), "seq")
    vectors = jnp.concatenate(
        [
            v.reshape(group, -1)
            for v in (gain1_part, offset1_part, out_bias_part, gain2_part, offset2_part, proj_bias_part, fc_bias_part)
        ],
        axis=1,
    )
    vectors = lax.psum_scatter(vectors, "fsdp")
    vectors = lax.psum(vectors, "seq")
    parts = [vectors[i * shard : (i + 1) * shard] for i in range(6)] + [vectors[6 * shard :]]
    f32 = jnp.float32
    return (
        layer_output, input_grad, parts[0], parts[1], qkv_grad, col, out_grad.astype(f32), parts[2], parts[3],
        parts[4], fc_grad.astype(f32), parts[6], proj_grad.astype(f32), parts[5],
    )


def cube_body(
    inputs, cotangent, segment_ids, norm1_gain, norm1_bias, qkv_weight, qv_bias, out_weight, out_bias,
    norm2_gain, norm2_bias, fc_weight, fc_bias, proj_weight, proj_bias,
):
    group = lax.axis_size("fsdp")
    seqs, local_rows, width = inputs.shape
    part_rows = local_rows * group
    heads = qkv_weight.shape[1] // (3 * HD)
    docs = segment_ids.shape[1] // (2 * WINDOW)
    seq_index = lax.axis_index("seq")
    me = lax.axis_index("fsdp")
    shard = norm1_gain.shape[0]
    f32, low = jnp.float32, jnp.bfloat16

    small = jnp.concatenate([norm1_gain, norm1_bias, out_bias, norm2_gain, norm2_bias, proj_bias, fc_bias])
    small = jnp.pad(small, (0, 16 * shard - small.shape[0])).reshape(16, shard)
    padded_ids = jnp.concatenate([jnp.full((seqs, WINDOW), -1, jnp.int32), segment_ids], axis=1)
    segment_ext = lax.dynamic_slice_in_dim(padded_ids, seq_index * part_rows, WINDOW + part_rows, 1)
    augk, augq = mask_features(segment_ext, docs)
    packed_weight = pack_columns(qkv_weight, heads)
    head_bias = qv_bias.astype(f32)
    head_bias = jnp.concatenate(
        [head_bias[:, :HD], jnp.zeros((heads, HD), f32), head_bias[:, HD:]], axis=1
    ).reshape(-1)
    packed_bias = pack_columns(head_bias, heads)

    x = inputs.reshape(seqs * local_rows, width)
    cot = cotangent.reshape(seqs * local_rows, width)
    all_small, z1, qkv = gather_project(x, small, packed_weight, packed_bias[None], group)
    head_out, q2, halo, merged, out_all, fc_near, proj_near = attend(
        qkv, augk, augq, out_weight, fc_weight, proj_weight, heads, group
    )
    full = lambda i: all_small[:, i].reshape(-1).astype(f32)
    vectors = jnp.stack([full(2), full(3), full(4), full(5)] + [jnp.zeros((width,), f32)] * 4)
    slots = jnp.stack([xor(me, r, group) for r in SLOT_AT])
    fc_off = jnp.take(all_small[:, 6:10].reshape(group, -1), slots, axis=0).astype(f32)[:, None]
    layer_output, g_resid, g_heads, kept, side, out_kept, gvec, gfcb = feed_forward(
        x, cot, merged.reshape(x.shape), out_all.reshape(width, width), fc_near, proj_near, fc_off, vectors
    )
    g_qkv, sums, out_sum = attend_back(
        qkv, halo, augk, q2, head_out, g_heads, kept, side, out_kept, heads, group
    )
    input_grad, sums, out_grad, qkv_grad, vecs = finish(
        g_qkv, packed_weight.T, x, g_resid, all_small, sums, out_sum, gvec, gfcb, z1
    )
    fc_grad, proj_grad = sums[0].astype(f32), sums[1].astype(f32)
    size = proj_grad.shape[0] // 2
    proj_grad = jnp.concatenate([proj_grad[:size], proj_grad[size:]], axis=1)
    qkv_grad = unpack_columns(qkv_grad.T.astype(f32), heads)
    return (
        layer_output.reshape(inputs.shape), input_grad.reshape(inputs.shape), vecs[0], vecs[1], qkv_grad,
        vecs[10 : 10 + heads], out_grad.astype(f32), vecs[2], vecs[3], vecs[4], fc_grad, vecs[6:10].reshape(-1),
        proj_grad, vecs[5],
    )


def solution(mesh):
    tokens = P(None, ("seq", "fsdp"), None)
    rows, cols, vec = P("fsdp", None), P(None, "fsdp"), P("fsdp")
    return jax.shard_map(
        cube_body if mesh.shape["fsdp"] == 8 and mesh.shape["seq"] == 4 else general_body,
        mesh=mesh,
        in_specs=(tokens, tokens, P(), vec, vec, cols, rows, rows, vec, vec, vec, cols, vec, rows, vec),
        out_specs=(tokens, tokens, vec, vec, cols, rows, rows, vec, vec, vec, cols, vec, rows, vec),
        check_vma=False,
    )
```

```python
import functools
import math

import jax
import jax.numpy as jnp
from jax import lax
from jax.experimental import pallas as pl
from jax.experimental.pallas import tpu as pltpu
from jax.sharding import PartitionSpec as P


def standardize(values):
    centre = values - jnp.mean(values, axis=-1, keepdims=True)
    spread = jnp.mean(centre * centre, axis=-1, keepdims=True)
    rate = lax.rsqrt(spread + norm_eps)
    return centre * rate, rate


def norm_grad(direction, z, rate):
    mean_d = jnp.mean(direction, axis=-1, keepdims=True)
    mean_dz = jnp.mean(direction * z, axis=-1, keepdims=True)
    return rate * (direction - mean_d - z * mean_dz)


norm_eps = 1e-05

HD = 64
WINDOW = 1024
BLK = 256
PENALTY = 1e30


def nt(a, b):
    return lax.dot_general(a, b, (((1,), (1,)), ((), ())), preferred_element_type=jnp.float32)


def nn(a, b):
    return lax.dot_general(a, b, (((1,), (0,)), ((), ())), preferred_element_type=jnp.float32)


def tn(a, b):
    return lax.dot_general(a, b, (((0,), (0,)), ((), ())), preferred_element_type=jnp.float32)


def split3(v):
    hi = v.astype(jnp.bfloat16).astype(jnp.float32)
    rest = v - hi
    mid = rest.astype(jnp.bfloat16).astype(jnp.float32)
    return hi, mid, rest - mid


def merge_edges(mask, tiles):
    return [jnp.where(mask, tiles[0], tiles[-1])] + tiles[1:-1]


def spread_edges(mask, tiles):
    zero = jnp.zeros_like(tiles[0])
    return [jnp.where(mask, tiles[0], zero)] + tiles[1:] + [jnp.where(mask, zero, tiles[0])]


def edge_mask():
    rows = lax.broadcasted_iota(jnp.int32, (BLK, BLK), 0)
    cols = lax.broadcasted_iota(jnp.int32, (BLK, BLK), 1)
    return rows > cols


def xor(a, b, size):
    total, bit = 0, 1
    while bit < size:
        total = total + bit * lax.rem(lax.div(a, bit) + lax.div(b, bit), 2)
        bit *= 2
    return total


MESH = pl.DeviceIdType.MESH
SLOT_AT = (3, 2, 5, 4, 1, 0, 7, 6)
STEP_OF = tuple(SLOT_AT.index(r) for r in range(8))
NEAR = 6


def enter(peers):
    barrier = pltpu.get_barrier_semaphore()
    for peer in peers:
        pl.semaphore_signal(barrier, inc=1, device_id={"fsdp": peer}, device_id_type=MESH)
    pl.semaphore_wait(barrier, len(peers))


def attend_kernel(
    heads, group, qkv_ref, augk_ref, augq_ref, out_w, fc_w, proj_w,
    out_ref, q2_ref, halo_ref, merged_ref, out_all, fc_all, proj_all,
    keys, values, values_t, sent, behind, own_sems, send_sems, recv_sems, halo_sems, w_own, w_send, w_recv,
):
    step = pl.program_id(0)
    last = pl.num_programs(0) - 1
    me = lax.axis_index("fsdp")
    line = lax.axis_index("seq")
    line_end = lax.axis_size("seq") - 1
    at = [xor(me, k, group) for k in range(group)]
    seqs, rows = qkv_ref.shape[0], qkv_ref.shape[1]
    half = group // 2
    seq = lax.rem(lax.div(step, half), 2)
    lower = lax.div(step, group)
    place = (1 - lower) * half + lax.rem(step + me, half)
    width = heads * 2 * HD
    low = jnp.bfloat16

    def halo_copy():
        return pltpu.make_async_remote_copy(
            src_ref=qkv_ref.at[:, pl.ds(rows - WINDOW, WINDOW), pl.ds(0, width)],
            dst_ref=behind, send_sem=halo_sems.at[0], recv_sem=halo_sems.at[1],
            device_id={"seq": lax.rem(line + 1, line_end + 1)}, device_id_type=MESH,
        )

    weights = ((out_w, out_all, False), (fc_w, fc_all, True), (proj_w, proj_all, True))

    def slot(a, r):
        return weights[a][1].at[STEP_OF[r] if weights[a][2] else r]

    def w_copy(a, r, second=False):
        to = at[1] if r % 2 else at[r]
        src = weights[a][0] if r in (1, 2, 4) else slot(a, r - 1) if r % 2 else None
        dst, sem = slot(a, r), r
        if r == 6:
            size = weights[a][0].shape[0] // 2
            part = pl.ds(size if second else 0, size)
            src = slot(a, 4 if second else 2).at[part]
            to = at[2] if second else at[4]
            dst, sem = dst.at[part], 0 if second else 6
        return pltpu.make_async_remote_copy(
            src_ref=src, dst_ref=dst, send_sem=w_send.at[a, sem], recv_sem=w_recv.at[a, sem],
            device_id={"fsdp": to}, device_id_type=MESH,
        )

    def w_keep(a):
        return pltpu.make_async_copy(weights[a][0], slot(a, 0), w_own.at[a])

    even = lax.rem(line, 2)
    partner = line + 1 - 2 * even
    p_size = proj_w.shape[0] // 2
    p_part = pl.ds(pl.multiple_of(even * p_size, p_size), p_size)

    def p_near(r):
        return pltpu.make_async_remote_copy(
            src_ref=proj_w.at[p_part], dst_ref=slot(2, r).at[p_part], send_sem=w_send.at[2, r],
            recv_sem=w_recv.at[2, r], device_id={"fsdp": at[r]}, device_id_type=MESH,
        )

    def p_line(r):
        sem = 5 + r // 2
        return pltpu.make_async_remote_copy(
            src_ref=slot(2, r).at[p_part], dst_ref=slot(2, r).at[p_part], send_sem=w_send.at[2, sem],
            recv_sem=w_recv.at[2, sem], device_id={"seq": partner}, device_id_type=MESH,
        )

    def forward(a):
        w_copy(a, 2).wait_recv()
        w_copy(a, 3).start()
        w_copy(a, 4).wait_recv()
        w_copy(a, 5).start()
        if not weights[a][2]:
            w_copy(a, 6).start()
            w_copy(a, 6, True).start()

    @pl.when(step == 0)
    def _():
        barrier = pltpu.get_barrier_semaphore()
        for peer in at[1:]:
            pl.semaphore_signal(barrier, inc=1, device_id={"fsdp": peer}, device_id_type=MESH)

        pl.semaphore_signal(
            barrier, inc=1, device_id={"seq": lax.rem(line + line_end, line_end + 1)}, device_id_type=MESH
        )
        pl.semaphore_signal(barrier, inc=1, device_id={"seq": partner}, device_id_type=MESH)
        pl.semaphore_wait(barrier, group + 1)

        @pl.when(line < line_end)
        def _():
            halo_copy().start()

        for r in (2, 4, 1):
            w_copy(0, r).start()
        for r in (2, 4):
            p_near(r).start()
        w_copy(2, 1).start()
        w_keep(0).start()
        for s in range(seqs):
            fill_keys(s, heads, qkv_ref, augk_ref, WINDOW, keys, values, values_t, None)

    @pl.when(step == group)
    def _():
        @pl.when(line > 0)
        def _():
            halo_copy().wait_recv()

        @pl.when(line == 0)
        def _():
            behind[...] = jnp.zeros_like(behind)

        halo_ref[...] = behind[...]
        for s in range(seqs):
            fill_keys(s, heads, behind, augk_ref, 0, keys, values, values_t, None)

    mask = edge_mask()
    tiles = WINDOW // BLK + 1
    start = pl.multiple_of(place * BLK, BLK)
    lane = lax.broadcasted_iota(jnp.int32, (BLK, 2 * HD), 1)
    lse_lane = augq_ref.shape[2] + HD - 3
    slot_k = xor(me, place, group)
    spans = [pl.ds(pl.multiple_of(start + b * BLK, BLK), BLK) for b in range(tiles)]
    for h in range(heads):
        sh = seq * heads + h
        qc = heads * 2 * HD + h * HD
        q = jnp.concatenate(
            [qkv_ref[seq, pl.ds(start, BLK), qc : qc + HD] * 0.125, augq_ref[seq, pl.ds(start, BLK), :]], axis=1
        )
        scores = merge_edges(mask, [nt(keys[sh, s, :], q) for s in spans])
        peak = functools.reduce(jnp.maximum, scores)
        peak = jnp.max(peak, axis=0, keepdims=True)
        weights_ = spread_edges(mask, [jnp.exp(s - peak).astype(low) for s in scores])
        total = sum(nn(values_t[sh, :, s], w) for s, w in zip(spans, weights_))
        sub = lax.broadcasted_iota(jnp.int32, total.shape, 0)
        total = jnp.where(sub == HD + 1, peak, total).T
        norm = total[:, HD : HD + 1]
        part = (total[:, :HD] / norm).astype(low)
        out_ref[seq, pl.ds(start, BLK), h * HD : (h + 1) * HD] = part
        sent[step, :, h * HD : (h + 1) * HD] = part
        lse = total[:, HD + 1 : HD + 2] + jnp.log(norm)
        hi, mid, lo = split3(-lse)
        q2 = q.astype(jnp.float32)
        q2 = jnp.where(lane == lse_lane, hi, q2)
        q2 = jnp.where(lane == lse_lane + 1, mid, q2)
        q2 = jnp.where(lane == lse_lane + 2, lo, q2)
        q2_ref[seq, h, pl.ds(start, BLK), :] = q2.astype(low)

    span = sent.shape[2]

    def landing(s, k):
        return merged_ref.at[s, :, pl.ds(pl.multiple_of(k * span, span), span)]

    def own(s):
        return pltpu.make_async_copy(sent.at[step], landing(s, 0), own_sems.at[s])

    def away(s, k, to):
        return pltpu.make_async_remote_copy(
            src_ref=sent.at[step], dst_ref=landing(s, k), send_sem=send_sems.at[s, k], recv_sem=recv_sems.at[s, k],
            device_id={"fsdp": to}, device_id_type=MESH,
        )

    @pl.when(place == me)
    def _():
        own(seq).start()

    @pl.when(place != me)
    def _():
        away(seq, slot_k, place).start()

    @pl.when(step == 3)
    def _():
        forward(0)
        for r in (2, 4, 1):
            w_copy(1, r).start()

    @pl.when(step == 6)
    def _():
        for r in (2, 4):
            p_near(r).wait_recv()
            p_line(r).start()

    @pl.when(step == 10)
    def _():
        w_copy(0, 6).wait_recv()
        w_copy(0, 6, True).wait_recv()
        w_copy(0, 7).start()

    @pl.when(step == last)
    def _():
        forward(1)
        for r in (2, 4):
            p_line(r).wait_recv()
            w_copy(2, r + 1).start()
        for s in range(seqs):
            own(s).wait()
            for k in range(1, group):
                away(s, k, at[k]).wait()
        w_keep(0).wait()
        for a in range(2):
            for r in (1, 2, 3, 4, 5):
                w_copy(a, r).wait_send()
            for r in (1, 3, 5):
                w_copy(a, r).wait_recv()
        for r in (2, 4):
            p_near(r).wait_send()
            p_line(r).wait_send()
        for r in (1, 3, 5):
            w_copy(2, r).wait()
        w_copy(0, 6).wait_send()
        w_copy(0, 6, True).wait_send()
        w_copy(0, 7).wait()

        @pl.when(line < line_end)
        def _():
            halo_copy().wait_send()


def fill_keys(s, heads, source, augk_ref, base, keys, values, values_t, keys_t):
    size = BLK
    ones = jnp.ones((size, HD), jnp.bfloat16)
    first = source.shape[1] - WINDOW if base == 0 else 0
    for h in range(heads):
        c = h * 2 * HD
        for i in range(source.shape[1] // size):
            pair = source[s, i * size : (i + 1) * size, c : c + 2 * HD]
            span = slice(base + i * size, base + (i + 1) * size)
            k = jnp.concatenate([pair[:, :HD], augk_ref[s, span, :]], axis=1)
            v = jnp.concatenate([pair[:, HD:], ones], axis=1)
            keys[s * heads + h, span, :] = k
            values[s * heads + h, span, :] = v
            if values_t is not None:
                values_t[s * heads + h, :, span] = v.T
            if keys_t is not None:
                keys_t[s * heads + h, :, span] = k.T


def attend(qkv, augk, augq, out_w, fc_w, proj_w, heads, group):
    seqs, rows, cols = qkv.shape
    ext = augk.shape[1]
    assert rows // BLK == group
    low = jnp.bfloat16
    vmem = pl.BlockSpec(memory_space=pltpu.VMEM)
    hbm = pl.BlockSpec(memory_space=pl.ANY)
    every = seqs * heads
    return pl.pallas_call(
        functools.partial(attend_kernel, heads, group),
        grid=(seqs * rows // BLK,),
        in_specs=[vmem] * 3 + [hbm] * 3,
        out_specs=[vmem] * 3 + [hbm] * 4,
        out_shape=[
            jax.ShapeDtypeStruct((seqs, rows, heads * HD), low),
            jax.ShapeDtypeStruct((seqs, heads, rows, 2 * HD), low),
            jax.ShapeDtypeStruct((seqs, WINDOW, heads * 2 * HD), low),
            jax.ShapeDtypeStruct((seqs, BLK, group * heads * HD), low),
        ]
        + [jax.ShapeDtypeStruct((n,) + w.shape, low) for n, w in ((group, out_w), (NEAR - 1, fc_w), (NEAR - 1, proj_w))],
        scratch_shapes=[
            pltpu.VMEM((every, ext, 2 * HD), low),
            pltpu.VMEM((every, ext, 2 * HD), low),
            pltpu.VMEM((every, 2 * HD, ext), low),
            pltpu.VMEM((seqs * rows // BLK, BLK, heads * HD), low),
            pltpu.VMEM((seqs, WINDOW, heads * 2 * HD), low),
            pltpu.SemaphoreType.DMA((seqs,)),
            pltpu.SemaphoreType.DMA((seqs, group)),
            pltpu.SemaphoreType.DMA((seqs, group)),
            pltpu.SemaphoreType.DMA((2,)),
            pltpu.SemaphoreType.DMA((1,)),
            pltpu.SemaphoreType.DMA((3, group)),
            pltpu.SemaphoreType.DMA((3, group)),
        ],
        compiler_params=pltpu.CompilerParams(vmem_limit_bytes=56 * 2**20, collective_id=1, has_side_effects=True),
        name="attend",
    )(qkv, augk, augq, out_w, fc_w, proj_w)


def mask_features(segment_ext, docs):
    doc = jnp.arange(docs, dtype=jnp.int32)
    hot = (segment_ext[..., None] == doc).astype(jnp.bfloat16)
    rows = segment_ext.shape[1]
    outside = (segment_ext < 0).astype(jnp.bfloat16)[..., None]
    pad = HD - docs - 4
    one = jnp.ones(segment_ext.shape + (3,), jnp.bfloat16)
    zero = jnp.zeros(segment_ext.shape + (pad,), jnp.bfloat16)
    keys = jnp.concatenate([-hot, -outside, zero, one], axis=-1)
    own = hot[:, WINDOW:]
    queries = jnp.concatenate(
        [
            (1 - own) * jnp.bfloat16(PENALTY),
            jnp.full(own.shape[:2] + (1,), PENALTY, jnp.bfloat16),
            jnp.zeros(own.shape[:2] + (pad + 3,), jnp.bfloat16),
        ],
        axis=-1,
    )
    return keys, queries


def gather_project_kernel(
    x_ref, *rest,
):
    parts, rest = rest[:7], rest[7:]
    project_kernel(x_ref, parts, *rest)


def project_kernel(
    x_ref, parts, w_ref, b_ref, all_small_ref, pieces_out, qkv_ref,
    z1, pieces, smalls, small_ref, small_send, small_recv, send_sems, recv_sems, out_sems,
):
    group = all_small_ref.shape[0]
    me = lax.axis_index("fsdp")
    at = [xor(me, k, group) for k in range(group)]
    rows = x_ref.shape[0] // 2
    f32, low = jnp.float32, jnp.bfloat16
    enter(at[1:])

    def small_copy(k):
        return pltpu.make_async_remote_copy(
            src_ref=small_ref, dst_ref=smalls.at[me], send_sem=small_send.at[k], recv_sem=small_recv.at[k],
            device_id={"fsdp": at[k]}, device_id_type=MESH,
        )

    row = 0
    small_ref[...] = jnp.zeros_like(small_ref)
    for part in parts:
        small_ref[row : row + part.shape[0], :] = part[...]
        row += part.shape[0]
    for k in range(1, group):
        small_copy(k).start()
    smalls[me] = small_ref[...]

    def chunk(p, s):
        return pieces.at[p, s]

    def move(r, s):
        if r % 2:
            piece, to = at[r - 1], at[1]
        elif r == 6:
            piece, to = (at[2], at[4]) if s == 0 else (at[4], at[2])
        else:
            piece, to = me, at[r]
        return pltpu.make_async_remote_copy(
            src_ref=chunk(piece, s), dst_ref=chunk(piece, s), send_sem=send_sems.at[r, s], recv_sem=recv_sems.at[r, s],
            device_id={"fsdp": to}, device_id_type=MESH,
        )

    def keep(k, s):
        return pltpu.make_async_copy(chunk(at[k], s), pieces_out.at[s, pl.ds(pl.multiple_of(at[k] * rows, rows), rows)], out_sems.at[k, s])

    def project(k, s):
        keep(k, s).start()
        start = pl.multiple_of(at[k] * rows, rows)
        qkv_ref[s, pl.ds(start, rows), :] = (nn(pieces[at[k], s], w_ref[...]) + b_ref[...]).astype(low)

    for s in range(2):
        z1[s * rows : (s + 1) * rows, :] = standardize(x_ref[s * rows : (s + 1) * rows, :].astype(f32))[0]
    for k in range(1, group):
        small_copy(k).wait()
    gain = jnp.concatenate([smalls[f, 0:1, :] for f in range(group)], axis=1).astype(f32)
    offset = jnp.concatenate([smalls[f, 1:2, :] for f in range(group)], axis=1).astype(f32)
    for s in range(2):
        pieces[me, s] = (z1[s * rows : (s + 1) * rows, :] * gain + offset).astype(low)
        move(2, s).start()
        move(4, s).start()
        move(1, s).start()
    all_small_ref[...] = smalls[...]
    for s in range(2):
        project(0, s)
    for s in range(2):
        move(1, s).wait_recv()
        project(1, s)
    for s in range(2):
        move(2, s).wait_recv()
        if s == 0:
            move(6, 0).start()
        move(3, s).start()
        move(4, s).wait_recv()
        if s == 1:
            move(6, 1).start()
        move(5, s).start()
        project(2, s)
        project(4, s)
    for s in range(2):
        move(3, s).wait_recv()
        project(3, s)
        move(5, s).wait_recv()
        project(5, s)
    for s in range(2):
        move(6, s).wait_recv()
        move(7, s).start()
        project(6, s)
    for s in range(2):
        move(7, s).wait_recv()
        project(7, s)
    for s in range(2):
        for r in range(1, group):
            move(r, s).wait_send()
        for k in range(group):
            keep(k, s).wait()


def gather_project(x, smalls, weight, bias, group):
    rows, width = x.shape
    cols = weight.shape[1]
    half = rows // 2
    span = smalls[0].shape[1]
    vmem = pl.BlockSpec(memory_space=pltpu.VMEM)
    low = jnp.bfloat16
    return pl.pallas_call(
        gather_project_kernel,
        in_specs=[vmem] * 10,
        out_specs=[vmem, pl.BlockSpec(memory_space=pl.ANY), vmem],
        out_shape=[
            jax.ShapeDtypeStruct((group, 16, span), low),
            jax.ShapeDtypeStruct((2, group * half, width), low),
            jax.ShapeDtypeStruct((2, group * half, cols), low),
        ],
        scratch_shapes=[
            pltpu.VMEM((rows, width), jnp.float32),
            pltpu.VMEM((group, 2, half, width), low),
            pltpu.VMEM((group, 16, span), low),
            pltpu.VMEM((16, span), low),
            pltpu.SemaphoreType.DMA((group,)),
            pltpu.SemaphoreType.DMA((group,)),
            pltpu.SemaphoreType.DMA((group, 2)),
            pltpu.SemaphoreType.DMA((group, 2)),
            pltpu.SemaphoreType.DMA((group, 2)),
        ],
        compiler_params=pltpu.CompilerParams(
            vmem_limit_bytes=48 * 2**20, collective_id=2, has_side_effects=True
        ),
        name="gather_project",
    )(x, *smalls, weight, bias)


def gelu_both(v):
    c = math.sqrt(2.0 / math.pi)
    square = v * v
    t = jnp.tanh(v * (c + (c * 0.044715) * square))
    half = 0.5 * (1.0 + t)
    slope = half + (0.5 * v) * (1.0 - t * t) * (c + (3.0 * 0.044715 * c) * square)
    return v * half, slope


def column_sums(array):
    return jnp.sum(array, axis=0, keepdims=True)


def feed_forward_kernel(
    group, x_ref, cot_ref, merged_ref, out_ref, fc_near, proj_near, fc_own, proj_own, fcb_ref, vec_ref,
    layer_ref, gres_ref, gheads_ref, keep_ref, side_ref, gout_ref, gvec_ref, gfcb_ref,
    resid, z2, rate, normed, total, gnormed, fc_w, proj_w, given, taken, gmerged, gout_given, gout_taken,
    load_sems, far_send, far_recv, pair_send, pair_recv, side_send, side_recv, keep_sems, head_send, head_recv,
    own_sem, gout_sems,
):
    step = pl.program_id(0)
    last = group - 1
    me = lax.axis_index("fsdp")
    at = [xor(me, k, group) for k in range(group)]
    rows = x_ref.shape[0]
    block = rows // 2
    f32, low = jnp.float32, jnp.bfloat16
    span = merged_ref.shape[1] // group

    def load(a, i):
        near, here = ((fc_near, fc_w), (proj_near, proj_w))[a]
        return pltpu.make_async_copy(near.at[i], here.at[lax.rem(i, 2)], load_sems.at[a, lax.rem(i, 2)])

    def load_own(a):
        i = (NEAR - 1) % 2
        return pltpu.make_async_copy((fc_own, proj_own)[a], (fc_w, proj_w)[a].at[i], load_sems.at[a, i])

    def far_copy(a, way):
        near, here = ((fc_near, fc_w), (proj_near, proj_w))[a]
        size = near.shape[1] // 2
        if way == 2:
            src, dst, to = here.at[3], here.at[2], at[1]
        else:
            part = pl.ds(way * size, size)
            src, dst = near.at[STEP_OF[(2, 4)[way]], part], here.at[3, part]
            to = at[(4, 2)[way]]
        return pltpu.make_async_remote_copy(
            src_ref=src, dst_ref=dst, send_sem=far_send.at[a, way], recv_sem=far_recv.at[a, way],
            device_id={"fsdp": to}, device_id_type=MESH,
        )

    def pair_copy(j):
        return pltpu.make_async_remote_copy(
            src_ref=given.at[lax.rem(j, 2)], dst_ref=taken.at[j], send_sem=pair_send.at[j], recv_sem=pair_recv.at[j],
            device_id={"fsdp": at[1]}, device_id_type=MESH,
        )

    def side_copy(a):
        return pltpu.make_async_remote_copy(
            src_ref=taken.at[a, a], dst_ref=side_ref.at[a], send_sem=side_send.at[a], recv_sem=side_recv.at[a],
            device_id={"fsdp": at[(2, 4)[a]]}, device_id_type=MESH,
        )

    def keep_copy(j):
        return pltpu.make_async_copy(taken.at[j], keep_ref.at[j], keep_sems.at[j])

    def head_copy(k):
        src = gmerged.at[:, :, pl.ds(k * span, span)]
        dst = gheads_ref.at[:, pl.ds(pl.multiple_of(me * block, block), block), :]
        if k == 0:
            return pltpu.make_async_copy(src, dst, own_sem)
        return pltpu.make_async_remote_copy(
            src_ref=src, dst_ref=dst, send_sem=head_send.at[k], recv_sem=head_recv.at[k],
            device_id={"fsdp": at[k]}, device_id_type=MESH,
        )

    def gout_copy():
        return pltpu.make_async_remote_copy(
            src_ref=gout_given, dst_ref=gout_taken, send_sem=gout_sems.at[0], recv_sem=gout_sems.at[1],
            device_id={"fsdp": at[1]}, device_id_type=MESH,
        )

    @pl.when(step == 0)
    def _():
        enter(at[1:])
        for a in range(2):
            load(a, 0).start()
        for a in range(2):
            far_copy(a, 0).start()
            far_copy(a, 1).start()
        acc = x_ref[...].astype(f32) + vec_ref[0:1, :] + nn(merged_ref[...], out_ref[...])
        resid[...] = acc
        z, r = standardize(acc)
        z2[...] = z
        rate[...] = jnp.broadcast_to(r, rate.shape)
        normed[...] = (z * vec_ref[1:2, :] + vec_ref[2:3, :]).astype(low)
        total[...] = jnp.zeros_like(total)
        gnormed[...] = jnp.zeros_like(gnormed)

    j = lax.div(step, 2)
    odd = lax.rem(step, 2)

    @pl.when(step < NEAR - 1)
    def _():
        for a in range(2):
            load(a, step).wait()

    @pl.when(step == NEAR - 1)
    def _():
        for a in range(2):
            load_own(a).wait()

    @pl.when(step + 1 < NEAR - 1)
    def _():
        for a in range(2):
            load(a, step + 1).start()

    @pl.when(step + 1 == NEAR - 1)
    def _():
        for a in range(2):
            load_own(a).start()

    @pl.when(step == NEAR)
    def _():
        for a in range(2):
            far_copy(a, 2).wait_recv()

    @pl.when((odd == 0) & (j >= 2))
    def _():
        pair_copy(j - 2).wait_send()

    here = jnp.where(step < NEAR, lax.rem(step, 2), step - NEAR + 2)
    fresh = jnp.where(odd == 0, lax.rem(j, 2), 2)
    hidden = nn(normed[...], fc_w[here]) + fcb_ref[0]
    gactive = nt(cot_ref[...], proj_w[here])
    active, slope = gelu_both(hidden)
    active = active.astype(low)
    ghidden = gactive * slope
    gfcb_ref[0] = column_sums(ghidden)
    ghidden = ghidden.astype(low)
    total[...] += nn(active, proj_w[here])
    gnormed[...] += nt(ghidden, fc_w[here])
    given[fresh, 0] = tn(normed[...], ghidden).astype(low)
    gproj = tn(active, cot_ref[...]).astype(low)
    size, part = gproj.shape[0], fc_w.shape[2]
    for i in range(gproj.shape[1] // part):
        given[fresh, 1, i * size : (i + 1) * size, :] = gproj[:, i * part : (i + 1) * part]

    @pl.when(odd == 0)
    def _():
        pair_copy(j).start()

    @pl.when(odd == 1)
    def _():
        pair_copy(j).wait_recv()

        def add(i, _):
            part = pl.ds(pl.multiple_of(lax.rem(i, 8) * 128, 128), 128)
            a = lax.div(i, 8)
            taken[j, a, part, :] = (taken[j, a, part, :].astype(f32) + given[2, a, part, :].astype(f32)).astype(low)
            return 0

        lax.fori_loop(0, 16, add, 0)
        keep_copy(j).start()

    for a in range(2):
        @pl.when(step == 1 + 2 * a)
        def _(a=a):
            side_copy(a).start()

    @pl.when(step == 3)
    def _():
        for a in range(2):
            far_copy(a, 0).wait_recv()
            far_copy(a, 1).wait_recv()
            far_copy(a, 2).start()

    @pl.when(step == last)
    def _():
        cot32 = cot_ref[...].astype(f32)
        g, z = gnormed[...], z2[...]
        gres = cot32 + norm_grad(g * vec_ref[1:2, :], z, rate[:, :1])
        gres_ref[...] = gres
        gattn = gres.astype(low)
        back = nt(gattn, out_ref[...]).astype(low)
        for s in range(2):
            gmerged[s] = back[s * block : (s + 1) * block, :]
        for k in (6, 2, 4, 3, 5, 7, 1, 0):
            head_copy(k).start()
        gout = tn(merged_ref[...], gattn)
        for k in range(1, group, 2):
            gout_given[k // 2] = gout[k * span : (k + 1) * span, :].astype(low)
        gout_copy().start()
        layer_ref[...] = (resid[...] + total[...] + vec_ref[3:4, :]).astype(low)
        gvec_ref[0:1, :] = column_sums(gattn.astype(f32))
        gvec_ref[1:2, :] = column_sums(g * z)
        gvec_ref[2:3, :] = column_sums(g)
        gvec_ref[3:4, :] = column_sums(cot32)
        gout_copy().wait_recv()
        for k in range(0, group, 2):
            mine = gout[k * span : (k + 1) * span, :].astype(low).astype(f32)
            gout_ref[k // 2] = (mine + gout_taken[k // 2].astype(f32)).astype(low)
        for k in range(group):
            head_copy(k).wait()
        gout_copy().wait_send()
        for a in range(2):
            for way in range(3):
                far_copy(a, way).wait_send()
        pair_copy(2).wait_send()
        pair_copy(3).wait_send()
        side_copy(0).wait()
        side_copy(1).wait()
        for i in range(group // 2):
            keep_copy(i).wait()


def feed_forward(x, cot, merged, out_all, fc_near, proj_near, fc_own, proj_own, fc_bias, vectors):
    rows, width = x.shape
    group, part = fc_bias.shape[0], fc_near.shape[2]
    span = width // group
    f32, low = jnp.float32, jnp.bfloat16
    vmem = pl.BlockSpec(memory_space=pltpu.VMEM)
    hbm = pl.BlockSpec(memory_space=pl.ANY)
    return pl.pallas_call(
        functools.partial(feed_forward_kernel, group),
        grid=(group,),
        in_specs=[
            vmem, vmem, vmem, vmem,
            hbm, hbm, hbm, hbm,
            pl.BlockSpec((1, 1, part), lambda i: (i, 0, 0)),
            vmem,
        ],
        out_specs=[
            vmem, vmem, hbm,
            hbm, hbm, vmem, vmem,
            pl.BlockSpec((1, 1, part), lambda i: (i, 0, 0)),
        ],
        out_shape=[
            jax.ShapeDtypeStruct((rows, width), low),
            jax.ShapeDtypeStruct((rows, width), f32),
            jax.ShapeDtypeStruct((2, group * rows // 2, span), low),
            jax.ShapeDtypeStruct((group // 2, 2, width, part), low),
            jax.ShapeDtypeStruct((2, width, part), low),
            jax.ShapeDtypeStruct((group // 2, span, width), low),
            jax.ShapeDtypeStruct((8, width), f32),
            jax.ShapeDtypeStruct((group, 1, part), f32),
        ],
        scratch_shapes=[
            pltpu.VMEM((rows, width), f32),
            pltpu.VMEM((rows, width), f32),
            pltpu.VMEM((rows, 128), f32),
            pltpu.VMEM((rows, width), low),
            pltpu.VMEM((rows, width), f32),
            pltpu.VMEM((rows, width), f32),
            pltpu.VMEM((4, width, part), low),
            pltpu.VMEM((4, part, width), low),
            pltpu.VMEM((3, 2, width, part), low),
            pltpu.VMEM((group // 2, 2, width, part), low),
            pltpu.VMEM((2, rows // 2, width), low),
            pltpu.VMEM((group // 2, span, width), low),
            pltpu.VMEM((group // 2, span, width), low),
            pltpu.SemaphoreType.DMA((2, 2)),
            pltpu.SemaphoreType.DMA((2, 3)),
            pltpu.SemaphoreType.DMA((2, 3)),
            pltpu.SemaphoreType.DMA((group // 2,)),
            pltpu.SemaphoreType.DMA((group // 2,)),
            pltpu.SemaphoreType.DMA((2,)),
            pltpu.SemaphoreType.DMA((2,)),
            pltpu.SemaphoreType.DMA((group // 2,)),
            pltpu.SemaphoreType.DMA((group,)),
            pltpu.SemaphoreType.DMA((group,)),
            pltpu.SemaphoreType.DMA,
            pltpu.SemaphoreType.DMA((2,)),
        ],
        compiler_params=pltpu.CompilerParams(vmem_limit_bytes=62 * 2**20, collective_id=3, has_side_effects=True),
        name="feed_forward",
    )(x, cot, merged, out_all, fc_near, proj_near, fc_own, proj_own, fc_bias, vectors)


def attend_back_kernel(
    heads, group, qkv_ref, halo_ref, augk_ref, q2_ref, out_ref, grad_ref, kept, side,
    gqkv_ref, sums_ref,
    keys, values, keys_t, dkeys, dvalues, edge, ahead, mid, near, far, mine, met,
    edge_sems, load_sems, near_send, near_recv, far_send, far_recv,
):
    step = pl.program_id(0)
    last = pl.num_programs(0) - 1
    me = lax.axis_index("fsdp")
    line = lax.axis_index("seq")
    line_end = lax.axis_size("seq") - 1
    at = [xor(me, k, group) for k in range(group)]
    seqs, rows = qkv_ref.shape[0], qkv_ref.shape[1]
    half = group // 2
    seq = lax.rem(lax.div(step, half), 2)
    place = lax.div(step, group) * half + lax.rem(step, half)
    f32, low = jnp.float32, jnp.bfloat16
    pieces = 2
    size = mid.shape[1] // pieces

    def edge_copy(s):
        return pltpu.make_async_remote_copy(
            src_ref=edge.at[s], dst_ref=ahead.at[s], send_sem=edge_sems.at[0, s], recv_sem=edge_sems.at[1, s],
            device_id={"seq": lax.rem(line + line_end, line_end + 1)}, device_id_type=MESH,
        )

    first, second = (at[2], at[4]), (at[4], at[2])

    def near_copy(a, h):
        part = pl.ds(h * size, size)
        return pltpu.make_async_remote_copy(
            src_ref=kept.at[3, a, part], dst_ref=near.at[a, part], send_sem=near_send.at[a, h],
            recv_sem=near_recv.at[a, h], device_id={"fsdp": first[a]}, device_id_type=MESH,
        )

    def far_copy(a, h):
        part = pl.ds(h * size, size)
        return pltpu.make_async_remote_copy(
            src_ref=mid.at[a, part], dst_ref=far.at[a, part], send_sem=far_send.at[a, h],
            recv_sem=far_recv.at[a, h], device_id={"fsdp": second[a]}, device_id_type=MESH,
        )

    def loads():
        for a in range(2):
            yield pltpu.make_async_copy(kept.at[1 - a, a], mid.at[a], load_sems.at[0, a])
            yield pltpu.make_async_copy(kept.at[2, a], mine.at[a], load_sems.at[1, a])
            yield pltpu.make_async_copy(side.at[a], met.at[a], load_sems.at[2, a])

    def plus(u, *more):
        total = u.astype(f32)
        for v in more:
            total += v.astype(f32)
        return total.astype(low)

    @pl.when(step == 0)
    def _():
        barrier = pltpu.get_barrier_semaphore()
        for peer in (at[2], at[4]):
            pl.semaphore_signal(barrier, inc=1, device_id={"fsdp": peer}, device_id_type=MESH)
        pl.semaphore_signal(
            barrier, inc=1, device_id={"seq": lax.rem(line + 1, line_end + 1)}, device_id_type=MESH
        )
        pl.semaphore_wait(barrier, 3)
        for h in range(pieces):
            for a in range(2):
                near_copy(a, h).start()
        for load in loads():
            load.start()
        for s in range(seqs):
            fill_keys(s, heads, halo_ref, augk_ref, 0, keys, values, None, keys_t)
            fill_keys(s, heads, qkv_ref, augk_ref, WINDOW, keys, values, None, keys_t)
        dkeys[...] = jnp.zeros_like(dkeys)
        dvalues[...] = jnp.zeros_like(dvalues)

    for s in range(seqs):
        @pl.when((step == (s + 1) * half) & (line > 0))
        def _(s=s):
            for h in range(heads):
                c = h * 2 * HD
                edge[s, :, c : c + 2 * HD] = jnp.concatenate(
                    [dkeys[s * heads + h, :WINDOW, :HD], dvalues[s * heads + h, :WINDOW, :HD]], axis=1
                ).astype(low)
            edge_copy(s).start()

    mask = edge_mask()
    tiles = WINDOW // BLK + 1
    start = pl.multiple_of(place * BLK, BLK)
    lane = lax.broadcasted_iota(jnp.int32, (BLK, 2 * HD), 1)
    spans = [pl.ds(pl.multiple_of(start + b * BLK, BLK), BLK) for b in range(tiles)]
    for h in range(heads):
        sh = seq * heads + h
        q = q2_ref[0, h]
        g32 = grad_ref[0, :, h * HD : (h + 1) * HD].astype(f32)
        centre = jnp.sum(g32 * out_ref[0, :, h * HD : (h + 1) * HD].astype(f32), axis=1, keepdims=True)
        hi, md, lo = split3(-centre)
        g2 = jnp.concatenate([g32, jnp.zeros((BLK, HD), f32)], axis=1)
        g2 = jnp.where(lane == HD, hi, g2)
        g2 = jnp.where(lane == HD + 1, md, g2)
        g2 = jnp.where(lane == HD + 2, lo, g2).astype(low)
        scores = merge_edges(mask, [nt(keys[sh, s, :], q) for s in spans])
        wgrads = merge_edges(mask, [nt(values[sh, s, :], g2) for s in spans])
        weights = [jnp.exp(s) for s in scores]
        sgrads = spread_edges(mask, [(w * d).astype(low) for w, d in zip(weights, wgrads)])
        weights = spread_edges(mask, [w.astype(low) for w in weights])
        for s, w, d in zip(spans, weights, sgrads):
            dvalues[sh, s, :] += nn(w, g2)
            dkeys[sh, s, :] += nn(d, q)
        dq = sum(nn(keys_t[sh, :, s], d) for s, d in zip(spans, sgrads))
        qc = heads * 2 * HD + h * HD
        gqkv_ref[seq, pl.ds(start, BLK), qc : qc + HD] = (dq.T[:, :HD] * 0.125).astype(low)

    def relay(h):
        part = slice(h * size, (h + 1) * size)
        for a in range(2):
            near_copy(a, h).wait_recv()
            mid[a, part] = plus(mid[a, part], near[a, part])
            far_copy(a, h).start()

    @pl.when(step == 4)
    def _():
        for load in loads():
            load.wait()
        relay(0)

    @pl.when(step == 8)
    def _():
        relay(1)

    @pl.when(step == last)
    def _():
        for s in range(seqs):
            for h in range(heads):
                c = h * 2 * HD
                own = jnp.concatenate(
                    [dkeys[s * heads + h, WINDOW:, :HD], dvalues[s * heads + h, WINDOW:, :HD]], axis=1
                )
                gqkv_ref[s, : rows - WINDOW, c : c + 2 * HD] = own[: rows - WINDOW].astype(low)
                dkeys[s * heads + h, WINDOW:, :] = own

        @pl.when(line < line_end)
        def _():
            for s in range(seqs):
                edge_copy(s).wait_recv()

        @pl.when(line == line_end)
        def _():
            ahead[...] = jnp.zeros_like(ahead)

        for s in range(seqs):
            for h in range(heads):
                c = h * 2 * HD
                own = dkeys[s * heads + h, rows:, :]
                gqkv_ref[s, rows - WINDOW :, c : c + 2 * HD] = (
                    own + ahead[s, :, c : c + 2 * HD].astype(f32)
                ).astype(low)

        for h in range(pieces):
            part = slice(h * size, (h + 1) * size)
            for a in range(2):
                far_copy(a, h).wait_recv()
                sums_ref[a, part] = plus(mine[a, part], met[a, part], far[a, part])
        for a in range(2):
            for h in range(pieces):
                near_copy(a, h).wait_send()
                far_copy(a, h).wait_send()

        @pl.when(line > 0)
        def _():
            for s in range(seqs):
                edge_copy(s).wait_send()


def attend_back(qkv, halo, augk, q2, out, grad, kept, side, heads, group):
    seqs, rows, cols = qkv.shape
    ext = augk.shape[1]
    half = group // 2
    f32, low = jnp.float32, jnp.bfloat16
    vmem = pl.BlockSpec(memory_space=pltpu.VMEM)
    hbm = pl.BlockSpec(memory_space=pl.ANY)
    every = seqs * heads
    part = kept.shape[2:]
    seq_of = lambda i: lax.rem(lax.div(i, half), 2)
    place_of = lambda i: lax.div(i, group) * half + lax.rem(i, half)
    edge = pltpu.VMEM((seqs, WINDOW, heads * 2 * HD), low)
    pair = pltpu.VMEM((2,) + part, low)
    return pl.pallas_call(
        functools.partial(attend_back_kernel, heads, group),
        grid=(seqs * rows // BLK,),
        in_specs=[
            vmem, vmem, vmem,
            pl.BlockSpec((1, heads, BLK, 2 * HD), lambda i: (seq_of(i), 0, place_of(i), 0)),
            pl.BlockSpec((1, BLK, heads * HD), lambda i: (seq_of(i), place_of(i), 0)),
            pl.BlockSpec((1, BLK, heads * HD), lambda i: (seq_of(i), place_of(i), 0)),
            hbm, hbm,
        ],
        out_specs=[vmem, vmem],
        out_shape=[
            jax.ShapeDtypeStruct((seqs, rows, cols), low),
            jax.ShapeDtypeStruct((2,) + part, low),
        ],
        scratch_shapes=[
            pltpu.VMEM((every, ext, 2 * HD), low),
            pltpu.VMEM((every, ext, 2 * HD), low),
            pltpu.VMEM((every, 2 * HD, ext), low),
            pltpu.VMEM((every, ext, 2 * HD), f32),
            pltpu.VMEM((every, ext, 2 * HD), f32),
            edge, edge, pair, pair, pair, pair, pair,
            pltpu.SemaphoreType.DMA((2, seqs)),
            pltpu.SemaphoreType.DMA((3, 2)),
            pltpu.SemaphoreType.DMA((2, 2)),
            pltpu.SemaphoreType.DMA((2, 2)),
            pltpu.SemaphoreType.DMA((2, 2)),
            pltpu.SemaphoreType.DMA((2, 2)),
        ],
        compiler_params=pltpu.CompilerParams(vmem_limit_bytes=62 * 2**20, collective_id=4, has_side_effects=True),
        name="attend_back",
    )(qkv, halo, augk, q2, out, grad, kept, side)


def finish_kernel(
    g_ref, wt_ref, x_ref, gres_ref, small_ref, sums_ref, out_kept, gvec_ref, gfcb_ref, z_hbm,
    input_grad_ref, fc_total_ref, proj_total_ref, out_total_ref, qkv_total_ref, vec_ref,
    z_all, odd, odd_in, even, mine, first_in, second_in, mt, rows6, vec_out, vec_in, vec_line,
    acc, acc_out, acc_q, left, left_out, left_q, right, right_out, right_q, out_near, out_far, out_mid,
    z_sem, odd_send, odd_recv, near_send, near_recv, far_send, far_recv,
    vec_send, vec_recv, vl_send, vl_recv, line_send, line_recv, out_send, out_recv,
):
    group = small_ref.shape[0]
    me = lax.axis_index("fsdp")
    line = lax.axis_index("seq")
    line_size = 4
    at = [xor(me, k, group) for k in range(group)]
    block = x_ref.shape[0] // 2
    f32, low = jnp.float32, jnp.bfloat16
    width = x_ref.shape[1]
    span = small_ref.shape[2]
    heads = wt_ref.shape[0] // (3 * HD)
    outer = (line == 0) | (line == line_size - 1)
    inner = (line > 0) & (line < line_size - 1)

    def remote(src, dst, send, recv, to):
        return pltpu.make_async_remote_copy(
            src_ref=src, dst_ref=dst, send_sem=send, recv_sem=recv, device_id=to, device_id_type=MESH
        )

    barrier = pltpu.get_barrier_semaphore()
    for peer in at[1:]:
        pl.semaphore_signal(barrier, inc=1, device_id={"fsdp": peer}, device_id_type=MESH)
    others = [lax.rem(line + d, line_size) for d in range(1, line_size)]
    for other in others:
        pl.semaphore_signal(barrier, inc=1, device_id={"seq": other}, device_id_type=MESH)
    pl.semaphore_wait(barrier, group - 1 + line_size - 1)

    cut = sums_ref.shape[1] // 4
    fc_chunks, proj_chunks = [], []
    for i in range(4):
        part = pl.ds(i * cut, cut)
        fc_chunks.append([r.at[0, part] for r in (sums_ref, acc, left, right)] + [fc_total_ref.at[part]])
        there = proj_total_ref.at[pl.ds(i % 2 * cut, cut), pl.ds(i // 2 * sums_ref.shape[2], sums_ref.shape[2])]
        proj_chunks.append([r.at[1, part] for r in (sums_ref, acc, left, right)] + [there])
    cut = acc_q.shape[0] // 3
    qkv_chunks = [
        [r.at[pl.ds(i * cut, cut)] for r in (acc_q, acc_q, left_q, right_q, qkv_total_ref)] for i in range(3)
    ]
    out_chunk = [acc_out, acc_out, left_out, right_out, out_total_ref]
    chunks = fc_chunks + proj_chunks[:1] + qkv_chunks + proj_chunks[1:] + [out_chunk]
    early = 5

    def inwards(c):
        return remote(
            chunks[c][0], chunks[c][2], line_send.at[0, c], line_recv.at[0, c], {"seq": 1 + lax.div(line, line_size - 1)}
        )

    def across(c):
        return remote(
            chunks[c][1], chunks[c][3], line_send.at[1, c], line_recv.at[1, c], {"seq": line_size - 1 - line}
        )

    def outwards(c):
        return remote(
            chunks[c][4], chunks[c][3], line_send.at[2, c], line_recv.at[2, c],
            {"seq": lax.rem((line + line_size - 1) * (line_size - 1), 2 * (line_size - 1))},
        )

    def begin(cs):
        @pl.when(outer)
        def _():
            for c in cs:
                inwards(c).start()

    def collect(c):
        @pl.when(inner)
        def _():
            inwards(c).wait_recv()
            own, acc_c, left_c = chunks[c][:3]
            acc_c[...] = (own[...].astype(f32) + left_c[...].astype(f32)).astype(low)
            across(c).start()

    def settle(c):
        @pl.when(inner)
        def _():
            across(c).wait_recv()
            chunks[c][4][...] = (chunks[c][1][...].astype(f32) + chunks[c][3][...].astype(f32)).astype(low)
            outwards(c).start()

    def receive(c):
        @pl.when(outer)
        def _():
            outwards(c).wait_recv()
            chunks[c][4][...] = chunks[c][3][...]

    def advance(first, last):
        for c in range(first, last):
            collect(c)
            if c >= 1:
                settle(c - 1)
            if c >= 2:
                receive(c - 2)

    begin(range(early))
    load = pltpu.make_async_copy(z_hbm, z_all, z_sem)
    load.start()

    ways = (at[2], at[4])
    out_cut = out_kept.shape[1] // 2
    out_first = ((0, 1, 0), (0, 3, 1), (1, 2, 0), (1, 3, 1))

    def out_near_copy(n):
        h, slot, j = out_first[n]
        return pltpu.make_async_remote_copy(
            src_ref=out_kept.at[slot, pl.ds(h * out_cut, out_cut)], dst_ref=out_near.at[h, j], send_sem=out_send.at[n],
            recv_sem=out_recv.at[n], device_id={"fsdp": ways[h]}, device_id_type=MESH,
        )

    def out_far_copy(h):
        return pltpu.make_async_remote_copy(
            src_ref=out_mid.at[h], dst_ref=out_far.at[h], send_sem=out_send.at[4 + h],
            recv_sem=out_recv.at[4 + h], device_id={"fsdp": ways[1 - h]}, device_id_type=MESH,
        )

    for n in range(4):
        out_near_copy(n).start()

    def product(r, s):
        start = pl.multiple_of(at[r] * block, block)
        return nn(g_ref[s, pl.ds(start, block), :], wt_ref[...])

    def odd_copy(j):
        return remote(odd.at[j], odd_in.at[j], odd_send.at[j], odd_recv.at[j], {"fsdp": at[1]})

    for j in (3, 1, 2, 0):
        for s in range(2):
            odd[j, s] = product(2 * j + 1, s).astype(low)
        odd_copy(j).start()
    advance(0, 1)

    def near_copy(s, i):
        j = 3 if i == 0 else 1 + s
        return remote(even.at[j, s], first_in.at[s, i], near_send.at[s, i], near_recv.at[s, i], {"fsdp": ways[s]})

    def far_copy(s):
        return remote(even.at[2 - s, s], second_in.at[s], far_send.at[s], far_recv.at[s], {"fsdp": ways[1 - s]})

    for j in (3, 1, 2, 0):
        for s in range(2):
            part = product(2 * j, s)
            if s == 0:
                odd_copy(j).wait_recv()
            part += odd_in[j, s].astype(f32)
            if j == 0:
                mine[s] = part
            else:
                even[j, s] = part.astype(low)
                if j == 3:
                    near_copy(s, 0).start()
                elif j == 1 + s:
                    near_copy(s, 1).start()
        if j == 1:
            advance(1, 2)
    advance(2, 3)

    def wide(index):
        return jnp.concatenate([small_ref[f, index : index + 1, :] for f in range(group)], axis=1).astype(f32)

    gain = wide(0)
    load.wait()
    mt[...] = jnp.zeros_like(mt)
    steps = z_all.shape[1] // 512
    ones = jnp.ones((512, 128), low)

    def add_product(i, sums):
        rows = pl.ds(pl.multiple_of(lax.rem(i, steps) * 512, 512), 512)
        g = g_ref[lax.div(i, steps), rows, :]
        mt[...] += tn(g, z_all[lax.div(i, steps), rows, :])
        return sums + tn(g, ones)

    column = lax.fori_loop(0, steps // 2, add_product, jnp.zeros((g_ref.shape[2], 128), f32))
    advance(3, 4)
    column = lax.fori_loop(steps // 2, steps, add_product, column)
    for h in range(2):
        part = slice(h * out_cut, (h + 1) * out_cut)
        out_near_copy(2 * h + 1).wait_recv()
        out_mid[h] = (out_kept[2 - h, part].astype(f32) + out_near[h, 1].astype(f32)).astype(low)
        out_far_copy(h).start()
    advance(4, 5)
    column = lax.fori_loop(steps, 2 * steps, add_product, column)
    acc_q[...] = mt[...].astype(low)
    begin(range(early, len(chunks) - 1))

    def vec_copy(k):
        return remote(vec_out.at[k], vec_in.at[k], vec_send.at[k], vec_recv.at[k], {"fsdp": at[k]})

    for s in range(2):
        near_copy(s, 0).wait_recv()
        even[2 - s, s] = (even[2 - s, s].astype(f32) + first_in[s, 0].astype(f32)).astype(low)
        far_copy(s).start()

    advance(5, 6)
    for h in range(2):
        part = slice(h * out_cut, (h + 1) * out_cut)
        out_near_copy(2 * h).wait_recv()
        out_far_copy(h).wait_recv()
        acc_out[part] = (
            out_kept[0, part].astype(f32) + out_near[h, 0].astype(f32) + out_far[h].astype(f32)
        ).astype(low)
    begin([len(chunks) - 1])

    def line_copy(d):
        return remote(vec_line.at[line], vec_line.at[line], vl_send.at[d], vl_recv.at[d], {"seq": others[d]})

    advance(6, 7)
    gain_grad = offset_grad = jnp.zeros((1, width), f32)
    for s in range(2):
        near_copy(s, 1).wait_recv()
        far_copy(s).wait_recv()
        rows = slice(s * block, (s + 1) * block)
        e = mine[s] + first_in[s, 1].astype(f32) + second_in[s].astype(f32)
        z, rate = standardize(x_ref[rows, :].astype(f32))
        gain_grad += column_sums(e * z)
        offset_grad += column_sums(e)
        input_grad_ref[rows, :] = (gres_ref[rows, :] + norm_grad(e * gain, z, rate)).astype(low)
    rows6[0:1, :] = gain_grad
    rows6[1:2, :] = offset_grad
    rows6[2:6, :] = gvec_ref[0:4, :]
    row = column.T[0:1, :]
    vec_out[...] = jnp.zeros_like(vec_out)
    for k in range(group):
        vec_out[k, 0:6, :] = rows6[0:6, pl.ds(pl.multiple_of(at[k] * span, span), span)]
        for i in range(4):
            vec_out[k, 6 + i : 7 + i, :] = gfcb_ref[STEP_OF[k], :, i * span : (i + 1) * span]
    for h in range(heads):
        base = heads * 2 * HD + h * HD
        vec_out[0, 10 + h : 11 + h, :] = jnp.concatenate(
            [row[:, base : base + HD], row[:, h * 2 * HD + HD : (h + 1) * 2 * HD]], axis=1
        )

    for k in range(1, group):
        vec_copy(k).start()

    advance(7, 9)
    total = vec_out[0]
    for k in range(1, group):
        vec_copy(k).wait_recv()
        total += vec_in[k]
    vec_line[line] = total

    for d in range(line_size - 1):
        line_copy(d).start()

    advance(9, 11)
    for d in range(line_size - 1):
        line_copy(d).wait_recv()
    vec_ref[...] = vec_line[0] + vec_line[1] + vec_line[2] + vec_line[3]
    advance(11, 12)
    settle(11)
    receive(10)
    receive(11)
    for j in range(4):
        odd_copy(j).wait_send()
    for s in range(2):
        near_copy(s, 0).wait_send()
        near_copy(s, 1).wait_send()
        far_copy(s).wait_send()
    for n in range(4):
        out_near_copy(n).wait_send()
    for h in range(2):
        out_far_copy(h).wait_send()
    for k in range(1, group):
        vec_copy(k).wait_send()
    for d in range(line_size - 1):
        line_copy(d).wait_send()

    @pl.when(outer)
    def _():
        for c in range(len(chunks)):
            inwards(c).wait_send()

    @pl.when(inner)
    def _():
        for c in range(len(chunks)):
            across(c).wait_send()
            outwards(c).wait_send()


def finish(g, wt, x, gres, small, sums, out_kept, gvec, gfcb, z_all):
    rows, width = x.shape
    group = small.shape[0]
    half = rows // 2
    span = small.shape[2]
    f32, low = jnp.float32, jnp.bfloat16
    vmem = pl.BlockSpec(memory_space=pltpu.VMEM)
    dma = pltpu.SemaphoreType.DMA
    out_part = out_kept.shape[1:]
    half_out = (out_part[0] // 2, out_part[1])
    buffers = [pltpu.VMEM(sums.shape, low), pltpu.VMEM(out_part, low), pltpu.VMEM(wt.shape, low)]
    return pl.pallas_call(
        finish_kernel,
        in_specs=[vmem] * 9 + [pl.BlockSpec(memory_space=pl.ANY)],
        out_specs=[vmem] * 6,
        out_shape=[
            jax.ShapeDtypeStruct((rows, width), low),
            jax.ShapeDtypeStruct(sums.shape[1:], low),
            jax.ShapeDtypeStruct((sums.shape[2], sums.shape[1]), low),
            jax.ShapeDtypeStruct(out_part, low),
            jax.ShapeDtypeStruct(wt.shape, low),
            jax.ShapeDtypeStruct((16, span), f32),
        ],
        scratch_shapes=[
            pltpu.VMEM(z_all.shape, low),
            pltpu.VMEM((group // 2, 2, half, width), low),
            pltpu.VMEM((group // 2, 2, half, width), low),
            pltpu.VMEM((group // 2, 2, half, width), low),
            pltpu.VMEM((2, half, width), f32),
            pltpu.VMEM((2, 2, half, width), low),
            pltpu.VMEM((2, half, width), low),
            pltpu.VMEM(wt.shape, f32),
            pltpu.VMEM((8, width), f32),
            pltpu.VMEM((group, 16, span), f32),
            pltpu.VMEM((group, 16, span), f32),
            pltpu.VMEM((4, 16, span), f32),
        ]
        + buffers * 3
        + [pltpu.VMEM((2, 2) + half_out, low), pltpu.VMEM((2,) + half_out, low), pltpu.VMEM((2,) + half_out, low)]
        + [dma, dma((4,)), dma((4,)), dma((2, 2)), dma((2, 2)), dma((2,)), dma((2,))]
        + [dma((group,)), dma((group,)), dma((3,)), dma((3,)), dma((3, 12)), dma((3, 12)), dma((6,)), dma((6,))],
        compiler_params=pltpu.CompilerParams(vmem_limit_bytes=62 * 2**20, collective_id=5, has_side_effects=True),
        name="finish",
    )(g, wt, x, gres, small, sums, out_kept, gvec, gfcb, z_all)


def plain_fill_keys(heads, qkv_ref, halo_ref, augk_ref, keys, values):
    halo_rows = halo_ref.shape[1]
    rows = qkv_ref.shape[1]
    ones = jnp.ones((1, HD), jnp.bfloat16)
    for h in range(heads):
        c = h * 2 * HD
        for source, base, size in ((halo_ref, 0, halo_rows), (qkv_ref, halo_rows, rows)):
            pair = source[0, :, c : c + 2 * HD]
            keys[h, base : base + size, :] = jnp.concatenate(
                [pair[:, :HD], augk_ref[0, base : base + size, :]], axis=1
            )
            values[h, base : base + size, :] = jnp.concatenate(
                [pair[:, HD:], jnp.broadcast_to(ones, (size, HD))], axis=1
            )


def plain_attend_kernel(heads, qkv_ref, halo_ref, augk_ref, augq_ref, out_ref, q2_ref, keys, values, values_t):
    step = pl.program_id(1)
    nkeys = keys.shape[1]

    @pl.when(step == 0)
    def _():
        plain_fill_keys(heads, qkv_ref, halo_ref, augk_ref, keys, values)
        for h in range(heads):
            for b in range(nkeys // BLK):
                values_t[h, :, b * BLK : (b + 1) * BLK] = values[h, b * BLK : (b + 1) * BLK, :].T

    mask = edge_mask()
    tiles = WINDOW // BLK + 1
    start = pl.multiple_of(step * BLK, BLK)
    lane = lax.broadcasted_iota(jnp.int32, (BLK, 2 * HD), 1)
    lse_lane = augq_ref.shape[2] + HD - 3
    for h in range(heads):
        qc = heads * 2 * HD + h * HD
        q = jnp.concatenate([qkv_ref[0, pl.ds(start, BLK), qc : qc + HD] * 0.125, augq_ref[0]], axis=1)
        scores = [nt(keys[h, pl.ds(start + b * BLK, BLK), :], q) for b in range(tiles)]
        scores = merge_edges(mask, scores)
        peak = functools.reduce(jnp.maximum, scores)
        peak = jnp.max(peak, axis=0, keepdims=True)
        weights = spread_edges(mask, [jnp.exp(s - peak).astype(jnp.bfloat16) for s in scores])
        total = sum(
            nn(values_t[h, :, pl.ds(pl.multiple_of(start + b * BLK, BLK), BLK)], w) for b, w in enumerate(weights)
        )
        sub = lax.broadcasted_iota(jnp.int32, total.shape, 0)
        total = jnp.where(sub == HD + 1, peak, total).T
        norm = total[:, HD : HD + 1]
        out_ref[0, :, h * HD : (h + 1) * HD] = (total[:, :HD] / norm).astype(out_ref.dtype)
        lse = total[:, HD + 1 : HD + 2] + jnp.log(norm)
        hi, mid, low = split3(-lse)
        q2 = q.astype(jnp.float32)
        q2 = jnp.where(lane == lse_lane, hi, q2)
        q2 = jnp.where(lane == lse_lane + 1, mid, q2)
        q2 = jnp.where(lane == lse_lane + 2, low, q2)
        q2_ref[0, h] = q2.astype(jnp.bfloat16)


def plain_attend(qkv, halo, augk, augq, heads):
    seqs, rows, cols = qkv.shape
    ext = augk.shape[1]
    return pl.pallas_call(
        functools.partial(plain_attend_kernel, heads),
        grid=(seqs, rows // BLK),
        in_specs=[
            pl.BlockSpec((1, rows, cols), lambda s, i: (s, 0, 0)),
            pl.BlockSpec((1, WINDOW, heads * 2 * HD), lambda s, i: (s, 0, 0)),
            pl.BlockSpec((1, ext, HD), lambda s, i: (s, 0, 0)),
            pl.BlockSpec((1, BLK, HD), lambda s, i: (s, i, 0)),
        ],
        out_specs=[
            pl.BlockSpec((1, BLK, heads * HD), lambda s, i: (s, i, 0)),
            pl.BlockSpec((1, heads, BLK, 2 * HD), lambda s, i: (s, 0, i, 0)),
        ],
        out_shape=[
            jax.ShapeDtypeStruct((seqs, rows, heads * HD), jnp.bfloat16),
            jax.ShapeDtypeStruct((seqs, heads, rows, 2 * HD), jnp.bfloat16),
        ],
        scratch_shapes=[
            pltpu.VMEM((heads, ext, 2 * HD), jnp.bfloat16),
            pltpu.VMEM((heads, ext, 2 * HD), jnp.bfloat16),
            pltpu.VMEM((heads, 2 * HD, ext), jnp.bfloat16),
        ],
        compiler_params=pltpu.CompilerParams(vmem_limit_bytes=48 * 2**20),
        name="plain_attend",
    )(qkv, halo, augk, augq)


def plain_attend_back_kernel(
    heads, qkv_ref, halo_ref, augk_ref, q2_ref, out_ref, grad_ref, dq_ref, dkv_ref, dhalo_ref,
    keys, values, keys_t, dkeys, dvalues,
):
    step = pl.program_id(1)
    nkeys = keys.shape[1]

    @pl.when(step == 0)
    def _():
        plain_fill_keys(heads, qkv_ref, halo_ref, augk_ref, keys, values)
        for h in range(heads):
            for b in range(nkeys // BLK):
                keys_t[h, :, b * BLK : (b + 1) * BLK] = keys[h, b * BLK : (b + 1) * BLK, :].T
        dkeys[...] = jnp.zeros_like(dkeys)
        dvalues[...] = jnp.zeros_like(dvalues)

    mask = edge_mask()
    tiles = WINDOW // BLK + 1
    start = pl.multiple_of(step * BLK, BLK)
    lane = lax.broadcasted_iota(jnp.int32, (BLK, 2 * HD), 1)
    for h in range(heads):
        q = q2_ref[0, h]
        g = grad_ref[0, :, h * HD : (h + 1) * HD]
        g32 = g.astype(jnp.float32)
        centre = jnp.sum(g32 * out_ref[0, :, h * HD : (h + 1) * HD].astype(jnp.float32), axis=1, keepdims=True)
        hi, mid, low = split3(-centre)
        g2 = jnp.concatenate([g32, jnp.zeros((BLK, HD), jnp.float32)], axis=1)
        g2 = jnp.where(lane == HD, hi, g2)
        g2 = jnp.where(lane == HD + 1, mid, g2)
        g2 = jnp.where(lane == HD + 2, low, g2).astype(jnp.bfloat16)
        spans = [pl.ds(pl.multiple_of(start + b * BLK, BLK), BLK) for b in range(tiles)]
        scores = merge_edges(mask, [nt(keys[h, s, :], q) for s in spans])
        wgrads = merge_edges(mask, [nt(values[h, s, :], g2) for s in spans])
        weights = [jnp.exp(s) for s in scores]
        sgrads = spread_edges(mask, [(w * d).astype(jnp.bfloat16) for w, d in zip(weights, wgrads)])
        weights = spread_edges(mask, [w.astype(jnp.bfloat16) for w in weights])
        for s, w, d in zip(spans, weights, sgrads):
            dvalues[h, s, :] += nn(w, g2)
            dkeys[h, s, :] += nn(d, q)
        dq = sum(nn(keys_t[h, :, s], d) for s, d in zip(spans, sgrads))
        dq_ref[0, :, h * HD : (h + 1) * HD] = (dq.T[:, :HD] * 0.125).astype(dq_ref.dtype)

    @pl.when(step == pl.num_programs(1) - 1)
    def _():
        for h in range(heads):
            c = h * 2 * HD
            dhalo_ref[0, :, c : c + 2 * HD] = jnp.concatenate(
                [dkeys[h, :WINDOW, :HD], dvalues[h, :WINDOW, :HD]], axis=1
            ).astype(dhalo_ref.dtype)
            dkv_ref[0, :, c : c + 2 * HD] = jnp.concatenate(
                [dkeys[h, WINDOW:, :HD], dvalues[h, WINDOW:, :HD]], axis=1
            ).astype(dkv_ref.dtype)


def plain_attend_back(qkv, halo, augk, q2, out, grad, heads):
    seqs, rows, cols = qkv.shape
    ext = augk.shape[1]
    return pl.pallas_call(
        functools.partial(plain_attend_back_kernel, heads),
        grid=(seqs, rows // BLK),
        in_specs=[
            pl.BlockSpec((1, rows, cols), lambda s, i: (s, 0, 0)),
            pl.BlockSpec((1, WINDOW, heads * 2 * HD), lambda s, i: (s, 0, 0)),
            pl.BlockSpec((1, ext, HD), lambda s, i: (s, 0, 0)),
            pl.BlockSpec((1, heads, BLK, 2 * HD), lambda s, i: (s, 0, i, 0)),
            pl.BlockSpec((1, BLK, heads * HD), lambda s, i: (s, i, 0)),
            pl.BlockSpec((1, BLK, heads * HD), lambda s, i: (s, i, 0)),
        ],
        out_specs=[
            pl.BlockSpec((1, BLK, heads * HD), lambda s, i: (s, i, 0)),
            pl.BlockSpec((1, rows, heads * 2 * HD), lambda s, i: (s, 0, 0)),
            pl.BlockSpec((1, WINDOW, heads * 2 * HD), lambda s, i: (s, 0, 0)),
        ],
        out_shape=[
            jax.ShapeDtypeStruct((seqs, rows, heads * HD), jnp.bfloat16),
            jax.ShapeDtypeStruct((seqs, rows, heads * 2 * HD), jnp.float32),
            jax.ShapeDtypeStruct((seqs, WINDOW, heads * 2 * HD), jnp.bfloat16),
        ],
        scratch_shapes=[
            pltpu.VMEM((heads, ext, 2 * HD), jnp.bfloat16),
            pltpu.VMEM((heads, ext, 2 * HD), jnp.bfloat16),
            pltpu.VMEM((heads, 2 * HD, ext), jnp.bfloat16),
            pltpu.VMEM((heads, ext, 2 * HD), jnp.float32),
            pltpu.VMEM((heads, ext, 2 * HD), jnp.float32),
        ],
        compiler_params=pltpu.CompilerParams(vmem_limit_bytes=56 * 2**20),
        name="plain_attend_back",
    )(qkv, halo, augk, q2, out, grad)


def from_behind(block, axis, distance):
    devices = range(lax.axis_size(axis))
    route = [(i - distance, i) for i in devices if i - distance in devices]
    return lax.ppermute(block, axis, route)


def pack_columns(array, heads):
    parts = array.reshape(array.shape[:-1] + (heads, 3 * HD))
    lead = array.shape[:-1]
    return jnp.concatenate(
        [parts[..., HD:].reshape(lead + (-1,)), parts[..., :HD].reshape(lead + (-1,))], axis=-1
    )


def unpack_columns(array, heads):
    lead = array.shape[:-1]
    pairs = array[..., : heads * 2 * HD].reshape(lead + (heads, 2 * HD))
    queries = array[..., heads * 2 * HD :].reshape(lead + (heads, HD))
    return jnp.concatenate([queries, pairs], axis=-1).reshape(lead + (-1,))


def dot(subscripts, a, b):
    return jnp.einsum(subscripts, a, b, preferred_element_type=jnp.float32)


def general_body(
    inputs, cotangent, segment_ids, norm1_gain, norm1_bias, qkv_weight, qv_bias, out_weight, out_bias,
    norm2_gain, norm2_bias, fc_weight, fc_bias, proj_weight, proj_bias,
):
    group = lax.axis_size("fsdp")
    seqs, local_rows, width = inputs.shape
    part_rows = local_rows * group
    heads = qkv_weight.shape[1] // (3 * HD)
    docs = segment_ids.shape[1] // (2 * WINDOW)
    seq_index = lax.axis_index("seq")
    shard = norm1_gain.shape[0]

    small = jnp.concatenate([norm1_gain, norm1_bias, out_bias, norm2_gain, norm2_bias, proj_bias, fc_bias])
    small = lax.all_gather(small, "fsdp")
    gain1, offset1, out_off, gain2, offset2, proj_off = (
        small[:, i * shard : (i + 1) * shard].reshape(-1).astype(jnp.float32) for i in range(6)
    )
    fc_off = small[:, 6 * shard :].reshape(-1).astype(jnp.float32)
    out_all = lax.all_gather(out_weight, "fsdp", axis=0, tiled=True)
    fc_all = lax.all_gather(fc_weight, "fsdp")
    proj_all = lax.all_gather(proj_weight, "fsdp")

    padded_ids = jnp.concatenate([jnp.full((seqs, WINDOW), -1, jnp.int32), segment_ids], axis=1)
    segment_ext = lax.dynamic_slice_in_dim(padded_ids, seq_index * part_rows, WINDOW + part_rows, 1)
    augk, augq = mask_features(segment_ext, docs)

    x = inputs.astype(jnp.float32)
    z1, rate1 = standardize(x)
    normed1 = (z1 * gain1 + offset1).astype(jnp.bfloat16)
    normed1 = lax.all_gather(normed1, "fsdp", axis=1, tiled=True)
    packed_weight = pack_columns(qkv_weight, heads)
    head_bias = qv_bias.astype(jnp.float32)
    head_bias = jnp.concatenate(
        [head_bias[:, :HD], jnp.zeros((heads, HD), jnp.float32), head_bias[:, HD:]], axis=1
    ).reshape(-1)
    packed_bias = pack_columns(head_bias, heads)
    qkv = (dot("sre,ef->srf", normed1, packed_weight) + packed_bias).astype(jnp.bfloat16)
    halo = from_behind(qkv[:, part_rows - WINDOW :, : heads * 2 * HD], "seq", 1)
    head_out, q2 = plain_attend(qkv, halo, augk, augq, heads)
    merged = lax.all_to_all(head_out, "fsdp", split_axis=1, concat_axis=2, tiled=True)
    resid = x + dot("sre,ef->srf", merged, out_all) + out_off
    z2, rate2 = standardize(resid)
    normed2 = (z2 * gain2 + offset2).astype(jnp.bfloat16)
    fc_offset = fc_off.reshape(group, -1)
    hidden = dot("sre,gef->gsrf", normed2, fc_all) + fc_offset[:, None, None]
    active, gelu_back = jax.vjp(lambda v: jax.nn.gelu(v, approximate=True), hidden)
    active = active.astype(jnp.bfloat16)
    layer_output = (resid + dot("gsrf,gfd->srd", active, proj_all) + proj_off).astype(jnp.bfloat16)

    cot32 = cotangent.astype(jnp.float32)
    proj_bias_part = jnp.sum(cot32, axis=(0, 1))
    proj_weight_part = dot("gsrf,srd->gfd", active, cotangent)
    g_hidden = gelu_back(dot("srd,gfd->gsrf", cotangent, proj_all))[0].astype(jnp.bfloat16)
    fc_bias_part = jnp.sum(g_hidden, axis=(1, 2), dtype=jnp.float32).reshape(-1)
    fc_weight_part = dot("sre,gsrf->gef", normed2, g_hidden)
    g_norm2 = dot("gsrf,gef->sre", g_hidden, fc_all)
    gain2_part = jnp.sum(g_norm2 * z2, axis=(0, 1))
    offset2_part = jnp.sum(g_norm2, axis=(0, 1))
    g_resid = cot32 + norm_grad(g_norm2 * gain2, z2, rate2)
    g_attn = g_resid.astype(jnp.bfloat16)
    out_bias_part = jnp.sum(g_attn, axis=(0, 1), dtype=jnp.float32)
    out_weight_part = dot("sre,srd->ed", merged, g_attn)
    g_merged = dot("srd,ed->sre", g_attn, out_all).astype(jnp.bfloat16)
    g_heads = lax.all_to_all(g_merged, "fsdp", split_axis=2, concat_axis=1, tiled=True)

    low = jnp.bfloat16
    fc_grad = lax.psum_scatter(fc_weight_part.astype(low), "fsdp")
    proj_grad = lax.psum_scatter(proj_weight_part.astype(low), "fsdp")
    out_grad = lax.psum_scatter(out_weight_part.astype(low), "fsdp", scatter_dimension=0, tiled=True)
    fc_grad, proj_grad, out_grad = lax.psum((fc_grad, proj_grad, out_grad), "seq")

    dq, dkv, dhalo = plain_attend_back(qkv, halo, augk, q2, head_out, g_heads, heads)
    edge = from_behind(dhalo, "seq", -1)
    edge = jnp.pad(edge.astype(jnp.float32), ((0, 0), (part_rows - WINDOW, 0), (0, 0)))
    g_qkv = jnp.concatenate([(dkv + edge).astype(jnp.bfloat16), dq], axis=-1)
    qkv_grad = dot("sre,srf->ef", normed1, g_qkv)
    qkv_colsum = jnp.sum(g_qkv, axis=(0, 1), dtype=jnp.float32)
    g_norm1 = dot("srf,ef->sre", g_qkv, packed_weight).astype(jnp.bfloat16)
    g_norm1 = lax.psum_scatter(g_norm1, "fsdp", scatter_dimension=1, tiled=True).astype(jnp.float32)
    gain1_part = jnp.sum(g_norm1 * z1, axis=(0, 1))
    offset1_part = jnp.sum(g_norm1, axis=(0, 1))
    input_grad = (g_resid + norm_grad(g_norm1 * gain1, z1, rate1)).astype(jnp.bfloat16)

    qkv_grad = lax.psum(qkv_grad.astype(low), "seq").astype(jnp.float32)
    qkv_grad = unpack_columns(qkv_grad, heads)
    col = unpack_columns(qkv_colsum, heads).reshape(heads, 3 * HD)
    col = lax.psum(jnp.concatenate([col[:, :HD], col[:, 2 * HD :]], axis=1), "seq")
    vectors = jnp.concatenate(
        [
            v.reshape(group, -1)
            for v in (gain1_part, offset1_part, out_bias_part, gain2_part, offset2_part, proj_bias_part, fc_bias_part)
        ],
        axis=1,
    )
    vectors = lax.psum_scatter(vectors, "fsdp")
    vectors = lax.psum(vectors, "seq")
    parts = [vectors[i * shard : (i + 1) * shard] for i in range(6)] + [vectors[6 * shard :]]
    f32 = jnp.float32
    return (
        layer_output, input_grad, parts[0], parts[1], qkv_grad, col, out_grad.astype(f32), parts[2], parts[3],
        parts[4], fc_grad.astype(f32), parts[6], proj_grad.astype(f32), parts[5],
    )


def cube_body(
    inputs, cotangent, segment_ids, norm1_gain, norm1_bias, qkv_weight, qv_bias, out_weight, out_bias,
    norm2_gain, norm2_bias, fc_weight, fc_bias, proj_weight, proj_bias,
):
    group = lax.axis_size("fsdp")
    seqs, local_rows, width = inputs.shape
    part_rows = local_rows * group
    heads = qkv_weight.shape[1] // (3 * HD)
    docs = segment_ids.shape[1] // (2 * WINDOW)
    seq_index = lax.axis_index("seq")
    me = lax.axis_index("fsdp")
    shard = norm1_gain.shape[0]
    f32, low = jnp.float32, jnp.bfloat16

    smalls = [norm1_gain, norm1_bias, out_bias, norm2_gain, norm2_bias, proj_bias, fc_bias]
    smalls = [v.reshape(-1, shard) for v in smalls]
    padded_ids = jnp.concatenate([jnp.full((seqs, WINDOW), -1, jnp.int32), segment_ids], axis=1)
    segment_ext = lax.dynamic_slice_in_dim(padded_ids, seq_index * part_rows, WINDOW + part_rows, 1)
    augk, augq = mask_features(segment_ext, docs)
    packed_weight = pack_columns(qkv_weight, heads)
    head_bias = qv_bias.astype(f32)
    head_bias = jnp.concatenate(
        [head_bias[:, :HD], jnp.zeros((heads, HD), f32), head_bias[:, HD:]], axis=1
    ).reshape(-1)
    packed_bias = pack_columns(head_bias, heads)

    x = inputs.reshape(seqs * local_rows, width)
    cot = cotangent.reshape(seqs * local_rows, width)
    all_small, z1, qkv = gather_project(x, smalls, packed_weight, packed_bias[None], group)
    head_out, q2, halo, merged, out_all, fc_near, proj_near = attend(
        qkv, augk, augq, out_weight, fc_weight, proj_weight, heads, group
    )
    full = lambda i: all_small[:, i].reshape(-1).astype(f32)
    vectors = jnp.stack([full(2), full(3), full(4), full(5)] + [jnp.zeros((width,), f32)] * 4)
    slots = jnp.stack([xor(me, r, group) for r in SLOT_AT])
    fc_off = jnp.take(all_small[:, 6:10].reshape(group, -1), slots, axis=0).astype(f32)[:, None]
    layer_output, g_resid, g_heads, kept, side, out_kept, gvec, gfcb = feed_forward(
        x, cot, merged.reshape(x.shape), out_all.reshape(width, width), fc_near, proj_near, fc_weight, proj_weight, fc_off, vectors
    )
    g_qkv, sums = attend_back(qkv, halo, augk, q2, head_out, g_heads, kept, side, heads, group)
    input_grad, fc_grad, proj_grad, out_grad, qkv_grad, vecs = finish(
        g_qkv, packed_weight.T, x, g_resid, all_small, sums, out_kept, gvec, gfcb, z1
    )
    qkv_grad = unpack_columns(qkv_grad.T.astype(f32), heads)
    return (
        layer_output.reshape(inputs.shape), input_grad.reshape(inputs.shape), vecs[0], vecs[1], qkv_grad,
        vecs[10 : 10 + heads], out_grad.astype(f32), vecs[2], vecs[3], vecs[4], fc_grad.astype(f32), vecs[6:10].reshape(-1),
        proj_grad.astype(f32), vecs[5],
    )


def solution(mesh):
    tokens = P(None, ("seq", "fsdp"), None)
    rows, cols, vec = P("fsdp", None), P(None, "fsdp"), P("fsdp")
    return jax.shard_map(
        cube_body if mesh.shape["fsdp"] == 8 and mesh.shape["seq"] == 4 else general_body,
        mesh=mesh,
        in_specs=(tokens, tokens, P(), vec, vec, cols, rows, rows, vec, vec, vec, cols, vec, rows, vec),
        out_specs=(tokens, tokens, vec, vec, cols, rows, rows, vec, vec, vec, cols, vec, rows, vec),
        check_vma=False,
    )
```

```python
import functools
import math

import jax
import jax.numpy as jnp
from jax import lax
from jax.experimental import pallas as pl
from jax.experimental.pallas import tpu as pltpu
from jax.sharding import PartitionSpec as P


def standardize(values):
    centre = values - jnp.mean(values, axis=-1, keepdims=True)
    spread = jnp.mean(centre * centre, axis=-1, keepdims=True)
    rate = lax.rsqrt(spread + norm_eps)
    return centre * rate, rate


def norm_grad(direction, z, rate):
    mean_d = jnp.mean(direction, axis=-1, keepdims=True)
    mean_dz = jnp.mean(direction * z, axis=-1, keepdims=True)
    return rate * (direction - mean_d - z * mean_dz)


norm_eps = 1e-05

HD = 64
WINDOW = 1024
BLK = 256
PENALTY = 1e30


def nt(a, b):
    return lax.dot_general(a, b, (((1,), (1,)), ((), ())), preferred_element_type=jnp.float32)


def nn(a, b):
    return lax.dot_general(a, b, (((1,), (0,)), ((), ())), preferred_element_type=jnp.float32)


def tn(a, b):
    return lax.dot_general(a, b, (((0,), (0,)), ((), ())), preferred_element_type=jnp.float32)


def split3(v):
    hi = v.astype(jnp.bfloat16).astype(jnp.float32)
    rest = v - hi
    mid = rest.astype(jnp.bfloat16).astype(jnp.float32)
    return hi, mid, rest - mid


def merge_edges(mask, tiles):
    return [jnp.where(mask, tiles[0], tiles[-1])] + tiles[1:-1]


def spread_edges(mask, tiles):
    zero = jnp.zeros_like(tiles[0])
    return [jnp.where(mask, tiles[0], zero)] + tiles[1:] + [jnp.where(mask, zero, tiles[0])]


def edge_mask():
    rows = lax.broadcasted_iota(jnp.int32, (BLK, BLK), 0)
    cols = lax.broadcasted_iota(jnp.int32, (BLK, BLK), 1)
    return rows > cols


def xor(a, b, size):
    total, bit = 0, 1
    while bit < size:
        total = total + bit * lax.rem(lax.div(a, bit) + lax.div(b, bit), 2)
        bit *= 2
    return total


MESH = pl.DeviceIdType.MESH
SLOT_AT = (3, 2, 5, 4, 1, 0, 7, 6)
STEP_OF = tuple(SLOT_AT.index(r) for r in range(8))
NEAR = 6


def enter(peers):
    barrier = pltpu.get_barrier_semaphore()
    for peer in peers:
        pl.semaphore_signal(barrier, inc=1, device_id={"fsdp": peer}, device_id_type=MESH)
    pl.semaphore_wait(barrier, len(peers))


def attend_kernel(
    heads, group, docs, qkv_ref, ids_ref, out_w, fc_w, proj_w,
    out_ref, q2_ref, halo_ref, merged_ref, out_all, fc_all, proj_all,
    keys, values, values_t, sent, behind, own_sems, send_sems, recv_sems, halo_sems, w_own, w_send, w_recv,
):
    step = pl.program_id(0)
    last = pl.num_programs(0) - 1
    me = lax.axis_index("fsdp")
    line = lax.axis_index("seq")
    line_end = lax.axis_size("seq") - 1
    at = [xor(me, k, group) for k in range(group)]
    seqs, rows = qkv_ref.shape[0], qkv_ref.shape[1]
    half = group // 2
    seq = lax.rem(lax.div(step, half), 2)
    lower = lax.div(step, group)
    place = (1 - lower) * half + lax.rem(step + me, half)
    width = heads * 2 * HD
    low = jnp.bfloat16

    def halo_copy():
        return pltpu.make_async_remote_copy(
            src_ref=qkv_ref.at[:, pl.ds(rows - WINDOW, WINDOW), pl.ds(0, width)],
            dst_ref=behind, send_sem=halo_sems.at[0], recv_sem=halo_sems.at[1],
            device_id={"seq": lax.rem(line + 1, line_end + 1)}, device_id_type=MESH,
        )

    weights = ((out_w, out_all, False), (fc_w, fc_all, True), (proj_w, proj_all, True))

    def slot(a, r):
        return weights[a][1].at[STEP_OF[r] if weights[a][2] else r]

    def w_copy(a, r, second=False):
        to = at[1] if r % 2 else at[r]
        src = weights[a][0] if r in (1, 2, 4) else slot(a, r - 1) if r % 2 else None
        dst, sem = slot(a, r), r
        if r == 6:
            size = weights[a][0].shape[0] // 2
            part = pl.ds(size if second else 0, size)
            src = slot(a, 4 if second else 2).at[part]
            to = at[2] if second else at[4]
            dst, sem = dst.at[part], 0 if second else 6
        return pltpu.make_async_remote_copy(
            src_ref=src, dst_ref=dst, send_sem=w_send.at[a, sem], recv_sem=w_recv.at[a, sem],
            device_id={"fsdp": to}, device_id_type=MESH,
        )

    def w_keep(a):
        return pltpu.make_async_copy(weights[a][0], slot(a, 0), w_own.at[a])

    even = lax.rem(line, 2)
    partner = line + 1 - 2 * even
    p_size = proj_w.shape[0] // 2
    p_part = pl.ds(pl.multiple_of(even * p_size, p_size), p_size)

    def p_near(r):
        return pltpu.make_async_remote_copy(
            src_ref=proj_w.at[p_part], dst_ref=slot(2, r).at[p_part], send_sem=w_send.at[2, r],
            recv_sem=w_recv.at[2, r], device_id={"fsdp": at[r]}, device_id_type=MESH,
        )

    def p_line(r):
        sem = 5 + r // 2
        return pltpu.make_async_remote_copy(
            src_ref=slot(2, r).at[p_part], dst_ref=slot(2, r).at[p_part], send_sem=w_send.at[2, sem],
            recv_sem=w_recv.at[2, sem], device_id={"seq": partner}, device_id_type=MESH,
        )

    def forward(a):
        w_copy(a, 2).wait_recv()
        w_copy(a, 3).start()
        w_copy(a, 4).wait_recv()
        w_copy(a, 5).start()
        if not weights[a][2]:
            w_copy(a, 6).start()
            w_copy(a, 6, True).start()

    @pl.when(step == 0)
    def _():
        barrier = pltpu.get_barrier_semaphore()
        for peer in at[1:]:
            pl.semaphore_signal(barrier, inc=1, device_id={"fsdp": peer}, device_id_type=MESH)

        pl.semaphore_signal(
            barrier, inc=1, device_id={"seq": lax.rem(line + line_end, line_end + 1)}, device_id_type=MESH
        )
        pl.semaphore_signal(barrier, inc=1, device_id={"seq": partner}, device_id_type=MESH)
        pl.semaphore_wait(barrier, group + 1)

        @pl.when(line < line_end)
        def _():
            halo_copy().start()

        for r in (2, 4, 1):
            w_copy(0, r).start()
        for r in (2, 4):
            p_near(r).start()
        w_copy(2, 1).start()
        w_keep(0).start()
        for s in range(seqs):
            fill_keys(s, heads, qkv_ref, ids_ref, docs, WINDOW, keys, values, values_t, None)

    @pl.when(step == group)
    def _():
        @pl.when(line > 0)
        def _():
            halo_copy().wait_recv()

        @pl.when(line == 0)
        def _():
            behind[...] = jnp.zeros_like(behind)

        halo_ref[...] = behind[...]
        for s in range(seqs):
            fill_keys(s, heads, behind, ids_ref, docs, 0, keys, values, values_t, None)

    mask = edge_mask()
    tiles = WINDOW // BLK + 1
    start = pl.multiple_of(place * BLK, BLK)
    lane = lax.broadcasted_iota(jnp.int32, (BLK, 2 * HD), 1)
    lse_lane = 2 * HD - 3
    slot_k = xor(me, place, group)
    spans = [pl.ds(pl.multiple_of(start + b * BLK, BLK), BLK) for b in range(tiles)]
    q_marks = query_marks(ids_ref[seq, pl.ds(start + WINDOW, BLK), :], docs)
    for h in range(heads):
        sh = seq * heads + h
        qc = heads * 2 * HD + h * HD
        q = jnp.concatenate([qkv_ref[seq, pl.ds(start, BLK), qc : qc + HD] * 0.125, q_marks], axis=1)
        scores = merge_edges(mask, [nt(keys[sh, s, :], q) for s in spans])
        peak = functools.reduce(jnp.maximum, scores)
        peak = jnp.max(peak, axis=0, keepdims=True)
        weights_ = spread_edges(mask, [jnp.exp(s - peak).astype(low) for s in scores])
        total = sum(nn(values_t[sh, :, s], w) for s, w in zip(spans, weights_))
        sub = lax.broadcasted_iota(jnp.int32, total.shape, 0)
        total = jnp.where(sub == HD + 1, peak, total).T
        norm = total[:, HD : HD + 1]
        part = (total[:, :HD] / norm).astype(low)
        out_ref[seq, pl.ds(start, BLK), h * HD : (h + 1) * HD] = part
        sent[step, :, h * HD : (h + 1) * HD] = part
        lse = total[:, HD + 1 : HD + 2] + jnp.log(norm)
        hi, mid, lo = split3(-lse)
        q2 = q.astype(jnp.float32)
        q2 = jnp.where(lane == lse_lane, hi, q2)
        q2 = jnp.where(lane == lse_lane + 1, mid, q2)
        q2 = jnp.where(lane == lse_lane + 2, lo, q2)
        q2_ref[seq, h, pl.ds(start, BLK), :] = q2.astype(low)

    span = sent.shape[2]

    def landing(s, k):
        return merged_ref.at[s, :, pl.ds(pl.multiple_of(k * span, span), span)]

    def own(s):
        return pltpu.make_async_copy(sent.at[step], landing(s, 0), own_sems.at[s])

    def away(s, k, to):
        return pltpu.make_async_remote_copy(
            src_ref=sent.at[step], dst_ref=landing(s, k), send_sem=send_sems.at[s, k], recv_sem=recv_sems.at[s, k],
            device_id={"fsdp": to}, device_id_type=MESH,
        )

    @pl.when(place == me)
    def _():
        own(seq).start()

    @pl.when(place != me)
    def _():
        away(seq, slot_k, place).start()

    @pl.when(step == 3)
    def _():
        forward(0)
        for r in (2, 4, 1):
            w_copy(1, r).start()

    @pl.when(step == 6)
    def _():
        for r in (2, 4):
            p_near(r).wait_recv()
            p_line(r).start()

    @pl.when(step == 10)
    def _():
        w_copy(0, 6).wait_recv()
        w_copy(0, 6, True).wait_recv()
        w_copy(0, 7).start()

    @pl.when(step == last)
    def _():
        forward(1)
        for r in (2, 4):
            p_line(r).wait_recv()
            w_copy(2, r + 1).start()
        for s in range(seqs):
            own(s).wait()
            for k in range(1, group):
                away(s, k, at[k]).wait()
        w_keep(0).wait()
        for a in range(2):
            for r in (1, 2, 3, 4, 5):
                w_copy(a, r).wait_send()
            for r in (1, 3, 5):
                w_copy(a, r).wait_recv()
        for r in (2, 4):
            p_near(r).wait_send()
            p_line(r).wait_send()
        for r in (1, 3, 5):
            w_copy(2, r).wait()
        w_copy(0, 6).wait_send()
        w_copy(0, 6, True).wait_send()
        w_copy(0, 7).wait()

        @pl.when(line < line_end)
        def _():
            halo_copy().wait_send()


def key_marks(ids, docs):
    lane = lax.broadcasted_iota(jnp.int32, (ids.shape[0], HD), 1)
    ids = jnp.broadcast_to(ids, lane.shape)
    hidden = (lane == ids) | ((lane == docs) & (ids < 0))
    return jnp.where(hidden, -1.0, jnp.where(lane >= HD - 3, 1.0, 0.0)).astype(jnp.bfloat16)


def query_marks(ids, docs):
    lane = lax.broadcasted_iota(jnp.int32, (ids.shape[0], HD), 1)
    ids = jnp.broadcast_to(ids, lane.shape)
    return jnp.where((lane <= docs) & (lane != ids), PENALTY, 0.0).astype(jnp.bfloat16)


def fill_keys(s, heads, source, ids_ref, docs, base, keys, values, values_t, keys_t):
    size = BLK
    ones = jnp.ones((size, HD), jnp.bfloat16)
    for i in range(source.shape[1] // size):
        span = slice(base + i * size, base + (i + 1) * size)
        marks = key_marks(ids_ref[s, span, :], docs)
        for h in range(heads):
            c = h * 2 * HD
            pair = source[s, i * size : (i + 1) * size, c : c + 2 * HD]
            k = jnp.concatenate([pair[:, :HD], marks], axis=1)
            v = jnp.concatenate([pair[:, HD:], ones], axis=1)
            keys[s * heads + h, span, :] = k
            values[s * heads + h, span, :] = v
            if values_t is not None:
                values_t[s * heads + h, :, span] = v.T
            if keys_t is not None:
                keys_t[s * heads + h, :, span] = k.T


def attend(qkv, ids, docs, out_w, fc_w, proj_w, heads, group):
    seqs, rows, cols = qkv.shape
    ext = ids.shape[1]
    assert rows // BLK == group
    low = jnp.bfloat16
    vmem = pl.BlockSpec(memory_space=pltpu.VMEM)
    hbm = pl.BlockSpec(memory_space=pl.ANY)
    every = seqs * heads
    return pl.pallas_call(
        functools.partial(attend_kernel, heads, group, docs),
        grid=(seqs * rows // BLK,),
        in_specs=[vmem] * 2 + [hbm] * 3,
        out_specs=[vmem] * 3 + [hbm] * 4,
        out_shape=[
            jax.ShapeDtypeStruct((seqs, rows, heads * HD), low),
            jax.ShapeDtypeStruct((seqs, heads, rows, 2 * HD), low),
            jax.ShapeDtypeStruct((seqs, WINDOW, heads * 2 * HD), low),
            jax.ShapeDtypeStruct((seqs, BLK, group * heads * HD), low),
        ]
        + [jax.ShapeDtypeStruct((n,) + w.shape, low) for n, w in ((group, out_w), (NEAR - 1, fc_w), (NEAR - 1, proj_w))],
        scratch_shapes=[
            pltpu.VMEM((every, ext, 2 * HD), low),
            pltpu.VMEM((every, ext, 2 * HD), low),
            pltpu.VMEM((every, 2 * HD, ext), low),
            pltpu.VMEM((seqs * rows // BLK, BLK, heads * HD), low),
            pltpu.VMEM((seqs, WINDOW, heads * 2 * HD), low),
            pltpu.SemaphoreType.DMA((seqs,)),
            pltpu.SemaphoreType.DMA((seqs, group)),
            pltpu.SemaphoreType.DMA((seqs, group)),
            pltpu.SemaphoreType.DMA((2,)),
            pltpu.SemaphoreType.DMA((1,)),
            pltpu.SemaphoreType.DMA((3, group)),
            pltpu.SemaphoreType.DMA((3, group)),
        ],
        compiler_params=pltpu.CompilerParams(vmem_limit_bytes=56 * 2**20, collective_id=1, has_side_effects=True),
        name="attend",
    )(qkv, ids, out_w, fc_w, proj_w)


def mask_features(segment_ext, docs):
    low = jnp.bfloat16
    lane = lax.broadcasted_iota(jnp.int32, segment_ext.shape + (HD,), 2)
    ids = segment_ext[..., None]
    hidden = (lane == ids) | ((lane == docs) & (ids < 0))
    keys = jnp.where(hidden, -1.0, jnp.where(lane >= HD - 3, 1.0, 0.0)).astype(low)
    queries = jnp.where((lane <= docs) & (lane != ids), PENALTY, 0.0).astype(low)
    return keys, queries[:, WINDOW:]


def gather_project_kernel(
    x_ref, *rest,
):
    parts, rest = rest[:7], rest[7:]
    project_kernel(x_ref, parts, *rest)


def project_kernel(
    x_ref, parts, w_ref, b_ref, all_small_ref, pieces_out, qkv_ref,
    z1, pieces, smalls, small_ref, small_send, small_recv, send_sems, recv_sems, out_sems,
):
    group = all_small_ref.shape[0]
    me = lax.axis_index("fsdp")
    at = [xor(me, k, group) for k in range(group)]
    rows = x_ref.shape[0] // 2
    f32, low = jnp.float32, jnp.bfloat16
    enter(at[1:])

    def small_copy(k):
        return pltpu.make_async_remote_copy(
            src_ref=small_ref, dst_ref=smalls.at[me], send_sem=small_send.at[k], recv_sem=small_recv.at[k],
            device_id={"fsdp": at[k]}, device_id_type=MESH,
        )

    row = 0
    small_ref[...] = jnp.zeros_like(small_ref)
    for part in parts:
        small_ref[row : row + part.shape[0], :] = part[...]
        row += part.shape[0]
    for k in range(1, group):
        small_copy(k).start()
    smalls[me] = small_ref[...]

    def chunk(p, s):
        return pieces.at[p, s]

    def move(r, s):
        if r % 2:
            piece, to = at[r - 1], at[1]
        elif r == 6:
            piece, to = (at[2], at[4]) if s == 0 else (at[4], at[2])
        else:
            piece, to = me, at[r]
        return pltpu.make_async_remote_copy(
            src_ref=chunk(piece, s), dst_ref=chunk(piece, s), send_sem=send_sems.at[r, s], recv_sem=recv_sems.at[r, s],
            device_id={"fsdp": to}, device_id_type=MESH,
        )

    def keep(k, s):
        return pltpu.make_async_copy(chunk(at[k], s), pieces_out.at[s, pl.ds(pl.multiple_of(at[k] * rows, rows), rows)], out_sems.at[k, s])

    def project(k, s):
        keep(k, s).start()
        start = pl.multiple_of(at[k] * rows, rows)
        made = (nn(pieces[at[k], s], w_ref[...]) + bias).astype(low)
        head = [made[:, h * 3 * HD : (h + 1) * 3 * HD] for h in range(heads)]
        made = jnp.concatenate([h[:, HD:] for h in head] + [h[:, :HD] for h in head], axis=1)
        qkv_ref[s, pl.ds(start, rows), :] = made

    for s in range(2):
        z1[s * rows : (s + 1) * rows, :] = standardize(x_ref[s * rows : (s + 1) * rows, :].astype(f32))[0]
    for k in range(1, group):
        small_copy(k).wait()
    gain = jnp.concatenate([smalls[f, 0:1, :] for f in range(group)], axis=1).astype(f32)
    offset = jnp.concatenate([smalls[f, 1:2, :] for f in range(group)], axis=1).astype(f32)
    for s in range(2):
        pieces[me, s] = (z1[s * rows : (s + 1) * rows, :] * gain + offset).astype(low)
        move(2, s).start()
        move(4, s).start()
        move(1, s).start()
    all_small_ref[...] = smalls[...]
    heads = b_ref.shape[0]
    none = jnp.zeros((1, HD), f32)
    bias = [p for h in range(heads) for p in (b_ref[h : h + 1, :HD].astype(f32), none, b_ref[h : h + 1, HD:].astype(f32))]
    bias = jnp.concatenate(bias, axis=1)
    for s in range(2):
        project(0, s)
    for s in range(2):
        move(1, s).wait_recv()
        project(1, s)
    for s in range(2):
        move(2, s).wait_recv()
        if s == 0:
            move(6, 0).start()
        move(3, s).start()
        move(4, s).wait_recv()
        if s == 1:
            move(6, 1).start()
        move(5, s).start()
        project(2, s)
        project(4, s)
    for s in range(2):
        move(3, s).wait_recv()
        project(3, s)
        move(5, s).wait_recv()
        project(5, s)
    for s in range(2):
        move(6, s).wait_recv()
        move(7, s).start()
        project(6, s)
    for s in range(2):
        move(7, s).wait_recv()
        project(7, s)
    for s in range(2):
        for r in range(1, group):
            move(r, s).wait_send()
        for k in range(group):
            keep(k, s).wait()


def gather_project(x, smalls, weight, bias, group):
    rows, width = x.shape
    cols = weight.shape[1]
    half = rows // 2
    span = smalls[0].shape[1]
    vmem = pl.BlockSpec(memory_space=pltpu.VMEM)
    low = jnp.bfloat16
    return pl.pallas_call(
        gather_project_kernel,
        in_specs=[vmem] * 10,
        out_specs=[vmem, pl.BlockSpec(memory_space=pl.ANY), vmem],
        out_shape=[
            jax.ShapeDtypeStruct((group, 16, span), low),
            jax.ShapeDtypeStruct((2, group * half, width), low),
            jax.ShapeDtypeStruct((2, group * half, cols), low),
        ],
        scratch_shapes=[
            pltpu.VMEM((rows, width), jnp.float32),
            pltpu.VMEM((group, 2, half, width), low),
            pltpu.VMEM((group, 16, span), low),
            pltpu.VMEM((16, span), low),
            pltpu.SemaphoreType.DMA((group,)),
            pltpu.SemaphoreType.DMA((group,)),
            pltpu.SemaphoreType.DMA((group, 2)),
            pltpu.SemaphoreType.DMA((group, 2)),
            pltpu.SemaphoreType.DMA((group, 2)),
        ],
        compiler_params=pltpu.CompilerParams(
            vmem_limit_bytes=48 * 2**20, collective_id=2, has_side_effects=True
        ),
        name="gather_project",
    )(x, *smalls, weight, bias)


def gelu_both(v):
    c = math.sqrt(2.0 / math.pi)
    square = v * v
    t = jnp.tanh(v * (c + (c * 0.044715) * square))
    half = 0.5 * (1.0 + t)
    slope = half + (0.5 * v) * (1.0 - t * t) * (c + (3.0 * 0.044715 * c) * square)
    return v * half, slope


def column_sums(array):
    return jnp.sum(array, axis=0, keepdims=True)


def feed_forward_kernel(
    group, x_ref, cot_ref, merged_ref, out_ref, fc_near, proj_near, fc_own, proj_own, small_ref,
    layer_ref, gres_ref, gheads_ref, keep_ref, side_ref, gout_ref, gvec_ref, gfcb_ref,
    resid, z2, rate, vec_ref, normed, total, gnormed, fc_w, proj_w, given, taken, gmerged, gout_given, gout_taken,
    load_sems, far_send, far_recv, pair_send, pair_recv, side_send, side_recv, keep_sems, head_send, head_recv,
    own_sem, gout_sems,
):
    step = pl.program_id(0)
    last = group - 1
    me = lax.axis_index("fsdp")
    at = [xor(me, k, group) for k in range(group)]
    rows = x_ref.shape[0]
    block = rows // 2
    f32, low = jnp.float32, jnp.bfloat16
    span = merged_ref.shape[1] // group

    def load(a, i):
        near, here = ((fc_near, fc_w), (proj_near, proj_w))[a]
        return pltpu.make_async_copy(near.at[i], here.at[lax.rem(i, 2)], load_sems.at[a, lax.rem(i, 2)])

    def load_own(a):
        i = (NEAR - 1) % 2
        return pltpu.make_async_copy((fc_own, proj_own)[a], (fc_w, proj_w)[a].at[i], load_sems.at[a, i])

    def far_copy(a, way):
        near, here = ((fc_near, fc_w), (proj_near, proj_w))[a]
        size = near.shape[1] // 2
        if way == 2:
            src, dst, to = here.at[3], here.at[2], at[1]
        else:
            part = pl.ds(way * size, size)
            src, dst = near.at[STEP_OF[(2, 4)[way]], part], here.at[3, part]
            to = at[(4, 2)[way]]
        return pltpu.make_async_remote_copy(
            src_ref=src, dst_ref=dst, send_sem=far_send.at[a, way], recv_sem=far_recv.at[a, way],
            device_id={"fsdp": to}, device_id_type=MESH,
        )

    def pair_copy(j):
        return pltpu.make_async_remote_copy(
            src_ref=given.at[lax.rem(j, 2)], dst_ref=taken.at[j], send_sem=pair_send.at[j], recv_sem=pair_recv.at[j],
            device_id={"fsdp": at[1]}, device_id_type=MESH,
        )

    def side_copy(a):
        return pltpu.make_async_remote_copy(
            src_ref=taken.at[a, a], dst_ref=side_ref.at[a], send_sem=side_send.at[a], recv_sem=side_recv.at[a],
            device_id={"fsdp": at[(2, 4)[a]]}, device_id_type=MESH,
        )

    def keep_copy(j):
        return pltpu.make_async_copy(taken.at[j], keep_ref.at[j], keep_sems.at[j])

    def head_copy(k):
        src = gmerged.at[:, :, pl.ds(k * span, span)]
        dst = gheads_ref.at[:, pl.ds(pl.multiple_of(me * block, block), block), :]
        if k == 0:
            return pltpu.make_async_copy(src, dst, own_sem)
        return pltpu.make_async_remote_copy(
            src_ref=src, dst_ref=dst, send_sem=head_send.at[k], recv_sem=head_recv.at[k],
            device_id={"fsdp": at[k]}, device_id_type=MESH,
        )

    def gout_copy():
        return pltpu.make_async_remote_copy(
            src_ref=gout_given, dst_ref=gout_taken, send_sem=gout_sems.at[0], recv_sem=gout_sems.at[1],
            device_id={"fsdp": at[1]}, device_id_type=MESH,
        )

    @pl.when(step == 0)
    def _():
        enter(at[1:])
        for a in range(2):
            load(a, 0).start()
        for a in range(2):
            far_copy(a, 0).start()
            far_copy(a, 1).start()
        for i in range(4):
            vec_ref[i : i + 1, :] = jnp.concatenate(
                [small_ref[f, 2 + i : 3 + i, :] for f in range(group)], axis=1
            ).astype(f32)
        acc = x_ref[...].astype(f32) + vec_ref[0:1, :] + nn(merged_ref[...], out_ref[...])
        resid[...] = acc
        z, r = standardize(acc)
        z2[...] = z
        rate[...] = jnp.broadcast_to(r, rate.shape)
        normed[...] = (z * vec_ref[1:2, :] + vec_ref[2:3, :]).astype(low)
        total[...] = jnp.zeros_like(total)
        gnormed[...] = jnp.zeros_like(gnormed)

    j = lax.div(step, 2)
    odd = lax.rem(step, 2)

    @pl.when(step < NEAR - 1)
    def _():
        for a in range(2):
            load(a, step).wait()

    @pl.when(step == NEAR - 1)
    def _():
        for a in range(2):
            load_own(a).wait()

    @pl.when(step + 1 < NEAR - 1)
    def _():
        for a in range(2):
            load(a, step + 1).start()

    @pl.when(step + 1 == NEAR - 1)
    def _():
        for a in range(2):
            load_own(a).start()

    @pl.when(step == NEAR)
    def _():
        for a in range(2):
            far_copy(a, 2).wait_recv()

    @pl.when((odd == 0) & (j >= 2))
    def _():
        pair_copy(j - 2).wait_send()

    here = jnp.where(step < NEAR, lax.rem(step, 2), step - NEAR + 2)
    fresh = jnp.where(odd == 0, lax.rem(j, 2), 2)
    owner = sum(jnp.where(step == i, at[SLOT_AT[i]], 0) for i in range(group))
    fc_bias = jnp.concatenate([small_ref[owner, 6 + i : 7 + i, :] for i in range(4)], axis=1).astype(f32)
    hidden = nn(normed[...], fc_w[here]) + fc_bias
    gactive = nt(cot_ref[...], proj_w[here])
    active, slope = gelu_both(hidden)
    active = active.astype(low)
    ghidden = gactive * slope
    gfcb_ref[0] = column_sums(ghidden)
    ghidden = ghidden.astype(low)
    total[...] += nn(active, proj_w[here])
    gnormed[...] += nt(ghidden, fc_w[here])
    given[fresh, 0] = tn(normed[...], ghidden).astype(low)
    gproj = tn(active, cot_ref[...]).astype(low)
    size, part = gproj.shape[0], fc_w.shape[2]
    for i in range(gproj.shape[1] // part):
        given[fresh, 1, i * size : (i + 1) * size, :] = gproj[:, i * part : (i + 1) * part]

    @pl.when(odd == 0)
    def _():
        pair_copy(j).start()

    @pl.when(odd == 1)
    def _():
        pair_copy(j).wait_recv()

        def add(i, _):
            part = pl.ds(pl.multiple_of(lax.rem(i, 8) * 128, 128), 128)
            a = lax.div(i, 8)
            taken[j, a, part, :] = (taken[j, a, part, :].astype(f32) + given[2, a, part, :].astype(f32)).astype(low)
            return 0

        lax.fori_loop(0, 16, add, 0)
        keep_copy(j).start()

    for a in range(2):
        @pl.when(step == 1 + 2 * a)
        def _(a=a):
            side_copy(a).start()

    @pl.when(step == 3)
    def _():
        for a in range(2):
            far_copy(a, 0).wait_recv()
            far_copy(a, 1).wait_recv()
            far_copy(a, 2).start()

    @pl.when(step == last)
    def _():
        cot32 = cot_ref[...].astype(f32)
        g, z = gnormed[...], z2[...]
        gres = cot32 + norm_grad(g * vec_ref[1:2, :], z, rate[:, :1])
        gres_ref[...] = gres
        gattn = gres.astype(low)
        back = nt(gattn, out_ref[...]).astype(low)
        for s in range(2):
            gmerged[s] = back[s * block : (s + 1) * block, :]
        for k in (6, 2, 4, 3, 5, 7, 1, 0):
            head_copy(k).start()
        gout = tn(merged_ref[...], gattn)
        for k in range(1, group, 2):
            gout_given[k // 2] = gout[k * span : (k + 1) * span, :].astype(low)
        gout_copy().start()
        layer_ref[...] = (resid[...] + total[...] + vec_ref[3:4, :]).astype(low)
        gvec_ref[0:1, :] = column_sums(gattn.astype(f32))
        gvec_ref[1:2, :] = column_sums(g * z)
        gvec_ref[2:3, :] = column_sums(g)
        gvec_ref[3:4, :] = column_sums(cot32)
        gout_copy().wait_recv()
        for k in range(0, group, 2):
            mine = gout[k * span : (k + 1) * span, :].astype(low).astype(f32)
            gout_ref[k // 2] = (mine + gout_taken[k // 2].astype(f32)).astype(low)
        for k in range(group):
            head_copy(k).wait()
        gout_copy().wait_send()
        for a in range(2):
            for way in range(3):
                far_copy(a, way).wait_send()
        pair_copy(2).wait_send()
        pair_copy(3).wait_send()
        side_copy(0).wait()
        side_copy(1).wait()
        for i in range(group // 2):
            keep_copy(i).wait()


def feed_forward(x, cot, merged, out_all, fc_near, proj_near, fc_own, proj_own, small):
    rows, width = x.shape
    group, part = small.shape[0], fc_near.shape[2]
    span = width // group
    f32, low = jnp.float32, jnp.bfloat16
    vmem = pl.BlockSpec(memory_space=pltpu.VMEM)
    hbm = pl.BlockSpec(memory_space=pl.ANY)
    return pl.pallas_call(
        functools.partial(feed_forward_kernel, group),
        grid=(group,),
        in_specs=[
            vmem, vmem, vmem, vmem,
            hbm, hbm, hbm, hbm,
            vmem,
        ],
        out_specs=[
            vmem, vmem, hbm,
            hbm, hbm, vmem, vmem,
            pl.BlockSpec((1, 1, part), lambda i: (i, 0, 0)),
        ],
        out_shape=[
            jax.ShapeDtypeStruct((rows, width), low),
            jax.ShapeDtypeStruct((rows, width), f32),
            jax.ShapeDtypeStruct((2, group * rows // 2, span), low),
            jax.ShapeDtypeStruct((group // 2, 2, width, part), low),
            jax.ShapeDtypeStruct((2, width, part), low),
            jax.ShapeDtypeStruct((group // 2, span, width), low),
            jax.ShapeDtypeStruct((8, width), f32),
            jax.ShapeDtypeStruct((group, 1, part), f32),
        ],
        scratch_shapes=[
            pltpu.VMEM((rows, width), f32),
            pltpu.VMEM((rows, width), f32),
            pltpu.VMEM((rows, 128), f32),
            pltpu.VMEM((8, width), f32),
            pltpu.VMEM((rows, width), low),
            pltpu.VMEM((rows, width), f32),
            pltpu.VMEM((rows, width), f32),
            pltpu.VMEM((4, width, part), low),
            pltpu.VMEM((4, part, width), low),
            pltpu.VMEM((3, 2, width, part), low),
            pltpu.VMEM((group // 2, 2, width, part), low),
            pltpu.VMEM((2, rows // 2, width), low),
            pltpu.VMEM((group // 2, span, width), low),
            pltpu.VMEM((group // 2, span, width), low),
            pltpu.SemaphoreType.DMA((2, 2)),
            pltpu.SemaphoreType.DMA((2, 3)),
            pltpu.SemaphoreType.DMA((2, 3)),
            pltpu.SemaphoreType.DMA((group // 2,)),
            pltpu.SemaphoreType.DMA((group // 2,)),
            pltpu.SemaphoreType.DMA((2,)),
            pltpu.SemaphoreType.DMA((2,)),
            pltpu.SemaphoreType.DMA((group // 2,)),
            pltpu.SemaphoreType.DMA((group,)),
            pltpu.SemaphoreType.DMA((group,)),
            pltpu.SemaphoreType.DMA,
            pltpu.SemaphoreType.DMA((2,)),
        ],
        compiler_params=pltpu.CompilerParams(vmem_limit_bytes=62 * 2**20, collective_id=3, has_side_effects=True),
        name="feed_forward",
    )(x, cot, merged, out_all, fc_near, proj_near, fc_own, proj_own, small)


def attend_back_kernel(
    heads, group, docs, qkv_ref, halo_ref, ids_ref, q2_ref, out_ref, grad_ref, kept, side,
    gqkv_ref, sums_ref,
    keys, values, keys_t, dkeys, dvalues, edge, ahead, mid, near, far, mine, met,
    edge_sems, load_sems, near_send, near_recv, far_send, far_recv,
):
    step = pl.program_id(0)
    last = pl.num_programs(0) - 1
    me = lax.axis_index("fsdp")
    line = lax.axis_index("seq")
    line_end = lax.axis_size("seq") - 1
    at = [xor(me, k, group) for k in range(group)]
    seqs, rows = qkv_ref.shape[0], qkv_ref.shape[1]
    half = group // 2
    seq = lax.rem(lax.div(step, half), 2)
    place = lax.div(step, group) * half + lax.rem(step, half)
    f32, low = jnp.float32, jnp.bfloat16
    pieces = 2
    size = mid.shape[1] // pieces

    def edge_copy(s):
        return pltpu.make_async_remote_copy(
            src_ref=edge.at[s], dst_ref=ahead.at[s], send_sem=edge_sems.at[0, s], recv_sem=edge_sems.at[1, s],
            device_id={"seq": lax.rem(line + line_end, line_end + 1)}, device_id_type=MESH,
        )

    first, second = (at[2], at[4]), (at[4], at[2])

    def near_copy(a, h):
        part = pl.ds(h * size, size)
        return pltpu.make_async_remote_copy(
            src_ref=kept.at[3, a, part], dst_ref=near.at[a, part], send_sem=near_send.at[a, h],
            recv_sem=near_recv.at[a, h], device_id={"fsdp": first[a]}, device_id_type=MESH,
        )

    def far_copy(a, h):
        part = pl.ds(h * size, size)
        return pltpu.make_async_remote_copy(
            src_ref=mid.at[a, part], dst_ref=far.at[a, part], send_sem=far_send.at[a, h],
            recv_sem=far_recv.at[a, h], device_id={"fsdp": second[a]}, device_id_type=MESH,
        )

    def loads():
        for a in range(2):
            yield pltpu.make_async_copy(kept.at[1 - a, a], mid.at[a], load_sems.at[0, a])
            yield pltpu.make_async_copy(kept.at[2, a], mine.at[a], load_sems.at[1, a])
            yield pltpu.make_async_copy(side.at[a], met.at[a], load_sems.at[2, a])

    def plus(u, *more):
        total = u.astype(f32)
        for v in more:
            total += v.astype(f32)
        return total.astype(low)

    @pl.when(step == 0)
    def _():
        barrier = pltpu.get_barrier_semaphore()
        for peer in (at[2], at[4]):
            pl.semaphore_signal(barrier, inc=1, device_id={"fsdp": peer}, device_id_type=MESH)
        pl.semaphore_signal(
            barrier, inc=1, device_id={"seq": lax.rem(line + 1, line_end + 1)}, device_id_type=MESH
        )
        pl.semaphore_wait(barrier, 3)
        for h in range(pieces):
            for a in range(2):
                near_copy(a, h).start()
        for load in loads():
            load.start()
        for s in range(seqs):
            fill_keys(s, heads, halo_ref, ids_ref, docs, 0, keys, values, None, keys_t)
            fill_keys(s, heads, qkv_ref, ids_ref, docs, WINDOW, keys, values, None, keys_t)
        dkeys[...] = jnp.zeros_like(dkeys)
        dvalues[...] = jnp.zeros_like(dvalues)

    for s in range(seqs):
        @pl.when((step == (s + 1) * half) & (line > 0))
        def _(s=s):
            for h in range(heads):
                c = h * 2 * HD
                edge[s, :, c : c + 2 * HD] = jnp.concatenate(
                    [dkeys[s * heads + h, :WINDOW, :HD], dvalues[s * heads + h, :WINDOW, :HD]], axis=1
                ).astype(low)
            edge_copy(s).start()

    mask = edge_mask()
    tiles = WINDOW // BLK + 1
    start = pl.multiple_of(place * BLK, BLK)
    lane = lax.broadcasted_iota(jnp.int32, (BLK, 2 * HD), 1)
    spans = [pl.ds(pl.multiple_of(start + b * BLK, BLK), BLK) for b in range(tiles)]
    for h in range(heads):
        sh = seq * heads + h
        q = q2_ref[0, h]
        g32 = grad_ref[0, :, h * HD : (h + 1) * HD].astype(f32)
        centre = jnp.sum(g32 * out_ref[0, :, h * HD : (h + 1) * HD].astype(f32), axis=1, keepdims=True)
        hi, md, lo = split3(-centre)
        g2 = jnp.concatenate([g32, jnp.zeros((BLK, HD), f32)], axis=1)
        g2 = jnp.where(lane == HD, hi, g2)
        g2 = jnp.where(lane == HD + 1, md, g2)
        g2 = jnp.where(lane == HD + 2, lo, g2).astype(low)
        scores = merge_edges(mask, [nt(keys[sh, s, :], q) for s in spans])
        wgrads = merge_edges(mask, [nt(values[sh, s, :], g2) for s in spans])
        weights = [jnp.exp(s) for s in scores]
        sgrads = spread_edges(mask, [(w * d).astype(low) for w, d in zip(weights, wgrads)])
        weights = spread_edges(mask, [w.astype(low) for w in weights])
        for s, w, d in zip(spans, weights, sgrads):
            dvalues[sh, s, :] += nn(w, g2)
            dkeys[sh, s, :] += nn(d, q)
        dq = sum(nn(keys_t[sh, :, s], d) for s, d in zip(spans, sgrads))
        qc = heads * 2 * HD + h * HD
        gqkv_ref[seq, pl.ds(start, BLK), qc : qc + HD] = (dq.T[:, :HD] * 0.125).astype(low)

    def relay(h):
        part = slice(h * size, (h + 1) * size)
        for a in range(2):
            near_copy(a, h).wait_recv()
            mid[a, part] = plus(mid[a, part], near[a, part])
            far_copy(a, h).start()

    @pl.when(step == 4)
    def _():
        for load in loads():
            load.wait()
        relay(0)

    @pl.when(step == 8)
    def _():
        relay(1)

    @pl.when(step == last)
    def _():
        def own(s, h, first, count):
            span = slice(WINDOW + first, WINDOW + first + count)
            return jnp.concatenate([dkeys[s * heads + h, span, :HD], dvalues[s * heads + h, span, :HD]], axis=1)

        for s in range(seqs):
            for h in range(heads):
                c = h * 2 * HD
                gqkv_ref[s, : rows - WINDOW, c : c + 2 * HD] = own(s, h, 0, rows - WINDOW).astype(low)

        @pl.when(line < line_end)
        def _():
            for s in range(seqs):
                edge_copy(s).wait_recv()

        @pl.when(line == line_end)
        def _():
            ahead[...] = jnp.zeros_like(ahead)

        for s in range(seqs):
            for h in range(heads):
                c = h * 2 * HD
                gqkv_ref[s, rows - WINDOW :, c : c + 2 * HD] = (
                    own(s, h, rows - WINDOW, WINDOW) + ahead[s, :, c : c + 2 * HD].astype(f32)
                ).astype(low)

        for h in range(pieces):
            part = slice(h * size, (h + 1) * size)
            for a in range(2):
                far_copy(a, h).wait_recv()
                sums_ref[a, part] = plus(mine[a, part], met[a, part], far[a, part])
        for a in range(2):
            for h in range(pieces):
                near_copy(a, h).wait_send()
                far_copy(a, h).wait_send()

        @pl.when(line > 0)
        def _():
            for s in range(seqs):
                edge_copy(s).wait_send()


def attend_back(qkv, halo, ids, docs, q2, out, grad, kept, side, heads, group):
    seqs, rows, cols = qkv.shape
    ext = ids.shape[1]
    half = group // 2
    f32, low = jnp.float32, jnp.bfloat16
    vmem = pl.BlockSpec(memory_space=pltpu.VMEM)
    hbm = pl.BlockSpec(memory_space=pl.ANY)
    every = seqs * heads
    part = kept.shape[2:]
    seq_of = lambda i: lax.rem(lax.div(i, half), 2)
    place_of = lambda i: lax.div(i, group) * half + lax.rem(i, half)
    edge = pltpu.VMEM((seqs, WINDOW, heads * 2 * HD), low)
    pair = pltpu.VMEM((2,) + part, low)
    return pl.pallas_call(
        functools.partial(attend_back_kernel, heads, group, docs),
        grid=(seqs * rows // BLK,),
        in_specs=[
            vmem, vmem, vmem,
            pl.BlockSpec((1, heads, BLK, 2 * HD), lambda i: (seq_of(i), 0, place_of(i), 0)),
            pl.BlockSpec((1, BLK, heads * HD), lambda i: (seq_of(i), place_of(i), 0)),
            pl.BlockSpec((1, BLK, heads * HD), lambda i: (seq_of(i), place_of(i), 0)),
            hbm, hbm,
        ],
        out_specs=[vmem, vmem],
        out_shape=[
            jax.ShapeDtypeStruct((seqs, rows, cols), low),
            jax.ShapeDtypeStruct((2,) + part, low),
        ],
        scratch_shapes=[
            pltpu.VMEM((every, ext, 2 * HD), low),
            pltpu.VMEM((every, ext, 2 * HD), low),
            pltpu.VMEM((every, 2 * HD, ext), low),
            pltpu.VMEM((every, ext, 2 * HD), f32),
            pltpu.VMEM((every, ext, 2 * HD), f32),
            edge, edge, pair, pair, pair, pair, pair,
            pltpu.SemaphoreType.DMA((2, seqs)),
            pltpu.SemaphoreType.DMA((3, 2)),
            pltpu.SemaphoreType.DMA((2, 2)),
            pltpu.SemaphoreType.DMA((2, 2)),
            pltpu.SemaphoreType.DMA((2, 2)),
            pltpu.SemaphoreType.DMA((2, 2)),
        ],
        compiler_params=pltpu.CompilerParams(vmem_limit_bytes=62 * 2**20, collective_id=4, has_side_effects=True),
        name="attend_back",
    )(qkv, halo, ids, q2, out, grad, kept, side)


def finish_kernel(
    g_ref, wt_ref, x_ref, gres_ref, small_ref, sums_ref, out_kept, gvec_ref, gfcb_ref, z_hbm,
    input_grad_ref, fc_total_ref, proj_total_ref, out_total_ref, qkv_total_ref, vec_ref,
    z_all, odd, odd_in, even, mine, first_in, second_in, mt, rows6, vec_out, vec_in, vec_line,
    acc, acc_out, acc_q, left, left_out, left_q, right, right_out, right_q, total_q, out_near, out_far, out_mid,
    z_sem, odd_send, odd_recv, near_send, near_recv, far_send, far_recv,
    vec_send, vec_recv, vl_send, vl_recv, line_send, line_recv, out_send, out_recv,
):
    group = small_ref.shape[0]
    me = lax.axis_index("fsdp")
    line = lax.axis_index("seq")
    line_size = 4
    at = [xor(me, k, group) for k in range(group)]
    block = x_ref.shape[0] // 2
    f32, low = jnp.float32, jnp.bfloat16
    width = x_ref.shape[1]
    span = small_ref.shape[2]
    heads = wt_ref.shape[0] // (3 * HD)
    outer = (line == 0) | (line == line_size - 1)
    inner = (line > 0) & (line < line_size - 1)

    def remote(src, dst, send, recv, to):
        return pltpu.make_async_remote_copy(
            src_ref=src, dst_ref=dst, send_sem=send, recv_sem=recv, device_id=to, device_id_type=MESH
        )

    barrier = pltpu.get_barrier_semaphore()
    for peer in at[1:]:
        pl.semaphore_signal(barrier, inc=1, device_id={"fsdp": peer}, device_id_type=MESH)
    others = [lax.rem(line + d, line_size) for d in range(1, line_size)]
    for other in others:
        pl.semaphore_signal(barrier, inc=1, device_id={"seq": other}, device_id_type=MESH)
    pl.semaphore_wait(barrier, group - 1 + line_size - 1)

    cut = sums_ref.shape[1] // 4
    fc_chunks, proj_chunks = [], []
    for i in range(4):
        part = pl.ds(i * cut, cut)
        fc_chunks.append([r.at[0, part] for r in (sums_ref, acc, left, right)] + [fc_total_ref.at[part]])
        there = proj_total_ref.at[pl.ds(i % 2 * cut, cut), pl.ds(i // 2 * sums_ref.shape[2], sums_ref.shape[2])]
        proj_chunks.append([r.at[1, part] for r in (sums_ref, acc, left, right)] + [there])
    cut = acc_q.shape[0] // 3
    qkv_chunks = [
        [r.at[pl.ds(i * cut, cut)] for r in (acc_q, acc_q, left_q, right_q, total_q)] for i in range(3)
    ]
    out_chunk = [acc_out, acc_out, left_out, right_out, out_total_ref]
    chunks = fc_chunks + proj_chunks[:2] + qkv_chunks + proj_chunks[2:] + [out_chunk]
    early = 6

    def inwards(c):
        return remote(
            chunks[c][0], chunks[c][2], line_send.at[0, c], line_recv.at[0, c], {"seq": 1 + lax.div(line, line_size - 1)}
        )

    def across(c):
        return remote(
            chunks[c][1], chunks[c][3], line_send.at[1, c], line_recv.at[1, c], {"seq": line_size - 1 - line}
        )

    def outwards(c):
        return remote(
            chunks[c][4], chunks[c][3], line_send.at[2, c], line_recv.at[2, c],
            {"seq": lax.rem((line + line_size - 1) * (line_size - 1), 2 * (line_size - 1))},
        )

    def begin(cs):
        @pl.when(outer)
        def _():
            for c in cs:
                inwards(c).start()

    def collect(c):
        @pl.when(inner)
        def _():
            inwards(c).wait_recv()
            own, acc_c, left_c = chunks[c][:3]
            acc_c[...] = (own[...].astype(f32) + left_c[...].astype(f32)).astype(low)
            across(c).start()

    def settle(c):
        @pl.when(inner)
        def _():
            across(c).wait_recv()
            chunks[c][4][...] = (chunks[c][1][...].astype(f32) + chunks[c][3][...].astype(f32)).astype(low)
            outwards(c).start()

    def receive(c):
        @pl.when(outer)
        def _():
            outwards(c).wait_recv()
            chunks[c][4][...] = chunks[c][3][...]

    def advance(first, last):
        for c in range(first, last):
            collect(c)
            if c >= 1:
                settle(c - 1)
            if c >= 2:
                receive(c - 2)

    begin(range(early))
    load = pltpu.make_async_copy(z_hbm, z_all, z_sem)
    load.start()

    ways = (at[2], at[4])
    out_cut = out_kept.shape[1] // 2
    out_first = ((0, 1, 0), (0, 3, 1), (1, 2, 0), (1, 3, 1))

    def out_near_copy(n):
        h, slot, j = out_first[n]
        return pltpu.make_async_remote_copy(
            src_ref=out_kept.at[slot, pl.ds(h * out_cut, out_cut)], dst_ref=out_near.at[h, j], send_sem=out_send.at[n],
            recv_sem=out_recv.at[n], device_id={"fsdp": ways[h]}, device_id_type=MESH,
        )

    def out_far_copy(h):
        return pltpu.make_async_remote_copy(
            src_ref=out_mid.at[h], dst_ref=out_far.at[h], send_sem=out_send.at[4 + h],
            recv_sem=out_recv.at[4 + h], device_id={"fsdp": ways[1 - h]}, device_id_type=MESH,
        )

    for n in range(4):
        out_near_copy(n).start()

    def product(r, s):
        start = pl.multiple_of(at[r] * block, block)
        return nn(g_ref[s, pl.ds(start, block), :], wt_ref[...])

    def odd_copy(j):
        return remote(odd.at[j], odd_in.at[j], odd_send.at[j], odd_recv.at[j], {"fsdp": at[1]})

    def make_odd(j):
        for s in range(2):
            odd[j, s] = product(2 * j + 1, s).astype(low)
        odd_copy(j).start()

    make_odd(3)
    make_odd(1)
    advance(0, 1)
    make_odd(2)
    make_odd(0)

    def near_copy(s, i):
        j = 3 if i == 0 else 1 + s
        return remote(even.at[j, s], first_in.at[s, i], near_send.at[s, i], near_recv.at[s, i], {"fsdp": ways[s]})

    def far_copy(s):
        return remote(even.at[2 - s, s], second_in.at[s], far_send.at[s], far_recv.at[s], {"fsdp": ways[1 - s]})

    def make_even(j):
        odd_copy(j).wait_recv()
        for s in range(2):
            part = product(2 * j, s) + odd_in[j, s].astype(f32)
            if j == 0:
                mine[s] = part
            else:
                even[j, s] = part.astype(low)
                if j == 3:
                    near_copy(s, 0).start()
                elif j == 1 + s:
                    near_copy(s, 1).start()

    make_even(3)
    advance(1, 2)
    make_even(1)
    make_even(2)
    advance(2, 3)
    make_even(0)

    def wide(index):
        return jnp.concatenate([small_ref[f, index : index + 1, :] for f in range(group)], axis=1).astype(f32)

    gain = wide(0)
    load.wait()
    mt[...] = jnp.zeros_like(mt)
    steps = z_all.shape[1] // 512
    ones = jnp.ones((512, 128), low)

    def add_product(i, sums):
        rows = pl.ds(pl.multiple_of(lax.rem(i, steps) * 512, 512), 512)
        g = g_ref[lax.div(i, steps), rows, :]
        mt[...] += tn(g, z_all[lax.div(i, steps), rows, :])
        return sums + tn(g, ones)

    column = lax.fori_loop(0, steps // 2, add_product, jnp.zeros((g_ref.shape[2], 128), f32))
    advance(3, 4)
    for h in range(2):
        part = slice(h * out_cut, (h + 1) * out_cut)
        out_near_copy(2 * h + 1).wait_recv()
        out_mid[h] = (out_kept[2 - h, part].astype(f32) + out_near[h, 1].astype(f32)).astype(low)
        out_far_copy(h).start()
    column = lax.fori_loop(steps // 2, steps, add_product, column)
    advance(4, 5)
    column = lax.fori_loop(steps, 2 * steps, add_product, column)
    acc_q[...] = mt[...].astype(low)
    begin(range(early, len(chunks) - 1))
    advance(5, 6)

    def vec_copy(k):
        return remote(vec_out.at[k], vec_in.at[k], vec_send.at[k], vec_recv.at[k], {"fsdp": at[k]})

    for s in range(2):
        near_copy(s, 0).wait_recv()
        even[2 - s, s] = (even[2 - s, s].astype(f32) + first_in[s, 0].astype(f32)).astype(low)
        far_copy(s).start()

    for h in range(2):
        part = slice(h * out_cut, (h + 1) * out_cut)
        out_near_copy(2 * h).wait_recv()
        out_far_copy(h).wait_recv()
        acc_out[part] = (
            out_kept[0, part].astype(f32) + out_near[h, 0].astype(f32) + out_far[h].astype(f32)
        ).astype(low)
    begin([len(chunks) - 1])

    def line_copy(d):
        return remote(vec_line.at[line], vec_line.at[line], vl_send.at[d], vl_recv.at[d], {"seq": others[d]})

    advance(6, 7)
    gain_grad = offset_grad = jnp.zeros((1, width), f32)
    for s in range(2):
        near_copy(s, 1).wait_recv()
        far_copy(s).wait_recv()
        rows = slice(s * block, (s + 1) * block)
        e = mine[s] + first_in[s, 1].astype(f32) + second_in[s].astype(f32)
        z, rate = standardize(x_ref[rows, :].astype(f32))
        gain_grad += column_sums(e * z)
        offset_grad += column_sums(e)
        input_grad_ref[rows, :] = (gres_ref[rows, :] + norm_grad(e * gain, z, rate)).astype(low)
    rows6[0:1, :] = gain_grad
    rows6[1:2, :] = offset_grad
    rows6[2:6, :] = gvec_ref[0:4, :]
    row = column.T[0:1, :]
    vec_out[...] = jnp.zeros_like(vec_out)
    for k in range(group):
        vec_out[k, 0:6, :] = rows6[0:6, pl.ds(pl.multiple_of(at[k] * span, span), span)]
        for i in range(4):
            vec_out[k, 6 + i : 7 + i, :] = gfcb_ref[STEP_OF[k], :, i * span : (i + 1) * span]
    for h in range(heads):
        base = heads * 2 * HD + h * HD
        vec_out[0, 10 + h : 11 + h, :] = jnp.concatenate(
            [row[:, base : base + HD], row[:, h * 2 * HD + HD : (h + 1) * 2 * HD]], axis=1
        )

    for k in range(1, group):
        vec_copy(k).start()

    advance(7, 9)
    total = vec_out[0]
    for k in range(1, group):
        vec_copy(k).wait_recv()
        total += vec_in[k]
    vec_line[line] = total

    for d in range(line_size - 1):
        line_copy(d).start()

    advance(9, 11)
    for d in range(line_size - 1):
        line_copy(d).wait_recv()
    vec_ref[...] = vec_line[0] + vec_line[1] + vec_line[2] + vec_line[3]
    advance(11, 12)
    turned = total_q[...].T
    pairs = heads * 2 * HD
    turned = [
        p
        for h in range(heads)
        for p in (turned[:, pairs + h * HD : pairs + (h + 1) * HD], turned[:, h * 2 * HD : (h + 1) * 2 * HD])
    ]
    qkv_total_ref[...] = jnp.concatenate(turned, axis=1)
    settle(11)
    receive(10)
    receive(11)
    for j in range(4):
        odd_copy(j).wait_send()
    for s in range(2):
        near_copy(s, 0).wait_send()
        near_copy(s, 1).wait_send()
        far_copy(s).wait_send()
    for n in range(4):
        out_near_copy(n).wait_send()
    for h in range(2):
        out_far_copy(h).wait_send()
    for k in range(1, group):
        vec_copy(k).wait_send()
    for d in range(line_size - 1):
        line_copy(d).wait_send()

    @pl.when(outer)
    def _():
        for c in range(len(chunks)):
            inwards(c).wait_send()

    @pl.when(inner)
    def _():
        for c in range(len(chunks)):
            across(c).wait_send()
            outwards(c).wait_send()


def finish(g, wt, x, gres, small, sums, out_kept, gvec, gfcb, z_all):
    rows, width = x.shape
    group = small.shape[0]
    half = rows // 2
    span = small.shape[2]
    f32, low = jnp.float32, jnp.bfloat16
    vmem = pl.BlockSpec(memory_space=pltpu.VMEM)
    dma = pltpu.SemaphoreType.DMA
    out_part = out_kept.shape[1:]
    half_out = (out_part[0] // 2, out_part[1])
    buffers = [pltpu.VMEM(sums.shape, low), pltpu.VMEM(out_part, low), pltpu.VMEM(wt.shape, low)]
    return pl.pallas_call(
        finish_kernel,
        in_specs=[vmem] * 9 + [pl.BlockSpec(memory_space=pl.ANY)],
        out_specs=[vmem] * 6,
        out_shape=[
            jax.ShapeDtypeStruct((rows, width), low),
            jax.ShapeDtypeStruct(sums.shape[1:], low),
            jax.ShapeDtypeStruct((sums.shape[2], sums.shape[1]), low),
            jax.ShapeDtypeStruct(out_part, low),
            jax.ShapeDtypeStruct(wt.shape[::-1], low),
            jax.ShapeDtypeStruct((16, span), f32),
        ],
        scratch_shapes=[
            pltpu.VMEM(z_all.shape, low),
            pltpu.VMEM((group // 2, 2, half, width), low),
            pltpu.VMEM((group // 2, 2, half, width), low),
            pltpu.VMEM((group // 2, 2, half, width), low),
            pltpu.VMEM((2, half, width), f32),
            pltpu.VMEM((2, 2, half, width), low),
            pltpu.VMEM((2, half, width), low),
            pltpu.VMEM(wt.shape, f32),
            pltpu.VMEM((8, width), f32),
            pltpu.VMEM((group, 16, span), f32),
            pltpu.VMEM((group, 16, span), f32),
            pltpu.VMEM((4, 16, span), f32),
        ]
        + buffers * 3
        + [pltpu.VMEM(wt.shape, low)]
        + [pltpu.VMEM((2, 2) + half_out, low), pltpu.VMEM((2,) + half_out, low), pltpu.VMEM((2,) + half_out, low)]
        + [dma, dma((4,)), dma((4,)), dma((2, 2)), dma((2, 2)), dma((2,)), dma((2,))]
        + [dma((group,)), dma((group,)), dma((3,)), dma((3,)), dma((3, 12)), dma((3, 12)), dma((6,)), dma((6,))],
        compiler_params=pltpu.CompilerParams(vmem_limit_bytes=62 * 2**20, collective_id=5, has_side_effects=True),
        name="finish",
    )(g, wt, x, gres, small, sums, out_kept, gvec, gfcb, z_all)


def plain_fill_keys(heads, qkv_ref, halo_ref, augk_ref, keys, values):
    halo_rows = halo_ref.shape[1]
    rows = qkv_ref.shape[1]
    ones = jnp.ones((1, HD), jnp.bfloat16)
    for h in range(heads):
        c = h * 2 * HD
        for source, base, size in ((halo_ref, 0, halo_rows), (qkv_ref, halo_rows, rows)):
            pair = source[0, :, c : c + 2 * HD]
            keys[h, base : base + size, :] = jnp.concatenate(
                [pair[:, :HD], augk_ref[0, base : base + size, :]], axis=1
            )
            values[h, base : base + size, :] = jnp.concatenate(
                [pair[:, HD:], jnp.broadcast_to(ones, (size, HD))], axis=1
            )


def plain_attend_kernel(heads, qkv_ref, halo_ref, augk_ref, augq_ref, out_ref, q2_ref, keys, values, values_t):
    step = pl.program_id(1)
    nkeys = keys.shape[1]

    @pl.when(step == 0)
    def _():
        plain_fill_keys(heads, qkv_ref, halo_ref, augk_ref, keys, values)
        for h in range(heads):
            for b in range(nkeys // BLK):
                values_t[h, :, b * BLK : (b + 1) * BLK] = values[h, b * BLK : (b + 1) * BLK, :].T

    mask = edge_mask()
    tiles = WINDOW // BLK + 1
    start = pl.multiple_of(step * BLK, BLK)
    lane = lax.broadcasted_iota(jnp.int32, (BLK, 2 * HD), 1)
    lse_lane = augq_ref.shape[2] + HD - 3
    for h in range(heads):
        qc = heads * 2 * HD + h * HD
        q = jnp.concatenate([qkv_ref[0, pl.ds(start, BLK), qc : qc + HD] * 0.125, augq_ref[0]], axis=1)
        scores = [nt(keys[h, pl.ds(start + b * BLK, BLK), :], q) for b in range(tiles)]
        scores = merge_edges(mask, scores)
        peak = functools.reduce(jnp.maximum, scores)
        peak = jnp.max(peak, axis=0, keepdims=True)
        weights = spread_edges(mask, [jnp.exp(s - peak).astype(jnp.bfloat16) for s in scores])
        total = sum(
            nn(values_t[h, :, pl.ds(pl.multiple_of(start + b * BLK, BLK), BLK)], w) for b, w in enumerate(weights)
        )
        sub = lax.broadcasted_iota(jnp.int32, total.shape, 0)
        total = jnp.where(sub == HD + 1, peak, total).T
        norm = total[:, HD : HD + 1]
        out_ref[0, :, h * HD : (h + 1) * HD] = (total[:, :HD] / norm).astype(out_ref.dtype)
        lse = total[:, HD + 1 : HD + 2] + jnp.log(norm)
        hi, mid, low = split3(-lse)
        q2 = q.astype(jnp.float32)
        q2 = jnp.where(lane == lse_lane, hi, q2)
        q2 = jnp.where(lane == lse_lane + 1, mid, q2)
        q2 = jnp.where(lane == lse_lane + 2, low, q2)
        q2_ref[0, h] = q2.astype(jnp.bfloat16)


def plain_attend(qkv, halo, augk, augq, heads):
    seqs, rows, cols = qkv.shape
    ext = augk.shape[1]
    return pl.pallas_call(
        functools.partial(plain_attend_kernel, heads),
        grid=(seqs, rows // BLK),
        in_specs=[
            pl.BlockSpec((1, rows, cols), lambda s, i: (s, 0, 0)),
            pl.BlockSpec((1, WINDOW, heads * 2 * HD), lambda s, i: (s, 0, 0)),
            pl.BlockSpec((1, ext, HD), lambda s, i: (s, 0, 0)),
            pl.BlockSpec((1, BLK, HD), lambda s, i: (s, i, 0)),
        ],
        out_specs=[
            pl.BlockSpec((1, BLK, heads * HD), lambda s, i: (s, i, 0)),
            pl.BlockSpec((1, heads, BLK, 2 * HD), lambda s, i: (s, 0, i, 0)),
        ],
        out_shape=[
            jax.ShapeDtypeStruct((seqs, rows, heads * HD), jnp.bfloat16),
            jax.ShapeDtypeStruct((seqs, heads, rows, 2 * HD), jnp.bfloat16),
        ],
        scratch_shapes=[
            pltpu.VMEM((heads, ext, 2 * HD), jnp.bfloat16),
            pltpu.VMEM((heads, ext, 2 * HD), jnp.bfloat16),
            pltpu.VMEM((heads, 2 * HD, ext), jnp.bfloat16),
        ],
        compiler_params=pltpu.CompilerParams(vmem_limit_bytes=48 * 2**20),
        name="plain_attend",
    )(qkv, halo, augk, augq)


def plain_attend_back_kernel(
    heads, qkv_ref, halo_ref, augk_ref, q2_ref, out_ref, grad_ref, dq_ref, dkv_ref, dhalo_ref,
    keys, values, keys_t, dkeys, dvalues,
):
    step = pl.program_id(1)
    nkeys = keys.shape[1]

    @pl.when(step == 0)
    def _():
        plain_fill_keys(heads, qkv_ref, halo_ref, augk_ref, keys, values)
        for h in range(heads):
            for b in range(nkeys // BLK):
                keys_t[h, :, b * BLK : (b + 1) * BLK] = keys[h, b * BLK : (b + 1) * BLK, :].T
        dkeys[...] = jnp.zeros_like(dkeys)
        dvalues[...] = jnp.zeros_like(dvalues)

    mask = edge_mask()
    tiles = WINDOW // BLK + 1
    start = pl.multiple_of(step * BLK, BLK)
    lane = lax.broadcasted_iota(jnp.int32, (BLK, 2 * HD), 1)
    for h in range(heads):
        q = q2_ref[0, h]
        g = grad_ref[0, :, h * HD : (h + 1) * HD]
        g32 = g.astype(jnp.float32)
        centre = jnp.sum(g32 * out_ref[0, :, h * HD : (h + 1) * HD].astype(jnp.float32), axis=1, keepdims=True)
        hi, mid, low = split3(-centre)
        g2 = jnp.concatenate([g32, jnp.zeros((BLK, HD), jnp.float32)], axis=1)
        g2 = jnp.where(lane == HD, hi, g2)
        g2 = jnp.where(lane == HD + 1, mid, g2)
        g2 = jnp.where(lane == HD + 2, low, g2).astype(jnp.bfloat16)
        spans = [pl.ds(pl.multiple_of(start + b * BLK, BLK), BLK) for b in range(tiles)]
        scores = merge_edges(mask, [nt(keys[h, s, :], q) for s in spans])
        wgrads = merge_edges(mask, [nt(values[h, s, :], g2) for s in spans])
        weights = [jnp.exp(s) for s in scores]
        sgrads = spread_edges(mask, [(w * d).astype(jnp.bfloat16) for w, d in zip(weights, wgrads)])
        weights = spread_edges(mask, [w.astype(jnp.bfloat16) for w in weights])
        for s, w, d in zip(spans, weights, sgrads):
            dvalues[h, s, :] += nn(w, g2)
            dkeys[h, s, :] += nn(d, q)
        dq = sum(nn(keys_t[h, :, s], d) for s, d in zip(spans, sgrads))
        dq_ref[0, :, h * HD : (h + 1) * HD] = (dq.T[:, :HD] * 0.125).astype(dq_ref.dtype)

    @pl.when(step == pl.num_programs(1) - 1)
    def _():
        for h in range(heads):
            c = h * 2 * HD
            dhalo_ref[0, :, c : c + 2 * HD] = jnp.concatenate(
                [dkeys[h, :WINDOW, :HD], dvalues[h, :WINDOW, :HD]], axis=1
            ).astype(dhalo_ref.dtype)
            dkv_ref[0, :, c : c + 2 * HD] = jnp.concatenate(
                [dkeys[h, WINDOW:, :HD], dvalues[h, WINDOW:, :HD]], axis=1
            ).astype(dkv_ref.dtype)


def plain_attend_back(qkv, halo, augk, q2, out, grad, heads):
    seqs, rows, cols = qkv.shape
    ext = augk.shape[1]
    return pl.pallas_call(
        functools.partial(plain_attend_back_kernel, heads),
        grid=(seqs, rows // BLK),
        in_specs=[
            pl.BlockSpec((1, rows, cols), lambda s, i: (s, 0, 0)),
            pl.BlockSpec((1, WINDOW, heads * 2 * HD), lambda s, i: (s, 0, 0)),
            pl.BlockSpec((1, ext, HD), lambda s, i: (s, 0, 0)),
            pl.BlockSpec((1, heads, BLK, 2 * HD), lambda s, i: (s, 0, i, 0)),
            pl.BlockSpec((1, BLK, heads * HD), lambda s, i: (s, i, 0)),
            pl.BlockSpec((1, BLK, heads * HD), lambda s, i: (s, i, 0)),
        ],
        out_specs=[
            pl.BlockSpec((1, BLK, heads * HD), lambda s, i: (s, i, 0)),
            pl.BlockSpec((1, rows, heads * 2 * HD), lambda s, i: (s, 0, 0)),
            pl.BlockSpec((1, WINDOW, heads * 2 * HD), lambda s, i: (s, 0, 0)),
        ],
        out_shape=[
            jax.ShapeDtypeStruct((seqs, rows, heads * HD), jnp.bfloat16),
            jax.ShapeDtypeStruct((seqs, rows, heads * 2 * HD), jnp.float32),
            jax.ShapeDtypeStruct((seqs, WINDOW, heads * 2 * HD), jnp.bfloat16),
        ],
        scratch_shapes=[
            pltpu.VMEM((heads, ext, 2 * HD), jnp.bfloat16),
            pltpu.VMEM((heads, ext, 2 * HD), jnp.bfloat16),
            pltpu.VMEM((heads, 2 * HD, ext), jnp.bfloat16),
            pltpu.VMEM((heads, ext, 2 * HD), jnp.float32),
            pltpu.VMEM((heads, ext, 2 * HD), jnp.float32),
        ],
        compiler_params=pltpu.CompilerParams(vmem_limit_bytes=56 * 2**20),
        name="plain_attend_back",
    )(qkv, halo, augk, q2, out, grad)


def from_behind(block, axis, distance):
    devices = range(lax.axis_size(axis))
    route = [(i - distance, i) for i in devices if i - distance in devices]
    return lax.ppermute(block, axis, route)


def pack_columns(array, heads):
    parts = array.reshape(array.shape[:-1] + (heads, 3 * HD))
    lead = array.shape[:-1]
    return jnp.concatenate(
        [parts[..., HD:].reshape(lead + (-1,)), parts[..., :HD].reshape(lead + (-1,))], axis=-1
    )


def unpack_columns(array, heads):
    lead = array.shape[:-1]
    pairs = array[..., : heads * 2 * HD].reshape(lead + (heads, 2 * HD))
    queries = array[..., heads * 2 * HD :].reshape(lead + (heads, HD))
    return jnp.concatenate([queries, pairs], axis=-1).reshape(lead + (-1,))


def dot(subscripts, a, b):
    return jnp.einsum(subscripts, a, b, preferred_element_type=jnp.float32)


def general_body(
    inputs, cotangent, segment_ids, norm1_gain, norm1_bias, qkv_weight, qv_bias, out_weight, out_bias,
    norm2_gain, norm2_bias, fc_weight, fc_bias, proj_weight, proj_bias,
):
    group = lax.axis_size("fsdp")
    seqs, local_rows, width = inputs.shape
    part_rows = local_rows * group
    heads = qkv_weight.shape[1] // (3 * HD)
    docs = segment_ids.shape[1] // (2 * WINDOW)
    seq_index = lax.axis_index("seq")
    shard = norm1_gain.shape[0]

    small = jnp.concatenate([norm1_gain, norm1_bias, out_bias, norm2_gain, norm2_bias, proj_bias, fc_bias])
    small = lax.all_gather(small, "fsdp")
    gain1, offset1, out_off, gain2, offset2, proj_off = (
        small[:, i * shard : (i + 1) * shard].reshape(-1).astype(jnp.float32) for i in range(6)
    )
    fc_off = small[:, 6 * shard :].reshape(-1).astype(jnp.float32)
    out_all = lax.all_gather(out_weight, "fsdp", axis=0, tiled=True)
    fc_all = lax.all_gather(fc_weight, "fsdp")
    proj_all = lax.all_gather(proj_weight, "fsdp")

    padded_ids = jnp.concatenate([jnp.full((seqs, WINDOW), -1, jnp.int32), segment_ids], axis=1)
    segment_ext = lax.dynamic_slice_in_dim(padded_ids, seq_index * part_rows, WINDOW + part_rows, 1)
    augk, augq = mask_features(segment_ext, docs)

    x = inputs.astype(jnp.float32)
    z1, rate1 = standardize(x)
    normed1 = (z1 * gain1 + offset1).astype(jnp.bfloat16)
    normed1 = lax.all_gather(normed1, "fsdp", axis=1, tiled=True)
    packed_weight = pack_columns(qkv_weight, heads)
    head_bias = qv_bias.astype(jnp.float32)
    head_bias = jnp.concatenate(
        [head_bias[:, :HD], jnp.zeros((heads, HD), jnp.float32), head_bias[:, HD:]], axis=1
    ).reshape(-1)
    packed_bias = pack_columns(head_bias, heads)
    qkv = (dot("sre,ef->srf", normed1, packed_weight) + packed_bias).astype(jnp.bfloat16)
    halo = from_behind(qkv[:, part_rows - WINDOW :, : heads * 2 * HD], "seq", 1)
    head_out, q2 = plain_attend(qkv, halo, augk, augq, heads)
    merged = lax.all_to_all(head_out, "fsdp", split_axis=1, concat_axis=2, tiled=True)
    resid = x + dot("sre,ef->srf", merged, out_all) + out_off
    z2, rate2 = standardize(resid)
    normed2 = (z2 * gain2 + offset2).astype(jnp.bfloat16)
    fc_offset = fc_off.reshape(group, -1)
    hidden = dot("sre,gef->gsrf", normed2, fc_all) + fc_offset[:, None, None]
    active, gelu_back = jax.vjp(lambda v: jax.nn.gelu(v, approximate=True), hidden)
    active = active.astype(jnp.bfloat16)
    layer_output = (resid + dot("gsrf,gfd->srd", active, proj_all) + proj_off).astype(jnp.bfloat16)

    cot32 = cotangent.astype(jnp.float32)
    proj_bias_part = jnp.sum(cot32, axis=(0, 1))
    proj_weight_part = dot("gsrf,srd->gfd", active, cotangent)
    g_hidden = gelu_back(dot("srd,gfd->gsrf", cotangent, proj_all))[0].astype(jnp.bfloat16)
    fc_bias_part = jnp.sum(g_hidden, axis=(1, 2), dtype=jnp.float32).reshape(-1)
    fc_weight_part = dot("sre,gsrf->gef", normed2, g_hidden)
    g_norm2 = dot("gsrf,gef->sre", g_hidden, fc_all)
    gain2_part = jnp.sum(g_norm2 * z2, axis=(0, 1))
    offset2_part = jnp.sum(g_norm2, axis=(0, 1))
    g_resid = cot32 + norm_grad(g_norm2 * gain2, z2, rate2)
    g_attn = g_resid.astype(jnp.bfloat16)
    out_bias_part = jnp.sum(g_attn, axis=(0, 1), dtype=jnp.float32)
    out_weight_part = dot("sre,srd->ed", merged, g_attn)
    g_merged = dot("srd,ed->sre", g_attn, out_all).astype(jnp.bfloat16)
    g_heads = lax.all_to_all(g_merged, "fsdp", split_axis=2, concat_axis=1, tiled=True)

    low = jnp.bfloat16
    fc_grad = lax.psum_scatter(fc_weight_part.astype(low), "fsdp")
    proj_grad = lax.psum_scatter(proj_weight_part.astype(low), "fsdp")
    out_grad = lax.psum_scatter(out_weight_part.astype(low), "fsdp", scatter_dimension=0, tiled=True)
    fc_grad, proj_grad, out_grad = lax.psum((fc_grad, proj_grad, out_grad), "seq")

    dq, dkv, dhalo = plain_attend_back(qkv, halo, augk, q2, head_out, g_heads, heads)
    edge = from_behind(dhalo, "seq", -1)
    edge = jnp.pad(edge.astype(jnp.float32), ((0, 0), (part_rows - WINDOW, 0), (0, 0)))
    g_qkv = jnp.concatenate([(dkv + edge).astype(jnp.bfloat16), dq], axis=-1)
    qkv_grad = dot("sre,srf->ef", normed1, g_qkv)
    qkv_colsum = jnp.sum(g_qkv, axis=(0, 1), dtype=jnp.float32)
    g_norm1 = dot("srf,ef->sre", g_qkv, packed_weight).astype(jnp.bfloat16)
    g_norm1 = lax.psum_scatter(g_norm1, "fsdp", scatter_dimension=1, tiled=True).astype(jnp.float32)
    gain1_part = jnp.sum(g_norm1 * z1, axis=(0, 1))
    offset1_part = jnp.sum(g_norm1, axis=(0, 1))
    input_grad = (g_resid + norm_grad(g_norm1 * gain1, z1, rate1)).astype(jnp.bfloat16)

    qkv_grad = lax.psum(qkv_grad.astype(low), "seq").astype(jnp.float32)
    qkv_grad = unpack_columns(qkv_grad, heads)
    col = unpack_columns(qkv_colsum, heads).reshape(heads, 3 * HD)
    col = lax.psum(jnp.concatenate([col[:, :HD], col[:, 2 * HD :]], axis=1), "seq")
    vectors = jnp.concatenate(
        [
            v.reshape(group, -1)
            for v in (gain1_part, offset1_part, out_bias_part, gain2_part, offset2_part, proj_bias_part, fc_bias_part)
        ],
        axis=1,
    )
    vectors = lax.psum_scatter(vectors, "fsdp")
    vectors = lax.psum(vectors, "seq")
    parts = [vectors[i * shard : (i + 1) * shard] for i in range(6)] + [vectors[6 * shard :]]
    f32 = jnp.float32
    return (
        layer_output, input_grad, parts[0], parts[1], qkv_grad, col, out_grad.astype(f32), parts[2], parts[3],
        parts[4], fc_grad.astype(f32), parts[6], proj_grad.astype(f32), parts[5],
    )


def cube_body(
    inputs, cotangent, segment_ids, norm1_gain, norm1_bias, qkv_weight, qv_bias, out_weight, out_bias,
    norm2_gain, norm2_bias, fc_weight, fc_bias, proj_weight, proj_bias,
):
    group = lax.axis_size("fsdp")
    seqs, local_rows, width = inputs.shape
    part_rows = local_rows * group
    heads = qkv_weight.shape[1] // (3 * HD)
    docs = segment_ids.shape[1] // (2 * WINDOW)
    seq_index = lax.axis_index("seq")
    shard = norm1_gain.shape[0]
    f32, low = jnp.float32, jnp.bfloat16

    smalls = [norm1_gain, norm1_bias, out_bias, norm2_gain, norm2_bias, proj_bias, fc_bias]
    smalls = [v.reshape(-1, shard) for v in smalls]
    padded_ids = jnp.concatenate([jnp.full((seqs, WINDOW), -1, jnp.int32), segment_ids], axis=1)
    segment_ext = lax.dynamic_slice_in_dim(padded_ids, seq_index * part_rows, WINDOW + part_rows, 1)
    ids = segment_ext[..., None]
    x = inputs.reshape(seqs * local_rows, width)
    cot = cotangent.reshape(seqs * local_rows, width)
    all_small, z1, qkv = gather_project(x, smalls, qkv_weight, qv_bias, group)
    head_out, q2, halo, merged, out_all, fc_near, proj_near = attend(
        qkv, ids, docs, out_weight, fc_weight, proj_weight, heads, group
    )
    layer_output, g_resid, g_heads, kept, side, out_kept, gvec, gfcb = feed_forward(
        x, cot, merged.reshape(x.shape), out_all.reshape(width, width), fc_near, proj_near, fc_weight, proj_weight, all_small
    )
    g_qkv, sums = attend_back(qkv, halo, ids, docs, q2, head_out, g_heads, kept, side, heads, group)
    input_grad, fc_grad, proj_grad, out_grad, qkv_grad, vecs = finish(
        g_qkv, pack_columns(qkv_weight, heads).T, x, g_resid, all_small, sums, out_kept, gvec, gfcb, z1
    )
    return (
        layer_output.reshape(inputs.shape), input_grad.reshape(inputs.shape), vecs[0], vecs[1], qkv_grad.astype(f32),
        vecs[10 : 10 + heads], out_grad.astype(f32), vecs[2], vecs[3], vecs[4], fc_grad.astype(f32), vecs[6:10].reshape(-1),
        proj_grad.astype(f32), vecs[5],
    )


def solution(mesh):
    tokens = P(None, ("seq", "fsdp"), None)
    rows, cols, vec = P("fsdp", None), P(None, "fsdp"), P("fsdp")
    return jax.shard_map(
        cube_body if mesh.shape["fsdp"] == 8 and mesh.shape["seq"] == 4 else general_body,
        mesh=mesh,
        in_specs=(tokens, tokens, P(), vec, vec, cols, rows, rows, vec, vec, vec, cols, vec, rows, vec),
        out_specs=(tokens, tokens, vec, vec, cols, rows, rows, vec, vec, vec, cols, vec, rows, vec),
        check_vma=False,
    )
```

```python
import functools
import math

import jax
import jax.numpy as jnp
from jax import lax
from jax.experimental import pallas as pl
from jax.experimental.pallas import tpu as pltpu
from jax.sharding import PartitionSpec as P


def standardize(values):
    centre = values - jnp.mean(values, axis=-1, keepdims=True)
    spread = jnp.mean(centre * centre, axis=-1, keepdims=True)
    rate = lax.rsqrt(spread + norm_eps)
    return centre * rate, rate


def norm_grad(direction, z, rate):
    mean_d = jnp.mean(direction, axis=-1, keepdims=True)
    mean_dz = jnp.mean(direction * z, axis=-1, keepdims=True)
    return rate * (direction - mean_d - z * mean_dz)


norm_eps = 1e-05

HD = 64
WINDOW = 1024
BLK = 256
PENALTY = 1e30


def nt(a, b):
    return lax.dot_general(a, b, (((1,), (1,)), ((), ())), preferred_element_type=jnp.float32)


def nn(a, b):
    return lax.dot_general(a, b, (((1,), (0,)), ((), ())), preferred_element_type=jnp.float32)


def tn(a, b):
    return lax.dot_general(a, b, (((0,), (0,)), ((), ())), preferred_element_type=jnp.float32)


def split3(v):
    hi = v.astype(jnp.bfloat16).astype(jnp.float32)
    rest = v - hi
    mid = rest.astype(jnp.bfloat16).astype(jnp.float32)
    return hi, mid, rest - mid


def merge_edges(mask, tiles):
    return [jnp.where(mask, tiles[0], tiles[-1])] + tiles[1:-1]


def spread_edges(mask, tiles):
    zero = jnp.zeros_like(tiles[0])
    return [jnp.where(mask, tiles[0], zero)] + tiles[1:] + [jnp.where(mask, zero, tiles[0])]


def edge_mask():
    rows = lax.broadcasted_iota(jnp.int32, (BLK, BLK), 0)
    cols = lax.broadcasted_iota(jnp.int32, (BLK, BLK), 1)
    return rows > cols


def xor(a, b, size):
    total, bit = 0, 1
    while bit < size:
        total = total + bit * lax.rem(lax.div(a, bit) + lax.div(b, bit), 2)
        bit *= 2
    return total


MESH = pl.DeviceIdType.MESH
SLOT_AT = (3, 2, 5, 4, 1, 0, 7, 6)
STEP_OF = tuple(SLOT_AT.index(r) for r in range(8))
NEAR = 6


def enter(peers):
    barrier = pltpu.get_barrier_semaphore()
    for peer in peers:
        pl.semaphore_signal(barrier, inc=1, device_id={"fsdp": peer}, device_id_type=MESH)
    pl.semaphore_wait(barrier, len(peers))


def attend_kernel(
    heads, group, docs, qkv_hbm, ids_hbm, out_w, fc_w, proj_w,
    out_ref, q2_ref, halo_ref, merged_ref, out_all, fc_all, proj_all,
    qkv_ref, ids_ref, in_sems, keys, values, values_t, sent, behind, own_sems, send_sems, recv_sems, halo_sems, w_own, w_send, w_recv,
):
    step = pl.program_id(0)
    last = pl.num_programs(0) - 1
    me = lax.axis_index("fsdp")
    line = lax.axis_index("seq")
    line_end = lax.axis_size("seq") - 1
    at = [xor(me, k, group) for k in range(group)]
    seqs, rows = qkv_ref.shape[0], qkv_ref.shape[1]
    half = group // 2
    seq = lax.rem(lax.div(step, half), 2)
    lower = lax.div(step, group)
    place = (1 - lower) * half + lax.rem(step + me, half)
    width = heads * 2 * HD
    low = jnp.bfloat16

    def halo_copy():
        return pltpu.make_async_remote_copy(
            src_ref=qkv_hbm.at[:, pl.ds(rows - WINDOW, WINDOW), pl.ds(0, width)],
            dst_ref=behind, send_sem=halo_sems.at[0], recv_sem=halo_sems.at[1],
            device_id={"seq": lax.rem(line + 1, line_end + 1)}, device_id_type=MESH,
        )

    weights = ((out_w, out_all, False), (fc_w, fc_all, True), (proj_w, proj_all, True))

    def slot(a, r):
        return weights[a][1].at[STEP_OF[r] if weights[a][2] else r]

    def w_copy(a, r, second=False):
        to = at[1] if r % 2 else at[r]
        src = weights[a][0] if r in (1, 2, 4) else slot(a, r - 1) if r % 2 else None
        dst, sem = slot(a, r), r
        if r == 6:
            size = weights[a][0].shape[0] // 2
            part = pl.ds(size if second else 0, size)
            src = slot(a, 4 if second else 2).at[part]
            to = at[2] if second else at[4]
            dst, sem = dst.at[part], 0 if second else 6
        return pltpu.make_async_remote_copy(
            src_ref=src, dst_ref=dst, send_sem=w_send.at[a, sem], recv_sem=w_recv.at[a, sem],
            device_id={"fsdp": to}, device_id_type=MESH,
        )

    def w_keep(a):
        return pltpu.make_async_copy(weights[a][0], slot(a, 0), w_own.at[a])

    even = lax.rem(line, 2)
    partner = line + 1 - 2 * even
    p_size = proj_w.shape[0] // 2
    p_part = pl.ds(pl.multiple_of(even * p_size, p_size), p_size)

    def p_near(r):
        return pltpu.make_async_remote_copy(
            src_ref=proj_w.at[p_part], dst_ref=slot(2, r).at[p_part], send_sem=w_send.at[2, r],
            recv_sem=w_recv.at[2, r], device_id={"fsdp": at[r]}, device_id_type=MESH,
        )

    def p_line(r):
        sem = 5 + r // 2
        return pltpu.make_async_remote_copy(
            src_ref=slot(2, r).at[p_part], dst_ref=slot(2, r).at[p_part], send_sem=w_send.at[2, sem],
            recv_sem=w_recv.at[2, sem], device_id={"seq": partner}, device_id_type=MESH,
        )

    def forward(a):
        w_copy(a, 2).wait_recv()
        w_copy(a, 3).start()
        w_copy(a, 4).wait_recv()
        w_copy(a, 5).start()
        if not weights[a][2]:
            w_copy(a, 6).start()
            w_copy(a, 6, True).start()

    @pl.when(step == 0)
    def _():
        loads = [
            pltpu.make_async_copy(qkv_hbm, qkv_ref, in_sems.at[0]),
            pltpu.make_async_copy(ids_hbm, ids_ref, in_sems.at[1]),
        ]
        for load in loads:
            load.start()
        barrier = pltpu.get_barrier_semaphore()
        for peer in at[1:]:
            pl.semaphore_signal(barrier, inc=1, device_id={"fsdp": peer}, device_id_type=MESH)

        pl.semaphore_signal(
            barrier, inc=1, device_id={"seq": lax.rem(line + line_end, line_end + 1)}, device_id_type=MESH
        )
        pl.semaphore_signal(barrier, inc=1, device_id={"seq": partner}, device_id_type=MESH)
        pl.semaphore_wait(barrier, group + 1)

        @pl.when(line < line_end)
        def _():
            halo_copy().start()

        for r in (2, 4, 1):
            w_copy(0, r).start()
        for r in (2, 4):
            p_near(r).start()
        w_copy(2, 1).start()
        w_keep(0).start()
        for load in loads:
            load.wait()
        for s in range(seqs):
            fill_keys(s, heads, qkv_ref, ids_ref, docs, WINDOW, keys, values, values_t, None)

    @pl.when(step == group)
    def _():
        @pl.when(line > 0)
        def _():
            halo_copy().wait_recv()

        @pl.when(line == 0)
        def _():
            behind[...] = jnp.zeros_like(behind)

        halo_ref[...] = behind[...]
        for s in range(seqs):
            fill_keys(s, heads, behind, ids_ref, docs, 0, keys, values, values_t, None)

    mask = edge_mask()
    tiles = WINDOW // BLK + 1
    start = pl.multiple_of(place * BLK, BLK)
    lane = lax.broadcasted_iota(jnp.int32, (BLK, 2 * HD), 1)
    lse_lane = 2 * HD - 3
    slot_k = xor(me, place, group)
    spans = [pl.ds(pl.multiple_of(start + b * BLK, BLK), BLK) for b in range(tiles)]
    q_marks = query_marks(ids_ref[seq, pl.ds(start + WINDOW, BLK), :], docs)
    for h in range(heads):
        sh = seq * heads + h
        qc = heads * 2 * HD + h * HD
        q = jnp.concatenate([qkv_ref[seq, pl.ds(start, BLK), qc : qc + HD] * 0.125, q_marks], axis=1)
        scores = merge_edges(mask, [nt(keys[sh, s, :], q) for s in spans])
        peak = functools.reduce(jnp.maximum, scores)
        peak = jnp.max(peak, axis=0, keepdims=True)
        weights_ = spread_edges(mask, [jnp.exp(s - peak).astype(low) for s in scores])
        total = sum(nn(values_t[sh, :, s], w) for s, w in zip(spans, weights_))
        sub = lax.broadcasted_iota(jnp.int32, total.shape, 0)
        total = jnp.where(sub == HD + 1, peak, total).T
        norm = total[:, HD : HD + 1]
        part = (total[:, :HD] / norm).astype(low)
        out_ref[seq, pl.ds(start, BLK), h * HD : (h + 1) * HD] = part
        sent[step, :, h * HD : (h + 1) * HD] = part
        lse = total[:, HD + 1 : HD + 2] + jnp.log(norm)
        hi, mid, lo = split3(-lse)
        q2 = q.astype(jnp.float32)
        q2 = jnp.where(lane == lse_lane, hi, q2)
        q2 = jnp.where(lane == lse_lane + 1, mid, q2)
        q2 = jnp.where(lane == lse_lane + 2, lo, q2)
        q2_ref[seq, h, pl.ds(start, BLK), :] = q2.astype(low)

    span = sent.shape[2]

    def landing(s, k):
        return merged_ref.at[s, :, pl.ds(pl.multiple_of(k * span, span), span)]

    def own(s):
        return pltpu.make_async_copy(sent.at[step], landing(s, 0), own_sems.at[s])

    def away(s, k, to):
        return pltpu.make_async_remote_copy(
            src_ref=sent.at[step], dst_ref=landing(s, k), send_sem=send_sems.at[s, k], recv_sem=recv_sems.at[s, k],
            device_id={"fsdp": to}, device_id_type=MESH,
        )

    @pl.when(place == me)
    def _():
        own(seq).start()

    @pl.when(place != me)
    def _():
        away(seq, slot_k, place).start()

    @pl.when(step == 3)
    def _():
        forward(0)
        for r in (2, 4, 1):
            w_copy(1, r).start()

    @pl.when(step == 6)
    def _():
        for r in (2, 4):
            p_near(r).wait_recv()
            p_line(r).start()

    @pl.when(step == 10)
    def _():
        w_copy(0, 6).wait_recv()
        w_copy(0, 6, True).wait_recv()
        w_copy(0, 7).start()

    @pl.when(step == last)
    def _():
        forward(1)
        for r in (2, 4):
            p_line(r).wait_recv()
            w_copy(2, r + 1).start()
        for s in range(seqs):
            own(s).wait()
            for k in range(1, group):
                away(s, k, at[k]).wait()
        w_keep(0).wait()
        for a in range(2):
            for r in (1, 2, 3, 4, 5):
                w_copy(a, r).wait_send()
            for r in (1, 3, 5):
                w_copy(a, r).wait_recv()
        for r in (2, 4):
            p_near(r).wait_send()
            p_line(r).wait_send()
        for r in (1, 3, 5):
            w_copy(2, r).wait()
        w_copy(0, 6).wait_send()
        w_copy(0, 6, True).wait_send()
        w_copy(0, 7).wait()

        @pl.when(line < line_end)
        def _():
            halo_copy().wait_send()


def key_marks(ids, docs):
    lane = lax.broadcasted_iota(jnp.int32, (ids.shape[0], HD), 1)
    ids = jnp.broadcast_to(ids, lane.shape)
    hidden = (lane == ids) | ((lane == docs) & (ids < 0))
    return jnp.where(hidden, -1.0, jnp.where(lane >= HD - 3, 1.0, 0.0)).astype(jnp.bfloat16)


def query_marks(ids, docs):
    lane = lax.broadcasted_iota(jnp.int32, (ids.shape[0], HD), 1)
    ids = jnp.broadcast_to(ids, lane.shape)
    return jnp.where((lane <= docs) & (lane != ids), PENALTY, 0.0).astype(jnp.bfloat16)


def fill_keys(s, heads, source, ids_ref, docs, base, keys, values, values_t, keys_t):
    size = BLK
    ones = jnp.ones((size, HD), jnp.bfloat16)
    for i in range(source.shape[1] // size):
        span = slice(base + i * size, base + (i + 1) * size)
        marks = key_marks(ids_ref[s, span, :], docs)
        for h in range(heads):
            c = h * 2 * HD
            pair = source[s, i * size : (i + 1) * size, c : c + 2 * HD]
            k = jnp.concatenate([pair[:, :HD], marks], axis=1)
            v = jnp.concatenate([pair[:, HD:], ones], axis=1)
            keys[s * heads + h, span, :] = k
            values[s * heads + h, span, :] = v
            if values_t is not None:
                values_t[s * heads + h, :, span] = v.T
            if keys_t is not None:
                keys_t[s * heads + h, :, span] = k.T


def attend(qkv, ids, docs, out_w, fc_w, proj_w, heads, group):
    seqs, rows, cols = qkv.shape
    ext = ids.shape[1]
    assert rows // BLK == group
    low = jnp.bfloat16
    vmem = pl.BlockSpec(memory_space=pltpu.VMEM)
    hbm = pl.BlockSpec(memory_space=pl.ANY)
    every = seqs * heads
    return pl.pallas_call(
        functools.partial(attend_kernel, heads, group, docs),
        grid=(seqs * rows // BLK,),
        in_specs=[hbm] * 5,
        out_specs=[vmem] * 3 + [hbm] * 4,
        out_shape=[
            jax.ShapeDtypeStruct((seqs, rows, heads * HD), low),
            jax.ShapeDtypeStruct((seqs, heads, rows, 2 * HD), low),
            jax.ShapeDtypeStruct((seqs, WINDOW, heads * 2 * HD), low),
            jax.ShapeDtypeStruct((seqs, BLK, group * heads * HD), low),
        ]
        + [jax.ShapeDtypeStruct((n,) + w.shape, low) for n, w in ((group, out_w), (NEAR - 1, fc_w), (NEAR - 1, proj_w))],
        scratch_shapes=[
            pltpu.VMEM(qkv.shape, low),
            pltpu.VMEM(ids.shape, jnp.int32),
            pltpu.SemaphoreType.DMA((2,)),
            pltpu.VMEM((every, ext, 2 * HD), low),
            pltpu.VMEM((every, ext, 2 * HD), low),
            pltpu.VMEM((every, 2 * HD, ext), low),
            pltpu.VMEM((seqs * rows // BLK, BLK, heads * HD), low),
            pltpu.VMEM((seqs, WINDOW, heads * 2 * HD), low),
            pltpu.SemaphoreType.DMA((seqs,)),
            pltpu.SemaphoreType.DMA((seqs, group)),
            pltpu.SemaphoreType.DMA((seqs, group)),
            pltpu.SemaphoreType.DMA((2,)),
            pltpu.SemaphoreType.DMA((1,)),
            pltpu.SemaphoreType.DMA((3, group)),
            pltpu.SemaphoreType.DMA((3, group)),
        ],
        compiler_params=pltpu.CompilerParams(vmem_limit_bytes=56 * 2**20, collective_id=1, has_side_effects=True),
        name="attend",
    )(qkv, ids, out_w, fc_w, proj_w)


def mask_features(segment_ext, docs):
    low = jnp.bfloat16
    lane = lax.broadcasted_iota(jnp.int32, segment_ext.shape + (HD,), 2)
    ids = segment_ext[..., None]
    hidden = (lane == ids) | ((lane == docs) & (ids < 0))
    keys = jnp.where(hidden, -1.0, jnp.where(lane >= HD - 3, 1.0, 0.0)).astype(low)
    queries = jnp.where((lane <= docs) & (lane != ids), PENALTY, 0.0).astype(low)
    return keys, queries[:, WINDOW:]


def gather_project_kernel(
    x_ref, *rest,
):
    parts, rest = rest[:7], rest[7:]
    project_kernel(x_ref, parts, *rest)


def project_kernel(
    x_ref, parts, w_ref, b_ref, all_small_ref, pieces_out, qkv_ref,
    z1, pieces, smalls, small_ref, small_send, small_recv, send_sems, recv_sems, out_sems,
):
    group = all_small_ref.shape[0]
    me = lax.axis_index("fsdp")
    at = [xor(me, k, group) for k in range(group)]
    rows = x_ref.shape[0] // 2
    f32, low = jnp.float32, jnp.bfloat16
    enter(at[1:])

    def small_copy(k):
        return pltpu.make_async_remote_copy(
            src_ref=small_ref, dst_ref=smalls.at[me], send_sem=small_send.at[k], recv_sem=small_recv.at[k],
            device_id={"fsdp": at[k]}, device_id_type=MESH,
        )

    row = 0
    small_ref[...] = jnp.zeros_like(small_ref)
    for part in parts:
        small_ref[row : row + part.shape[0], :] = part[...]
        row += part.shape[0]
    for k in range(1, group):
        small_copy(k).start()
    smalls[me] = small_ref[...]

    def chunk(p, s):
        return pieces.at[p, s]

    def move(r, s):
        if r % 2:
            piece, to = at[r - 1], at[1]
        elif r == 6:
            piece, to = (at[2], at[4]) if s == 0 else (at[4], at[2])
        else:
            piece, to = me, at[r]
        return pltpu.make_async_remote_copy(
            src_ref=chunk(piece, s), dst_ref=chunk(piece, s), send_sem=send_sems.at[r, s], recv_sem=recv_sems.at[r, s],
            device_id={"fsdp": to}, device_id_type=MESH,
        )

    def keep(k, s):
        return pltpu.make_async_copy(chunk(at[k], s), pieces_out.at[s, pl.ds(pl.multiple_of(at[k] * rows, rows), rows)], out_sems.at[k, s])

    def project(k, s):
        keep(k, s).start()
        start = pl.multiple_of(at[k] * rows, rows)
        made = (nn(pieces[at[k], s], w_ref[...]) + bias).astype(low)
        head = [made[:, h * 3 * HD : (h + 1) * 3 * HD] for h in range(heads)]
        made = jnp.concatenate([h[:, HD:] for h in head] + [h[:, :HD] for h in head], axis=1)
        qkv_ref[s, pl.ds(start, rows), :] = made

    z1[...] = standardize(x_ref[:rows, :].astype(f32))[0]
    for k in range(1, group):
        small_copy(k).wait()
    gain = jnp.concatenate([smalls[f, 0:1, :] for f in range(group)], axis=1).astype(f32)
    offset = jnp.concatenate([smalls[f, 1:2, :] for f in range(group)], axis=1).astype(f32)
    for s in range(2):
        if s == 1:
            z1[...] = standardize(x_ref[rows:, :].astype(f32))[0]
        pieces[me, s] = (z1[...] * gain + offset).astype(low)
        move(2, s).start()
        move(4, s).start()
        move(1, s).start()
    all_small_ref[...] = smalls[...]
    heads = b_ref.shape[0]
    none = jnp.zeros((1, HD), f32)
    bias = [p for h in range(heads) for p in (b_ref[h : h + 1, :HD].astype(f32), none, b_ref[h : h + 1, HD:].astype(f32))]
    bias = jnp.concatenate(bias, axis=1)
    for s in range(2):
        project(0, s)
    for s in range(2):
        move(1, s).wait_recv()
        project(1, s)
    for s in range(2):
        move(2, s).wait_recv()
        if s == 0:
            move(6, 0).start()
        move(3, s).start()
        move(4, s).wait_recv()
        if s == 1:
            move(6, 1).start()
        move(5, s).start()
        project(2, s)
        project(4, s)
    for s in range(2):
        move(3, s).wait_recv()
        project(3, s)
        move(5, s).wait_recv()
        project(5, s)
    for s in range(2):
        move(6, s).wait_recv()
        move(7, s).start()
        project(6, s)
    for s in range(2):
        move(7, s).wait_recv()
        project(7, s)
    for s in range(2):
        for r in range(1, group):
            move(r, s).wait_send()
        for k in range(group):
            keep(k, s).wait()


def gather_project(x, smalls, weight, bias, group):
    rows, width = x.shape
    cols = weight.shape[1]
    half = rows // 2
    span = smalls[0].shape[1]
    vmem = pl.BlockSpec(memory_space=pltpu.VMEM)
    low = jnp.bfloat16
    return pl.pallas_call(
        gather_project_kernel,
        in_specs=[vmem] * 10,
        out_specs=[vmem, pl.BlockSpec(memory_space=pl.ANY), vmem],
        out_shape=[
            jax.ShapeDtypeStruct((group, 16, span), low),
            jax.ShapeDtypeStruct((2, group * half, width), low),
            jax.ShapeDtypeStruct((2, group * half, cols), low),
        ],
        scratch_shapes=[
            pltpu.VMEM((half, width), jnp.float32),
            pltpu.VMEM((group, 2, half, width), low),
            pltpu.VMEM((group, 16, span), low),
            pltpu.VMEM((16, span), low),
            pltpu.SemaphoreType.DMA((group,)),
            pltpu.SemaphoreType.DMA((group,)),
            pltpu.SemaphoreType.DMA((group, 2)),
            pltpu.SemaphoreType.DMA((group, 2)),
            pltpu.SemaphoreType.DMA((group, 2)),
        ],
        compiler_params=pltpu.CompilerParams(
            vmem_limit_bytes=48 * 2**20, collective_id=2, has_side_effects=True
        ),
        name="gather_project",
    )(x, *smalls, weight, bias)


def gelu_both(v):
    c = math.sqrt(2.0 / math.pi)
    square = v * v
    t = jnp.tanh(v * (c + (c * 0.044715) * square))
    half = 0.5 * (1.0 + t)
    slope = half + (0.5 * v) * (1.0 - t * t) * (c + (3.0 * 0.044715 * c) * square)
    return v * half, slope


def column_sums(array):
    return jnp.sum(array, axis=0, keepdims=True)


def feed_forward_kernel(
    group, x_hbm, cot_hbm, merged_hbm, out_hbm, fc_near, proj_near, fc_own, proj_own, small_ref,
    layer_ref, gres_ref, gheads_ref, keep_ref, side_ref, gout_ref, gvec_ref, gfcb_ref,
    x_ref, cot_ref, merged_ref, out_ref, in_sems, resid, z2, rate, vec_ref, normed, total, gnormed, fc_w, proj_w, given, taken, gmerged, gout_given, gout_taken,
    load_sems, far_send, far_recv, pair_send, pair_recv, side_send, side_recv, keep_sems, head_send, head_recv,
    own_sem, gout_sems,
):
    step = pl.program_id(0)
    last = group - 1
    me = lax.axis_index("fsdp")
    at = [xor(me, k, group) for k in range(group)]
    rows = x_hbm.shape[0]
    block = rows // 2
    f32, low = jnp.float32, jnp.bfloat16
    span = merged_ref.shape[1] // group

    def load(a, i):
        near, here = ((fc_near, fc_w), (proj_near, proj_w))[a]
        return pltpu.make_async_copy(near.at[i], here.at[lax.rem(i, 2)], load_sems.at[a, lax.rem(i, 2)])

    def load_own(a):
        i = (NEAR - 1) % 2
        return pltpu.make_async_copy((fc_own, proj_own)[a], (fc_w, proj_w)[a].at[i], load_sems.at[a, i])

    def far_copy(a, way):
        near, here = ((fc_near, fc_w), (proj_near, proj_w))[a]
        size = near.shape[1] // 2
        if way == 2:
            src, dst, to = here.at[3], here.at[2], at[1]
        else:
            part = pl.ds(way * size, size)
            src, dst = near.at[STEP_OF[(2, 4)[way]], part], here.at[3, part]
            to = at[(4, 2)[way]]
        return pltpu.make_async_remote_copy(
            src_ref=src, dst_ref=dst, send_sem=far_send.at[a, way], recv_sem=far_recv.at[a, way],
            device_id={"fsdp": to}, device_id_type=MESH,
        )

    def pair_copy(j):
        return pltpu.make_async_remote_copy(
            src_ref=given.at[lax.rem(j, 2)], dst_ref=taken.at[j], send_sem=pair_send.at[j], recv_sem=pair_recv.at[j],
            device_id={"fsdp": at[1]}, device_id_type=MESH,
        )

    def side_copy(a):
        return pltpu.make_async_remote_copy(
            src_ref=taken.at[a, a], dst_ref=side_ref.at[a], send_sem=side_send.at[a], recv_sem=side_recv.at[a],
            device_id={"fsdp": at[(2, 4)[a]]}, device_id_type=MESH,
        )

    def keep_copy(j):
        return pltpu.make_async_copy(taken.at[j], keep_ref.at[j], keep_sems.at[j])

    def head_copy(k):
        src = gmerged.at[:, :, pl.ds(k * span, span)]
        dst = gheads_ref.at[:, pl.ds(pl.multiple_of(me * block, block), block), :]
        if k == 0:
            return pltpu.make_async_copy(src, dst, own_sem)
        return pltpu.make_async_remote_copy(
            src_ref=src, dst_ref=dst, send_sem=head_send.at[k], recv_sem=head_recv.at[k],
            device_id={"fsdp": at[k]}, device_id_type=MESH,
        )

    def gout_copy():
        return pltpu.make_async_remote_copy(
            src_ref=gout_given, dst_ref=gout_taken, send_sem=gout_sems.at[0], recv_sem=gout_sems.at[1],
            device_id={"fsdp": at[1]}, device_id_type=MESH,
        )

    @pl.when(step == 0)
    def _():
        brought = [
            pltpu.make_async_copy(src, dst, in_sems.at[i])
            for i, (src, dst) in enumerate(
                ((merged_hbm, merged_ref), (out_hbm, out_ref), (x_hbm, x_ref), (cot_hbm, cot_ref))
            )
        ]
        for copy in brought:
            copy.start()
        enter(at[1:])
        for a in range(2):
            load(a, 0).start()
        for a in range(2):
            far_copy(a, 0).start()
            far_copy(a, 1).start()
        for copy in brought:
            copy.wait()
        for i in range(4):
            vec_ref[i : i + 1, :] = jnp.concatenate(
                [small_ref[f, 2 + i : 3 + i, :] for f in range(group)], axis=1
            ).astype(f32)
        acc = x_ref[...].astype(f32) + vec_ref[0:1, :] + nn(merged_ref[...], out_ref[...])
        resid[...] = acc
        z, r = standardize(acc)
        z2[...] = z
        rate[...] = jnp.broadcast_to(r, rate.shape)
        normed[...] = (z * vec_ref[1:2, :] + vec_ref[2:3, :]).astype(low)
        total[...] = jnp.zeros_like(total)
        gnormed[...] = jnp.zeros_like(gnormed)

    j = lax.div(step, 2)
    odd = lax.rem(step, 2)

    @pl.when(step < NEAR - 1)
    def _():
        for a in range(2):
            load(a, step).wait()

    @pl.when(step == NEAR - 1)
    def _():
        for a in range(2):
            load_own(a).wait()

    @pl.when(step + 1 < NEAR - 1)
    def _():
        for a in range(2):
            load(a, step + 1).start()

    @pl.when(step + 1 == NEAR - 1)
    def _():
        for a in range(2):
            load_own(a).start()

    @pl.when(step == NEAR)
    def _():
        for a in range(2):
            far_copy(a, 2).wait_recv()

    @pl.when((odd == 0) & (j >= 2))
    def _():
        pair_copy(j - 2).wait_send()

    here = jnp.where(step < NEAR, lax.rem(step, 2), step - NEAR + 2)
    fresh = jnp.where(odd == 0, lax.rem(j, 2), 2)
    owner = sum(jnp.where(step == i, at[SLOT_AT[i]], 0) for i in range(group))
    fc_bias = jnp.concatenate([small_ref[owner, 6 + i : 7 + i, :] for i in range(4)], axis=1).astype(f32)
    hidden = nn(normed[...], fc_w[here]) + fc_bias
    gactive = nt(cot_ref[...], proj_w[here])
    active, slope = gelu_both(hidden)
    active = active.astype(low)
    ghidden = gactive * slope
    gfcb_ref[0] = column_sums(ghidden)
    ghidden = ghidden.astype(low)
    total[...] += nn(active, proj_w[here])
    gnormed[...] += nt(ghidden, fc_w[here])
    given[fresh, 0] = tn(normed[...], ghidden).astype(low)
    gproj = tn(active, cot_ref[...]).astype(low)
    size, part = gproj.shape[0], fc_w.shape[2]
    for i in range(gproj.shape[1] // part):
        given[fresh, 1, i * size : (i + 1) * size, :] = gproj[:, i * part : (i + 1) * part]

    @pl.when(odd == 0)
    def _():
        pair_copy(j).start()

    @pl.when(odd == 1)
    def _():
        pair_copy(j).wait_recv()

        def add(i, _):
            part = pl.ds(pl.multiple_of(lax.rem(i, 8) * 128, 128), 128)
            a = lax.div(i, 8)
            taken[j, a, part, :] = (taken[j, a, part, :].astype(f32) + given[2, a, part, :].astype(f32)).astype(low)
            return 0

        lax.fori_loop(0, 16, add, 0)
        keep_copy(j).start()

    for a in range(2):
        @pl.when(step == 1 + 2 * a)
        def _(a=a):
            side_copy(a).start()

    @pl.when(step == 3)
    def _():
        for a in range(2):
            far_copy(a, 0).wait_recv()
            far_copy(a, 1).wait_recv()
            far_copy(a, 2).start()

    @pl.when(step == last)
    def _():
        cot32 = cot_ref[...].astype(f32)
        g, z = gnormed[...], z2[...]
        gres = cot32 + norm_grad(g * vec_ref[1:2, :], z, rate[:, :1])
        gres_ref[...] = gres
        gattn = gres.astype(low)
        back = nt(gattn, out_ref[...]).astype(low)
        for s in range(2):
            gmerged[s] = back[s * block : (s + 1) * block, :]
        for k in (6, 2, 4, 3, 5, 7, 1, 0):
            head_copy(k).start()
        gout = tn(merged_ref[...], gattn)
        for k in range(1, group, 2):
            gout_given[k // 2] = gout[k * span : (k + 1) * span, :].astype(low)
        gout_copy().start()
        layer_ref[...] = (resid[...] + total[...] + vec_ref[3:4, :]).astype(low)
        gvec_ref[0:1, :] = column_sums(gattn.astype(f32))
        gvec_ref[1:2, :] = column_sums(g * z)
        gvec_ref[2:3, :] = column_sums(g)
        gvec_ref[3:4, :] = column_sums(cot32)
        gout_copy().wait_recv()
        for k in range(0, group, 2):
            mine = gout[k * span : (k + 1) * span, :].astype(low).astype(f32)
            gout_ref[k // 2] = (mine + gout_taken[k // 2].astype(f32)).astype(low)
        for k in range(group):
            head_copy(k).wait()
        gout_copy().wait_send()
        for a in range(2):
            for way in range(3):
                far_copy(a, way).wait_send()
        pair_copy(2).wait_send()
        pair_copy(3).wait_send()
        side_copy(0).wait()
        side_copy(1).wait()
        for i in range(group // 2):
            keep_copy(i).wait()


def feed_forward(x, cot, merged, out_all, fc_near, proj_near, fc_own, proj_own, small):
    rows, width = x.shape
    group, part = small.shape[0], fc_near.shape[2]
    span = width // group
    f32, low = jnp.float32, jnp.bfloat16
    vmem = pl.BlockSpec(memory_space=pltpu.VMEM)
    hbm = pl.BlockSpec(memory_space=pl.ANY)
    return pl.pallas_call(
        functools.partial(feed_forward_kernel, group),
        grid=(group,),
        in_specs=[
            hbm, hbm, hbm, hbm,
            hbm, hbm, hbm, hbm,
            vmem,
        ],
        out_specs=[
            vmem, vmem, hbm,
            hbm, hbm, vmem, vmem,
            pl.BlockSpec((1, 1, part), lambda i: (i, 0, 0)),
        ],
        out_shape=[
            jax.ShapeDtypeStruct((rows, width), low),
            jax.ShapeDtypeStruct((rows, width), f32),
            jax.ShapeDtypeStruct((2, group * rows // 2, span), low),
            jax.ShapeDtypeStruct((group // 2, 2, width, part), low),
            jax.ShapeDtypeStruct((2, width, part), low),
            jax.ShapeDtypeStruct((group // 2, span, width), low),
            jax.ShapeDtypeStruct((8, width), f32),
            jax.ShapeDtypeStruct((group, 1, part), f32),
        ],
        scratch_shapes=[
            pltpu.VMEM((rows, width), low),
            pltpu.VMEM((rows, width), low),
            pltpu.VMEM((rows, width), low),
            pltpu.VMEM((width, width), low),
            pltpu.SemaphoreType.DMA((4,)),
            pltpu.VMEM((rows, width), f32),
            pltpu.VMEM((rows, width), f32),
            pltpu.VMEM((rows, 128), f32),
            pltpu.VMEM((8, width), f32),
            pltpu.VMEM((rows, width), low),
            pltpu.VMEM((rows, width), f32),
            pltpu.VMEM((rows, width), f32),
            pltpu.VMEM((4, width, part), low),
            pltpu.VMEM((4, part, width), low),
            pltpu.VMEM((3, 2, width, part), low),
            pltpu.VMEM((group // 2, 2, width, part), low),
            pltpu.VMEM((2, rows // 2, width), low),
            pltpu.VMEM((group // 2, span, width), low),
            pltpu.VMEM((group // 2, span, width), low),
            pltpu.SemaphoreType.DMA((2, 2)),
            pltpu.SemaphoreType.DMA((2, 3)),
            pltpu.SemaphoreType.DMA((2, 3)),
            pltpu.SemaphoreType.DMA((group // 2,)),
            pltpu.SemaphoreType.DMA((group // 2,)),
            pltpu.SemaphoreType.DMA((2,)),
            pltpu.SemaphoreType.DMA((2,)),
            pltpu.SemaphoreType.DMA((group // 2,)),
            pltpu.SemaphoreType.DMA((group,)),
            pltpu.SemaphoreType.DMA((group,)),
            pltpu.SemaphoreType.DMA,
            pltpu.SemaphoreType.DMA((2,)),
        ],
        compiler_params=pltpu.CompilerParams(vmem_limit_bytes=62 * 2**20, collective_id=3, has_side_effects=True),
        name="feed_forward",
    )(x, cot, merged, out_all, fc_near, proj_near, fc_own, proj_own, small)


def attend_back_kernel(
    heads, group, docs, qkv_hbm, halo_hbm, ids_hbm, q2_ref, out_ref, grad_ref, kept, side,
    gqkv_ref, sums_ref,
    qkv_ref, halo_ref, ids_ref, in_sems, keys, values, keys_t, dkeys, dvalues, edge, ahead, mid, near, far, mine, met,
    edge_sems, load_sems, near_send, near_recv, far_send, far_recv,
):
    step = pl.program_id(0)
    last = pl.num_programs(0) - 1
    me = lax.axis_index("fsdp")
    line = lax.axis_index("seq")
    line_end = lax.axis_size("seq") - 1
    at = [xor(me, k, group) for k in range(group)]
    seqs, rows = qkv_hbm.shape[0], qkv_hbm.shape[1]
    half = group // 2
    seq = lax.rem(lax.div(step, half), 2)
    place = lax.div(step, group) * half + lax.rem(step, half)
    f32, low = jnp.float32, jnp.bfloat16
    pieces = 2
    size = mid.shape[1] // pieces

    def edge_copy(s):
        return pltpu.make_async_remote_copy(
            src_ref=edge.at[s], dst_ref=ahead.at[s], send_sem=edge_sems.at[0, s], recv_sem=edge_sems.at[1, s],
            device_id={"seq": lax.rem(line + line_end, line_end + 1)}, device_id_type=MESH,
        )

    first, second = (at[2], at[4]), (at[4], at[2])

    def near_copy(a, h):
        part = pl.ds(h * size, size)
        return pltpu.make_async_remote_copy(
            src_ref=kept.at[3, a, part], dst_ref=near.at[a, part], send_sem=near_send.at[a, h],
            recv_sem=near_recv.at[a, h], device_id={"fsdp": first[a]}, device_id_type=MESH,
        )

    def far_copy(a, h):
        part = pl.ds(h * size, size)
        return pltpu.make_async_remote_copy(
            src_ref=mid.at[a, part], dst_ref=far.at[a, part], send_sem=far_send.at[a, h],
            recv_sem=far_recv.at[a, h], device_id={"fsdp": second[a]}, device_id_type=MESH,
        )

    def loads():
        for a in range(2):
            yield pltpu.make_async_copy(kept.at[1 - a, a], mid.at[a], load_sems.at[0, a])
            yield pltpu.make_async_copy(kept.at[2, a], mine.at[a], load_sems.at[1, a])
            yield pltpu.make_async_copy(side.at[a], met.at[a], load_sems.at[2, a])

    def plus(u, *more):
        total = u.astype(f32)
        for v in more:
            total += v.astype(f32)
        return total.astype(low)

    @pl.when(step == 0)
    def _():
        brought = [
            pltpu.make_async_copy(src, dst, in_sems.at[i])
            for i, (src, dst) in enumerate(((qkv_hbm, qkv_ref), (halo_hbm, halo_ref), (ids_hbm, ids_ref)))
        ]
        for load in brought:
            load.start()
        dkeys[...] = jnp.zeros_like(dkeys)
        dvalues[...] = jnp.zeros_like(dvalues)
        barrier = pltpu.get_barrier_semaphore()
        for peer in (at[2], at[4]):
            pl.semaphore_signal(barrier, inc=1, device_id={"fsdp": peer}, device_id_type=MESH)
        pl.semaphore_signal(
            barrier, inc=1, device_id={"seq": lax.rem(line + 1, line_end + 1)}, device_id_type=MESH
        )
        pl.semaphore_wait(barrier, 3)
        for h in range(pieces):
            for a in range(2):
                near_copy(a, h).start()
        for load in loads():
            load.start()
        for load in brought:
            load.wait()
        for s in range(seqs):
            fill_keys(s, heads, halo_ref, ids_ref, docs, 0, keys, values, None, keys_t)
            fill_keys(s, heads, qkv_ref, ids_ref, docs, WINDOW, keys, values, None, keys_t)

    for s in range(seqs):
        @pl.when((step == (s + 1) * half) & (line > 0))
        def _(s=s):
            for h in range(heads):
                c = h * 2 * HD
                edge[s, :, c : c + 2 * HD] = jnp.concatenate(
                    [dkeys[s * heads + h, :WINDOW, :HD], dvalues[s * heads + h, :WINDOW, :HD]], axis=1
                ).astype(low)
            edge_copy(s).start()

    mask = edge_mask()
    tiles = WINDOW // BLK + 1
    start = pl.multiple_of(place * BLK, BLK)
    lane = lax.broadcasted_iota(jnp.int32, (BLK, 2 * HD), 1)
    spans = [pl.ds(pl.multiple_of(start + b * BLK, BLK), BLK) for b in range(tiles)]
    for h in range(heads):
        sh = seq * heads + h
        q = q2_ref[0, h]
        g32 = grad_ref[0, :, h * HD : (h + 1) * HD].astype(f32)
        centre = jnp.sum(g32 * out_ref[0, :, h * HD : (h + 1) * HD].astype(f32), axis=1, keepdims=True)
        hi, md, lo = split3(-centre)
        g2 = jnp.concatenate([g32, jnp.zeros((BLK, HD), f32)], axis=1)
        g2 = jnp.where(lane == HD, hi, g2)
        g2 = jnp.where(lane == HD + 1, md, g2)
        g2 = jnp.where(lane == HD + 2, lo, g2).astype(low)
        scores = merge_edges(mask, [nt(keys[sh, s, :], q) for s in spans])
        wgrads = merge_edges(mask, [nt(values[sh, s, :], g2) for s in spans])
        weights = [jnp.exp(s) for s in scores]
        sgrads = spread_edges(mask, [(w * d).astype(low) for w, d in zip(weights, wgrads)])
        weights = spread_edges(mask, [w.astype(low) for w in weights])
        for s, w, d in zip(spans, weights, sgrads):
            dvalues[sh, s, :] += nn(w, g2)
            dkeys[sh, s, :] += nn(d, q)
        dq = sum(nn(keys_t[sh, :, s], d) for s, d in zip(spans, sgrads))
        qc = heads * 2 * HD + h * HD
        gqkv_ref[seq, pl.ds(start, BLK), qc : qc + HD] = (dq.T[:, :HD] * 0.125).astype(low)

    def relay(h):
        part = slice(h * size, (h + 1) * size)
        for a in range(2):
            near_copy(a, h).wait_recv()
            mid[a, part] = plus(mid[a, part], near[a, part])
            far_copy(a, h).start()

    @pl.when(step == 4)
    def _():
        for load in loads():
            load.wait()
        relay(0)

    @pl.when(step == 8)
    def _():
        relay(1)

    @pl.when(step == last)
    def _():
        def own(s, h, first, count):
            span = slice(WINDOW + first, WINDOW + first + count)
            return jnp.concatenate([dkeys[s * heads + h, span, :HD], dvalues[s * heads + h, span, :HD]], axis=1)

        for s in range(seqs):
            for h in range(heads):
                c = h * 2 * HD
                gqkv_ref[s, : rows - WINDOW, c : c + 2 * HD] = own(s, h, 0, rows - WINDOW).astype(low)

        @pl.when(line < line_end)
        def _():
            for s in range(seqs):
                edge_copy(s).wait_recv()

        @pl.when(line == line_end)
        def _():
            ahead[...] = jnp.zeros_like(ahead)

        for s in range(seqs):
            for h in range(heads):
                c = h * 2 * HD
                gqkv_ref[s, rows - WINDOW :, c : c + 2 * HD] = (
                    own(s, h, rows - WINDOW, WINDOW) + ahead[s, :, c : c + 2 * HD].astype(f32)
                ).astype(low)

        for h in range(pieces):
            part = slice(h * size, (h + 1) * size)
            for a in range(2):
                far_copy(a, h).wait_recv()
                sums_ref[a, part] = plus(mine[a, part], met[a, part], far[a, part])
        for a in range(2):
            for h in range(pieces):
                near_copy(a, h).wait_send()
                far_copy(a, h).wait_send()

        @pl.when(line > 0)
        def _():
            for s in range(seqs):
                edge_copy(s).wait_send()


def attend_back(qkv, halo, ids, docs, q2, out, grad, kept, side, heads, group):
    seqs, rows, cols = qkv.shape
    ext = ids.shape[1]
    half = group // 2
    f32, low = jnp.float32, jnp.bfloat16
    vmem = pl.BlockSpec(memory_space=pltpu.VMEM)
    hbm = pl.BlockSpec(memory_space=pl.ANY)
    every = seqs * heads
    part = kept.shape[2:]
    seq_of = lambda i: lax.rem(lax.div(i, half), 2)
    place_of = lambda i: lax.div(i, group) * half + lax.rem(i, half)
    edge = pltpu.VMEM((seqs, WINDOW, heads * 2 * HD), low)
    pair = pltpu.VMEM((2,) + part, low)
    return pl.pallas_call(
        functools.partial(attend_back_kernel, heads, group, docs),
        grid=(seqs * rows // BLK,),
        in_specs=[
            hbm, hbm, hbm,
            pl.BlockSpec((1, heads, BLK, 2 * HD), lambda i: (seq_of(i), 0, place_of(i), 0)),
            pl.BlockSpec((1, BLK, heads * HD), lambda i: (seq_of(i), place_of(i), 0)),
            pl.BlockSpec((1, BLK, heads * HD), lambda i: (seq_of(i), place_of(i), 0)),
            hbm, hbm,
        ],
        out_specs=[vmem, vmem],
        out_shape=[
            jax.ShapeDtypeStruct((seqs, rows, cols), low),
            jax.ShapeDtypeStruct((2,) + part, low),
        ],
        scratch_shapes=[
            pltpu.VMEM(qkv.shape, low),
            pltpu.VMEM(halo.shape, low),
            pltpu.VMEM(ids.shape, jnp.int32),
            pltpu.SemaphoreType.DMA((3,)),
            pltpu.VMEM((every, ext, 2 * HD), low),
            pltpu.VMEM((every, ext, 2 * HD), low),
            pltpu.VMEM((every, 2 * HD, ext), low),
            pltpu.VMEM((every, ext, 2 * HD), f32),
            pltpu.VMEM((every, ext, 2 * HD), f32),
            edge, edge, pair, pair, pair, pair, pair,
            pltpu.SemaphoreType.DMA((2, seqs)),
            pltpu.SemaphoreType.DMA((3, 2)),
            pltpu.SemaphoreType.DMA((2, 2)),
            pltpu.SemaphoreType.DMA((2, 2)),
            pltpu.SemaphoreType.DMA((2, 2)),
            pltpu.SemaphoreType.DMA((2, 2)),
        ],
        compiler_params=pltpu.CompilerParams(vmem_limit_bytes=62 * 2**20, collective_id=4, has_side_effects=True),
        name="attend_back",
    )(qkv, halo, ids, q2, out, grad, kept, side)


def finish_kernel(
    g_hbm, wt_hbm, x_hbm, gres_hbm, small_ref, sums_hbm, out_hbm, gvec_ref, gfcb_ref, z_hbm,
    input_grad_ref, fc_total_ref, proj_total_ref, out_total_ref, qkv_total_ref, vec_ref,
    g_ref, wt_ref, x_ref, gres_ref, sums_ref, out_kept, in_sems, z_all, odd, odd_in, even, mine, first_in, second_in, mt, rows6, vec_out, vec_in, vec_line,
    acc, acc_out, acc_q, left, left_out, left_q, right, right_out, right_q, total_q, out_near, out_far, out_mid,
    z_sem, odd_send, odd_recv, near_send, near_recv, far_send, far_recv,
    vec_send, vec_recv, vl_send, vl_recv, line_send, line_recv, out_send, out_recv,
):
    group = small_ref.shape[0]
    me = lax.axis_index("fsdp")
    line = lax.axis_index("seq")
    line_size = 4
    at = [xor(me, k, group) for k in range(group)]
    block = x_hbm.shape[0] // 2
    f32, low = jnp.float32, jnp.bfloat16
    width = x_hbm.shape[1]
    span = small_ref.shape[2]
    heads = wt_hbm.shape[0] // (3 * HD)
    outer = (line == 0) | (line == line_size - 1)
    inner = (line > 0) & (line < line_size - 1)

    def remote(src, dst, send, recv, to):
        return pltpu.make_async_remote_copy(
            src_ref=src, dst_ref=dst, send_sem=send, recv_sem=recv, device_id=to, device_id_type=MESH
        )

    brought = [
        pltpu.make_async_copy(src, dst, in_sems.at[i])
        for i, (src, dst) in enumerate(
            (
                (g_hbm, g_ref), (wt_hbm, wt_ref), (sums_hbm, sums_ref), (out_hbm, out_kept), (x_hbm, x_ref),
                (gres_hbm, gres_ref),
            )
        )
    ]
    for copy in brought:
        copy.start()
    barrier = pltpu.get_barrier_semaphore()
    for peer in at[1:]:
        pl.semaphore_signal(barrier, inc=1, device_id={"fsdp": peer}, device_id_type=MESH)
    others = [lax.rem(line + d, line_size) for d in range(1, line_size)]
    for other in others:
        pl.semaphore_signal(barrier, inc=1, device_id={"seq": other}, device_id_type=MESH)
    pl.semaphore_wait(barrier, group - 1 + line_size - 1)

    cut = sums_hbm.shape[1] // 4
    fc_chunks, proj_chunks = [], []
    for i in range(4):
        part = pl.ds(i * cut, cut)
        fc_chunks.append([r.at[0, part] for r in (sums_hbm, acc, left, right)] + [fc_total_ref.at[part], sums_ref.at[0, part]])
        there = proj_total_ref.at[pl.ds(i % 2 * cut, cut), pl.ds(i // 2 * sums_ref.shape[2], sums_ref.shape[2])]
        proj_chunks.append([r.at[1, part] for r in (sums_hbm, acc, left, right)] + [there, sums_ref.at[1, part]])
    cut = acc_q.shape[0] // 3
    qkv_chunks = [
        [r.at[pl.ds(i * cut, cut)] for r in (acc_q, acc_q, left_q, right_q, total_q, acc_q)] for i in range(3)
    ]
    cut = acc_out.shape[0] // 2
    out_chunks = [
        [r.at[pl.ds(i * cut, cut)] for r in (acc_out, acc_out, left_out, right_out, out_total_ref, acc_out)]
        for i in range(2)
    ]
    chunks = fc_chunks + proj_chunks[:2] + qkv_chunks + proj_chunks[2:] + out_chunks
    early = 6

    def inwards(c):
        return remote(
            chunks[c][0], chunks[c][2], line_send.at[0, c], line_recv.at[0, c], {"seq": 1 + lax.div(line, line_size - 1)}
        )

    def across(c):
        return remote(
            chunks[c][1], chunks[c][3], line_send.at[1, c], line_recv.at[1, c], {"seq": line_size - 1 - line}
        )

    def outwards(c):
        return remote(
            chunks[c][4], chunks[c][3], line_send.at[2, c], line_recv.at[2, c],
            {"seq": lax.rem((line + line_size - 1) * (line_size - 1), 2 * (line_size - 1))},
        )

    def begin(cs):
        @pl.when(outer)
        def _():
            for c in cs:
                inwards(c).start()

    def collect(c):
        @pl.when(inner)
        def _():
            inwards(c).wait_recv()
            acc_c, left_c, own = chunks[c][1], chunks[c][2], chunks[c][5]
            acc_c[...] = (own[...].astype(f32) + left_c[...].astype(f32)).astype(low)
            across(c).start()

    def settle(c):
        @pl.when(inner)
        def _():
            across(c).wait_recv()
            chunks[c][4][...] = (chunks[c][1][...].astype(f32) + chunks[c][3][...].astype(f32)).astype(low)
            outwards(c).start()

    def receive(c):
        @pl.when(outer)
        def _():
            outwards(c).wait_recv()
            chunks[c][4][...] = chunks[c][3][...]

    def advance(first, last):
        for c in range(first, last):
            collect(c)
            if c >= 1:
                settle(c - 1)
            if c >= 2:
                receive(c - 2)

    begin(range(early))
    load = pltpu.make_async_copy(z_hbm, z_all, z_sem)
    load.start()

    ways = (at[2], at[4])
    out_cut = out_hbm.shape[1] // 2
    out_first = ((0, 1, 0), (0, 3, 1), (1, 2, 0), (1, 3, 1))

    def out_near_copy(n):
        h, slot, j = out_first[n]
        return pltpu.make_async_remote_copy(
            src_ref=out_hbm.at[slot, pl.ds(h * out_cut, out_cut)], dst_ref=out_near.at[h, j], send_sem=out_send.at[n],
            recv_sem=out_recv.at[n], device_id={"fsdp": ways[h]}, device_id_type=MESH,
        )

    def out_far_copy(h):
        return pltpu.make_async_remote_copy(
            src_ref=out_mid.at[h], dst_ref=out_far.at[h], send_sem=out_send.at[4 + h],
            recv_sem=out_recv.at[4 + h], device_id={"fsdp": ways[1 - h]}, device_id_type=MESH,
        )

    for n in range(4):
        out_near_copy(n).start()

    def product(r, s):
        start = pl.multiple_of(at[r] * block, block)
        return nn(g_ref[s, pl.ds(start, block), :], wt_ref[...])

    def odd_copy(j):
        return remote(odd.at[j], odd_in.at[j], odd_send.at[j], odd_recv.at[j], {"fsdp": at[1]})

    def make_odd(j):
        for s in range(2):
            odd[j, s] = product(2 * j + 1, s).astype(low)
        odd_copy(j).start()

    for copy in brought:
        copy.wait()
    make_odd(3)
    make_odd(1)
    advance(0, 1)
    make_odd(2)
    make_odd(0)

    def near_copy(s, i):
        j = 3 if i == 0 else 1 + s
        return remote(even.at[j, s], first_in.at[s, i], near_send.at[s, i], near_recv.at[s, i], {"fsdp": ways[s]})

    def far_copy(s):
        return remote(even.at[2 - s, s], second_in.at[s], far_send.at[s], far_recv.at[s], {"fsdp": ways[1 - s]})

    def make_even(j):
        odd_copy(j).wait_recv()
        for s in range(2):
            part = product(2 * j, s) + odd_in[j, s].astype(f32)
            if j == 0:
                mine[s] = part
            else:
                even[j, s] = part.astype(low)
                if j == 3:
                    near_copy(s, 0).start()
                elif j == 1 + s:
                    near_copy(s, 1).start()

    make_even(3)
    advance(1, 2)
    make_even(1)
    make_even(2)
    advance(2, 3)
    make_even(0)

    def wide(index):
        return jnp.concatenate([small_ref[f, index : index + 1, :] for f in range(group)], axis=1).astype(f32)

    gain = wide(0)
    load.wait()
    mt[...] = jnp.zeros_like(mt)
    steps = z_all.shape[1] // 512
    ones = jnp.ones((512, 128), low)

    def add_product(i, sums):
        rows = pl.ds(pl.multiple_of(lax.rem(i, steps) * 512, 512), 512)
        g = g_ref[lax.div(i, steps), rows, :]
        mt[...] += tn(g, z_all[lax.div(i, steps), rows, :])
        return sums + tn(g, ones)

    column = lax.fori_loop(0, steps // 2, add_product, jnp.zeros((g_ref.shape[2], 128), f32))
    advance(3, 4)
    for h in range(2):
        part = slice(h * out_cut, (h + 1) * out_cut)
        out_near_copy(2 * h + 1).wait_recv()
        out_mid[h] = (out_kept[2 - h, part].astype(f32) + out_near[h, 1].astype(f32)).astype(low)
        out_far_copy(h).start()
    column = lax.fori_loop(steps // 2, steps, add_product, column)
    for s in range(2):
        near_copy(s, 0).wait_recv()
        even[2 - s, s] = (even[2 - s, s].astype(f32) + first_in[s, 0].astype(f32)).astype(low)
        far_copy(s).start()

    advance(4, 5)
    column = lax.fori_loop(steps, 2 * steps, add_product, column)
    acc_q[...] = mt[...].astype(low)
    begin(range(early, len(chunks) - 2))
    advance(5, 6)

    def vec_copy(k):
        return remote(vec_out.at[k], vec_in.at[k], vec_send.at[k], vec_recv.at[k], {"fsdp": at[k]})

    for h in range(2):
        part = slice(h * out_cut, (h + 1) * out_cut)
        out_near_copy(2 * h).wait_recv()
        out_far_copy(h).wait_recv()
        acc_out[part] = (
            out_kept[0, part].astype(f32) + out_near[h, 0].astype(f32) + out_far[h].astype(f32)
        ).astype(low)
    begin([len(chunks) - 2, len(chunks) - 1])

    def line_copy(d):
        return remote(vec_line.at[line], vec_line.at[line], vl_send.at[d], vl_recv.at[d], {"seq": others[d]})

    advance(6, 7)
    gain_grad = offset_grad = jnp.zeros((1, width), f32)
    for s in range(2):
        near_copy(s, 1).wait_recv()
        far_copy(s).wait_recv()
        rows = slice(s * block, (s + 1) * block)
        e = mine[s] + first_in[s, 1].astype(f32) + second_in[s].astype(f32)
        z, rate = standardize(x_ref[rows, :].astype(f32))
        gain_grad += column_sums(e * z)
        offset_grad += column_sums(e)
        input_grad_ref[rows, :] = (gres_ref[rows, :] + norm_grad(e * gain, z, rate)).astype(low)
    rows6[0:1, :] = gain_grad
    rows6[1:2, :] = offset_grad
    rows6[2:6, :] = gvec_ref[0:4, :]
    row = column.T[0:1, :]
    vec_out[...] = jnp.zeros_like(vec_out)
    for k in range(group):
        vec_out[k, 0:6, :] = rows6[0:6, pl.ds(pl.multiple_of(at[k] * span, span), span)]
        for i in range(4):
            vec_out[k, 6 + i : 7 + i, :] = gfcb_ref[STEP_OF[k], :, i * span : (i + 1) * span]
    for h in range(heads):
        base = heads * 2 * HD + h * HD
        vec_out[0, 10 + h : 11 + h, :] = jnp.concatenate(
            [row[:, base : base + HD], row[:, h * 2 * HD + HD : (h + 1) * 2 * HD]], axis=1
        )

    for k in range(1, group):
        vec_copy(k).start()

    advance(7, 9)
    total = vec_out[0]
    for k in range(1, group):
        vec_copy(k).wait_recv()
        total += vec_in[k]
    vec_line[line] = total

    for d in range(line_size - 1):
        line_copy(d).start()

    advance(9, 11)
    for d in range(line_size - 1):
        line_copy(d).wait_recv()
    vec_ref[...] = vec_line[0] + vec_line[1] + vec_line[2] + vec_line[3]
    advance(11, 13)
    turned = total_q[...].T
    pairs = heads * 2 * HD
    turned = [
        p
        for h in range(heads)
        for p in (turned[:, pairs + h * HD : pairs + (h + 1) * HD], turned[:, h * 2 * HD : (h + 1) * 2 * HD])
    ]
    qkv_total_ref[...] = jnp.concatenate(turned, axis=1)
    settle(12)
    receive(11)
    receive(12)
    for j in range(4):
        odd_copy(j).wait_send()
    for s in range(2):
        near_copy(s, 0).wait_send()
        near_copy(s, 1).wait_send()
        far_copy(s).wait_send()
    for n in range(4):
        out_near_copy(n).wait_send()
    for h in range(2):
        out_far_copy(h).wait_send()
    for k in range(1, group):
        vec_copy(k).wait_send()
    for d in range(line_size - 1):
        line_copy(d).wait_send()

    @pl.when(outer)
    def _():
        for c in range(len(chunks)):
            inwards(c).wait_send()

    @pl.when(inner)
    def _():
        for c in range(len(chunks)):
            across(c).wait_send()
            outwards(c).wait_send()


def finish(g, wt, x, gres, small, sums, out_kept, gvec, gfcb, z_all):
    rows, width = x.shape
    group = small.shape[0]
    half = rows // 2
    span = small.shape[2]
    f32, low = jnp.float32, jnp.bfloat16
    vmem = pl.BlockSpec(memory_space=pltpu.VMEM)
    hbm = pl.BlockSpec(memory_space=pl.ANY)
    dma = pltpu.SemaphoreType.DMA
    out_part = out_kept.shape[1:]
    half_out = (out_part[0] // 2, out_part[1])
    buffers = [pltpu.VMEM(sums.shape, low), pltpu.VMEM(out_part, low), pltpu.VMEM(wt.shape, low)]
    return pl.pallas_call(
        finish_kernel,
        in_specs=[hbm] * 4 + [vmem, hbm, hbm, vmem, vmem, hbm],
        out_specs=[vmem] * 6,
        out_shape=[
            jax.ShapeDtypeStruct((rows, width), low),
            jax.ShapeDtypeStruct(sums.shape[1:], low),
            jax.ShapeDtypeStruct((sums.shape[2], sums.shape[1]), low),
            jax.ShapeDtypeStruct(out_part, low),
            jax.ShapeDtypeStruct(wt.shape[::-1], low),
            jax.ShapeDtypeStruct((16, span), f32),
        ],
        scratch_shapes=[
            pltpu.VMEM(g.shape, low),
            pltpu.VMEM(wt.shape, low),
            pltpu.VMEM(x.shape, low),
            pltpu.VMEM(gres.shape, f32),
            pltpu.VMEM(sums.shape, low),
            pltpu.VMEM(out_kept.shape, low),
            dma((6,)),
            pltpu.VMEM(z_all.shape, low),
            pltpu.VMEM((group // 2, 2, half, width), low),
            pltpu.VMEM((group // 2, 2, half, width), low),
            pltpu.VMEM((group // 2, 2, half, width), low),
            pltpu.VMEM((2, half, width), f32),
            pltpu.VMEM((2, 2, half, width), low),
            pltpu.VMEM((2, half, width), low),
            pltpu.VMEM(wt.shape, f32),
            pltpu.VMEM((8, width), f32),
            pltpu.VMEM((group, 16, span), f32),
            pltpu.VMEM((group, 16, span), f32),
            pltpu.VMEM((4, 16, span), f32),
        ]
        + buffers * 3
        + [pltpu.VMEM(wt.shape, low)]
        + [pltpu.VMEM((2, 2) + half_out, low), pltpu.VMEM((2,) + half_out, low), pltpu.VMEM((2,) + half_out, low)]
        + [dma, dma((4,)), dma((4,)), dma((2, 2)), dma((2, 2)), dma((2,)), dma((2,))]
        + [dma((group,)), dma((group,)), dma((3,)), dma((3,)), dma((3, 13)), dma((3, 13)), dma((6,)), dma((6,))],
        compiler_params=pltpu.CompilerParams(vmem_limit_bytes=62 * 2**20, collective_id=5, has_side_effects=True),
        name="finish",
    )(g, wt, x, gres, small, sums, out_kept, gvec, gfcb, z_all)


def plain_fill_keys(heads, qkv_ref, halo_ref, augk_ref, keys, values):
    halo_rows = halo_ref.shape[1]
    rows = qkv_ref.shape[1]
    ones = jnp.ones((1, HD), jnp.bfloat16)
    for h in range(heads):
        c = h * 2 * HD
        for source, base, size in ((halo_ref, 0, halo_rows), (qkv_ref, halo_rows, rows)):
            pair = source[0, :, c : c + 2 * HD]
            keys[h, base : base + size, :] = jnp.concatenate(
                [pair[:, :HD], augk_ref[0, base : base + size, :]], axis=1
            )
            values[h, base : base + size, :] = jnp.concatenate(
                [pair[:, HD:], jnp.broadcast_to(ones, (size, HD))], axis=1
            )


def plain_attend_kernel(heads, qkv_ref, halo_ref, augk_ref, augq_ref, out_ref, q2_ref, keys, values, values_t):
    step = pl.program_id(1)
    nkeys = keys.shape[1]

    @pl.when(step == 0)
    def _():
        plain_fill_keys(heads, qkv_ref, halo_ref, augk_ref, keys, values)
        for h in range(heads):
            for b in range(nkeys // BLK):
                values_t[h, :, b * BLK : (b + 1) * BLK] = values[h, b * BLK : (b + 1) * BLK, :].T

    mask = edge_mask()
    tiles = WINDOW // BLK + 1
    start = pl.multiple_of(step * BLK, BLK)
    lane = lax.broadcasted_iota(jnp.int32, (BLK, 2 * HD), 1)
    lse_lane = augq_ref.shape[2] + HD - 3
    for h in range(heads):
        qc = heads * 2 * HD + h * HD
        q = jnp.concatenate([qkv_ref[0, pl.ds(start, BLK), qc : qc + HD] * 0.125, augq_ref[0]], axis=1)
        scores = [nt(keys[h, pl.ds(start + b * BLK, BLK), :], q) for b in range(tiles)]
        scores = merge_edges(mask, scores)
        peak = functools.reduce(jnp.maximum, scores)
        peak = jnp.max(peak, axis=0, keepdims=True)
        weights = spread_edges(mask, [jnp.exp(s - peak).astype(jnp.bfloat16) for s in scores])
        total = sum(
            nn(values_t[h, :, pl.ds(pl.multiple_of(start + b * BLK, BLK), BLK)], w) for b, w in enumerate(weights)
        )
        sub = lax.broadcasted_iota(jnp.int32, total.shape, 0)
        total = jnp.where(sub == HD + 1, peak, total).T
        norm = total[:, HD : HD + 1]
        out_ref[0, :, h * HD : (h + 1) * HD] = (total[:, :HD] / norm).astype(out_ref.dtype)
        lse = total[:, HD + 1 : HD + 2] + jnp.log(norm)
        hi, mid, low = split3(-lse)
        q2 = q.astype(jnp.float32)
        q2 = jnp.where(lane == lse_lane, hi, q2)
        q2 = jnp.where(lane == lse_lane + 1, mid, q2)
        q2 = jnp.where(lane == lse_lane + 2, low, q2)
        q2_ref[0, h] = q2.astype(jnp.bfloat16)


def plain_attend(qkv, halo, augk, augq, heads):
    seqs, rows, cols = qkv.shape
    ext = augk.shape[1]
    return pl.pallas_call(
        functools.partial(plain_attend_kernel, heads),
        grid=(seqs, rows // BLK),
        in_specs=[
            pl.BlockSpec((1, rows, cols), lambda s, i: (s, 0, 0)),
            pl.BlockSpec((1, WINDOW, heads * 2 * HD), lambda s, i: (s, 0, 0)),
            pl.BlockSpec((1, ext, HD), lambda s, i: (s, 0, 0)),
            pl.BlockSpec((1, BLK, HD), lambda s, i: (s, i, 0)),
        ],
        out_specs=[
            pl.BlockSpec((1, BLK, heads * HD), lambda s, i: (s, i, 0)),
            pl.BlockSpec((1, heads, BLK, 2 * HD), lambda s, i: (s, 0, i, 0)),
        ],
        out_shape=[
            jax.ShapeDtypeStruct((seqs, rows, heads * HD), jnp.bfloat16),
            jax.ShapeDtypeStruct((seqs, heads, rows, 2 * HD), jnp.bfloat16),
        ],
        scratch_shapes=[
            pltpu.VMEM((heads, ext, 2 * HD), jnp.bfloat16),
            pltpu.VMEM((heads, ext, 2 * HD), jnp.bfloat16),
            pltpu.VMEM((heads, 2 * HD, ext), jnp.bfloat16),
        ],
        compiler_params=pltpu.CompilerParams(vmem_limit_bytes=48 * 2**20),
        name="plain_attend",
    )(qkv, halo, augk, augq)


def plain_attend_back_kernel(
    heads, qkv_ref, halo_ref, augk_ref, q2_ref, out_ref, grad_ref, dq_ref, dkv_ref, dhalo_ref,
    keys, values, keys_t, dkeys, dvalues,
):
    step = pl.program_id(1)
    nkeys = keys.shape[1]

    @pl.when(step == 0)
    def _():
        plain_fill_keys(heads, qkv_ref, halo_ref, augk_ref, keys, values)
        for h in range(heads):
            for b in range(nkeys // BLK):
                keys_t[h, :, b * BLK : (b + 1) * BLK] = keys[h, b * BLK : (b + 1) * BLK, :].T
        dkeys[...] = jnp.zeros_like(dkeys)
        dvalues[...] = jnp.zeros_like(dvalues)

    mask = edge_mask()
    tiles = WINDOW // BLK + 1
    start = pl.multiple_of(step * BLK, BLK)
    lane = lax.broadcasted_iota(jnp.int32, (BLK, 2 * HD), 1)
    for h in range(heads):
        q = q2_ref[0, h]
        g = grad_ref[0, :, h * HD : (h + 1) * HD]
        g32 = g.astype(jnp.float32)
        centre = jnp.sum(g32 * out_ref[0, :, h * HD : (h + 1) * HD].astype(jnp.float32), axis=1, keepdims=True)
        hi, mid, low = split3(-centre)
        g2 = jnp.concatenate([g32, jnp.zeros((BLK, HD), jnp.float32)], axis=1)
        g2 = jnp.where(lane == HD, hi, g2)
        g2 = jnp.where(lane == HD + 1, mid, g2)
        g2 = jnp.where(lane == HD + 2, low, g2).astype(jnp.bfloat16)
        spans = [pl.ds(pl.multiple_of(start + b * BLK, BLK), BLK) for b in range(tiles)]
        scores = merge_edges(mask, [nt(keys[h, s, :], q) for s in spans])
        wgrads = merge_edges(mask, [nt(values[h, s, :], g2) for s in spans])
        weights = [jnp.exp(s) for s in scores]
        sgrads = spread_edges(mask, [(w * d).astype(jnp.bfloat16) for w, d in zip(weights, wgrads)])
        weights = spread_edges(mask, [w.astype(jnp.bfloat16) for w in weights])
        for s, w, d in zip(spans, weights, sgrads):
            dvalues[h, s, :] += nn(w, g2)
            dkeys[h, s, :] += nn(d, q)
        dq = sum(nn(keys_t[h, :, s], d) for s, d in zip(spans, sgrads))
        dq_ref[0, :, h * HD : (h + 1) * HD] = (dq.T[:, :HD] * 0.125).astype(dq_ref.dtype)

    @pl.when(step == pl.num_programs(1) - 1)
    def _():
        for h in range(heads):
            c = h * 2 * HD
            dhalo_ref[0, :, c : c + 2 * HD] = jnp.concatenate(
                [dkeys[h, :WINDOW, :HD], dvalues[h, :WINDOW, :HD]], axis=1
            ).astype(dhalo_ref.dtype)
            dkv_ref[0, :, c : c + 2 * HD] = jnp.concatenate(
                [dkeys[h, WINDOW:, :HD], dvalues[h, WINDOW:, :HD]], axis=1
            ).astype(dkv_ref.dtype)


def plain_attend_back(qkv, halo, augk, q2, out, grad, heads):
    seqs, rows, cols = qkv.shape
    ext = augk.shape[1]
    return pl.pallas_call(
        functools.partial(plain_attend_back_kernel, heads),
        grid=(seqs, rows // BLK),
        in_specs=[
            pl.BlockSpec((1, rows, cols), lambda s, i: (s, 0, 0)),
            pl.BlockSpec((1, WINDOW, heads * 2 * HD), lambda s, i: (s, 0, 0)),
            pl.BlockSpec((1, ext, HD), lambda s, i: (s, 0, 0)),
            pl.BlockSpec((1, heads, BLK, 2 * HD), lambda s, i: (s, 0, i, 0)),
            pl.BlockSpec((1, BLK, heads * HD), lambda s, i: (s, i, 0)),
            pl.BlockSpec((1, BLK, heads * HD), lambda s, i: (s, i, 0)),
        ],
        out_specs=[
            pl.BlockSpec((1, BLK, heads * HD), lambda s, i: (s, i, 0)),
            pl.BlockSpec((1, rows, heads * 2 * HD), lambda s, i: (s, 0, 0)),
            pl.BlockSpec((1, WINDOW, heads * 2 * HD), lambda s, i: (s, 0, 0)),
        ],
        out_shape=[
            jax.ShapeDtypeStruct((seqs, rows, heads * HD), jnp.bfloat16),
            jax.ShapeDtypeStruct((seqs, rows, heads * 2 * HD), jnp.float32),
            jax.ShapeDtypeStruct((seqs, WINDOW, heads * 2 * HD), jnp.bfloat16),
        ],
        scratch_shapes=[
            pltpu.VMEM((heads, ext, 2 * HD), jnp.bfloat16),
            pltpu.VMEM((heads, ext, 2 * HD), jnp.bfloat16),
            pltpu.VMEM((heads, 2 * HD, ext), jnp.bfloat16),
            pltpu.VMEM((heads, ext, 2 * HD), jnp.float32),
            pltpu.VMEM((heads, ext, 2 * HD), jnp.float32),
        ],
        compiler_params=pltpu.CompilerParams(vmem_limit_bytes=56 * 2**20),
        name="plain_attend_back",
    )(qkv, halo, augk, q2, out, grad)


def from_behind(block, axis, distance):
    devices = range(lax.axis_size(axis))
    route = [(i - distance, i) for i in devices if i - distance in devices]
    return lax.ppermute(block, axis, route)


def pack_columns(array, heads):
    parts = array.reshape(array.shape[:-1] + (heads, 3 * HD))
    lead = array.shape[:-1]
    return jnp.concatenate(
        [parts[..., HD:].reshape(lead + (-1,)), parts[..., :HD].reshape(lead + (-1,))], axis=-1
    )


def unpack_columns(array, heads):
    lead = array.shape[:-1]
    pairs = array[..., : heads * 2 * HD].reshape(lead + (heads, 2 * HD))
    queries = array[..., heads * 2 * HD :].reshape(lead + (heads, HD))
    return jnp.concatenate([queries, pairs], axis=-1).reshape(lead + (-1,))


def dot(subscripts, a, b):
    return jnp.einsum(subscripts, a, b, preferred_element_type=jnp.float32)


def general_body(
    inputs, cotangent, segment_ids, norm1_gain, norm1_bias, qkv_weight, qv_bias, out_weight, out_bias,
    norm2_gain, norm2_bias, fc_weight, fc_bias, proj_weight, proj_bias,
):
    group = lax.axis_size("fsdp")
    seqs, local_rows, width = inputs.shape
    part_rows = local_rows * group
    heads = qkv_weight.shape[1] // (3 * HD)
    docs = segment_ids.shape[1] // (2 * WINDOW)
    seq_index = lax.axis_index("seq")
    shard = norm1_gain.shape[0]

    small = jnp.concatenate([norm1_gain, norm1_bias, out_bias, norm2_gain, norm2_bias, proj_bias, fc_bias])
    small = lax.all_gather(small, "fsdp")
    gain1, offset1, out_off, gain2, offset2, proj_off = (
        small[:, i * shard : (i + 1) * shard].reshape(-1).astype(jnp.float32) for i in range(6)
    )
    fc_off = small[:, 6 * shard :].reshape(-1).astype(jnp.float32)
    out_all = lax.all_gather(out_weight, "fsdp", axis=0, tiled=True)
    fc_all = lax.all_gather(fc_weight, "fsdp")
    proj_all = lax.all_gather(proj_weight, "fsdp")

    padded_ids = jnp.concatenate([jnp.full((seqs, WINDOW), -1, jnp.int32), segment_ids], axis=1)
    segment_ext = lax.dynamic_slice_in_dim(padded_ids, seq_index * part_rows, WINDOW + part_rows, 1)
    augk, augq = mask_features(segment_ext, docs)

    x = inputs.astype(jnp.float32)
    z1, rate1 = standardize(x)
    normed1 = (z1 * gain1 + offset1).astype(jnp.bfloat16)
    normed1 = lax.all_gather(normed1, "fsdp", axis=1, tiled=True)
    packed_weight = pack_columns(qkv_weight, heads)
    head_bias = qv_bias.astype(jnp.float32)
    head_bias = jnp.concatenate(
        [head_bias[:, :HD], jnp.zeros((heads, HD), jnp.float32), head_bias[:, HD:]], axis=1
    ).reshape(-1)
    packed_bias = pack_columns(head_bias, heads)
    qkv = (dot("sre,ef->srf", normed1, packed_weight) + packed_bias).astype(jnp.bfloat16)
    halo = from_behind(qkv[:, part_rows - WINDOW :, : heads * 2 * HD], "seq", 1)
    head_out, q2 = plain_attend(qkv, halo, augk, augq, heads)
    merged = lax.all_to_all(head_out, "fsdp", split_axis=1, concat_axis=2, tiled=True)
    resid = x + dot("sre,ef->srf", merged, out_all) + out_off
    z2, rate2 = standardize(resid)
    normed2 = (z2 * gain2 + offset2).astype(jnp.bfloat16)
    fc_offset = fc_off.reshape(group, -1)
    hidden = dot("sre,gef->gsrf", normed2, fc_all) + fc_offset[:, None, None]
    active, gelu_back = jax.vjp(lambda v: jax.nn.gelu(v, approximate=True), hidden)
    active = active.astype(jnp.bfloat16)
    layer_output = (resid + dot("gsrf,gfd->srd", active, proj_all) + proj_off).astype(jnp.bfloat16)

    cot32 = cotangent.astype(jnp.float32)
    proj_bias_part = jnp.sum(cot32, axis=(0, 1))
    proj_weight_part = dot("gsrf,srd->gfd", active, cotangent)
    g_hidden = gelu_back(dot("srd,gfd->gsrf", cotangent, proj_all))[0].astype(jnp.bfloat16)
    fc_bias_part = jnp.sum(g_hidden, axis=(1, 2), dtype=jnp.float32).reshape(-1)
    fc_weight_part = dot("sre,gsrf->gef", normed2, g_hidden)
    g_norm2 = dot("gsrf,gef->sre", g_hidden, fc_all)
    gain2_part = jnp.sum(g_norm2 * z2, axis=(0, 1))
    offset2_part = jnp.sum(g_norm2, axis=(0, 1))
    g_resid = cot32 + norm_grad(g_norm2 * gain2, z2, rate2)
    g_attn = g_resid.astype(jnp.bfloat16)
    out_bias_part = jnp.sum(g_attn, axis=(0, 1), dtype=jnp.float32)
    out_weight_part = dot("sre,srd->ed", merged, g_attn)
    g_merged = dot("srd,ed->sre", g_attn, out_all).astype(jnp.bfloat16)
    g_heads = lax.all_to_all(g_merged, "fsdp", split_axis=2, concat_axis=1, tiled=True)

    low = jnp.bfloat16
    fc_grad = lax.psum_scatter(fc_weight_part.astype(low), "fsdp")
    proj_grad = lax.psum_scatter(proj_weight_part.astype(low), "fsdp")
    out_grad = lax.psum_scatter(out_weight_part.astype(low), "fsdp", scatter_dimension=0, tiled=True)
    fc_grad, proj_grad, out_grad = lax.psum((fc_grad, proj_grad, out_grad), "seq")

    dq, dkv, dhalo = plain_attend_back(qkv, halo, augk, q2, head_out, g_heads, heads)
    edge = from_behind(dhalo, "seq", -1)
    edge = jnp.pad(edge.astype(jnp.float32), ((0, 0), (part_rows - WINDOW, 0), (0, 0)))
    g_qkv = jnp.concatenate([(dkv + edge).astype(jnp.bfloat16), dq], axis=-1)
    qkv_grad = dot("sre,srf->ef", normed1, g_qkv)
    qkv_colsum = jnp.sum(g_qkv, axis=(0, 1), dtype=jnp.float32)
    g_norm1 = dot("srf,ef->sre", g_qkv, packed_weight).astype(jnp.bfloat16)
    g_norm1 = lax.psum_scatter(g_norm1, "fsdp", scatter_dimension=1, tiled=True).astype(jnp.float32)
    gain1_part = jnp.sum(g_norm1 * z1, axis=(0, 1))
    offset1_part = jnp.sum(g_norm1, axis=(0, 1))
    input_grad = (g_resid + norm_grad(g_norm1 * gain1, z1, rate1)).astype(jnp.bfloat16)

    qkv_grad = lax.psum(qkv_grad.astype(low), "seq").astype(jnp.float32)
    qkv_grad = unpack_columns(qkv_grad, heads)
    col = unpack_columns(qkv_colsum, heads).reshape(heads, 3 * HD)
    col = lax.psum(jnp.concatenate([col[:, :HD], col[:, 2 * HD :]], axis=1), "seq")
    vectors = jnp.concatenate(
        [
            v.reshape(group, -1)
            for v in (gain1_part, offset1_part, out_bias_part, gain2_part, offset2_part, proj_bias_part, fc_bias_part)
        ],
        axis=1,
    )
    vectors = lax.psum_scatter(vectors, "fsdp")
    vectors = lax.psum(vectors, "seq")
    parts = [vectors[i * shard : (i + 1) * shard] for i in range(6)] + [vectors[6 * shard :]]
    f32 = jnp.float32
    return (
        layer_output, input_grad, parts[0], parts[1], qkv_grad, col, out_grad.astype(f32), parts[2], parts[3],
        parts[4], fc_grad.astype(f32), parts[6], proj_grad.astype(f32), parts[5],
    )


def cube_body(
    inputs, cotangent, segment_ids, norm1_gain, norm1_bias, qkv_weight, qv_bias, out_weight, out_bias,
    norm2_gain, norm2_bias, fc_weight, fc_bias, proj_weight, proj_bias,
):
    group = lax.axis_size("fsdp")
    seqs, local_rows, width = inputs.shape
    part_rows = local_rows * group
    heads = qkv_weight.shape[1] // (3 * HD)
    docs = segment_ids.shape[1] // (2 * WINDOW)
    seq_index = lax.axis_index("seq")
    shard = norm1_gain.shape[0]
    f32, low = jnp.float32, jnp.bfloat16

    smalls = [norm1_gain, norm1_bias, out_bias, norm2_gain, norm2_bias, proj_bias, fc_bias]
    smalls = [v.reshape(-1, shard) for v in smalls]
    padded_ids = jnp.concatenate([jnp.full((seqs, WINDOW), -1, jnp.int32), segment_ids], axis=1)
    segment_ext = lax.dynamic_slice_in_dim(padded_ids, seq_index * part_rows, WINDOW + part_rows, 1)
    ids = segment_ext[..., None]
    x = inputs.reshape(seqs * local_rows, width)
    cot = cotangent.reshape(seqs * local_rows, width)
    all_small, z1, qkv = gather_project(x, smalls, qkv_weight, qv_bias, group)
    head_out, q2, halo, merged, out_all, fc_near, proj_near = attend(
        qkv, ids, docs, out_weight, fc_weight, proj_weight, heads, group
    )
    layer_output, g_resid, g_heads, kept, side, out_kept, gvec, gfcb = feed_forward(
        x, cot, merged.reshape(x.shape), out_all.reshape(width, width), fc_near, proj_near, fc_weight, proj_weight, all_small
    )
    g_qkv, sums = attend_back(qkv, halo, ids, docs, q2, head_out, g_heads, kept, side, heads, group)
    input_grad, fc_grad, proj_grad, out_grad, qkv_grad, vecs = finish(
        g_qkv, pack_columns(qkv_weight, heads).T, x, g_resid, all_small, sums, out_kept, gvec, gfcb, z1
    )
    return (
        layer_output.reshape(inputs.shape), input_grad.reshape(inputs.shape), vecs[0], vecs[1], qkv_grad.astype(f32),
        vecs[10 : 10 + heads], out_grad.astype(f32), vecs[2], vecs[3], vecs[4], fc_grad.astype(f32), vecs[6:10].reshape(-1),
        proj_grad.astype(f32), vecs[5],
    )


def solution(mesh):
    tokens = P(None, ("seq", "fsdp"), None)
    rows, cols, vec = P("fsdp", None), P(None, "fsdp"), P("fsdp")
    return jax.shard_map(
        cube_body if mesh.shape["fsdp"] == 8 and mesh.shape["seq"] == 4 else general_body,
        mesh=mesh,
        in_specs=(tokens, tokens, P(), vec, vec, cols, rows, rows, vec, vec, vec, cols, vec, rows, vec),
        out_specs=(tokens, tokens, vec, vec, cols, rows, rows, vec, vec, vec, cols, vec, rows, vec),
        check_vma=False,
    )
```

```python
import functools
import math

import jax
import jax.numpy as jnp
from jax import lax
from jax.experimental import pallas as pl
from jax.experimental.pallas import tpu as pltpu
from jax.sharding import PartitionSpec as P


def standardize(values):
    centre = values - jnp.mean(values, axis=-1, keepdims=True)
    spread = jnp.mean(centre * centre, axis=-1, keepdims=True)
    rate = lax.rsqrt(spread + norm_eps)
    return centre * rate, rate


def norm_grad(direction, z, rate):
    mean_d = jnp.mean(direction, axis=-1, keepdims=True)
    mean_dz = jnp.mean(direction * z, axis=-1, keepdims=True)
    return rate * (direction - mean_d - z * mean_dz)


norm_eps = 1e-05

HD = 64
WINDOW = 1024
BLK = 256
PENALTY = 1e30


def nt(a, b):
    return lax.dot_general(a, b, (((1,), (1,)), ((), ())), preferred_element_type=jnp.float32)


def nn(a, b):
    return lax.dot_general(a, b, (((1,), (0,)), ((), ())), preferred_element_type=jnp.float32)


def tn(a, b):
    return lax.dot_general(a, b, (((0,), (0,)), ((), ())), preferred_element_type=jnp.float32)


def split3(v):
    hi = v.astype(jnp.bfloat16).astype(jnp.float32)
    rest = v - hi
    mid = rest.astype(jnp.bfloat16).astype(jnp.float32)
    return hi, mid, rest - mid


def merge_edges(mask, tiles):
    return [jnp.where(mask, tiles[0], tiles[-1])] + tiles[1:-1]


def spread_edges(mask, tiles):
    zero = jnp.zeros_like(tiles[0])
    return [jnp.where(mask, tiles[0], zero)] + tiles[1:] + [jnp.where(mask, zero, tiles[0])]


def edge_mask():
    rows = lax.broadcasted_iota(jnp.int32, (BLK, BLK), 0)
    cols = lax.broadcasted_iota(jnp.int32, (BLK, BLK), 1)
    return rows > cols


def xor(a, b, size):
    total, bit = 0, 1
    while bit < size:
        total = total + bit * lax.rem(lax.div(a, bit) + lax.div(b, bit), 2)
        bit *= 2
    return total


MESH = pl.DeviceIdType.MESH
SLOT_AT = (3, 2, 5, 4, 1, 0, 7, 6)
STEP_OF = tuple(SLOT_AT.index(r) for r in range(8))
NEAR = 6


def enter(peers):
    barrier = pltpu.get_barrier_semaphore()
    for peer in peers:
        pl.semaphore_signal(barrier, inc=1, device_id={"fsdp": peer}, device_id_type=MESH)
    pl.semaphore_wait(barrier, len(peers))


def attend_kernel(
    heads, group, docs, qkv_hbm, row_ref, out_w, fc_w, proj_w,
    out_ref, q2_ref, halo_ref, merged_ref, out_all, fc_all, proj_all, ids_out,
    qkv_ref, ids_ref, in_sems, keys, values, values_t, sent, behind, own_sems, send_sems, recv_sems, halo_sems, w_own, w_send, w_recv,
):
    step = pl.program_id(0)
    last = pl.num_programs(0) - 1
    me = lax.axis_index("fsdp")
    line = lax.axis_index("seq")
    line_end = lax.axis_size("seq") - 1
    at = [xor(me, k, group) for k in range(group)]
    seqs, rows = qkv_ref.shape[0], qkv_ref.shape[1]
    half = group // 2
    seq = lax.rem(lax.div(step, half), 2)
    lower = lax.div(step, group)
    place = (1 - lower) * half + lax.rem(step + me, half)
    width = heads * 2 * HD
    low = jnp.bfloat16

    def halo_copy():
        return pltpu.make_async_remote_copy(
            src_ref=qkv_hbm.at[:, pl.ds(rows - WINDOW, WINDOW), pl.ds(0, width)],
            dst_ref=behind, send_sem=halo_sems.at[0], recv_sem=halo_sems.at[1],
            device_id={"seq": lax.rem(line + 1, line_end + 1)}, device_id_type=MESH,
        )

    weights = ((out_w, out_all, False), (fc_w, fc_all, True), (proj_w, proj_all, True))

    def slot(a, r):
        return weights[a][1].at[STEP_OF[r] if weights[a][2] else r]

    def w_copy(a, r, second=False):
        to = at[1] if r % 2 else at[r]
        src = weights[a][0] if r in (1, 2, 4) else slot(a, r - 1) if r % 2 else None
        dst, sem = slot(a, r), r
        if r == 6:
            size = weights[a][0].shape[0] // 2
            part = pl.ds(size if second else 0, size)
            src = slot(a, 4 if second else 2).at[part]
            to = at[2] if second else at[4]
            dst, sem = dst.at[part], 0 if second else 6
        return pltpu.make_async_remote_copy(
            src_ref=src, dst_ref=dst, send_sem=w_send.at[a, sem], recv_sem=w_recv.at[a, sem],
            device_id={"fsdp": to}, device_id_type=MESH,
        )

    def w_keep(a):
        return pltpu.make_async_copy(weights[a][0], slot(a, 0), w_own.at[a])

    even = lax.rem(line, 2)
    partner = line + 1 - 2 * even
    p_size = proj_w.shape[0] // 2
    p_part = pl.ds(pl.multiple_of(even * p_size, p_size), p_size)

    def p_near(r):
        return pltpu.make_async_remote_copy(
            src_ref=proj_w.at[p_part], dst_ref=slot(2, r).at[p_part], send_sem=w_send.at[2, r],
            recv_sem=w_recv.at[2, r], device_id={"fsdp": at[r]}, device_id_type=MESH,
        )

    def p_line(r):
        sem = 5 + r // 2
        return pltpu.make_async_remote_copy(
            src_ref=slot(2, r).at[p_part], dst_ref=slot(2, r).at[p_part], send_sem=w_send.at[2, sem],
            recv_sem=w_recv.at[2, sem], device_id={"seq": partner}, device_id_type=MESH,
        )

    def forward(a):
        w_copy(a, 2).wait_recv()
        w_copy(a, 3).start()
        w_copy(a, 4).wait_recv()
        w_copy(a, 5).start()
        if not weights[a][2]:
            w_copy(a, 6).start()
            w_copy(a, 6, True).start()

    halo_keep = pltpu.make_async_copy(behind, halo_ref, in_sems.at[2])
    ids_keep = pltpu.make_async_copy(ids_ref, ids_out, in_sems.at[1])

    @pl.when(step == 0)
    def _():
        load = pltpu.make_async_copy(qkv_hbm, qkv_ref, in_sems.at[0])
        load.start()
        barrier = pltpu.get_barrier_semaphore()
        for peer in at[1:]:
            pl.semaphore_signal(barrier, inc=1, device_id={"fsdp": peer}, device_id_type=MESH)

        pl.semaphore_signal(
            barrier, inc=1, device_id={"seq": lax.rem(line + line_end, line_end + 1)}, device_id_type=MESH
        )
        pl.semaphore_signal(barrier, inc=1, device_id={"seq": partner}, device_id_type=MESH)
        pl.semaphore_wait(barrier, group + 1)

        @pl.when(line < line_end)
        def _():
            halo_copy().start()

        for r in (2, 4, 1):
            w_copy(0, r).start()
        for r in (2, 4):
            p_near(r).start()
        w_copy(2, 1).start()
        w_keep(0).start()
        for s in range(seqs):
            for i in range(row_ref.shape[2] // BLK):
                span = slice(i * BLK, (i + 1) * BLK)
                row = jnp.broadcast_to(row_ref[s, :, span].astype(jnp.float32), (128, BLK))
                ids_ref[s, span, :] = row.T[:, 0:1].astype(jnp.int32)
        ids_keep.start()
        load.wait()
        for s in range(seqs):
            fill_keys(s, heads, qkv_ref, ids_ref, docs, WINDOW, keys, values, values_t, None)

    @pl.when(step == group)
    def _():
        @pl.when(line > 0)
        def _():
            halo_copy().wait_recv()

        @pl.when(line == 0)
        def _():
            behind[...] = jnp.zeros_like(behind)

        halo_keep.start()
        for s in range(seqs):
            fill_keys(s, heads, behind, ids_ref, docs, 0, keys, values, values_t, None)

    mask = edge_mask()
    tiles = WINDOW // BLK + 1
    start = pl.multiple_of(place * BLK, BLK)
    lane = lax.broadcasted_iota(jnp.int32, (BLK, 2 * HD), 1)
    lse_lane = 2 * HD - 3
    slot_k = xor(me, place, group)
    spans = [pl.ds(pl.multiple_of(start + b * BLK, BLK), BLK) for b in range(tiles)]
    q_marks = query_marks(ids_ref[seq, pl.ds(start + WINDOW, BLK), :], docs)
    for h in range(heads):
        sh = seq * heads + h
        qc = heads * 2 * HD + h * HD
        q = jnp.concatenate([qkv_ref[seq, pl.ds(start, BLK), qc : qc + HD] * 0.125, q_marks], axis=1)
        scores = merge_edges(mask, [nt(keys[sh, s, :], q) for s in spans])
        peak = functools.reduce(jnp.maximum, scores)
        peak = jnp.max(peak, axis=0, keepdims=True)
        weights_ = spread_edges(mask, [jnp.exp(s - peak).astype(low) for s in scores])
        total = sum(nn(values_t[sh, :, s], w) for s, w in zip(spans, weights_))
        sub = lax.broadcasted_iota(jnp.int32, total.shape, 0)
        total = jnp.where(sub == HD + 1, peak, total).T
        norm = total[:, HD : HD + 1]
        part = (total[:, :HD] / norm).astype(low)
        out_ref[0, :, h * HD : (h + 1) * HD] = part
        sent[step, :, h * HD : (h + 1) * HD] = part
        lse = total[:, HD + 1 : HD + 2] + jnp.log(norm)
        hi, mid, lo = split3(-lse)
        q2 = q.astype(jnp.float32)
        q2 = jnp.where(lane == lse_lane, hi, q2)
        q2 = jnp.where(lane == lse_lane + 1, mid, q2)
        q2 = jnp.where(lane == lse_lane + 2, lo, q2)
        q2_ref[0, h] = q2.astype(low)

    span = sent.shape[2]

    def landing(s, k):
        return merged_ref.at[s, :, pl.ds(pl.multiple_of(k * span, span), span)]

    def own(s):
        return pltpu.make_async_copy(sent.at[step], landing(s, 0), own_sems.at[s])

    def away(s, k, to):
        return pltpu.make_async_remote_copy(
            src_ref=sent.at[step], dst_ref=landing(s, k), send_sem=send_sems.at[s, k], recv_sem=recv_sems.at[s, k],
            device_id={"fsdp": to}, device_id_type=MESH,
        )

    @pl.when(place == me)
    def _():
        own(seq).start()

    @pl.when(place != me)
    def _():
        away(seq, slot_k, place).start()

    @pl.when(step == 3)
    def _():
        forward(0)
        for r in (2, 4, 1):
            w_copy(1, r).start()

    @pl.when(step == 6)
    def _():
        for r in (2, 4):
            p_near(r).wait_recv()
            p_line(r).start()

    @pl.when(step == 10)
    def _():
        w_copy(0, 6).wait_recv()
        w_copy(0, 6, True).wait_recv()
        w_copy(0, 7).start()

    @pl.when(step == last)
    def _():
        forward(1)
        for r in (2, 4):
            p_line(r).wait_recv()
            w_copy(2, r + 1).start()
        for s in range(seqs):
            own(s).wait()
            for k in range(1, group):
                away(s, k, at[k]).wait()
        halo_keep.wait()
        ids_keep.wait()
        w_keep(0).wait()
        for a in range(2):
            for r in (1, 2, 3, 4, 5):
                w_copy(a, r).wait_send()
            for r in (1, 3, 5):
                w_copy(a, r).wait_recv()
        for r in (2, 4):
            p_near(r).wait_send()
            p_line(r).wait_send()
        for r in (1, 3, 5):
            w_copy(2, r).wait()
        w_copy(0, 6).wait_send()
        w_copy(0, 6, True).wait_send()
        w_copy(0, 7).wait()

        @pl.when(line < line_end)
        def _():
            halo_copy().wait_send()


def key_marks(ids, docs):
    lane = lax.broadcasted_iota(jnp.int32, (ids.shape[0], HD), 1)
    ids = jnp.broadcast_to(ids, lane.shape)
    hidden = (lane == ids) | ((lane == docs) & (ids < 0))
    return jnp.where(hidden, -1.0, jnp.where(lane >= HD - 3, 1.0, 0.0)).astype(jnp.bfloat16)


def query_marks(ids, docs):
    lane = lax.broadcasted_iota(jnp.int32, (ids.shape[0], HD), 1)
    ids = jnp.broadcast_to(ids, lane.shape)
    return jnp.where((lane <= docs) & (lane != ids), PENALTY, 0.0).astype(jnp.bfloat16)


def fill_keys(s, heads, source, ids_ref, docs, base, keys, values, values_t, keys_t):
    size = BLK
    ones = jnp.ones((size, HD), jnp.bfloat16)
    for i in range(source.shape[1] // size):
        span = slice(base + i * size, base + (i + 1) * size)
        marks = key_marks(ids_ref[s, span, :], docs)
        for h in range(heads):
            c = h * 2 * HD
            pair = source[s, i * size : (i + 1) * size, c : c + 2 * HD]
            k = jnp.concatenate([pair[:, :HD], marks], axis=1)
            v = jnp.concatenate([pair[:, HD:], ones], axis=1)
            keys[s * heads + h, span, :] = k
            values[s * heads + h, span, :] = v
            if values_t is not None:
                values_t[s * heads + h, :, span] = v.T
            if keys_t is not None:
                keys_t[s * heads + h, :, span] = k.T


def attend(qkv, ids_row, docs, out_w, fc_w, proj_w, heads, group):
    seqs, rows, cols = qkv.shape
    ext = ids_row.shape[2]
    assert rows // BLK == group
    low = jnp.bfloat16
    vmem = pl.BlockSpec(memory_space=pltpu.VMEM)
    hbm = pl.BlockSpec(memory_space=pl.ANY)
    every = seqs * heads
    half = group // 2
    seq_of = lambda i: lax.rem(lax.div(i, half), 2)
    place_of = lambda i: (1 - lax.div(i, group)) * half + lax.rem(i + lax.axis_index("fsdp"), half)
    return pl.pallas_call(
        functools.partial(attend_kernel, heads, group, docs),
        grid=(seqs * rows // BLK,),
        in_specs=[hbm, vmem] + [hbm] * 3,
        out_specs=[
            pl.BlockSpec((1, BLK, heads * HD), lambda i: (seq_of(i), place_of(i), 0)),
            pl.BlockSpec((1, heads, BLK, 2 * HD), lambda i: (seq_of(i), 0, place_of(i), 0)),
        ]
        + [hbm] * 6,
        out_shape=[
            jax.ShapeDtypeStruct((seqs, rows, heads * HD), low),
            jax.ShapeDtypeStruct((seqs, heads, rows, 2 * HD), low),
            jax.ShapeDtypeStruct((seqs, WINDOW, heads * 2 * HD), low),
            jax.ShapeDtypeStruct((seqs, BLK, group * heads * HD), low),
        ]
        + [jax.ShapeDtypeStruct((n,) + w.shape, low) for n, w in ((group, out_w), (NEAR - 1, fc_w), (NEAR - 1, proj_w))]
        + [jax.ShapeDtypeStruct((seqs, ext, 1), jnp.int32)],
        scratch_shapes=[
            pltpu.VMEM(qkv.shape, low),
            pltpu.VMEM((seqs, ext, 1), jnp.int32),
            pltpu.SemaphoreType.DMA((3,)),
            pltpu.VMEM((every, ext, 2 * HD), low),
            pltpu.VMEM((every, ext, 2 * HD), low),
            pltpu.VMEM((every, 2 * HD, ext), low),
            pltpu.VMEM((seqs * rows // BLK, BLK, heads * HD), low),
            pltpu.VMEM((seqs, WINDOW, heads * 2 * HD), low),
            pltpu.SemaphoreType.DMA((seqs,)),
            pltpu.SemaphoreType.DMA((seqs, group)),
            pltpu.SemaphoreType.DMA((seqs, group)),
            pltpu.SemaphoreType.DMA((2,)),
            pltpu.SemaphoreType.DMA((1,)),
            pltpu.SemaphoreType.DMA((3, group)),
            pltpu.SemaphoreType.DMA((3, group)),
        ],
        compiler_params=pltpu.CompilerParams(vmem_limit_bytes=56 * 2**20, collective_id=1, has_side_effects=True),
        name="attend",
    )(qkv, ids_row, out_w, fc_w, proj_w)


def mask_features(segment_ext, docs):
    low = jnp.bfloat16
    lane = lax.broadcasted_iota(jnp.int32, segment_ext.shape + (HD,), 2)
    ids = segment_ext[..., None]
    hidden = (lane == ids) | ((lane == docs) & (ids < 0))
    keys = jnp.where(hidden, -1.0, jnp.where(lane >= HD - 3, 1.0, 0.0)).astype(low)
    queries = jnp.where((lane <= docs) & (lane != ids), PENALTY, 0.0).astype(low)
    return keys, queries[:, WINDOW:]


def gather_project_kernel(
    x_ref, *rest,
):
    parts, rest = rest[:7], rest[7:]
    project_kernel(x_ref, parts, *rest)


def project_kernel(
    x_ref, parts, w_ref, b_ref, all_small_ref, pieces_out, qkv_out,
    qkv_ref, give_sems, z1, pieces, smalls, small_ref, small_send, small_recv, send_sems, recv_sems, out_sems,
):
    group = all_small_ref.shape[0]
    me = lax.axis_index("fsdp")
    at = [xor(me, k, group) for k in range(group)]
    rows = x_ref.shape[0] // 2
    f32, low = jnp.float32, jnp.bfloat16
    enter(at[1:])

    def small_copy(k):
        return pltpu.make_async_remote_copy(
            src_ref=small_ref, dst_ref=smalls.at[me], send_sem=small_send.at[k], recv_sem=small_recv.at[k],
            device_id={"fsdp": at[k]}, device_id_type=MESH,
        )

    row = 0
    small_ref[...] = jnp.zeros_like(small_ref)
    for part in parts:
        small_ref[row : row + part.shape[0], :] = part[...]
        row += part.shape[0]
    for k in range(1, group):
        small_copy(k).start()
    smalls[me] = small_ref[...]

    def chunk(p, s):
        return pieces.at[p, s]

    def move(r, s):
        if r % 2:
            piece, to = at[r - 1], at[1]
        elif r == 6:
            piece, to = (at[2], at[4]) if s == 0 else (at[4], at[2])
        else:
            piece, to = me, at[r]
        return pltpu.make_async_remote_copy(
            src_ref=chunk(piece, s), dst_ref=chunk(piece, s), send_sem=send_sems.at[r, s], recv_sem=recv_sems.at[r, s],
            device_id={"fsdp": to}, device_id_type=MESH,
        )

    def keep(k, s):
        return pltpu.make_async_copy(chunk(at[k], s), pieces_out.at[s, pl.ds(pl.multiple_of(at[k] * rows, rows), rows)], out_sems.at[k, s])

    def give(k, s):
        span = pl.ds(pl.multiple_of(at[k] * rows, rows), rows)
        return pltpu.make_async_copy(qkv_ref.at[s, span], qkv_out.at[s, span], give_sems.at[k, s])

    def project(k, s):
        keep(k, s).start()
        start = pl.multiple_of(at[k] * rows, rows)
        made = (nn(pieces[at[k], s], w_ref[...]) + bias).astype(low)
        head = [made[:, h * 3 * HD : (h + 1) * 3 * HD] for h in range(heads)]
        made = jnp.concatenate([h[:, HD:] for h in head] + [h[:, :HD] for h in head], axis=1)
        qkv_ref[s, pl.ds(start, rows), :] = made
        give(k, s).start()

    z1[...] = standardize(x_ref[:rows, :].astype(f32))[0]
    for k in range(1, group):
        small_copy(k).wait()
    gain = jnp.concatenate([smalls[f, 0:1, :] for f in range(group)], axis=1).astype(f32)
    offset = jnp.concatenate([smalls[f, 1:2, :] for f in range(group)], axis=1).astype(f32)
    for s in range(2):
        if s == 1:
            z1[...] = standardize(x_ref[rows:, :].astype(f32))[0]
        pieces[me, s] = (z1[...] * gain + offset).astype(low)
        move(2, s).start()
        move(4, s).start()
        move(1, s).start()
    all_small_ref[...] = smalls[...]
    heads = b_ref.shape[0]
    none = jnp.zeros((1, HD), f32)
    bias = [p for h in range(heads) for p in (b_ref[h : h + 1, :HD].astype(f32), none, b_ref[h : h + 1, HD:].astype(f32))]
    bias = jnp.concatenate(bias, axis=1)
    for s in range(2):
        project(0, s)
    for s in range(2):
        move(1, s).wait_recv()
        project(1, s)
    for s in range(2):
        move(2, s).wait_recv()
        if s == 0:
            move(6, 0).start()
        move(3, s).start()
        move(4, s).wait_recv()
        if s == 1:
            move(6, 1).start()
        move(5, s).start()
        project(2, s)
        project(4, s)
    for s in range(2):
        move(3, s).wait_recv()
        project(3, s)
        move(5, s).wait_recv()
        project(5, s)
    for s in range(2):
        move(6, s).wait_recv()
        move(7, s).start()
        project(6, s)
    for s in range(2):
        move(7, s).wait_recv()
        project(7, s)
    for s in range(2):
        for r in range(1, group):
            move(r, s).wait_send()
        for k in range(group):
            keep(k, s).wait()
            give(k, s).wait()


def gather_project(x, smalls, weight, bias, group):
    rows, width = x.shape
    cols = weight.shape[1]
    half = rows // 2
    span = smalls[0].shape[1]
    vmem = pl.BlockSpec(memory_space=pltpu.VMEM)
    low = jnp.bfloat16
    return pl.pallas_call(
        gather_project_kernel,
        in_specs=[vmem] * 10,
        out_specs=[vmem, pl.BlockSpec(memory_space=pl.ANY), pl.BlockSpec(memory_space=pl.ANY)],
        out_shape=[
            jax.ShapeDtypeStruct((group, 16, span), low),
            jax.ShapeDtypeStruct((2, group * half, width), low),
            jax.ShapeDtypeStruct((2, group * half, cols), low),
        ],
        scratch_shapes=[
            pltpu.VMEM((2, group * half, cols), low),
            pltpu.SemaphoreType.DMA((group, 2)),
            pltpu.VMEM((half, width), jnp.float32),
            pltpu.VMEM((group, 2, half, width), low),
            pltpu.VMEM((group, 16, span), low),
            pltpu.VMEM((16, span), low),
            pltpu.SemaphoreType.DMA((group,)),
            pltpu.SemaphoreType.DMA((group,)),
            pltpu.SemaphoreType.DMA((group, 2)),
            pltpu.SemaphoreType.DMA((group, 2)),
            pltpu.SemaphoreType.DMA((group, 2)),
        ],
        compiler_params=pltpu.CompilerParams(
            vmem_limit_bytes=60 * 2**20, collective_id=2, has_side_effects=True
        ),
        name="gather_project",
    )(x, *smalls, weight, bias)


def gelu_both(v):
    c = math.sqrt(2.0 / math.pi)
    square = v * v
    t = jnp.tanh(v * (c + (c * 0.044715) * square))
    half = 0.5 * (1.0 + t)
    slope = half + (0.5 * v) * (1.0 - t * t) * (c + (3.0 * 0.044715 * c) * square)
    return v * half, slope


def column_sums(array):
    return jnp.sum(array, axis=0, keepdims=True)


def feed_forward_kernel(
    group, x_hbm, cot_hbm, merged_hbm, out_hbm, fc_near, proj_near, fc_own, proj_own, small_ref,
    layer_ref, gres_ref, gheads_ref, keep_ref, side_ref, gout_ref, gvec_ref, gfcb_ref,
    x_ref, cot_ref, merged_ref, out_ref, in_sems, resid, z2, rate, vec_ref, normed, total, gnormed, fc_w, proj_w, given, taken, gmerged, gout_given, gout_taken,
    load_sems, far_send, far_recv, pair_send, pair_recv, side_send, side_recv, keep_sems, head_send, head_recv,
    own_sem, gout_sems,
):
    step = pl.program_id(0)
    last = group - 1
    me = lax.axis_index("fsdp")
    at = [xor(me, k, group) for k in range(group)]
    rows = x_hbm.shape[0]
    block = rows // 2
    f32, low = jnp.float32, jnp.bfloat16
    span = merged_ref.shape[1] // group

    def load(a, i):
        near, here = ((fc_near, fc_w), (proj_near, proj_w))[a]
        return pltpu.make_async_copy(near.at[i], here.at[lax.rem(i, 2)], load_sems.at[a, lax.rem(i, 2)])

    def load_own(a):
        i = (NEAR - 1) % 2
        return pltpu.make_async_copy((fc_own, proj_own)[a], (fc_w, proj_w)[a].at[i], load_sems.at[a, i])

    def far_copy(a, way):
        near, here = ((fc_near, fc_w), (proj_near, proj_w))[a]
        size = near.shape[1] // 2
        if way == 2:
            src, dst, to = here.at[3], here.at[2], at[1]
        else:
            part = pl.ds(way * size, size)
            src, dst = near.at[STEP_OF[(2, 4)[way]], part], here.at[3, part]
            to = at[(4, 2)[way]]
        return pltpu.make_async_remote_copy(
            src_ref=src, dst_ref=dst, send_sem=far_send.at[a, way], recv_sem=far_recv.at[a, way],
            device_id={"fsdp": to}, device_id_type=MESH,
        )

    def pair_copy(j):
        return pltpu.make_async_remote_copy(
            src_ref=given.at[lax.rem(j, 2)], dst_ref=taken.at[j], send_sem=pair_send.at[j], recv_sem=pair_recv.at[j],
            device_id={"fsdp": at[1]}, device_id_type=MESH,
        )

    def side_copy(a):
        return pltpu.make_async_remote_copy(
            src_ref=taken.at[a, a], dst_ref=side_ref.at[a], send_sem=side_send.at[a], recv_sem=side_recv.at[a],
            device_id={"fsdp": at[(2, 4)[a]]}, device_id_type=MESH,
        )

    def keep_copy(j):
        return pltpu.make_async_copy(taken.at[j], keep_ref.at[j], keep_sems.at[j])

    def head_copy(k):
        src = gmerged.at[:, :, pl.ds(k * span, span)]
        dst = gheads_ref.at[:, pl.ds(pl.multiple_of(me * block, block), block), :]
        if k == 0:
            return pltpu.make_async_copy(src, dst, own_sem)
        return pltpu.make_async_remote_copy(
            src_ref=src, dst_ref=dst, send_sem=head_send.at[k], recv_sem=head_recv.at[k],
            device_id={"fsdp": at[k]}, device_id_type=MESH,
        )

    def gout_copy():
        return pltpu.make_async_remote_copy(
            src_ref=gout_given, dst_ref=gout_taken, send_sem=gout_sems.at[0], recv_sem=gout_sems.at[1],
            device_id={"fsdp": at[1]}, device_id_type=MESH,
        )

    @pl.when(step == 0)
    def _():
        brought = [
            pltpu.make_async_copy(src, dst, in_sems.at[i])
            for i, (src, dst) in enumerate(
                ((merged_hbm, merged_ref), (out_hbm, out_ref), (x_hbm, x_ref), (cot_hbm, cot_ref))
            )
        ]
        for copy in brought:
            copy.start()
        enter(at[1:])
        for a in range(2):
            load(a, 0).start()
        for a in range(2):
            far_copy(a, 0).start()
            far_copy(a, 1).start()
        for copy in brought:
            copy.wait()
        for i in range(4):
            vec_ref[i : i + 1, :] = jnp.concatenate(
                [small_ref[f, 2 + i : 3 + i, :] for f in range(group)], axis=1
            ).astype(f32)
        acc = x_ref[...].astype(f32) + vec_ref[0:1, :] + nn(merged_ref[...], out_ref[...])
        resid[...] = acc
        z, r = standardize(acc)
        z2[...] = z
        rate[...] = jnp.broadcast_to(r, rate.shape)
        normed[...] = (z * vec_ref[1:2, :] + vec_ref[2:3, :]).astype(low)
        total[...] = jnp.zeros_like(total)
        gnormed[...] = jnp.zeros_like(gnormed)

    j = lax.div(step, 2)
    odd = lax.rem(step, 2)

    @pl.when(step < NEAR - 1)
    def _():
        for a in range(2):
            load(a, step).wait()

    @pl.when(step == NEAR - 1)
    def _():
        for a in range(2):
            load_own(a).wait()

    @pl.when(step + 1 < NEAR - 1)
    def _():
        for a in range(2):
            load(a, step + 1).start()

    @pl.when(step + 1 == NEAR - 1)
    def _():
        for a in range(2):
            load_own(a).start()

    @pl.when(step == NEAR)
    def _():
        for a in range(2):
            far_copy(a, 2).wait_recv()

    @pl.when((odd == 0) & (j >= 2))
    def _():
        pair_copy(j - 2).wait_send()

    here = jnp.where(step < NEAR, lax.rem(step, 2), step - NEAR + 2)
    fresh = jnp.where(odd == 0, lax.rem(j, 2), 2)
    owner = sum(jnp.where(step == i, at[SLOT_AT[i]], 0) for i in range(group))
    fc_bias = jnp.concatenate([small_ref[owner, 6 + i : 7 + i, :] for i in range(4)], axis=1).astype(f32)
    hidden = nn(normed[...], fc_w[here]) + fc_bias
    gactive = nt(cot_ref[...], proj_w[here])
    active, slope = gelu_both(hidden)
    active = active.astype(low)
    ghidden = gactive * slope
    gfcb_ref[0] = column_sums(ghidden)
    ghidden = ghidden.astype(low)
    total[...] += nn(active, proj_w[here])
    gnormed[...] += nt(ghidden, fc_w[here])
    @pl.when(step == last)
    def _():
        cot32 = cot_ref[...].astype(f32)
        g, z = gnormed[...], z2[...]
        gres = cot32 + norm_grad(g * vec_ref[1:2, :], z, rate[:, :1])
        gres_ref[...] = gres
        gattn = gres.astype(low)
        back = nt(gattn, out_ref[...]).astype(low)
        for s in range(2):
            gmerged[s] = back[s * block : (s + 1) * block, :]
        for k in (6, 2, 4, 3, 5, 7, 1, 0):
            head_copy(k).start()

    given[fresh, 0] = tn(normed[...], ghidden).astype(low)
    gproj = tn(active, cot_ref[...]).astype(low)
    size, part = gproj.shape[0], fc_w.shape[2]
    for i in range(gproj.shape[1] // part):
        given[fresh, 1, i * size : (i + 1) * size, :] = gproj[:, i * part : (i + 1) * part]

    @pl.when(odd == 0)
    def _():
        pair_copy(j).start()

    @pl.when(odd == 1)
    def _():
        pair_copy(j).wait_recv()

        def add(i, _):
            part = pl.ds(pl.multiple_of(lax.rem(i, 8) * 128, 128), 128)
            a = lax.div(i, 8)
            taken[j, a, part, :] = (taken[j, a, part, :].astype(f32) + given[2, a, part, :].astype(f32)).astype(low)
            return 0

        lax.fori_loop(0, 16, add, 0)
        keep_copy(j).start()

    for a in range(2):
        @pl.when(step == 1 + 2 * a)
        def _(a=a):
            side_copy(a).start()

    @pl.when(step == 3)
    def _():
        for a in range(2):
            far_copy(a, 0).wait_recv()
            far_copy(a, 1).wait_recv()
            far_copy(a, 2).start()

    @pl.when(step == last)
    def _():
        gattn = gres_ref[...].astype(low)
        g, z = gnormed[...], z2[...]
        gout = tn(merged_ref[...], gattn)
        for k in range(1, group, 2):
            gout_given[k // 2] = gout[k * span : (k + 1) * span, :].astype(low)
        gout_copy().start()
        layer_ref[...] = (resid[...] + total[...] + vec_ref[3:4, :]).astype(low)
        gvec_ref[0:1, :] = column_sums(gattn.astype(f32))
        gvec_ref[1:2, :] = column_sums(g * z)
        gvec_ref[2:3, :] = column_sums(g)
        gvec_ref[3:4, :] = column_sums(cot_ref[...].astype(f32))
        gout_copy().wait_recv()
        for k in range(0, group, 2):
            mine = gout[k * span : (k + 1) * span, :].astype(low).astype(f32)
            gout_ref[k // 2] = (mine + gout_taken[k // 2].astype(f32)).astype(low)
        for k in range(group):
            head_copy(k).wait()
        gout_copy().wait_send()
        for a in range(2):
            for way in range(3):
                far_copy(a, way).wait_send()
        pair_copy(2).wait_send()
        pair_copy(3).wait_send()
        side_copy(0).wait()
        side_copy(1).wait()
        for i in range(group // 2):
            keep_copy(i).wait()


def feed_forward(x, cot, merged, out_all, fc_near, proj_near, fc_own, proj_own, small):
    rows, width = x.shape
    group, part = small.shape[0], fc_near.shape[2]
    span = width // group
    f32, low = jnp.float32, jnp.bfloat16
    vmem = pl.BlockSpec(memory_space=pltpu.VMEM)
    hbm = pl.BlockSpec(memory_space=pl.ANY)
    return pl.pallas_call(
        functools.partial(feed_forward_kernel, group),
        grid=(group,),
        in_specs=[
            hbm, hbm, hbm, hbm,
            hbm, hbm, hbm, hbm,
            vmem,
        ],
        out_specs=[
            vmem, vmem, hbm,
            hbm, hbm, vmem, vmem,
            pl.BlockSpec((1, 1, part), lambda i: (i, 0, 0)),
        ],
        out_shape=[
            jax.ShapeDtypeStruct((rows, width), low),
            jax.ShapeDtypeStruct((rows, width), f32),
            jax.ShapeDtypeStruct((2, group * rows // 2, span), low),
            jax.ShapeDtypeStruct((group // 2, 2, width, part), low),
            jax.ShapeDtypeStruct((2, width, part), low),
            jax.ShapeDtypeStruct((group // 2, span, width), low),
            jax.ShapeDtypeStruct((8, width), f32),
            jax.ShapeDtypeStruct((group, 1, part), f32),
        ],
        scratch_shapes=[
            pltpu.VMEM((rows, width), low),
            pltpu.VMEM((rows, width), low),
            pltpu.VMEM((rows, width), low),
            pltpu.VMEM((width, width), low),
            pltpu.SemaphoreType.DMA((4,)),
            pltpu.VMEM((rows, width), f32),
            pltpu.VMEM((rows, width), f32),
            pltpu.VMEM((rows, 128), f32),
            pltpu.VMEM((8, width), f32),
            pltpu.VMEM((rows, width), low),
            pltpu.VMEM((rows, width), f32),
            pltpu.VMEM((rows, width), f32),
            pltpu.VMEM((4, width, part), low),
            pltpu.VMEM((4, part, width), low),
            pltpu.VMEM((3, 2, width, part), low),
            pltpu.VMEM((group // 2, 2, width, part), low),
            pltpu.VMEM((2, rows // 2, width), low),
            pltpu.VMEM((group // 2, span, width), low),
            pltpu.VMEM((group // 2, span, width), low),
            pltpu.SemaphoreType.DMA((2, 2)),
            pltpu.SemaphoreType.DMA((2, 3)),
            pltpu.SemaphoreType.DMA((2, 3)),
            pltpu.SemaphoreType.DMA((group // 2,)),
            pltpu.SemaphoreType.DMA((group // 2,)),
            pltpu.SemaphoreType.DMA((2,)),
            pltpu.SemaphoreType.DMA((2,)),
            pltpu.SemaphoreType.DMA((group // 2,)),
            pltpu.SemaphoreType.DMA((group,)),
            pltpu.SemaphoreType.DMA((group,)),
            pltpu.SemaphoreType.DMA,
            pltpu.SemaphoreType.DMA((2,)),
        ],
        compiler_params=pltpu.CompilerParams(vmem_limit_bytes=62 * 2**20, collective_id=3, has_side_effects=True),
        name="feed_forward",
    )(x, cot, merged, out_all, fc_near, proj_near, fc_own, proj_own, small)


def attend_back_kernel(
    heads, group, docs, qkv_hbm, halo_hbm, ids_hbm, q2_ref, out_ref, grad_ref, kept, side,
    gqkv_ref, sums_ref,
    qkv_ref, halo_ref, ids_ref, in_sems, keys, values, keys_t, dkeys, dvalues, edge, ahead, mid, near, far, mine, met,
    edge_sems, load_sems, near_send, near_recv, far_send, far_recv,
):
    step = pl.program_id(0)
    last = pl.num_programs(0) - 1
    me = lax.axis_index("fsdp")
    line = lax.axis_index("seq")
    line_end = lax.axis_size("seq") - 1
    at = [xor(me, k, group) for k in range(group)]
    seqs, rows = qkv_hbm.shape[0], qkv_hbm.shape[1]
    half = group // 2
    seq = lax.rem(lax.div(step, half), 2)
    place = lax.div(step, group) * half + lax.rem(step, half)
    f32, low = jnp.float32, jnp.bfloat16
    pieces = 2
    size = mid.shape[1] // pieces

    def edge_copy(s):
        return pltpu.make_async_remote_copy(
            src_ref=edge.at[s], dst_ref=ahead.at[s], send_sem=edge_sems.at[0, s], recv_sem=edge_sems.at[1, s],
            device_id={"seq": lax.rem(line + line_end, line_end + 1)}, device_id_type=MESH,
        )

    first, second = (at[2], at[4]), (at[4], at[2])

    def near_copy(a, h):
        part = pl.ds(h * size, size)
        return pltpu.make_async_remote_copy(
            src_ref=kept.at[3, a, part], dst_ref=near.at[a, part], send_sem=near_send.at[a, h],
            recv_sem=near_recv.at[a, h], device_id={"fsdp": first[a]}, device_id_type=MESH,
        )

    def far_copy(a, h):
        part = pl.ds(h * size, size)
        return pltpu.make_async_remote_copy(
            src_ref=mid.at[a, part], dst_ref=far.at[a, part], send_sem=far_send.at[a, h],
            recv_sem=far_recv.at[a, h], device_id={"fsdp": second[a]}, device_id_type=MESH,
        )

    def loads():
        for a in range(2):
            yield pltpu.make_async_copy(kept.at[1 - a, a], mid.at[a], load_sems.at[0, a])
            yield pltpu.make_async_copy(kept.at[2, a], mine.at[a], load_sems.at[1, a])
            yield pltpu.make_async_copy(side.at[a], met.at[a], load_sems.at[2, a])

    def plus(u, *more):
        total = u.astype(f32)
        for v in more:
            total += v.astype(f32)
        return total.astype(low)

    @pl.when(step == 0)
    def _():
        brought = [
            pltpu.make_async_copy(src, dst, in_sems.at[i])
            for i, (src, dst) in enumerate(((qkv_hbm, qkv_ref), (halo_hbm, halo_ref), (ids_hbm, ids_ref)))
        ]
        for load in brought:
            load.start()
        dkeys[...] = jnp.zeros_like(dkeys)
        dvalues[...] = jnp.zeros_like(dvalues)
        barrier = pltpu.get_barrier_semaphore()
        for peer in (at[2], at[4]):
            pl.semaphore_signal(barrier, inc=1, device_id={"fsdp": peer}, device_id_type=MESH)
        pl.semaphore_signal(
            barrier, inc=1, device_id={"seq": lax.rem(line + 1, line_end + 1)}, device_id_type=MESH
        )
        pl.semaphore_wait(barrier, 3)
        for h in range(pieces):
            for a in range(2):
                near_copy(a, h).start()
        for load in loads():
            load.start()
        for load in brought:
            load.wait()
        for s in range(seqs):
            fill_keys(s, heads, halo_ref, ids_ref, docs, 0, keys, values, None, keys_t)
            fill_keys(s, heads, qkv_ref, ids_ref, docs, WINDOW, keys, values, None, keys_t)

    for s in range(seqs):
        @pl.when((step == (s + 1) * half) & (line > 0))
        def _(s=s):
            for h in range(heads):
                c = h * 2 * HD
                edge[s, :, c : c + 2 * HD] = jnp.concatenate(
                    [dkeys[s * heads + h, :WINDOW, :HD], dvalues[s * heads + h, :WINDOW, :HD]], axis=1
                ).astype(low)
            edge_copy(s).start()

    mask = edge_mask()
    tiles = WINDOW // BLK + 1
    start = pl.multiple_of(place * BLK, BLK)
    lane = lax.broadcasted_iota(jnp.int32, (BLK, 2 * HD), 1)
    spans = [pl.ds(pl.multiple_of(start + b * BLK, BLK), BLK) for b in range(tiles)]
    for h in range(heads):
        sh = seq * heads + h
        q = q2_ref[0, h]
        g32 = grad_ref[0, :, h * HD : (h + 1) * HD].astype(f32)
        centre = jnp.sum(g32 * out_ref[0, :, h * HD : (h + 1) * HD].astype(f32), axis=1, keepdims=True)
        hi, md, lo = split3(-centre)
        g2 = jnp.concatenate([g32, jnp.zeros((BLK, HD), f32)], axis=1)
        g2 = jnp.where(lane == HD, hi, g2)
        g2 = jnp.where(lane == HD + 1, md, g2)
        g2 = jnp.where(lane == HD + 2, lo, g2).astype(low)
        scores = merge_edges(mask, [nt(keys[sh, s, :], q) for s in spans])
        wgrads = merge_edges(mask, [nt(values[sh, s, :], g2) for s in spans])
        weights = [jnp.exp(s) for s in scores]
        sgrads = spread_edges(mask, [(w * d).astype(low) for w, d in zip(weights, wgrads)])
        weights = spread_edges(mask, [w.astype(low) for w in weights])
        for s, w, d in zip(spans, weights, sgrads):
            dvalues[sh, s, :] += nn(w, g2)
            dkeys[sh, s, :] += nn(d, q)
        dq = sum(nn(keys_t[sh, :, s], d) for s, d in zip(spans, sgrads))
        qc = heads * 2 * HD + h * HD
        gqkv_ref[seq, pl.ds(start, BLK), qc : qc + HD] = (dq.T[:, :HD] * 0.125).astype(low)

    def relay(h):
        part = slice(h * size, (h + 1) * size)
        for a in range(2):
            near_copy(a, h).wait_recv()
            mid[a, part] = plus(mid[a, part], near[a, part])
            far_copy(a, h).start()

    @pl.when(step == 4)
    def _():
        for load in loads():
            load.wait()
        relay(0)

    @pl.when(step == 8)
    def _():
        relay(1)

    @pl.when(step == last)
    def _():
        def own(s, h, first, count):
            span = slice(WINDOW + first, WINDOW + first + count)
            return jnp.concatenate([dkeys[s * heads + h, span, :HD], dvalues[s * heads + h, span, :HD]], axis=1)

        for s in range(seqs):
            for h in range(heads):
                c = h * 2 * HD
                gqkv_ref[s, : rows - WINDOW, c : c + 2 * HD] = own(s, h, 0, rows - WINDOW).astype(low)

        @pl.when(line < line_end)
        def _():
            for s in range(seqs):
                edge_copy(s).wait_recv()

        @pl.when(line == line_end)
        def _():
            ahead[...] = jnp.zeros_like(ahead)

        for s in range(seqs):
            for h in range(heads):
                c = h * 2 * HD
                gqkv_ref[s, rows - WINDOW :, c : c + 2 * HD] = (
                    own(s, h, rows - WINDOW, WINDOW) + ahead[s, :, c : c + 2 * HD].astype(f32)
                ).astype(low)

        for h in range(pieces):
            part = slice(h * size, (h + 1) * size)
            for a in range(2):
                far_copy(a, h).wait_recv()
                sums_ref[a, part] = plus(mine[a, part], met[a, part], far[a, part])
        for a in range(2):
            for h in range(pieces):
                near_copy(a, h).wait_send()
                far_copy(a, h).wait_send()

        @pl.when(line > 0)
        def _():
            for s in range(seqs):
                edge_copy(s).wait_send()


def attend_back(qkv, halo, ids, docs, q2, out, grad, kept, side, heads, group):
    seqs, rows, cols = qkv.shape
    ext = ids.shape[1]
    half = group // 2
    f32, low = jnp.float32, jnp.bfloat16
    vmem = pl.BlockSpec(memory_space=pltpu.VMEM)
    hbm = pl.BlockSpec(memory_space=pl.ANY)
    every = seqs * heads
    part = kept.shape[2:]
    seq_of = lambda i: lax.rem(lax.div(i, half), 2)
    place_of = lambda i: lax.div(i, group) * half + lax.rem(i, half)
    edge = pltpu.VMEM((seqs, WINDOW, heads * 2 * HD), low)
    pair = pltpu.VMEM((2,) + part, low)
    return pl.pallas_call(
        functools.partial(attend_back_kernel, heads, group, docs),
        grid=(seqs * rows // BLK,),
        in_specs=[
            hbm, hbm, hbm,
            pl.BlockSpec((1, heads, BLK, 2 * HD), lambda i: (seq_of(i), 0, place_of(i), 0)),
            pl.BlockSpec((1, BLK, heads * HD), lambda i: (seq_of(i), place_of(i), 0)),
            pl.BlockSpec((1, BLK, heads * HD), lambda i: (seq_of(i), place_of(i), 0)),
            hbm, hbm,
        ],
        out_specs=[vmem, vmem],
        out_shape=[
            jax.ShapeDtypeStruct((seqs, rows, cols), low),
            jax.ShapeDtypeStruct((2,) + part, low),
        ],
        scratch_shapes=[
            pltpu.VMEM(qkv.shape, low),
            pltpu.VMEM(halo.shape, low),
            pltpu.VMEM(ids.shape, jnp.int32),
            pltpu.SemaphoreType.DMA((3,)),
            pltpu.VMEM((every, ext, 2 * HD), low),
            pltpu.VMEM((every, ext, 2 * HD), low),
            pltpu.VMEM((every, 2 * HD, ext), low),
            pltpu.VMEM((every, ext, 2 * HD), f32),
            pltpu.VMEM((every, ext, 2 * HD), f32),
            edge, edge, pair, pair, pair, pair, pair,
            pltpu.SemaphoreType.DMA((2, seqs)),
            pltpu.SemaphoreType.DMA((3, 2)),
            pltpu.SemaphoreType.DMA((2, 2)),
            pltpu.SemaphoreType.DMA((2, 2)),
            pltpu.SemaphoreType.DMA((2, 2)),
            pltpu.SemaphoreType.DMA((2, 2)),
        ],
        compiler_params=pltpu.CompilerParams(vmem_limit_bytes=62 * 2**20, collective_id=4, has_side_effects=True),
        name="attend_back",
    )(qkv, halo, ids, q2, out, grad, kept, side)


def finish_kernel(
    g_hbm, wt_hbm, x_hbm, gres_hbm, small_ref, sums_hbm, out_hbm, gvec_ref, gfcb_ref, z_hbm,
    input_grad_ref, fc_total_ref, proj_total_ref, out_total_ref, qkv_total_ref, vec_ref,
    g_ref, wt_ref, x_ref, gres_ref, sums_ref, out_kept, in_sems, z_all, odd, odd_in, even, mine, first_in, second_in, mt, rows6, vec_out, vec_in, vec_line,
    acc, acc_out, acc_q, left, left_out, left_q, right, right_out, right_q, total_q, out_near, out_far, out_mid,
    z_sem, odd_send, odd_recv, near_send, near_recv, far_send, far_recv,
    vec_send, vec_recv, vl_send, vl_recv, line_send, line_recv, out_send, out_recv,
):
    group = small_ref.shape[0]
    me = lax.axis_index("fsdp")
    line = lax.axis_index("seq")
    line_size = 4
    at = [xor(me, k, group) for k in range(group)]
    block = x_hbm.shape[0] // 2
    f32, low = jnp.float32, jnp.bfloat16
    width = x_hbm.shape[1]
    span = small_ref.shape[2]
    heads = wt_hbm.shape[0] // (3 * HD)
    outer = (line == 0) | (line == line_size - 1)
    inner = (line > 0) & (line < line_size - 1)

    def remote(src, dst, send, recv, to):
        return pltpu.make_async_remote_copy(
            src_ref=src, dst_ref=dst, send_sem=send, recv_sem=recv, device_id=to, device_id_type=MESH
        )

    brought = [
        pltpu.make_async_copy(src, dst, in_sems.at[i])
        for i, (src, dst) in enumerate(
            (
                (g_hbm, g_ref), (wt_hbm, wt_ref), (sums_hbm, sums_ref), (out_hbm, out_kept), (x_hbm, x_ref),
                (gres_hbm, gres_ref),
            )
        )
    ]
    for copy in brought:
        copy.start()
    barrier = pltpu.get_barrier_semaphore()
    for peer in at[1:]:
        pl.semaphore_signal(barrier, inc=1, device_id={"fsdp": peer}, device_id_type=MESH)
    others = [lax.rem(line + d, line_size) for d in range(1, line_size)]
    for other in others:
        pl.semaphore_signal(barrier, inc=1, device_id={"seq": other}, device_id_type=MESH)
    pl.semaphore_wait(barrier, group - 1 + line_size - 1)

    cut = sums_hbm.shape[1] // 4
    fc_chunks, proj_chunks = [], []
    for i in range(4):
        part = pl.ds(i * cut, cut)
        fc_chunks.append([r.at[0, part] for r in (sums_hbm, acc, left, right)] + [fc_total_ref.at[part], sums_ref.at[0, part]])
        there = proj_total_ref.at[pl.ds(i % 2 * cut, cut), pl.ds(i // 2 * sums_ref.shape[2], sums_ref.shape[2])]
        proj_chunks.append([r.at[1, part] for r in (sums_hbm, acc, left, right)] + [there, sums_ref.at[1, part]])
    cut = acc_q.shape[0] // 3
    qkv_chunks = [
        [r.at[pl.ds(i * cut, cut)] for r in (acc_q, acc_q, left_q, right_q, total_q, acc_q)] for i in range(3)
    ]
    cut = acc_out.shape[0] // 2
    out_chunks = [
        [r.at[pl.ds(i * cut, cut)] for r in (acc_out, acc_out, left_out, right_out, out_total_ref, acc_out)]
        for i in range(2)
    ]
    chunks = fc_chunks + proj_chunks[:2] + qkv_chunks + proj_chunks[2:] + out_chunks
    early = 6

    def inwards(c):
        return remote(
            chunks[c][0], chunks[c][2], line_send.at[0, c], line_recv.at[0, c], {"seq": 1 + lax.div(line, line_size - 1)}
        )

    def across(c):
        return remote(
            chunks[c][1], chunks[c][3], line_send.at[1, c], line_recv.at[1, c], {"seq": line_size - 1 - line}
        )

    def outwards(c):
        return remote(
            chunks[c][4], chunks[c][3], line_send.at[2, c], line_recv.at[2, c],
            {"seq": lax.rem((line + line_size - 1) * (line_size - 1), 2 * (line_size - 1))},
        )

    def begin(cs):
        @pl.when(outer)
        def _():
            for c in cs:
                inwards(c).start()

    def collect(c):
        @pl.when(inner)
        def _():
            inwards(c).wait_recv()
            acc_c, left_c, own = chunks[c][1], chunks[c][2], chunks[c][5]
            acc_c[...] = (own[...].astype(f32) + left_c[...].astype(f32)).astype(low)
            across(c).start()

    def settle(c):
        @pl.when(inner)
        def _():
            across(c).wait_recv()
            chunks[c][4][...] = (chunks[c][1][...].astype(f32) + chunks[c][3][...].astype(f32)).astype(low)
            outwards(c).start()

    def receive(c):
        @pl.when(outer)
        def _():
            outwards(c).wait_recv()
            chunks[c][4][...] = chunks[c][3][...]

    def advance(first, last):
        for c in range(first, last):
            collect(c)
            if c >= 1:
                settle(c - 1)
            if c >= 2:
                receive(c - 2)

    begin(range(early))
    load = pltpu.make_async_copy(z_hbm, z_all, z_sem)
    load.start()

    ways = (at[2], at[4])
    out_cut = out_hbm.shape[1] // 2
    out_first = ((0, 1, 0), (0, 3, 1), (1, 2, 0), (1, 3, 1))

    def out_near_copy(n):
        h, slot, j = out_first[n]
        return pltpu.make_async_remote_copy(
            src_ref=out_hbm.at[slot, pl.ds(h * out_cut, out_cut)], dst_ref=out_near.at[h, j], send_sem=out_send.at[n],
            recv_sem=out_recv.at[n], device_id={"fsdp": ways[h]}, device_id_type=MESH,
        )

    def out_far_copy(h):
        return pltpu.make_async_remote_copy(
            src_ref=out_mid.at[h], dst_ref=out_far.at[h], send_sem=out_send.at[4 + h],
            recv_sem=out_recv.at[4 + h], device_id={"fsdp": ways[1 - h]}, device_id_type=MESH,
        )

    for n in range(4):
        out_near_copy(n).start()

    def product(r, s):
        start = pl.multiple_of(at[r] * block, block)
        return nn(g_ref[s, pl.ds(start, block), :], wt_ref[...])

    def odd_copy(j):
        return remote(odd.at[j], odd_in.at[j], odd_send.at[j], odd_recv.at[j], {"fsdp": at[1]})

    def make_odd(j):
        for s in range(2):
            odd[j, s] = product(2 * j + 1, s).astype(low)
        odd_copy(j).start()

    for copy in brought:
        copy.wait()
    make_odd(3)
    make_odd(1)
    advance(0, 1)
    make_odd(2)
    make_odd(0)

    def near_copy(s, i):
        j = 3 if i == 0 else 1 + s
        return remote(even.at[j, s], first_in.at[s, i], near_send.at[s, i], near_recv.at[s, i], {"fsdp": ways[s]})

    def far_copy(s):
        return remote(even.at[2 - s, s], second_in.at[s], far_send.at[s], far_recv.at[s], {"fsdp": ways[1 - s]})

    def make_even(j):
        odd_copy(j).wait_recv()
        for s in range(2):
            part = product(2 * j, s) + odd_in[j, s].astype(f32)
            if j == 0:
                mine[s] = part
            else:
                even[j, s] = part.astype(low)
                if j == 3:
                    near_copy(s, 0).start()
                elif j == 1 + s:
                    near_copy(s, 1).start()

    make_even(3)
    advance(1, 2)
    make_even(1)
    make_even(2)
    advance(2, 3)
    make_even(0)

    def wide(index):
        return jnp.concatenate([small_ref[f, index : index + 1, :] for f in range(group)], axis=1).astype(f32)

    gain = wide(0)
    load.wait()
    mt[...] = jnp.zeros_like(mt)
    steps = z_all.shape[1] // 512
    ones = jnp.ones((512, 128), low)

    def add_product(i, sums):
        rows = pl.ds(pl.multiple_of(lax.rem(i, steps) * 512, 512), 512)
        g = g_ref[lax.div(i, steps), rows, :]
        mt[...] += tn(g, z_all[lax.div(i, steps), rows, :])
        return sums + tn(g, ones)

    column = lax.fori_loop(0, steps // 2, add_product, jnp.zeros((g_ref.shape[2], 128), f32))
    advance(3, 4)
    for h in range(2):
        part = slice(h * out_cut, (h + 1) * out_cut)
        out_near_copy(2 * h + 1).wait_recv()
        out_mid[h] = (out_kept[2 - h, part].astype(f32) + out_near[h, 1].astype(f32)).astype(low)
        out_far_copy(h).start()
    column = lax.fori_loop(steps // 2, steps, add_product, column)
    for s in range(2):
        near_copy(s, 0).wait_recv()
        even[2 - s, s] = (even[2 - s, s].astype(f32) + first_in[s, 0].astype(f32)).astype(low)
        far_copy(s).start()

    advance(4, 5)
    column = lax.fori_loop(steps, 2 * steps, add_product, column)
    acc_q[...] = mt[...].astype(low)
    begin(range(early, len(chunks) - 2))
    advance(5, 6)

    def vec_copy(k):
        return remote(vec_out.at[k], vec_in.at[k], vec_send.at[k], vec_recv.at[k], {"fsdp": at[k]})

    for h in range(2):
        part = slice(h * out_cut, (h + 1) * out_cut)
        out_near_copy(2 * h).wait_recv()
        out_far_copy(h).wait_recv()
        acc_out[part] = (
            out_kept[0, part].astype(f32) + out_near[h, 0].astype(f32) + out_far[h].astype(f32)
        ).astype(low)
    begin([len(chunks) - 2, len(chunks) - 1])

    def line_copy(d):
        return remote(vec_line.at[line], vec_line.at[line], vl_send.at[d], vl_recv.at[d], {"seq": others[d]})

    advance(6, 7)
    gain_grad = offset_grad = jnp.zeros((1, width), f32)
    for s in range(2):
        near_copy(s, 1).wait_recv()
        far_copy(s).wait_recv()
        rows = slice(s * block, (s + 1) * block)
        e = mine[s] + first_in[s, 1].astype(f32) + second_in[s].astype(f32)
        z, rate = standardize(x_ref[rows, :].astype(f32))
        gain_grad += column_sums(e * z)
        offset_grad += column_sums(e)
        input_grad_ref[rows, :] = (gres_ref[rows, :] + norm_grad(e * gain, z, rate)).astype(low)
    rows6[0:1, :] = gain_grad
    rows6[1:2, :] = offset_grad
    rows6[2:6, :] = gvec_ref[0:4, :]
    row = column.T[0:1, :]
    vec_out[...] = jnp.zeros_like(vec_out)
    for k in range(group):
        vec_out[k, 0:6, :] = rows6[0:6, pl.ds(pl.multiple_of(at[k] * span, span), span)]
        for i in range(4):
            vec_out[k, 6 + i : 7 + i, :] = gfcb_ref[STEP_OF[k], :, i * span : (i + 1) * span]
    for h in range(heads):
        base = heads * 2 * HD + h * HD
        vec_out[0, 10 + h : 11 + h, :] = jnp.concatenate(
            [row[:, base : base + HD], row[:, h * 2 * HD + HD : (h + 1) * 2 * HD]], axis=1
        )

    for k in range(1, group):
        vec_copy(k).start()

    advance(7, 9)
    total = vec_out[0]
    for k in range(1, group):
        vec_copy(k).wait_recv()
        total += vec_in[k]
    vec_line[line] = total

    for d in range(line_size - 1):
        line_copy(d).start()

    advance(9, 11)
    for d in range(line_size - 1):
        line_copy(d).wait_recv()
    vec_ref[...] = vec_line[0] + vec_line[1] + vec_line[2] + vec_line[3]
    advance(11, 13)
    turned = total_q[...].T
    pairs = heads * 2 * HD
    turned = [
        p
        for h in range(heads)
        for p in (turned[:, pairs + h * HD : pairs + (h + 1) * HD], turned[:, h * 2 * HD : (h + 1) * 2 * HD])
    ]
    qkv_total_ref[...] = jnp.concatenate(turned, axis=1)
    settle(12)
    receive(11)
    receive(12)
    for j in range(4):
        odd_copy(j).wait_send()
    for s in range(2):
        near_copy(s, 0).wait_send()
        near_copy(s, 1).wait_send()
        far_copy(s).wait_send()
    for n in range(4):
        out_near_copy(n).wait_send()
    for h in range(2):
        out_far_copy(h).wait_send()
    for k in range(1, group):
        vec_copy(k).wait_send()
    for d in range(line_size - 1):
        line_copy(d).wait_send()

    @pl.when(outer)
    def _():
        for c in range(len(chunks)):
            inwards(c).wait_send()

    @pl.when(inner)
    def _():
        for c in range(len(chunks)):
            across(c).wait_send()
            outwards(c).wait_send()


def finish(g, wt, x, gres, small, sums, out_kept, gvec, gfcb, z_all):
    rows, width = x.shape
    group = small.shape[0]
    half = rows // 2
    span = small.shape[2]
    f32, low = jnp.float32, jnp.bfloat16
    vmem = pl.BlockSpec(memory_space=pltpu.VMEM)
    hbm = pl.BlockSpec(memory_space=pl.ANY)
    dma = pltpu.SemaphoreType.DMA
    out_part = out_kept.shape[1:]
    half_out = (out_part[0] // 2, out_part[1])
    buffers = [pltpu.VMEM(sums.shape, low), pltpu.VMEM(out_part, low), pltpu.VMEM(wt.shape, low)]
    return pl.pallas_call(
        finish_kernel,
        in_specs=[hbm] * 4 + [vmem, hbm, hbm, vmem, vmem, hbm],
        out_specs=[vmem] * 6,
        out_shape=[
            jax.ShapeDtypeStruct((rows, width), low),
            jax.ShapeDtypeStruct(sums.shape[1:], low),
            jax.ShapeDtypeStruct((sums.shape[2], sums.shape[1]), low),
            jax.ShapeDtypeStruct(out_part, low),
            jax.ShapeDtypeStruct(wt.shape[::-1], low),
            jax.ShapeDtypeStruct((16, span), f32),
        ],
        scratch_shapes=[
            pltpu.VMEM(g.shape, low),
            pltpu.VMEM(wt.shape, low),
            pltpu.VMEM(x.shape, low),
            pltpu.VMEM(gres.shape, f32),
            pltpu.VMEM(sums.shape, low),
            pltpu.VMEM(out_kept.shape, low),
            dma((6,)),
            pltpu.VMEM(z_all.shape, low),
            pltpu.VMEM((group // 2, 2, half, width), low),
            pltpu.VMEM((group // 2, 2, half, width), low),
            pltpu.VMEM((group // 2, 2, half, width), low),
            pltpu.VMEM((2, half, width), f32),
            pltpu.VMEM((2, 2, half, width), low),
            pltpu.VMEM((2, half, width), low),
            pltpu.VMEM(wt.shape, f32),
            pltpu.VMEM((8, width), f32),
            pltpu.VMEM((group, 16, span), f32),
            pltpu.VMEM((group, 16, span), f32),
            pltpu.VMEM((4, 16, span), f32),
        ]
        + buffers * 3
        + [pltpu.VMEM(wt.shape, low)]
        + [pltpu.VMEM((2, 2) + half_out, low), pltpu.VMEM((2,) + half_out, low), pltpu.VMEM((2,) + half_out, low)]
        + [dma, dma((4,)), dma((4,)), dma((2, 2)), dma((2, 2)), dma((2,)), dma((2,))]
        + [dma((group,)), dma((group,)), dma((3,)), dma((3,)), dma((3, 13)), dma((3, 13)), dma((6,)), dma((6,))],
        compiler_params=pltpu.CompilerParams(vmem_limit_bytes=62 * 2**20, collective_id=5, has_side_effects=True),
        name="finish",
    )(g, wt, x, gres, small, sums, out_kept, gvec, gfcb, z_all)


def plain_fill_keys(heads, qkv_ref, halo_ref, augk_ref, keys, values):
    halo_rows = halo_ref.shape[1]
    rows = qkv_ref.shape[1]
    ones = jnp.ones((1, HD), jnp.bfloat16)
    for h in range(heads):
        c = h * 2 * HD
        for source, base, size in ((halo_ref, 0, halo_rows), (qkv_ref, halo_rows, rows)):
            pair = source[0, :, c : c + 2 * HD]
            keys[h, base : base + size, :] = jnp.concatenate(
                [pair[:, :HD], augk_ref[0, base : base + size, :]], axis=1
            )
            values[h, base : base + size, :] = jnp.concatenate(
                [pair[:, HD:], jnp.broadcast_to(ones, (size, HD))], axis=1
            )


def plain_attend_kernel(heads, qkv_ref, halo_ref, augk_ref, augq_ref, out_ref, q2_ref, keys, values, values_t):
    step = pl.program_id(1)
    nkeys = keys.shape[1]

    @pl.when(step == 0)
    def _():
        plain_fill_keys(heads, qkv_ref, halo_ref, augk_ref, keys, values)
        for h in range(heads):
            for b in range(nkeys // BLK):
                values_t[h, :, b * BLK : (b + 1) * BLK] = values[h, b * BLK : (b + 1) * BLK, :].T

    mask = edge_mask()
    tiles = WINDOW // BLK + 1
    start = pl.multiple_of(step * BLK, BLK)
    lane = lax.broadcasted_iota(jnp.int32, (BLK, 2 * HD), 1)
    lse_lane = augq_ref.shape[2] + HD - 3
    for h in range(heads):
        qc = heads * 2 * HD + h * HD
        q = jnp.concatenate([qkv_ref[0, pl.ds(start, BLK), qc : qc + HD] * 0.125, augq_ref[0]], axis=1)
        scores = [nt(keys[h, pl.ds(start + b * BLK, BLK), :], q) for b in range(tiles)]
        scores = merge_edges(mask, scores)
        peak = functools.reduce(jnp.maximum, scores)
        peak = jnp.max(peak, axis=0, keepdims=True)
        weights = spread_edges(mask, [jnp.exp(s - peak).astype(jnp.bfloat16) for s in scores])
        total = sum(
            nn(values_t[h, :, pl.ds(pl.multiple_of(start + b * BLK, BLK), BLK)], w) for b, w in enumerate(weights)
        )
        sub = lax.broadcasted_iota(jnp.int32, total.shape, 0)
        total = jnp.where(sub == HD + 1, peak, total).T
        norm = total[:, HD : HD + 1]
        out_ref[0, :, h * HD : (h + 1) * HD] = (total[:, :HD] / norm).astype(out_ref.dtype)
        lse = total[:, HD + 1 : HD + 2] + jnp.log(norm)
        hi, mid, low = split3(-lse)
        q2 = q.astype(jnp.float32)
        q2 = jnp.where(lane == lse_lane, hi, q2)
        q2 = jnp.where(lane == lse_lane + 1, mid, q2)
        q2 = jnp.where(lane == lse_lane + 2, low, q2)
        q2_ref[0, h] = q2.astype(jnp.bfloat16)


def plain_attend(qkv, halo, augk, augq, heads):
    seqs, rows, cols = qkv.shape
    ext = augk.shape[1]
    return pl.pallas_call(
        functools.partial(plain_attend_kernel, heads),
        grid=(seqs, rows // BLK),
        in_specs=[
            pl.BlockSpec((1, rows, cols), lambda s, i: (s, 0, 0)),
            pl.BlockSpec((1, WINDOW, heads * 2 * HD), lambda s, i: (s, 0, 0)),
            pl.BlockSpec((1, ext, HD), lambda s, i: (s, 0, 0)),
            pl.BlockSpec((1, BLK, HD), lambda s, i: (s, i, 0)),
        ],
        out_specs=[
            pl.BlockSpec((1, BLK, heads * HD), lambda s, i: (s, i, 0)),
            pl.BlockSpec((1, heads, BLK, 2 * HD), lambda s, i: (s, 0, i, 0)),
        ],
        out_shape=[
            jax.ShapeDtypeStruct((seqs, rows, heads * HD), jnp.bfloat16),
            jax.ShapeDtypeStruct((seqs, heads, rows, 2 * HD), jnp.bfloat16),
        ],
        scratch_shapes=[
            pltpu.VMEM((heads, ext, 2 * HD), jnp.bfloat16),
            pltpu.VMEM((heads, ext, 2 * HD), jnp.bfloat16),
            pltpu.VMEM((heads, 2 * HD, ext), jnp.bfloat16),
        ],
        compiler_params=pltpu.CompilerParams(vmem_limit_bytes=48 * 2**20),
        name="plain_attend",
    )(qkv, halo, augk, augq)


def plain_attend_back_kernel(
    heads, qkv_ref, halo_ref, augk_ref, q2_ref, out_ref, grad_ref, dq_ref, dkv_ref, dhalo_ref,
    keys, values, keys_t, dkeys, dvalues,
):
    step = pl.program_id(1)
    nkeys = keys.shape[1]

    @pl.when(step == 0)
    def _():
        plain_fill_keys(heads, qkv_ref, halo_ref, augk_ref, keys, values)
        for h in range(heads):
            for b in range(nkeys // BLK):
                keys_t[h, :, b * BLK : (b + 1) * BLK] = keys[h, b * BLK : (b + 1) * BLK, :].T
        dkeys[...] = jnp.zeros_like(dkeys)
        dvalues[...] = jnp.zeros_like(dvalues)

    mask = edge_mask()
    tiles = WINDOW // BLK + 1
    start = pl.multiple_of(step * BLK, BLK)
    lane = lax.broadcasted_iota(jnp.int32, (BLK, 2 * HD), 1)
    for h in range(heads):
        q = q2_ref[0, h]
        g = grad_ref[0, :, h * HD : (h + 1) * HD]
        g32 = g.astype(jnp.float32)
        centre = jnp.sum(g32 * out_ref[0, :, h * HD : (h + 1) * HD].astype(jnp.float32), axis=1, keepdims=True)
        hi, mid, low = split3(-centre)
        g2 = jnp.concatenate([g32, jnp.zeros((BLK, HD), jnp.float32)], axis=1)
        g2 = jnp.where(lane == HD, hi, g2)
        g2 = jnp.where(lane == HD + 1, mid, g2)
        g2 = jnp.where(lane == HD + 2, low, g2).astype(jnp.bfloat16)
        spans = [pl.ds(pl.multiple_of(start + b * BLK, BLK), BLK) for b in range(tiles)]
        scores = merge_edges(mask, [nt(keys[h, s, :], q) for s in spans])
        wgrads = merge_edges(mask, [nt(values[h, s, :], g2) for s in spans])
        weights = [jnp.exp(s) for s in scores]
        sgrads = spread_edges(mask, [(w * d).astype(jnp.bfloat16) for w, d in zip(weights, wgrads)])
        weights = spread_edges(mask, [w.astype(jnp.bfloat16) for w in weights])
        for s, w, d in zip(spans, weights, sgrads):
            dvalues[h, s, :] += nn(w, g2)
            dkeys[h, s, :] += nn(d, q)
        dq = sum(nn(keys_t[h, :, s], d) for s, d in zip(spans, sgrads))
        dq_ref[0, :, h * HD : (h + 1) * HD] = (dq.T[:, :HD] * 0.125).astype(dq_ref.dtype)

    @pl.when(step == pl.num_programs(1) - 1)
    def _():
        for h in range(heads):
            c = h * 2 * HD
            dhalo_ref[0, :, c : c + 2 * HD] = jnp.concatenate(
                [dkeys[h, :WINDOW, :HD], dvalues[h, :WINDOW, :HD]], axis=1
            ).astype(dhalo_ref.dtype)
            dkv_ref[0, :, c : c + 2 * HD] = jnp.concatenate(
                [dkeys[h, WINDOW:, :HD], dvalues[h, WINDOW:, :HD]], axis=1
            ).astype(dkv_ref.dtype)


def plain_attend_back(qkv, halo, augk, q2, out, grad, heads):
    seqs, rows, cols = qkv.shape
    ext = augk.shape[1]
    return pl.pallas_call(
        functools.partial(plain_attend_back_kernel, heads),
        grid=(seqs, rows // BLK),
        in_specs=[
            pl.BlockSpec((1, rows, cols), lambda s, i: (s, 0, 0)),
            pl.BlockSpec((1, WINDOW, heads * 2 * HD), lambda s, i: (s, 0, 0)),
            pl.BlockSpec((1, ext, HD), lambda s, i: (s, 0, 0)),
            pl.BlockSpec((1, heads, BLK, 2 * HD), lambda s, i: (s, 0, i, 0)),
            pl.BlockSpec((1, BLK, heads * HD), lambda s, i: (s, i, 0)),
            pl.BlockSpec((1, BLK, heads * HD), lambda s, i: (s, i, 0)),
        ],
        out_specs=[
            pl.BlockSpec((1, BLK, heads * HD), lambda s, i: (s, i, 0)),
            pl.BlockSpec((1, rows, heads * 2 * HD), lambda s, i: (s, 0, 0)),
            pl.BlockSpec((1, WINDOW, heads * 2 * HD), lambda s, i: (s, 0, 0)),
        ],
        out_shape=[
            jax.ShapeDtypeStruct((seqs, rows, heads * HD), jnp.bfloat16),
            jax.ShapeDtypeStruct((seqs, rows, heads * 2 * HD), jnp.float32),
            jax.ShapeDtypeStruct((seqs, WINDOW, heads * 2 * HD), jnp.bfloat16),
        ],
        scratch_shapes=[
            pltpu.VMEM((heads, ext, 2 * HD), jnp.bfloat16),
            pltpu.VMEM((heads, ext, 2 * HD), jnp.bfloat16),
            pltpu.VMEM((heads, 2 * HD, ext), jnp.bfloat16),
            pltpu.VMEM((heads, ext, 2 * HD), jnp.float32),
            pltpu.VMEM((heads, ext, 2 * HD), jnp.float32),
        ],
        compiler_params=pltpu.CompilerParams(vmem_limit_bytes=56 * 2**20),
        name="plain_attend_back",
    )(qkv, halo, augk, q2, out, grad)


def from_behind(block, axis, distance):
    devices = range(lax.axis_size(axis))
    route = [(i - distance, i) for i in devices if i - distance in devices]
    return lax.ppermute(block, axis, route)


def pack_columns(array, heads):
    parts = array.reshape(array.shape[:-1] + (heads, 3 * HD))
    lead = array.shape[:-1]
    return jnp.concatenate(
        [parts[..., HD:].reshape(lead + (-1,)), parts[..., :HD].reshape(lead + (-1,))], axis=-1
    )


def unpack_columns(array, heads):
    lead = array.shape[:-1]
    pairs = array[..., : heads * 2 * HD].reshape(lead + (heads, 2 * HD))
    queries = array[..., heads * 2 * HD :].reshape(lead + (heads, HD))
    return jnp.concatenate([queries, pairs], axis=-1).reshape(lead + (-1,))


def dot(subscripts, a, b):
    return jnp.einsum(subscripts, a, b, preferred_element_type=jnp.float32)


def general_body(
    inputs, cotangent, segment_ids, norm1_gain, norm1_bias, qkv_weight, qv_bias, out_weight, out_bias,
    norm2_gain, norm2_bias, fc_weight, fc_bias, proj_weight, proj_bias,
):
    group = lax.axis_size("fsdp")
    seqs, local_rows, width = inputs.shape
    part_rows = local_rows * group
    heads = qkv_weight.shape[1] // (3 * HD)
    docs = segment_ids.shape[1] // (2 * WINDOW)
    seq_index = lax.axis_index("seq")
    shard = norm1_gain.shape[0]

    small = jnp.concatenate([norm1_gain, norm1_bias, out_bias, norm2_gain, norm2_bias, proj_bias, fc_bias])
    small = lax.all_gather(small, "fsdp")
    gain1, offset1, out_off, gain2, offset2, proj_off = (
        small[:, i * shard : (i + 1) * shard].reshape(-1).astype(jnp.float32) for i in range(6)
    )
    fc_off = small[:, 6 * shard :].reshape(-1).astype(jnp.float32)
    out_all = lax.all_gather(out_weight, "fsdp", axis=0, tiled=True)
    fc_all = lax.all_gather(fc_weight, "fsdp")
    proj_all = lax.all_gather(proj_weight, "fsdp")

    padded_ids = jnp.concatenate([jnp.full((seqs, WINDOW), -1, jnp.int32), segment_ids], axis=1)
    segment_ext = lax.dynamic_slice_in_dim(padded_ids, seq_index * part_rows, WINDOW + part_rows, 1)
    augk, augq = mask_features(segment_ext, docs)

    x = inputs.astype(jnp.float32)
    z1, rate1 = standardize(x)
    normed1 = (z1 * gain1 + offset1).astype(jnp.bfloat16)
    normed1 = lax.all_gather(normed1, "fsdp", axis=1, tiled=True)
    packed_weight = pack_columns(qkv_weight, heads)
    head_bias = qv_bias.astype(jnp.float32)
    head_bias = jnp.concatenate(
        [head_bias[:, :HD], jnp.zeros((heads, HD), jnp.float32), head_bias[:, HD:]], axis=1
    ).reshape(-1)
    packed_bias = pack_columns(head_bias, heads)
    qkv = (dot("sre,ef->srf", normed1, packed_weight) + packed_bias).astype(jnp.bfloat16)
    halo = from_behind(qkv[:, part_rows - WINDOW :, : heads * 2 * HD], "seq", 1)
    head_out, q2 = plain_attend(qkv, halo, augk, augq, heads)
    merged = lax.all_to_all(head_out, "fsdp", split_axis=1, concat_axis=2, tiled=True)
    resid = x + dot("sre,ef->srf", merged, out_all) + out_off
    z2, rate2 = standardize(resid)
    normed2 = (z2 * gain2 + offset2).astype(jnp.bfloat16)
    fc_offset = fc_off.reshape(group, -1)
    hidden = dot("sre,gef->gsrf", normed2, fc_all) + fc_offset[:, None, None]
    active, gelu_back = jax.vjp(lambda v: jax.nn.gelu(v, approximate=True), hidden)
    active = active.astype(jnp.bfloat16)
    layer_output = (resid + dot("gsrf,gfd->srd", active, proj_all) + proj_off).astype(jnp.bfloat16)

    cot32 = cotangent.astype(jnp.float32)
    proj_bias_part = jnp.sum(cot32, axis=(0, 1))
    proj_weight_part = dot("gsrf,srd->gfd", active, cotangent)
    g_hidden = gelu_back(dot("srd,gfd->gsrf", cotangent, proj_all))[0].astype(jnp.bfloat16)
    fc_bias_part = jnp.sum(g_hidden, axis=(1, 2), dtype=jnp.float32).reshape(-1)
    fc_weight_part = dot("sre,gsrf->gef", normed2, g_hidden)
    g_norm2 = dot("gsrf,gef->sre", g_hidden, fc_all)
    gain2_part = jnp.sum(g_norm2 * z2, axis=(0, 1))
    offset2_part = jnp.sum(g_norm2, axis=(0, 1))
    g_resid = cot32 + norm_grad(g_norm2 * gain2, z2, rate2)
    g_attn = g_resid.astype(jnp.bfloat16)
    out_bias_part = jnp.sum(g_attn, axis=(0, 1), dtype=jnp.float32)
    out_weight_part = dot("sre,srd->ed", merged, g_attn)
    g_merged = dot("srd,ed->sre", g_attn, out_all).astype(jnp.bfloat16)
    g_heads = lax.all_to_all(g_merged, "fsdp", split_axis=2, concat_axis=1, tiled=True)

    low = jnp.bfloat16
    fc_grad = lax.psum_scatter(fc_weight_part.astype(low), "fsdp")
    proj_grad = lax.psum_scatter(proj_weight_part.astype(low), "fsdp")
    out_grad = lax.psum_scatter(out_weight_part.astype(low), "fsdp", scatter_dimension=0, tiled=True)
    fc_grad, proj_grad, out_grad = lax.psum((fc_grad, proj_grad, out_grad), "seq")

    dq, dkv, dhalo = plain_attend_back(qkv, halo, augk, q2, head_out, g_heads, heads)
    edge = from_behind(dhalo, "seq", -1)
    edge = jnp.pad(edge.astype(jnp.float32), ((0, 0), (part_rows - WINDOW, 0), (0, 0)))
    g_qkv = jnp.concatenate([(dkv + edge).astype(jnp.bfloat16), dq], axis=-1)
    qkv_grad = dot("sre,srf->ef", normed1, g_qkv)
    qkv_colsum = jnp.sum(g_qkv, axis=(0, 1), dtype=jnp.float32)
    g_norm1 = dot("srf,ef->sre", g_qkv, packed_weight).astype(jnp.bfloat16)
    g_norm1 = lax.psum_scatter(g_norm1, "fsdp", scatter_dimension=1, tiled=True).astype(jnp.float32)
    gain1_part = jnp.sum(g_norm1 * z1, axis=(0, 1))
    offset1_part = jnp.sum(g_norm1, axis=(0, 1))
    input_grad = (g_resid + norm_grad(g_norm1 * gain1, z1, rate1)).astype(jnp.bfloat16)

    qkv_grad = lax.psum(qkv_grad.astype(low), "seq").astype(jnp.float32)
    qkv_grad = unpack_columns(qkv_grad, heads)
    col = unpack_columns(qkv_colsum, heads).reshape(heads, 3 * HD)
    col = lax.psum(jnp.concatenate([col[:, :HD], col[:, 2 * HD :]], axis=1), "seq")
    vectors = jnp.concatenate(
        [
            v.reshape(group, -1)
            for v in (gain1_part, offset1_part, out_bias_part, gain2_part, offset2_part, proj_bias_part, fc_bias_part)
        ],
        axis=1,
    )
    vectors = lax.psum_scatter(vectors, "fsdp")
    vectors = lax.psum(vectors, "seq")
    parts = [vectors[i * shard : (i + 1) * shard] for i in range(6)] + [vectors[6 * shard :]]
    f32 = jnp.float32
    return (
        layer_output, input_grad, parts[0], parts[1], qkv_grad, col, out_grad.astype(f32), parts[2], parts[3],
        parts[4], fc_grad.astype(f32), parts[6], proj_grad.astype(f32), parts[5],
    )


def cube_body(
    inputs, cotangent, segment_ids, norm1_gain, norm1_bias, qkv_weight, qv_bias, out_weight, out_bias,
    norm2_gain, norm2_bias, fc_weight, fc_bias, proj_weight, proj_bias,
):
    group = lax.axis_size("fsdp")
    seqs, local_rows, width = inputs.shape
    part_rows = local_rows * group
    heads = qkv_weight.shape[1] // (3 * HD)
    docs = segment_ids.shape[1] // (2 * WINDOW)
    seq_index = lax.axis_index("seq")
    shard = norm1_gain.shape[0]
    f32, low = jnp.float32, jnp.bfloat16

    smalls = [norm1_gain, norm1_bias, out_bias, norm2_gain, norm2_bias, proj_bias, fc_bias]
    smalls = [v.reshape(-1, shard) for v in smalls]
    padded_ids = jnp.concatenate([jnp.full((seqs, WINDOW), -1, jnp.int32), segment_ids], axis=1)
    segment_ext = lax.dynamic_slice_in_dim(padded_ids, seq_index * part_rows, WINDOW + part_rows, 1)
    x = inputs.reshape(seqs * local_rows, width)
    cot = cotangent.reshape(seqs * local_rows, width)
    all_small, z1, qkv = gather_project(x, smalls, qkv_weight, qv_bias, group)
    head_out, q2, halo, merged, out_all, fc_near, proj_near, ids = attend(
        qkv, segment_ext[:, None], docs, out_weight, fc_weight, proj_weight, heads, group
    )
    layer_output, g_resid, g_heads, kept, side, out_kept, gvec, gfcb = feed_forward(
        x, cot, merged.reshape(x.shape), out_all.reshape(width, width), fc_near, proj_near, fc_weight, proj_weight, all_small
    )
    g_qkv, sums = attend_back(qkv, halo, ids, docs, q2, head_out, g_heads, kept, side, heads, group)
    input_grad, fc_grad, proj_grad, out_grad, qkv_grad, vecs = finish(
        g_qkv, pack_columns(qkv_weight, heads).T, x, g_resid, all_small, sums, out_kept, gvec, gfcb, z1
    )
    return (
        layer_output.reshape(inputs.shape), input_grad.reshape(inputs.shape), vecs[0], vecs[1], qkv_grad.astype(f32),
        vecs[10 : 10 + heads], out_grad.astype(f32), vecs[2], vecs[3], vecs[4], fc_grad.astype(f32), vecs[6:10].reshape(-1),
        proj_grad.astype(f32), vecs[5],
    )


def solution(mesh):
    tokens = P(None, ("seq", "fsdp"), None)
    rows, cols, vec = P("fsdp", None), P(None, "fsdp"), P("fsdp")
    return jax.shard_map(
        cube_body if mesh.shape["fsdp"] == 8 and mesh.shape["seq"] == 4 else general_body,
        mesh=mesh,
        in_specs=(tokens, tokens, P(), vec, vec, cols, rows, rows, vec, vec, vec, cols, vec, rows, vec),
        out_specs=(tokens, tokens, vec, vec, cols, rows, rows, vec, vec, vec, cols, vec, rows, vec),
        check_vma=False,
    )
```
